32 devices in a mesh: dp: 8 (over z, y), vocab: 4 (over x, core).
Axes of the slice: x: 2, y: 2, z: 4, core: 2. Of those that a mesh axis runs over, the one named last changes fastest.
Arguments:
- token_ids: int32 [8, 1024], P('dp'), may hold values from 0 to 30521
- timesteps: int32 [8], P('dp'), may hold values from 0 to 1999, as said below
- pad_mask: int32 [8, 1024], P('dp'), may hold values from 0 to 1, as said below
- noise_draw: bfloat16 [8, 1024, 128], P('dp', 'vocab'), may hold values from -6 to 6
- owners: int32 [9], replicated, may hold values from 0 to 7, as said below
- emb_table: float32 [30528, 128], P('vocab', 'dp')
- table_first_moment: float32 [30528, 128], P('vocab', 'dp'), may hold values from -0.0068359375 to 0.0068359375
- table_second_moment: float32 [30528, 128], P('vocab', 'dp'), may hold values from 1.2207032e-07 to 4.882813e-07
- mat_slots: float32 [768, 24576], P('vocab', 'dp'), as said below
- slot_first: float32 [768, 24576], P('vocab', 'dp'), as said below
- slot_second: float32 [768, 24576], P('vocab', 'dp'), as said below
- vec_params: float32 [7680], replicated
- vec_first: float32 [7680], P('vocab'), may hold values from -0.01953125 to 0.01953125
- vec_second: float32 [7680], P('vocab'), may hold values from 1.0986328e-06 to 4.394531e-06
Outputs:
- loss_pair: float32 [2], replicated
- emb_norm: float32 [], replicated
- new_table: float32 [30528, 128], P('vocab', 'dp')
- table_first_new: float32 [30528, 128], P('vocab', 'dp')
- table_second_new: float32 [30528, 128], P('vocab', 'dp')
- new_slots: float32 [768, 24576], P('vocab', 'dp')
- slot_first_new: float32 [768, 24576], P('vocab', 'dp')
- slot_second_new: float32 [768, 24576], P('vocab', 'dp')
- new_vecs: float32 [7680], P('vocab')
- vec_first_new: float32 [7680], P('vocab')
- vec_second_new: float32 [7680], P('vocab')
The draws below stay inside these ranges and needn't reach their ends.
Inputs may be any that keep to these rules, and one draw needn't show every extreme that they name: Skewed toward small timesteps; some sequence has timestep 0 and some other 1999. `pad_mask`: each row's ones are a suffix of at least 341 positions; some row has no zero. `owners`: the rows of the matrices that one data index owns, in list order, number at most 3072, and some index owns exactly 3072. `mat_slots`: columns of a slot that no listed matrix covers are zero. `slot_first`: columns of a slot that no listed matrix covers are zero. `slot_second`: columns of a slot that no listed matrix covers are zero; the others are positive.
All inputs are finite; a program needn't handle non-finite values.
Results may differ from the reference program's by a relative error of at most 0.0009.
The reference program's roundings to bfloat16 on the way count: a program that leaves them out, or rounds other values in their place, can miss the bound.
Values may be sent and summed in bfloat16 or wider, within the bound.
A program may use at most 256 MiB of HBM per device.

```python
import math
import jax
import jax.numpy as jnp
import numpy as np
from jax import lax

D = 768
HEADS = 12
HDIM = 64
FF = 3072
EMBED_WIDTH = 128
VOCAB = 30522
TABLE_ROWS = 30528
LAYERS = 1
SEQUENCE_TOKENS = 1024
DIFF = 2000
STEP = 10
SEQUENCE_COUNT = 8
CAP = 3072
ROWS = 9600
VEC = 7680
N_DP = 8


def matrix_rows_drawn():
    return [D, D, D, D, FF, FF] * LAYERS + [EMBED_WIDTH, EMBED_WIDTH, EMBED_WIDTH]


def slot_starts_drawn(owners):
    counts = jnp.array(matrix_rows_drawn(), jnp.int32)
    mat_total = counts.shape[0]
    same_owner = (owners[:, None] == owners[None, :]).astype(jnp.int32)
    earlier_mask = jnp.tril(jnp.ones((mat_total, mat_total), jnp.int32), -1)
    return (owners * CAP + jnp.sum(same_owner * earlier_mask * counts[None, :], 1)).astype(jnp.int32)


def owner_list(key):
    device_order = jax.random.permutation(jax.random.fold_in(key, 101), N_DP)
    pair_coin = jax.random.randint(jax.random.fold_in(key, 102), (), 0, 2)
    owner_parts = []
    for layer_idx in range(LAYERS):
        owner_parts = owner_parts + [device_order[3 * layer_idx]] * 4 + [device_order[3 * layer_idx + 1], device_order[3 * layer_idx + 2]]
    tail_at = 3 * LAYERS
    owner_parts = owner_parts + [device_order[tail_at], device_order[tail_at + pair_coin], device_order[tail_at + 2]]
    return jnp.stack(owner_parts).astype(jnp.int32)


def row_scales():
    per_layer = [D ** (-0.5)] * 3 + [8.0 * D ** (-0.5), D ** (-0.5), FF ** (-0.5)]
    scale_list = per_layer * LAYERS + [EMBED_WIDTH ** (-0.5), EMBED_WIDTH ** (-0.5), D ** (-0.5)]
    return jnp.concatenate([jnp.full((count_rows,), scale_val, jnp.float32) for count_rows, scale_val in zip(matrix_rows_drawn(), scale_list)])


def place_rows(value_entries, owners):
    starts = slot_starts_drawn(owners)
    slots = jnp.zeros((N_DP * CAP, D), jnp.float32)
    cursor = 0
    for mat_idx, count_rows in enumerate(matrix_rows_drawn()):
        slots = lax.dynamic_update_slice_in_dim(slots, value_entries[cursor:cursor + count_rows], starts[mat_idx], 0)
        cursor = cursor + count_rows
    return slots.T


def draw_owners(key, part):
    return owner_list(key)


def draw_timesteps(key, part):
    key = jax.random.fold_in(key, 3)
    samples = jax.random.randint(jax.random.fold_in(key, 1), (3, SEQUENCE_COUNT), 0, DIFF)
    skewed = jnp.min(samples, 0).astype(jnp.int32)
    order = jax.random.permutation(jax.random.fold_in(key, 2), SEQUENCE_COUNT)
    places = jnp.arange(SEQUENCE_COUNT, dtype=jnp.int32)
    skewed = jnp.where(places == order[0], DIFF - 1, skewed)
    skewed = jnp.where(places == order[1], 0, skewed)
    return skewed.astype(jnp.int32)


def draw_pad_mask(key, part):
    key = jax.random.fold_in(key, 5)
    seq_index = jnp.arange(SEQUENCE_COUNT, dtype=jnp.int32)
    spread_den = max(N_DP - 1, 1)
    base_len = SEQUENCE_TOKENS * (spread_den + 2 * seq_index) // (3 * spread_den)
    jitter = jax.random.randint(key, (SEQUENCE_COUNT,), 0, SEQUENCE_TOKENS // 8 + 1)
    lengths = jnp.minimum(base_len + jitter, SEQUENCE_TOKENS)
    places = jnp.arange(SEQUENCE_TOKENS, dtype=jnp.int32)
    return (places[None, :] >= SEQUENCE_TOKENS - lengths[:, None]).astype(jnp.int32)


def draw_emb_table(key, part):
    key = jax.random.fold_in(key, 21)
    row_location = jnp.arange(TABLE_ROWS, dtype=jnp.float32)[:, None] / TABLE_ROWS
    value_entries = jax.random.normal(key, (TABLE_ROWS, EMBED_WIDTH), jnp.float32)
    return value_entries * 0.09 * (1.0 + 2.0 * row_location)


def draw_mat_slots(key, part):
    owners = owner_list(key)
    key = jax.random.fold_in(key, 11)
    value_entries = jax.random.normal(key, (ROWS, D), jnp.float32)
    return place_rows(value_entries * row_scales()[:, None], owners)


def draw_slot_first(key, part):
    owners = owner_list(key)
    key = jax.random.fold_in(key, 12)
    value_entries = jax.random.normal(key, (ROWS, D), jnp.float32)
    return place_rows(value_entries * 0.33 * (SEQUENCE_COUNT * SEQUENCE_TOKENS) ** (-0.5), owners)


def draw_slot_second(key, part):
    owners = owner_list(key)
    key = jax.random.fold_in(key, 13)
    value_entries = jnp.exp(jax.random.uniform(key, (ROWS, D), jnp.float32, math.log(0.009), math.log(0.036))) / (SEQUENCE_COUNT * SEQUENCE_TOKENS)
    return place_rows(value_entries, owners)


def draw_vec_params(key, part):
    key = jax.random.fold_in(key, 31)
    value_entries = jax.random.normal(key, (VEC,), jnp.float32)
    one_layer = jnp.concatenate([jnp.ones((D,), jnp.float32), jnp.zeros((D,), jnp.float32), jnp.ones((D,), jnp.float32), jnp.zeros((D,), jnp.float32), jnp.zeros((FF,), jnp.float32)])
    centers = jnp.concatenate([one_layer] * LAYERS + [jnp.ones((D,), jnp.float32), jnp.zeros((D,), jnp.float32)])
    return centers + 0.2 * value_entries


def plant(values, own_key, low, high):
    spot = [jax.random.randint(jax.random.fold_in(own_key, axis), (), 0, length) for axis, length in enumerate(values.shape)]
    widest = values.shape.index(max(values.shape))
    neighbour = spot[:widest] + [(spot[widest] + 1) % values.shape[widest]] + spot[widest + 1:]
    return values.at[tuple(spot)].set(low).at[tuple(neighbour)].set(high)


def levels(rng, extent, split, low, high):
    factor_of = 1.0
    for dim, parts in split:
        heights = jax.random.uniform(jax.random.fold_in(jax.random.fold_in(rng, 6), dim), (parts,), jnp.float32, low / len(split), high / len(split))
        factor_of = factor_of * jnp.repeat(jnp.exp(heights), extent[dim] // parts).reshape((-1,) + (1,) * (len(extent) - 1 - dim))
    return factor_of


def rank_table(amount, lean):
    loads = [(1 << 20) // math.isqrt(standing ** lean) + 1 for standing in range(1, amount + 1)]
    scale = 1 + sum(loads) // (1 << 30)
    return np.cumsum(np.array([max(1, weight // scale) for weight in loads]))


def skewed_ids(own_key, extent, count, skew):
    listing = rank_table(count, skew)
    lot = jax.random.randint(jax.random.fold_in(own_key, 1), extent, 0, int(listing[count - 1]))
    grade = jnp.searchsorted(jnp.asarray(listing, jnp.int32), lot, side="right")
    return jax.random.permutation(jax.random.fold_in(own_key, 2), count)[grade].astype(jnp.int32)


def centred(rng, dims, deviation, limit, shards=(), kind=jnp.bfloat16):
    drawn = deviation * jax.random.normal(rng, dims, jnp.float32)
    if shards:
        drawn = drawn * levels(rng, dims, shards, -0.22, 0.18)
    return jnp.clip(drawn, -limit, limit).astype(kind)


def setup_inputs(seed: int = 0) -> dict:
    streams_of = jax.random.split(jax.random.key(seed), 15)
    return {
        "token_ids": plant(skewed_ids(streams_of[0], (SEQUENCE_COUNT, SEQUENCE_TOKENS), VOCAB, 2), jax.random.fold_in(streams_of[0], 3), 0, VOCAB - 1).astype(jnp.int32),
        "timesteps": draw_timesteps(jax.random.fold_in(streams_of[14], 71), 0),
        "pad_mask": draw_pad_mask(jax.random.fold_in(streams_of[14], 71), 0),
        "noise_draw": centred(streams_of[3], (SEQUENCE_COUNT, SEQUENCE_TOKENS, EMBED_WIDTH), 1.0, 6.0, ((0, 8), (1, 4))),
        "owners": draw_owners(jax.random.fold_in(streams_of[14], 71), 0),
        "emb_table": draw_emb_table(jax.random.fold_in(streams_of[14], 71), 0),
        "table_first_moment": centred(streams_of[6], (TABLE_ROWS, EMBED_WIDTH), (0.1 / (SEQUENCE_COUNT * SEQUENCE_TOKENS) ** 0.5), 0.0068359375, ((0, 4), (1, 8)), jnp.float32),
        "table_second_moment": jnp.clip(jnp.exp(math.log(4.882812731921149e-07) - 1.3862944 * jax.random.uniform(streams_of[7], (TABLE_ROWS, EMBED_WIDTH), jnp.float32) ** levels(streams_of[7], (TABLE_ROWS, EMBED_WIDTH), ((0, 4), (1, 8)), -0.2, 0.2)), 1.2207031829802872e-07, 4.882812731921149e-07),
        "mat_slots": draw_mat_slots(jax.random.fold_in(streams_of[14], 71), 0),
        "slot_first": draw_slot_first(jax.random.fold_in(streams_of[14], 71), 0),
        "slot_second": draw_slot_second(jax.random.fold_in(streams_of[14], 71), 0),
        "vec_params": draw_vec_params(jax.random.fold_in(streams_of[14], 71), 0),
        "vec_first": centred(streams_of[12], (VEC,), (0.3 / (SEQUENCE_COUNT * SEQUENCE_TOKENS) ** 0.5), 0.01953125, ((0, 4),), jnp.float32),
        "vec_second": jnp.clip(jnp.exp(math.log(4.394531060825102e-06) - 1.3862944 * jax.random.uniform(streams_of[13], (VEC,), jnp.float32) ** levels(streams_of[13], (VEC,), ((0, 4),), -0.2, 0.2)), 1.0986327652062755e-06, 4.394531060825102e-06),
    }


@jax.custom_vjp
def low(v):
    return lax.optimization_barrier(v.astype(jnp.bfloat16)).astype(jnp.float32)

@jax.custom_vjp
def low_back(v):
    return v

def low_keep(v):
    return (low(v), None)

def low_pass(kept, grad):
    return (grad,)

def back_keep(v):
    return (v, None)

def back_low(kept, grad):
    return (low(grad),)
low.defvjp(low_keep, low_pass)
low_back.defvjp(back_keep, back_low)
beta_one = 0.9
beta_two = 0.999
learn_rate = 0.02
weight_decay = 0.01
eps_adam = 1e-08
eps_norm = 1e-05
highest = lax.Precision.HIGHEST

def matmul_nn(left, right):
    return jnp.dot(left, right, precision=highest)

def matrix_rows():
    return [D, D, D, D, FF, FF] * LAYERS + [EMBED_WIDTH, EMBED_WIDTH, EMBED_WIDTH]

def slot_starts(owners):
    counts = jnp.array(matrix_rows(), jnp.int32)
    mat_total = counts.shape[0]
    same_owner = (owners[:, None] == owners[None, :]).astype(jnp.int32)
    earlier_mask = jnp.tril(jnp.ones((mat_total, mat_total), jnp.int32), -1)
    return (owners * CAP + lax.optimization_barrier(jnp.sum(same_owner * earlier_mask * counts[None, :], 1))).astype(jnp.int32)

def waves(places, width):
    half_width = width // 2
    frequency = jnp.exp(-math.log(10000.0) * jnp.arange(half_width, dtype=jnp.float32) / half_width)
    angles = places[:, None] * frequency[None, :]
    return jnp.concatenate([jnp.sin(angles), jnp.cos(angles)], 1)

def norm_layer(value_entries, gain_vec, shift_vec):
    center = value_entries - lax.optimization_barrier(jnp.mean(value_entries, -1, keepdims=True))
    variance = lax.optimization_barrier(jnp.mean(center * center, -1, keepdims=True))
    return center * lax.rsqrt(variance + eps_norm) * gain_vec + shift_vec

def sequence_loss(params, seq_ids, step_num, seq_mask, seq_noise, count_all):
    table_low, pieces, vec_params = params
    clean_emb = jnp.take(table_low, seq_ids, axis=0)
    step_val = step_num.astype(jnp.float32)
    signal_level = 1.0 - jnp.sqrt(step_val / DIFF + 0.0001)
    noisy_emb = jnp.sqrt(signal_level) * clean_emb + jnp.sqrt(1.0 - signal_level) * seq_noise
    time_feat = jnp.broadcast_to(waves(step_val[None], EMBED_WIDTH), (SEQUENCE_TOKENS, EMBED_WIDTH))
    inputs = low(jnp.concatenate([noisy_emb, time_feat], 1))
    tail_at = 6 * LAYERS
    w_input = jnp.concatenate([pieces[tail_at], pieces[tail_at + 1]], 0)
    hidden = low_back(matmul_nn(inputs, w_input)) + waves(jnp.arange(SEQUENCE_TOKENS, dtype=jnp.float32), D)
    weight_row = seq_mask.astype(jnp.float32)
    keep_keys = seq_mask[None, None, :] > 0
    for layer_idx in range(LAYERS):
        w_query, w_key, w_value, w_out, w_up, w_down = pieces[6 * layer_idx:6 * layer_idx + 6]
        vec_at = layer_idx * (4 * D + FF)
        gain_rows = vec_params[vec_at:vec_at + 4 * D].reshape(4, D)
        bias_up = vec_params[vec_at + 4 * D:vec_at + 4 * D + FF]
        normed = low(norm_layer(hidden, gain_rows[0], gain_rows[1]))
        queries = low(low_back(matmul_nn(normed, w_query))).reshape(SEQUENCE_TOKENS, HEADS, HDIM)
        key_rows = low(low_back(matmul_nn(normed, w_key))).reshape(SEQUENCE_TOKENS, HEADS, HDIM)
        value_rows = low(low_back(matmul_nn(normed, w_value))).reshape(SEQUENCE_TOKENS, HEADS, HDIM)
        scores = low_back(jnp.einsum('qhd,khd->hqk', queries, key_rows, precision=highest) * HDIM ** (-0.5))
        scores = jnp.where(keep_keys, scores, -1000000000.0)
        row_max = lax.optimization_barrier(jnp.max(scores, -1, keepdims=True))
        expo = jnp.exp(scores - row_max)
        probabilities = expo / lax.optimization_barrier(jnp.sum(expo, -1, keepdims=True))
        mixed_out = jnp.einsum('hqk,khd->qhd', low(probabilities), value_rows, precision=highest).reshape(SEQUENCE_TOKENS, D)
        mixed_out = low(low_back(mixed_out))
        hidden = hidden + low_back(matmul_nn(mixed_out, w_out))
        normed_two = low(norm_layer(hidden, gain_rows[2], gain_rows[3]))
        up_proj = low_back(matmul_nn(normed_two, w_up.T) + bias_up)
        hidden = hidden + low_back(matmul_nn(low(jax.nn.gelu(up_proj)), w_down))
    final_norm = low(norm_layer(hidden, vec_params[VEC - 2 * D:VEC - D], vec_params[VEC - D:]))
    predicted = low_back(matmul_nn(final_norm, pieces[tail_at + 2].T))
    pred_error = predicted - clean_emb
    square = jnp.sum(weight_row[:, None] * pred_error * pred_error)
    logits = low_back(matmul_nn(low(predicted), table_low.T))
    row_max = lax.optimization_barrier(jnp.max(logits, -1, keepdims=True))
    log_total = row_max[:, 0] + jnp.log(lax.optimization_barrier(jnp.sum(jnp.exp(logits - row_max), -1)))
    target = jnp.take_along_axis(logits, seq_ids[:, None].astype(jnp.int32), 1)[:, 0]
    cross_sum = jnp.sum(weight_row * (log_total - target))
    return ((square + cross_sum) / count_all, (square, cross_sum))

def adamw(weight, gradient, moment_one, moment_two):
    moment_one = beta_one * moment_one + (1.0 - beta_one) * gradient
    moment_two = beta_two * moment_two + (1.0 - beta_two) * gradient * gradient
    fix_one = 1.0 - beta_one ** STEP
    fix_two = 1.0 - beta_two ** STEP
    update_dir = moment_one / fix_one / (jnp.sqrt(moment_two / fix_two) + eps_adam)
    return (weight - learn_rate * (update_dir + weight_decay * weight), moment_one, moment_two)

def reference(token_ids, timesteps, pad_mask, noise_draw, owners, emb_table, table_first_moment, table_second_moment, mat_slots, slot_first, slot_second, vec_params, vec_first, vec_second):
    starts = slot_starts(owners)
    row_counts = matrix_rows()
    table_low = emb_table.astype(jnp.bfloat16).astype(jnp.float32)
    pieces = [lax.dynamic_slice_in_dim(mat_slots, starts[mat_idx], row_counts[mat_idx], 1).T.astype(jnp.bfloat16).astype(jnp.float32) for mat_idx in range(len(row_counts))]
    weights_all = pad_mask.astype(jnp.float32)
    count_all = jnp.sum(weights_all)
    checked = jax.checkpoint(sequence_loss)

    def total_loss(params):

        def add_one(carry_sums, batch_data):
            loss_one, loss_parts = checked(params, batch_data[0], batch_data[1], batch_data[2], batch_data[3], count_all)
            return ((carry_sums[0] + loss_one, carry_sums[1] + loss_parts[0], carry_sums[2] + loss_parts[1]), None)
        zero_val = jnp.zeros((), jnp.float32)
        result, unused = lax.scan(add_one, (zero_val, zero_val, zero_val), (token_ids, timesteps, pad_mask, noise_draw.astype(jnp.float32)))
        return result
    sums, pull_back = jax.vjp(total_loss, (table_low, pieces, vec_params))
    zero_val = jnp.zeros((), jnp.float32)
    grad_table, grad_pieces, grad_vecs = pull_back((jnp.ones((), jnp.float32), zero_val, zero_val))[0]
    slot_grad = jnp.zeros_like(mat_slots)
    for mat_idx in range(len(row_counts)):
        slot_grad = lax.dynamic_update_slice_in_dim(slot_grad, grad_pieces[mat_idx].T, starts[mat_idx], 1)
    new_slots, slot_first_new, slot_second_new = adamw(mat_slots, slot_grad, slot_first, slot_second)
    new_table, table_first_new, table_second_new = adamw(emb_table, grad_table, table_first_moment, table_second_moment)
    new_vecs, vec_first_new, vec_second_new = adamw(vec_params, grad_vecs, vec_first, vec_second)
    clean_all = jnp.take(table_low, token_ids, axis=0)
    norms = jnp.sqrt(lax.optimization_barrier(jnp.sum(clean_all * clean_all, -1)) + 1e-06)
    emb_norm = jnp.sum(weights_all * norms) / count_all
    loss_pair = jnp.stack([sums[1] + sums[2], count_all])
    return (loss_pair, emb_norm, new_table, table_first_new, table_second_new, new_slots, slot_first_new, slot_second_new, new_vecs, vec_first_new, vec_second_new)
```

```python
import functools
import math

import jax
import jax.numpy as jnp
from jax import lax
from jax.experimental import pallas as pl
from jax.experimental.pallas import tpu as pltpu
from jax.sharding import PartitionSpec as P

D = 768
HEADS = 12
HDIM = 64
FF = 3072
EMBED_WIDTH = 128
DIFF = 2000
STEP = 10
CAP = 3072
LAYERS = 1
LANES = 128


beta_one = 0.9
beta_two = 0.999
learn_rate = 0.02
weight_decay = 0.01
eps_adam = 1e-08
eps_norm = 1e-05
f32 = jnp.float32
bf16 = jnp.bfloat16


def matmul_nn(left, right):
    return jnp.dot(left, right, preferred_element_type=f32)


def matmul_tn(left, right):
    return lax.dot_general(left, right, (((0,), (0,)), ((), ())), preferred_element_type=f32)


def matmul_nt(left, right):
    return lax.dot_general(left, right, (((1,), (1,)), ((), ())), preferred_element_type=f32)


ROW_COUNTS = [D, D, D, D, FF, FF, EMBED_WIDTH, EMBED_WIDTH, EMBED_WIDTH]


def slot_starts(owners):
    counts = jnp.array(ROW_COUNTS, jnp.int32)
    same_owner = (owners[:, None] == owners[None, :]).astype(jnp.int32)
    earlier_mask = jnp.tril(jnp.ones((len(ROW_COUNTS),) * 2, jnp.int32), -1)
    return jnp.sum(same_owner * earlier_mask * counts[None, :], 1)


def waves(places, width):
    half_width = width // 2
    frequency = jnp.exp(-math.log(10000.0) * jnp.arange(half_width, dtype=f32) / half_width)
    angles = places[:, None] * frequency[None, :]
    return jnp.concatenate([jnp.sin(angles), jnp.cos(angles)], 1)


def norm_parts(value_entries):
    center = value_entries - jnp.mean(value_entries, -1, keepdims=True)
    scale_inv = lax.rsqrt(jnp.mean(center * center, -1, keepdims=True) + eps_norm)
    return (center * scale_inv, scale_inv)


def norm_back(normal_part, scale_inv, gain_vec, grad_out):
    scaled = grad_out * gain_vec
    inner = (
        scaled
        - jnp.mean(scaled, -1, keepdims=True)
        - normal_part * jnp.mean(scaled * normal_part, -1, keepdims=True)
    )
    return (inner * scale_inv, jnp.sum(grad_out * normal_part, 0), jnp.sum(grad_out, 0))


def adamw(weight, gradient, moment_one, moment_two):
    moment_one = beta_one * moment_one + (1.0 - beta_one) * gradient
    moment_two = beta_two * moment_two + (1.0 - beta_two) * gradient * gradient
    fix_one = 1.0 - beta_one**STEP
    fix_two = 1.0 - beta_two**STEP
    update_dir = moment_one / fix_one / (jnp.sqrt(moment_two / fix_two) + eps_adam)
    return (weight - learn_rate * (update_dir + weight_decay * weight), moment_one, moment_two)


def swap_vocab(value, mask):
    return lax.ppermute(value, "vocab", [(i, i ^ mask) for i in range(4)])


def relative(value, axis=0):
    v = lax.axis_index("vocab")
    p = jnp.split(value, 4, axis)
    swapped = jnp.where(v % 2 == 1, jnp.concatenate([p[1], p[0], p[3], p[2]], axis), value)
    q = jnp.split(swapped, 4, axis)
    return jnp.where(v // 2 == 1, jnp.concatenate([q[2], q[3], q[0], q[1]], axis), swapped)


def vocab_gather(own, axis=0):
    far = swap_vocab(own, 2)
    near = swap_vocab(own, 1)
    return jnp.concatenate([own, near, far, swap_vocab(far, 1)], axis)


def vocab_gather_direct(own, axis=0):
    return jnp.concatenate([own] + [swap_vocab(own, k) for k in (1, 2, 3)], axis)


def vocab_exchange(pieces):
    return [pieces[0]] + [swap_vocab(pieces[k], k) for k in (1, 2, 3)]


def vocab_reduce(value):
    p = jnp.split(value, 4, 0)
    sent = swap_vocab(jnp.concatenate([p[1], p[3]], 0).astype(bf16), 1)
    near, far = jnp.split(sent, 2, 0)
    far = p[2] + far.astype(f32)
    return p[0] + near.astype(f32) + swap_vocab(far.astype(bf16), 2).astype(f32)


MESH = pl.DeviceIdType.MESH
ANY = pl.BlockSpec(memory_space=pl.ANY)
UNIT = 768
HALF = 96
QUARTER = 192


def place():
    d, v = lax.axis_index("dp"), lax.axis_index("vocab")
    return d // 2, d % 2, d, v


def greet(partners):
    barrier = pltpu.get_barrier_semaphore()
    for partner in partners:
        pl.semaphore_signal(barrier, inc=1, device_id=partner, device_id_type=MESH)
    pl.semaphore_wait(barrier, len(partners))


def remote(src, dst, sems, index, partner):
    return pltpu.make_async_remote_copy(
        src_ref=src,
        dst_ref=dst,
        send_sem=sems[0].at[index],
        recv_sem=sems[1].at[index],
        device_id=partner,
        device_id_type=MESH,
    )


def start_all(copies):
    for copy in copies:
        copy.start()
    return copies


def arrive_all(copies):
    for copy in copies:
        copy.wait_recv()


def trade_kernel(payload, arrived, send, recv, local):
    z, y, d, v = place()
    masks = (4, 6, 5, 7, 2, 3, 1)
    greet([(d ^ m, v) for m in masks])

    def part(m):
        other = d ^ m
        return payload.at[other // 2, pl.ds((other % 2) * HALF, HALF), :]

    copies = [
        remote(part(m), arrived.at[d], (send, recv), i, (d ^ m, v)) for i, m in enumerate(masks)
    ]
    start_all(copies)
    own = pltpu.make_async_copy(part(0), arrived.at[d], local)
    own.start()
    own.wait()
    for copy in copies:
        copy.wait()


def trade(payload):
    cols = payload.shape[2]
    return pl.pallas_call(
        trade_kernel,
        out_shape=jax.ShapeDtypeStruct((8, HALF, cols), payload.dtype),
        in_specs=[ANY],
        out_specs=ANY,
        scratch_shapes=[
            pltpu.SemaphoreType.DMA((7,)),
            pltpu.SemaphoreType.DMA((7,)),
            pltpu.SemaphoreType.DMA,
        ],
        compiler_params=pltpu.CompilerParams(collective_id=0, has_side_effects=True),
    )(payload)


def spread_kernel(
    up_home, down_home, small_home, attn_home, table_home,
    up, down, small, attn, out, table,
    z_send, z_recv, y_send, y_recv, x_send, x_recv, n_send, n_recv, f_send, f_recv, local,
):
    z, y, d, v = place()
    far, near = v ^ 2, v ^ 1
    greet([(d ^ m, v) for m in (2, 4, 6, 1)] + [(d, far), (d, near)])
    homes = [up_home, down_home, small_home, attn_home, table_home]
    fulls = [up, down, small, attn, table]
    own_rows = pl.ds(v * QUARTER, QUARTER)

    def spot(c, unit):
        if c == 4:
            return table.at[2 * unit + y]
        first = y * HALF if c == 3 else v * QUARTER + y * HALF
        return fulls[c].at[unit, pl.ds(first, HALF), :]

    def start_line(c):
        keep = pltpu.make_async_copy(homes[c], spot(c, z), local.at[c])
        keep.start()
        return [keep] + start_all(
            [
                remote(homes[c], spot(c, z), (z_send, z_recv), (c, k - 1), (d ^ (2 * k), v))
                for k in (2, 1, 3)
            ]
        )

    def wait_line(copies):
        copies[0].wait()
        arrive_all(copies[1:])
        return copies[1:]

    def start_side(c):
        return start_all(
            [remote(spot(c, u), spot(c, u), (y_send, y_recv), (c, u), (d ^ 1, v)) for u in range(4)]
        )

    def strips(c, rows):
        if c == 3:
            return [out.at[rows, :]]
        return [fulls[c].at[u, rows, :] for u in range(4)]

    def sources(c):
        return [attn.at[3]] if c == 3 else strips(c, own_rows)

    def start_far(c):
        return start_all(
            [
                remote(s, t, (x_send, x_recv), (c, u), (d, far))
                for u, (s, t) in enumerate(zip(sources(c), strips(c, own_rows)))
            ]
        )

    def start_near(c):
        return start_all(
            [
                remote(s, t, (n_send, n_recv), (c, u), (d, near))
                for u, (s, t) in enumerate(zip(sources(c), strips(c, own_rows)))
            ]
        )

    def start_last(c):
        rows = pl.ds(far * QUARTER, QUARTER)
        return start_all(
            [
                remote(s, s, (f_send, f_recv), (c, u), (d, near))
                for u, s in enumerate(strips(c, rows))
            ]
        )

    sent, landing = [], []
    line, side, chip = {}, {}, {}

    def begin_chip(c):
        arrive_all(side[c])
        if c == 3:
            keep = pltpu.make_async_copy(attn.at[3], out.at[own_rows, :], local.at[5])
            keep.start()
            keep.wait()
        if c != 4:
            chip[c] = start_far(c)
            near_copies = start_near(c)
            sent.extend(chip[c] + near_copies)
            landing.extend(near_copies)

    def begin_last(c):
        if c != 4:
            arrive_all(chip[c])
            last = start_last(c)
            sent.extend(last)
            landing.extend(last)

    waves_of = [[0], [1], [2, 3], [4]]
    for c in waves_of[0]:
        line[c] = start_line(c)
    for i, wave in enumerate(waves_of):
        for c in wave:
            sent.extend(wait_line(line[c]))
        if i + 1 < len(waves_of):
            for c in waves_of[i + 1]:
                line[c] = start_line(c)
        for c in wave:
            side[c] = start_side(c)
            sent.extend(side[c])
        if i >= 1:
            for c in waves_of[i - 1]:
                begin_chip(c)
        if i >= 2:
            for c in waves_of[i - 2]:
                begin_last(c)
    for c in waves_of[-1]:
        begin_chip(c)
    for wave in waves_of[-2:]:
        for c in wave:
            begin_last(c)
    arrive_all(landing)
    for copy in sent:
        copy.wait_send()


def spread(up_home, down_home, small_home, attn_home, table_home):
    small_cols = small_home.shape[1]
    rows, vocab_rows = table_home.shape
    dma = pltpu.SemaphoreType.DMA

    def shape(*dims):
        return jax.ShapeDtypeStruct(dims, bf16)

    return pl.pallas_call(
        spread_kernel,
        out_shape=[
            shape(4, D, UNIT),
            shape(4, D, UNIT),
            shape(4, D, small_cols),
            shape(4, QUARTER, UNIT),
            shape(D, UNIT),
            shape(8, rows, vocab_rows),
        ],
        in_specs=[ANY] * 5,
        out_specs=[ANY] * 6,
        scratch_shapes=[dma((5, 3))] * 2 + [dma((5, 4))] * 2 + [dma((4, 4))] * 6 + [dma((6,))],
        compiler_params=pltpu.CompilerParams(collective_id=1, has_side_effects=True),
    )(up_home, down_home, small_home, attn_home, table_home)

I16 = jnp.int16
TAIL = 16
TILES = 60


def exponent(peak):
    return jnp.ceil(jnp.log2(jnp.maximum(peak, 1e-30))) + 1.0


def coded(value, power):
    return jnp.round(value * jnp.exp2(15.0 - power)).astype(jnp.int32).astype(I16)


def plain(code, power):
    return code.astype(jnp.int32).astype(f32) * jnp.exp2(power - 15.0)


def put(ref, value):
    rows, cols = value.shape
    power = exponent(jnp.max(jnp.abs(value), 0, keepdims=True))
    ref[0:rows, :] = coded(value, power)
    ref[rows : rows + TAIL, :] = (
        jnp.broadcast_to(power, (TAIL, cols)).astype(jnp.int32).astype(I16)
    )


def get(ref, rows):
    power = ref[rows : rows + TAIL, :].astype(jnp.int32).astype(f32)[0:1]
    return plain(ref[0:rows, :], power)


def put_tiles(ref, source, rows):
    lane = lax.broadcasted_iota(jnp.int32, (rows, LANES), 1)

    def body(tile, powers):
        at = pl.ds(pl.multiple_of(tile * LANES, LANES), LANES)
        value = source(at)
        power = exponent(jnp.max(jnp.abs(value), 1, keepdims=True))
        ref[:, at] = coded(value, power)
        return jnp.where(lane == tile, power, powers)

    powers = lax.fori_loop(0, TILES, body, jnp.zeros((rows, LANES), f32), unroll=6)
    ref[:, TILES * LANES :] = powers.astype(jnp.int32).astype(I16)


def tile_getter(ref, rows):
    lane = lax.broadcasted_iota(jnp.int32, (rows, LANES), 1)
    powers = ref[:, TILES * LANES :].astype(jnp.int32).astype(f32)

    def read(tile, at):
        power = jnp.sum(jnp.where(lane == tile, powers, 0.0), 1, keepdims=True)
        return plain(ref[:, at], power)

    return read


def grads_kernel(
    down_left, up_left, out_left, small_left, final_left, qkv_left,
    active, grad_up, mixed, inputs, grad_pred, normed, table,
    big, small, table_sum,
    cs, cr, xs, xr, ys, yr, zs, zr, home, part, half,
    small_cs, small_cr, small_xs, small_xr, small_ys, small_yr, small_zs, small_zr, small_home, small_half,
    ts, tr, tzs, tzr,
    c_send, c_recv, x_send, x_recv, y_send, y_recv, z_send, z_recv, g_send, g_recv, f_send, f_recv, local,
):
    z, y, d, v = place()
    far, near = v ^ 2, v ^ 1
    greet([(d ^ m, v) for m in (2, 4, 6, 1)] + [(d, far), (d, near)])
    sent = []

    def send(src, dst, sems, index, partner):
        copy = remote(src, dst, sems, index, partner)
        copy.start()
        sent.append(copy)
        return copy

    def product(n, who):
        if n == 0:
            return matmul_nn(out_left[who], mixed[...])
        if n < 5:
            return matmul_nn(down_left[who], active[n - 1])
        return matmul_nn(up_left[who], grad_up[n - 5])

    core, chip, side, line, spread_line, spread_side = {}, {}, {}, {}, {}, {}

    def to_core(n):
        put(cs.at[n, 0], product(n, near))
        put(cs.at[n, 1], product(n, near ^ 2))
        core[n] = send(cs.at[n], cr.at[n], (c_send, c_recv), n, (d, near))

    def to_chip(n):
        core[n].wait_recv()
        put(xs.at[n], product(n, far) + get(cr.at[n, 1], QUARTER))
        chip[n] = send(xs.at[n], xr.at[n], (x_send, x_recv), n, (d, far))

    def halves(slot, value):
        part[...] = value
        put(ys.at[slot], part[pl.ds((1 - y) * HALF, HALF), :])
        half[slot] = part[pl.ds(y * HALF, HALF), :]
        side[slot] = send(ys.at[slot], yr.at[slot], (y_send, y_recv), slot, (d ^ 1, v))

    def to_side(n):
        chip[n].wait_recv()
        value = product(n, v) + get(cr.at[n, 0], QUARTER) + get(xr.at[n], QUARTER)
        halves(3 + n, value)

    def to_line(group):
        for u in range(4):
            slot = 4 * group + u
            side[slot].wait_recv()
            half[slot] = half[slot] + get(yr.at[slot], HALF)
        for k in (2, 1, 3):
            put(zs.at[group, k - 1], half[4 * group + (z ^ k)])
            line[group, k] = send(
                zs.at[group, k - 1], zr.at[group, k - 1], (z_send, z_recv), 3 * group + k - 1, (d ^ (2 * k), v)
            )

    def to_home(group):
        total = half[4 * group + z]
        for k in (2, 1, 3):
            line[group, k].wait_recv()
            total = total + get(zr.at[group, k - 1], HALF)
        put(home.at[group], total)
        keep = pltpu.make_async_copy(home.at[group], big.at[4 * group + z, y], local.at[group])
        keep.start()
        for k in (2, 1, 3):
            spread_line[group, k] = send(
                home.at[group], big.at[4 * group + z, y], (g_send, g_recv), 3 * group + k - 1, (d ^ (2 * k), v)
            )
        keep.wait()

    def to_all(group):
        for k in (2, 1, 3):
            spread_line[group, k].wait_recv()
        for u in range(4):
            slot = 4 * group + u
            spread_side[slot] = send(
                big.at[slot, y], big.at[slot, y], (f_send, f_recv), slot, (d ^ 1, v)
            )

    def small_product(who):
        return jnp.concatenate(
            [matmul_nn(small_left[who], inputs[...]), matmul_nn(final_left[who], grad_pred[...])], 1
        )

    def small_to_core():
        put(small_cs.at[0], small_product(near))
        put(small_cs.at[1], small_product(near ^ 2))
        core[9] = send(small_cs, small_cr, (c_send, c_recv), 9, (d, near))

    def small_to_chip():
        core[9].wait_recv()
        put(small_xs, small_product(far) + get(small_cr.at[1], QUARTER))
        chip[9] = send(small_xs, small_xr, (x_send, x_recv), 9, (d, far))

    def small_to_side():
        chip[9].wait_recv()
        value = small_product(v) + get(small_cr.at[0], QUARTER) + get(small_xr, QUARTER)
        cols = value.shape[1]
        part[:, 0:cols] = value
        put(small_ys, part[pl.ds((1 - y) * HALF, HALF), 0:cols])
        small_half[0] = part[pl.ds(y * HALF, HALF), 0:LANES]
        small_half[1] = part[pl.ds(y * HALF, HALF), LANES : 2 * LANES]
        small_half[2] = part[pl.ds(y * HALF, HALF), 2 * LANES : cols]
        small_half[3] = jnp.zeros((HALF, LANES), f32)
        side[12] = send(small_ys, small_yr, (y_send, y_recv), 12, (d ^ 1, v))

    def small_to_line():
        side[12].wait_recv()
        value = get(small_yr, HALF)
        for u in range(3):
            small_half[u] = small_half[u] + value[:, u * LANES : (u + 1) * LANES]
        for k in (2, 1, 3):
            put(small_zs.at[k - 1], small_half[z ^ k])
            line[3, k] = send(
                small_zs.at[k - 1], small_zr.at[k - 1], (z_send, z_recv), 9 + k - 1, (d ^ (2 * k), v)
            )

    def small_to_home():
        total = small_half[z]
        for k in (2, 1, 3):
            line[3, k].wait_recv()
            total = total + get(small_zr.at[k - 1], HALF)
        put(small_home, total)
        keep = pltpu.make_async_copy(small_home, small.at[z, y], local.at[3])
        keep.start()
        for k in (2, 1, 3):
            spread_line[3, k] = send(
                small_home, small.at[z, y], (g_send, g_recv), 9 + k - 1, (d ^ (2 * k), v)
            )
        keep.wait()

    def small_to_all():
        for k in (2, 1, 3):
            spread_line[3, k].wait_recv()
        spread_side[12] = send(
            small.at[:, y], small.at[:, y], (f_send, f_recv), 12, (d ^ 1, v)
        )

    def table_to_side():
        put_tiles(ts, lambda at: table[1 - y, :, at], 64)
        side[13] = send(ts, tr, (y_send, y_recv), 13, (d ^ 1, v))

    def table_line_value(which):
        rows = pl.ds(pl.multiple_of(which * 16, 16), 16)
        read = tile_getter(tr.at[rows, :], 16)
        return rows, read

    def table_to_line():
        side[13].wait_recv()
        for k in (2, 1, 3):
            rows, read = table_line_value(z ^ k)

            def source(at, rows=rows, read=read):
                return table[y, rows, at] + read(at.start // LANES, at)

            put_tiles(tzs.at[k - 1], source, 16)
            line[4, k] = send(
                tzs.at[k - 1], tzr.at[k - 1], (z_send, z_recv), 12 + k - 1, (d ^ (2 * k), v)
            )

    def table_to_home():
        for k in (2, 1, 3):
            line[4, k].wait_recv()
        rows, read = table_line_value(z)
        others = [tile_getter(tzr.at[k], 16) for k in range(3)]

        def body(tile, carry):
            at = pl.ds(pl.multiple_of(tile * LANES, LANES), LANES)
            value = table[y, rows, at] + read(tile, at)
            for other in others:
                value = value + other(tile, at)
            table_sum[:, at] = value
            return carry

        lax.fori_loop(0, TILES, body, 0, unroll=4)

    to_core(0)
    to_core(1)
    to_chip(0)
    to_core(2)
    to_chip(1)
    table_to_side()
    to_core(3)
    to_chip(2)
    for u in range(3):
        halves(u, matmul_nn(qkv_left[u], normed[...]))
    to_core(4)
    to_chip(3)
    small_to_core()
    to_side(0)
    to_core(5)
    to_chip(4)
    small_to_chip()
    to_side(1)
    table_to_line()
    to_core(6)
    to_chip(5)
    to_side(2)
    to_line(0)
    to_core(7)
    to_chip(6)
    to_side(3)
    to_core(8)
    to_chip(7)
    to_side(4)
    to_chip(8)
    small_to_side()
    to_line(1)
    table_to_home()
    to_home(0)
    to_side(5)
    small_to_line()
    to_side(6)
    to_home(1)
    to_all(0)
    to_side(7)
    small_to_home()
    to_side(8)
    to_line(2)
    to_all(1)
    small_to_all()
    to_home(2)
    to_all(2)
    for slot in range(13):
        spread_side[slot].wait_recv()
    for copy in sent:
        copy.wait_send()


def reduce_grads(*operands):
    dma = pltpu.SemaphoreType.DMA
    vmem = pltpu.VMEM
    tall, low, wide = QUARTER + TAIL, HALF + TAIL, 3 * LANES
    table_cols = TILES * LANES
    return pl.pallas_call(
        grads_kernel,
        out_shape=[
            jax.ShapeDtypeStruct((12, 2, low, UNIT), I16),
            jax.ShapeDtypeStruct((4, 2, low, LANES), I16),
            jax.ShapeDtypeStruct((16, table_cols), f32),
        ],
        in_specs=[pl.BlockSpec(memory_space=pltpu.VMEM)] * 13,
        out_specs=[ANY, ANY, pl.BlockSpec(memory_space=pltpu.VMEM)],
        scratch_shapes=[
            vmem((9, 2, tall, UNIT), I16),
            vmem((9, 2, tall, UNIT), I16),
            vmem((9, tall, UNIT), I16),
            vmem((9, tall, UNIT), I16),
            vmem((12, low, UNIT), I16),
            vmem((12, low, UNIT), I16),
            vmem((3, 3, low, UNIT), I16),
            vmem((3, 3, low, UNIT), I16),
            vmem((3, low, UNIT), I16),
            vmem((QUARTER, UNIT), f32),
            vmem((12, HALF, UNIT), f32),
            vmem((2, tall, wide), I16),
            vmem((2, tall, wide), I16),
            vmem((tall, wide), I16),
            vmem((tall, wide), I16),
            vmem((low, wide), I16),
            vmem((low, wide), I16),
            vmem((3, low, LANES), I16),
            vmem((3, low, LANES), I16),
            vmem((low, LANES), I16),
            vmem((4, HALF, LANES), f32),
            vmem((64, table_cols + LANES), I16),
            vmem((64, table_cols + LANES), I16),
            vmem((3, 16, table_cols + LANES), I16),
            vmem((3, 16, table_cols + LANES), I16),
        ]
        + [dma((10,))] * 4
        + [dma((14,))] * 2
        + [dma((15,))] * 2
        + [dma((12,))] * 2
        + [dma((13,))] * 2
        + [dma((4,))],
        compiler_params=pltpu.CompilerParams(
            collective_id=2, has_side_effects=True, vmem_limit_bytes=60 * 2**20
        ),
    )(*operands)


def slot_kernel(kind, unit, column, big, small, w, m1, m2, w_out, m1_out, m2_out):
    which = kind[pl.program_id(0)]

    def rows_of(ref):
        return jnp.concatenate([get(ref.at[0, 0], HALF), get(ref.at[0, 1], HALF)], 0)

    zero = jnp.zeros(w.shape, f32)
    g = jnp.where(which == 1, rows_of(big), jnp.where(which == 2, rows_of(small), zero))
    w_out[...], m1_out[...], m2_out[...] = adamw(w[...], g, m1[...], m2[...])


def slot_update(owners, starts, big, small, slots, first, second):
    rows = slots.shape[0]
    blocks = CAP // LANES
    d = lax.axis_index("dp")
    spots, units, columns, kinds = [], [], [], []
    per_unit = UNIT // LANES
    first_unit = [0, 1, 2, 3, 8, 4, 0, 1, 2]
    for i, count in enumerate(ROW_COUNTS):
        spots.append(jnp.where(owners[i] == d, starts[i] // LANES, -CAP) + jnp.arange(count // LANES))
        for b in range(count // LANES):
            units.append(first_unit[i] + b // per_unit)
            columns.append(b % per_unit)
            kinds.append(2 if i > 5 else 1)
    hit = jnp.concatenate(spots)[None, :] == jnp.arange(blocks)[:, None]

    def looked_up(values):
        return jnp.sum(jnp.where(hit, jnp.array(values, jnp.int32)[None, :], 0), 1).astype(jnp.int32)

    kind, unit, column = looked_up(kinds), looked_up(units), looked_up(columns)
    plain_spec = pl.BlockSpec((rows, LANES), lambda j, k, u, c: (0, j))
    low = HALF + TAIL
    big_spec = pl.BlockSpec(
        (1, 2, low, LANES),
        lambda j, k, u, c: (jnp.where(k[j] == 1, u[j], 0), 0, 0, jnp.where(k[j] == 1, c[j], 0)),
    )
    small_spec = pl.BlockSpec(
        (1, 2, low, LANES), lambda j, k, u, c: (jnp.where(k[j] == 2, u[j], 0), 0, 0, 0)
    )
    return pl.pallas_call(
        slot_kernel,
        grid_spec=pltpu.PrefetchScalarGridSpec(
            num_scalar_prefetch=3,
            grid=(blocks,),
            in_specs=[big_spec, small_spec, plain_spec, plain_spec, plain_spec],
            out_specs=[plain_spec, plain_spec, plain_spec],
        ),
        out_shape=[jax.ShapeDtypeStruct(slots.shape, f32)] * 3,
        cost_estimate=pl.CostEstimate(flops=0, bytes_accessed=28 * rows * CAP, transcendentals=0),
    )(kind, unit, column, big, small, slots, first, second)


def swap_dp(value, mask):
    return lax.ppermute(value, "dp", [(i, i ^ mask) for i in range(8)])


def sum_all(value, over_vocab=True):
    if over_vocab:
        for mask in (1, 2):
            value = value + swap_vocab(value, mask)
    for mask in (1, 2, 4):
        value = value + swap_dp(value, mask)
    return value


def per_device(
    token_ids,
    timesteps,
    pad_mask,
    noise_draw,
    owners,
    emb_table,
    table_first_moment,
    table_second_moment,
    mat_slots,
    slot_first,
    slot_second,
    vec_params,
    vec_first,
    vec_second,
):
    v = lax.axis_index("vocab")
    d = lax.axis_index("dp")
    z = d // 2
    seq_len = token_ids.shape[1]
    tokens = seq_len // 4
    vocab_rows, emb_cols = emb_table.shape
    heads_own = HEADS // 4
    score_scale = HDIM ** (-0.5)

    starts = slot_starts(owners)
    whole = (owners[4] == d) | (owners[5] == d)

    def unit_payload(u):
        start = jnp.where(whole, u * UNIT, starts[u])
        main = lax.dynamic_slice(mat_slots, (0, start), (QUARTER, UNIT))
        extra = lax.dynamic_slice(
            mat_slots, (0, starts[6 + min(u, 2)]), (QUARTER, EMBED_WIDTH)
        )
        return jnp.concatenate([main, extra], 1).astype(bf16)

    arrived = trade(jnp.stack([unit_payload(u) for u in range(4)]))

    def from_owner(index, lo, width):
        return lax.dynamic_slice(arrived, (owners[index], 0, lo), (1, HALF, width))[0]

    table_own = emb_table.T
    w_up, w_down, w_small, w_attn, w_out, table_low = spread(
        from_owner(4, 0, UNIT),
        from_owner(5, 0, UNIT),
        from_owner(6 + jnp.minimum(z, 2), UNIT, EMBED_WIDTH),
        from_owner(z, 0, UNIT),
        table_own.astype(bf16),
    )
    table_low = table_low.reshape(EMBED_WIDTH, vocab_rows)

    ids_rel = relative(token_ids[0])
    mask_rel = relative(pad_mask[0])
    keep_keys = mask_rel > 0
    weight_rel = mask_rel.astype(f32)
    mask_own = weight_rel[:tokens]
    count_all = sum_all(jnp.sum(weight_rel)[None], False)[0]
    local_row = ids_rel - v * vocab_rows
    valid_row = (local_row >= 0) & (local_row < vocab_rows)
    safe_row = jnp.clip(local_row, 0, vocab_rows - 1)
    found_rows = jnp.where(
        valid_row[:, None], jnp.take(table_low.T, safe_row, axis=0), jnp.zeros((), bf16)
    )
    pieces = vocab_exchange(jnp.split(found_rows, 4, 0))
    clean_emb = sum(piece.astype(f32) for piece in pieces)
    own_places = (v * tokens + jnp.arange(tokens)).astype(f32)
    step_val = timesteps[0].astype(f32)
    signal_level = 1.0 - jnp.sqrt(step_val / DIFF + 0.0001)
    noisy_emb = jnp.sqrt(signal_level) * clean_emb + jnp.sqrt(1.0 - signal_level) * noise_draw[
        0
    ].astype(f32)
    time_feat = jnp.broadcast_to(waves(step_val[None], EMBED_WIDTH), (tokens, EMBED_WIDTH))
    inputs = jnp.concatenate([noisy_emb, time_feat], 1).astype(bf16)

    g_one, b_one, g_two, b_two = [vec_params[i * D : (i + 1) * D] for i in range(4)]
    bias_up = vec_params[4 * D : 4 * D + FF].reshape(4, 1, UNIT)
    g_fin, b_fin = [vec_params[4 * D + FF + i * D : 4 * D + FF + (i + 1) * D] for i in range(2)]

    hidden = (
        matmul_nt(inputs[:, :EMBED_WIDTH], w_small[0])
        + matmul_nt(inputs[:, EMBED_WIDTH:], w_small[1])
        + waves(own_places, D)
    )
    norm_one, inv_one = norm_parts(hidden)
    normed_all = vocab_gather((norm_one * g_one + b_one).astype(bf16))
    queries, keys, values = [matmul_nt(normed_all, w_attn[i]).astype(bf16) for i in range(3)]

    def by_head(value):
        return value.reshape(seq_len, heads_own, HDIM)

    q_h, k_h, v_h = by_head(queries), by_head(keys), by_head(values)
    scores = jnp.einsum("qhd,khd->hqk", q_h, k_h, preferred_element_type=f32) * score_scale
    scores = jnp.where(keep_keys[None, None, :], scores, -1000000000.0)
    row_max = jnp.max(scores, -1, keepdims=True)
    expo = jnp.exp(scores - row_max)
    probs = expo / jnp.sum(expo, -1, keepdims=True)
    probs_low = probs.astype(bf16)
    mixed = jnp.einsum("hqk,khd->qhd", probs_low, v_h, preferred_element_type=f32)
    mixed = mixed.reshape(seq_len, QUARTER).astype(bf16)
    mixed_own = relative(jnp.concatenate(vocab_exchange(jnp.split(mixed, 4, 0)), 1), 1)
    middle = hidden + matmul_nt(mixed_own, w_out)
    norm_two, inv_two = norm_parts(middle)
    normed_two = (norm_two * g_two + b_two).astype(bf16)
    up_proj = (
        jnp.einsum("tk,jkn->jtn", normed_two, w_up, preferred_element_type=f32) + bias_up
    )
    active = jax.nn.gelu(up_proj).astype(bf16)
    hidden_two = middle + jnp.einsum("jtn,jon->to", active, w_down, preferred_element_type=f32)
    norm_final, inv_final = norm_parts(hidden_two)
    final_norm = (norm_final * g_fin + b_fin).astype(bf16)
    predicted = matmul_nn(final_norm, w_small[2])

    pred_all = vocab_gather_direct(predicted.astype(bf16))
    logits = matmul_nn(pred_all, table_low)
    columns = lax.broadcasted_iota(jnp.int32, (seq_len, vocab_rows), 1)
    chosen = columns == local_row[:, None]
    peak = jnp.max(logits, -1)
    exp_low = jnp.exp(logits - peak[:, None])
    exp_sum = jnp.sum(exp_low, -1)
    exp_low = exp_low.astype(bf16)
    target = jnp.sum(jnp.where(chosen, logits, 0.0), -1)
    mix_emb = matmul_nt(exp_low, table_low)
    stats = jnp.stack([peak, exp_sum, target]).reshape(3, 4, tokens)
    stat_list = [stats]
    for k in (1, 2, 3):
        got = swap_vocab(stats, k)
        stat_list.append(jnp.stack([got[:, j ^ k] for j in range(4)], 1))
    peak_all = functools.reduce(jnp.maximum, [s[0] for s in stat_list])
    total_all = sum(s[1] * jnp.exp(s[0] - peak_all) for s in stat_list)
    target_own = sum(s[2][0] for s in stat_list)
    lse = (peak_all + jnp.log(total_all)).reshape(seq_len)
    row_weight = weight_rel / count_all
    factor = jnp.exp(peak - lse) * row_weight
    grad_pred_local = mix_emb * factor[:, None] - found_rows.astype(f32) * row_weight[:, None]
    pieces = vocab_exchange(jnp.split(grad_pred_local.astype(bf16), 4, 0))
    pred_error = predicted - clean_emb
    error_grad = 2.0 * mask_own[:, None] * pred_error / count_all
    grad_pred_low = (sum(piece.astype(f32) for piece in pieces) + error_grad).astype(bf16)
    grad_logits = exp_low.astype(f32) * factor[:, None] - jnp.where(chosen, row_weight[:, None], 0.0)
    grad_table_head = matmul_tn(pred_all, grad_logits.astype(bf16))

    square_own = jnp.sum(mask_own[:, None] * pred_error * pred_error)
    cross_own = jnp.sum(mask_own * (lse[:tokens] - target_own))
    norm_own = jnp.sum(mask_own * jnp.sqrt(jnp.sum(clean_emb * clean_emb, -1) + 1e-06))
    square, cross_sum, norm_total = sum_all(jnp.stack([square_own, cross_own, norm_own]))

    grad_final = matmul_nt(grad_pred_low, w_small[2])
    grad_hidden, grad_gf, grad_bf = norm_back(norm_final, inv_final, g_fin, grad_final)
    grad_low = grad_hidden.astype(bf16)
    grad_active = jnp.einsum("to,jon->jtn", grad_low, w_down, preferred_element_type=f32)
    grad_up_proj = jax.vjp(jax.nn.gelu, up_proj)[1](grad_active)[0].astype(bf16)
    grad_bias = jnp.sum(grad_up_proj.astype(f32), 1).reshape(FF)
    grad_normed_two = jnp.einsum("jtn,jkn->tk", grad_up_proj, w_up, preferred_element_type=f32)
    grad_part, grad_g2, grad_b2 = norm_back(norm_two, inv_two, g_two, grad_normed_two)
    grad_middle = grad_hidden + grad_part
    grad_attn = grad_middle.astype(bf16)
    grad_mixed = relative(matmul_nn(grad_attn, w_out).astype(bf16), 1)
    grad_mixed = by_head(jnp.concatenate(vocab_exchange(jnp.split(grad_mixed, 4, 1)), 0))
    grad_probs = jnp.einsum("qhd,khd->hqk", grad_mixed, v_h, preferred_element_type=f32)
    inner_sum = jnp.sum(probs * grad_probs, -1, keepdims=True)
    grad_scores = (probs * (grad_probs - inner_sum)).astype(bf16)
    grad_q = jnp.einsum("hqk,khd->qhd", grad_scores, k_h, preferred_element_type=f32)
    grad_k = jnp.einsum("hqk,qhd->khd", grad_scores, q_h, preferred_element_type=f32)
    grad_v = jnp.einsum("hqk,qhd->khd", probs_low, grad_mixed, preferred_element_type=f32)
    grad_q = (grad_q * score_scale).astype(bf16).reshape(seq_len, QUARTER)
    grad_k = (grad_k * score_scale).astype(bf16).reshape(seq_len, QUARTER)
    grad_v = grad_v.astype(bf16).reshape(seq_len, QUARTER)
    grad_normed = vocab_reduce(
        matmul_nn(grad_q, w_attn[0]) + matmul_nn(grad_k, w_attn[1]) + matmul_nn(grad_v, w_attn[2])
    )
    grad_part_one, grad_g1, grad_b1 = norm_back(norm_one, inv_one, g_one, grad_normed)
    grad_hidden_low = (grad_middle + grad_part_one).astype(bf16)
    grad_inputs = matmul_nn(grad_hidden_low, w_small[0])
    grad_clean = jnp.sqrt(signal_level) * grad_inputs - error_grad
    grad_clean_all = vocab_gather_direct(grad_clean.astype(bf16))
    grad_table = grad_table_head + matmul_tn(grad_clean_all, chosen.astype(bf16))
    grad_table = jnp.pad(grad_table, ((0, 0), (0, TILES * LANES - vocab_rows)))
    grad_table = grad_table.reshape(4, 2, 16, TILES * LANES).transpose(1, 0, 2, 3)

    def left(value):
        return value.T.reshape(4, QUARTER, value.shape[0])

    big, small, table_grad = reduce_grads(
        left(grad_low),
        left(normed_two),
        left(grad_attn),
        left(grad_hidden_low),
        left(final_norm),
        jnp.stack([grad_q.T, grad_k.T, grad_v.T]),
        active,
        grad_up_proj,
        mixed_own,
        inputs,
        grad_pred_low,
        normed_all,
        grad_table.reshape(2, 64, TILES * LANES),
    )

    grad_vec = jnp.concatenate([grad_g1, grad_b1, grad_g2, grad_b2, grad_bias, grad_gf, grad_bf])
    grad_vec = sum_all(grad_vec)
    vec_share = vec_first.shape[0]
    own_grad = lax.dynamic_slice_in_dim(grad_vec, v * vec_share, vec_share)
    own_vecs = lax.dynamic_slice_in_dim(vec_params, v * vec_share, vec_share)

    new_slots, slot_first_new, slot_second_new = slot_update(
        owners, starts, big, small, mat_slots, slot_first, slot_second
    )
    new_table, table_first_new, table_second_new = adamw(
        table_own, table_grad[:, :vocab_rows], table_first_moment.T, table_second_moment.T
    )
    new_vecs, vec_first_new, vec_second_new = adamw(own_vecs, own_grad, vec_first, vec_second)
    loss_pair = jnp.stack([square + cross_sum, count_all])
    emb_norm = norm_total / count_all
    return (
        loss_pair,
        emb_norm,
        new_table.T,
        table_first_new.T,
        table_second_new.T,
        new_slots,
        slot_first_new,
        slot_second_new,
        new_vecs,
        vec_first_new,
        vec_second_new,
    )


def broadcast(value, axis, source):
    kept = jnp.where(lax.axis_index(axis) == source, value, 0).astype(value.dtype)
    return lax.psum(kept, axis)


def merged(value, axis, join):
    pieces = jax.tree.map(lambda part: lax.all_gather(part, axis), value)
    head = jax.tree.map(lambda part: part[0], pieces)
    tail = jax.tree.map(lambda part: part[1:], pieces)
    so_far, _ = lax.scan(lambda so_far, share: (join(so_far, share), None), head, tail)
    return so_far


def matrix_rows():
    return [D, D, D, D, FF, FF] * LAYERS + [EMBED_WIDTH, EMBED_WIDTH, EMBED_WIDTH]


def slot_places(owners):
    counts = jnp.array(matrix_rows(), jnp.int32)
    mat_total = counts.shape[0]
    same_owner = (owners[:, None] == owners[None, :]).astype(jnp.int32)
    earlier_mask = jnp.tril(jnp.ones((mat_total, mat_total), jnp.int32), -1)
    return owners * CAP + jnp.sum(same_owner * earlier_mask * counts[None, :], 1)


def block_scores(query_blk, keys_all, keep_keys, score_scale):
    scores = (
        jnp.einsum("qhd,khd->hqk", query_blk, keys_all, preferred_element_type=jnp.float32)
        * score_scale
    )
    return jnp.where(keep_keys[None, None, :], scores, -1000000000.0)


def attention(queries, keys_all, values_all, keep_keys, score_scale):
    tokens = queries.shape[0]
    width = min(512, tokens)
    query_blocks = queries.reshape(tokens // width, width, HEADS, HDIM)

    def one_block(query_blk):
        scores = block_scores(query_blk, keys_all, keep_keys, score_scale)
        row_max = jnp.max(scores, -1, keepdims=True)
        expo = jnp.exp(scores - row_max)
        exp_total = jnp.sum(expo, -1, keepdims=True)
        probabilities = (expo / exp_total).astype(jnp.bfloat16)
        mixed_out = jnp.einsum(
            "hqk,khd->qhd", probabilities, values_all, preferred_element_type=jnp.float32
        )
        return (mixed_out, (row_max + jnp.log(exp_total))[..., 0])

    mixed_out, log_total = lax.map(one_block, query_blocks)
    return (mixed_out.reshape(tokens, HEADS, HDIM), log_total)


def attention_back(queries, keys_all, values_all, keep_keys, log_total, grad_mixed, score_scale):
    tokens = queries.shape[0]
    width = min(512, tokens)
    query_blocks = queries.reshape(tokens // width, width, HEADS, HDIM)
    grad_blocks = grad_mixed.reshape(tokens // width, width, HEADS, HDIM)

    def one_block(carry_sums, block_data):
        query_blk, total_blk, grad_blk = block_data
        scores = block_scores(query_blk, keys_all, keep_keys, score_scale)
        probabilities = jnp.exp(scores - total_blk[..., None])
        grad_probs = jnp.einsum(
            "qhd,khd->hqk", grad_blk, values_all, preferred_element_type=jnp.float32
        )
        inner_sum = jnp.sum(probabilities * grad_probs, -1, keepdims=True)
        grad_scores = (probabilities * (grad_probs - inner_sum)).astype(jnp.bfloat16)
        grad_query = (
            jnp.einsum("hqk,khd->qhd", grad_scores, keys_all, preferred_element_type=jnp.float32)
            * score_scale
        )
        grad_key = (
            jnp.einsum("hqk,qhd->khd", grad_scores, query_blk, preferred_element_type=jnp.float32)
            * score_scale
        )
        grad_value = jnp.einsum(
            "hqk,qhd->khd",
            probabilities.astype(jnp.bfloat16),
            grad_blk,
            preferred_element_type=jnp.float32,
        )
        return ((carry_sums[0] + grad_key, carry_sums[1] + grad_value), grad_query)

    zero_keys = jnp.zeros(keys_all.shape, jnp.float32)
    grad_kv, grad_queries = lax.scan(
        one_block, (zero_keys, zero_keys), (query_blocks, log_total, grad_blocks)
    )
    return (grad_queries.reshape(tokens, D), grad_kv[0].reshape(-1, D), grad_kv[1].reshape(-1, D))


def send_matrix(piece_cols, root):
    return broadcast(piece_cols, "dp", root)


def fetch_keys(key_rows, value_rows):
    return (
        lax.all_gather(key_rows, "vocab", axis=0, tiled=True),
        lax.all_gather(value_rows, "vocab", axis=0, tiled=True),
    )


def layer_forward(hidden, weights, vec_layer, keep_keys, score_scale):
    w_query, w_key, w_value, w_out, w_up, w_down = weights
    tokens = hidden.shape[0]
    norm_one, inv_one = norm_parts(hidden)
    normed = (norm_one * vec_layer[0:D] + vec_layer[D : 2 * D]).astype(jnp.bfloat16)
    queries = matmul_nn(normed, w_query).astype(jnp.bfloat16)
    key_rows = matmul_nn(normed, w_key).astype(jnp.bfloat16)
    value_rows = matmul_nn(normed, w_value).astype(jnp.bfloat16)
    keys_all, values_all = fetch_keys(key_rows, value_rows)
    keys_all = keys_all.reshape(-1, HEADS, HDIM)
    values_all = values_all.reshape(-1, HEADS, HDIM)
    mixed_out, log_total = attention(
        queries.reshape(tokens, HEADS, HDIM), keys_all, values_all, keep_keys, score_scale
    )
    mixed_low = mixed_out.reshape(tokens, D).astype(jnp.bfloat16)
    middle = hidden + matmul_nn(mixed_low, w_out)
    norm_two, inv_two = norm_parts(middle)
    normed_two = (norm_two * vec_layer[2 * D : 3 * D] + vec_layer[3 * D : 4 * D]).astype(
        jnp.bfloat16
    )
    up_proj = matmul_nt(normed_two, w_up) + vec_layer[4 * D :]
    active = jax.nn.gelu(up_proj).astype(jnp.bfloat16)
    out_rows = middle + matmul_nn(active, w_down)
    kept_vals = (
        norm_one,
        inv_one,
        normed,
        queries,
        key_rows,
        value_rows,
        keys_all,
        values_all,
        log_total,
        mixed_low,
        norm_two,
        inv_two,
        normed_two,
        up_proj,
        active,
    )
    return (out_rows, kept_vals)


def layer_backward(grad_out, kept_vals, weights, vec_layer, keep_keys, score_scale):
    w_query, w_key, w_value, w_out, w_up, w_down = weights
    (
        norm_one,
        inv_one,
        normed,
        queries,
        key_rows,
        value_rows,
        keys_all,
        values_all,
        log_total,
        mixed_low,
        norm_two,
        inv_two,
        normed_two,
        up_proj,
        active,
    ) = kept_vals
    tokens = grad_out.shape[0]
    grad_low = grad_out.astype(jnp.bfloat16)
    grad_down = matmul_tn(active, grad_low)
    grad_active = matmul_nt(grad_low, w_down)
    grad_up_proj = jax.vjp(jax.nn.gelu, up_proj)[1](grad_active)[0].astype(jnp.bfloat16)
    grad_bias = jnp.sum(grad_up_proj.astype(jnp.float32), 0)
    grad_up = matmul_tn(grad_up_proj, normed_two)
    grad_normed_two = matmul_nn(grad_up_proj, w_up)
    grad_part, grad_gain_two, grad_shift_two = norm_back(
        norm_two, inv_two, vec_layer[2 * D : 3 * D], grad_normed_two
    )
    grad_middle = grad_out + grad_part
    grad_attn = grad_middle.astype(jnp.bfloat16)
    grad_out_w = matmul_tn(mixed_low, grad_attn)
    grad_mixed = matmul_nt(grad_attn, w_out).astype(jnp.bfloat16).reshape(tokens, HEADS, HDIM)
    grad_queries, grad_keys_all, grad_values_all = attention_back(
        queries.reshape(tokens, HEADS, HDIM),
        keys_all,
        values_all,
        keep_keys,
        log_total,
        grad_mixed,
        score_scale,
    )
    grad_key_rows, grad_value_rows = (
        lax.psum_scatter(
            grad_keys_all.astype(jnp.bfloat16), "vocab", scatter_dimension=0, tiled=True
        ).astype(jnp.float32),
        lax.psum_scatter(
            grad_values_all.astype(jnp.bfloat16), "vocab", scatter_dimension=0, tiled=True
        ).astype(jnp.float32),
    )
    grad_q_low = grad_queries.astype(jnp.bfloat16)
    grad_k_low = grad_key_rows.astype(jnp.bfloat16)
    grad_v_low = grad_value_rows.astype(jnp.bfloat16)
    grad_wq = matmul_tn(normed, grad_q_low)
    grad_wk = matmul_tn(normed, grad_k_low)
    grad_wv = matmul_tn(normed, grad_v_low)
    grad_normed = (
        matmul_nt(grad_q_low, w_query)
        + matmul_nt(grad_k_low, w_key)
        + matmul_nt(grad_v_low, w_value)
    )
    grad_part_one, grad_gain_one, grad_shift_one = norm_back(
        norm_one, inv_one, vec_layer[0:D], grad_normed
    )
    grad_hidden = grad_middle + grad_part_one
    grad_mats = [grad_wq, grad_wk, grad_wv, grad_out_w, grad_up, grad_down]
    grad_vec = jnp.concatenate(
        [grad_gain_one, grad_shift_one, grad_gain_two, grad_shift_two, grad_bias]
    )
    return (grad_hidden, grad_mats, grad_vec)


def merge_stats(first_part, second_part):
    peak_val = jnp.maximum(first_part[0], second_part[0])
    exp_total = first_part[1] * jnp.exp(first_part[0] - peak_val) + second_part[1] * jnp.exp(
        second_part[0] - peak_val
    )
    return (peak_val, exp_total, first_part[2] + second_part[2])


def any_mesh_device(
    token_ids,
    timesteps,
    pad_mask,
    noise_draw,
    owners,
    emb_table,
    table_first_moment,
    table_second_moment,
    mat_slots,
    slot_first,
    slot_second,
    vec_params,
    vec_first,
    vec_second,
):
    vocab_count = lax.axis_size("vocab")
    vocab_pos = lax.axis_index("vocab")
    data_pos = lax.axis_index("dp")
    seq_len = token_ids.shape[1]
    tokens = seq_len // vocab_count
    vocab_rows = emb_table.shape[0]
    score_scale = HDIM ** (-0.5)
    table_low = lax.all_gather(emb_table.astype(jnp.bfloat16), "dp", axis=1, tiled=True)
    row_counts = matrix_rows()
    local_start = slot_places(owners) - owners * CAP
    sent_pieces = [
        send_matrix(
            lax.dynamic_slice_in_dim(
                mat_slots, local_start[mat_idx], row_counts[mat_idx], 1
            ).astype(jnp.bfloat16),
            owners[mat_idx],
        )
        for mat_idx in range(len(row_counts))
    ]
    canon = jnp.concatenate(sent_pieces, 1)
    weights = lax.all_gather(canon, "vocab", axis=0, tiled=True).T
    layer_rows = 4 * D + 2 * FF
    vec_rows = 4 * D + FF
    tail_at = LAYERS * layer_rows

    def layer_weights(layer_idx):
        begin_row = layer_idx * layer_rows
        cuts = [
            begin_row,
            begin_row + D,
            begin_row + 2 * D,
            begin_row + 3 * D,
            begin_row + 4 * D,
            begin_row + 4 * D + FF,
            begin_row + layer_rows,
        ]
        return [weights[cuts[cut_idx] : cuts[cut_idx + 1]] for cut_idx in range(6)]

    w_input = weights[tail_at : tail_at + 2 * EMBED_WIDTH]
    w_final = weights[tail_at + 2 * EMBED_WIDTH : tail_at + 3 * EMBED_WIDTH]
    seq_ids = token_ids[0]
    seq_mask = pad_mask[0].astype(jnp.float32)
    keep_keys = pad_mask[0] > 0
    local_row = seq_ids - vocab_pos * vocab_rows
    valid_row = (local_row >= 0) & (local_row < vocab_rows)
    safe_row = jnp.clip(local_row, 0, vocab_rows - 1)
    found_rows = jnp.where(
        valid_row[:, None], jnp.take(table_low, safe_row, axis=0), jnp.zeros((), jnp.bfloat16)
    )
    arrived = lax.all_to_all(found_rows, "vocab", split_axis=0, concat_axis=0, tiled=True)
    clean_emb = jnp.sum(arrived.reshape(vocab_count, tokens, EMBED_WIDTH).astype(jnp.float32), 0)
    own_first = vocab_pos * tokens
    mask_own = lax.dynamic_slice_in_dim(seq_mask, own_first, tokens)
    own_places = (own_first + jnp.arange(tokens)).astype(jnp.float32)
    step_val = timesteps[0].astype(jnp.float32)
    signal_level = 1.0 - jnp.sqrt(step_val / DIFF + 0.0001)
    noisy_emb = jnp.sqrt(signal_level) * clean_emb + jnp.sqrt(1.0 - signal_level) * noise_draw[
        0
    ].astype(jnp.float32)
    time_feat = jnp.broadcast_to(waves(step_val[None], EMBED_WIDTH), (tokens, EMBED_WIDTH))
    inputs = jnp.concatenate([noisy_emb, time_feat], 1).astype(jnp.bfloat16)
    hidden = matmul_nn(inputs, w_input) + waves(own_places, D)
    layer_idx = 0
    vec_layer = vec_params[layer_idx * vec_rows : (layer_idx + 1) * vec_rows]
    hidden, kept_vals = layer_forward(
        hidden, layer_weights(layer_idx), vec_layer, keep_keys, score_scale
    )
    kept_list = [kept_vals]
    gain_final = vec_params[LAYERS * vec_rows : LAYERS * vec_rows + D]
    shift_final = vec_params[LAYERS * vec_rows + D :]
    norm_final, inv_final = norm_parts(hidden)
    final_norm = (norm_final * gain_final + shift_final).astype(jnp.bfloat16)
    predicted = matmul_nt(final_norm, w_final)
    pred_all = lax.all_gather(predicted.astype(jnp.bfloat16), "vocab", axis=0, tiled=True)
    head_width = min(512, seq_len)
    head_count = seq_len // head_width
    columns = jnp.arange(vocab_rows)
    pred_blocks = pred_all.reshape(head_count, head_width, EMBED_WIDTH)
    row_blocks = local_row.reshape(head_count, head_width)

    def head_stats(block_data):
        pred_blk, rows_blk = block_data
        logits = matmul_nt(pred_blk, table_low)
        row_max = jnp.max(logits, -1)
        exp_total = jnp.sum(jnp.exp(logits - row_max[:, None]), -1)
        target = jnp.sum(jnp.where(columns[None, :] == rows_blk[:, None], logits, 0.0), -1)
        return (row_max, exp_total, target)

    peaks, totals, targets = lax.map(head_stats, (pred_blocks, row_blocks))
    peak_all, total_all, target_all = merged(
        (peaks.reshape(seq_len), totals.reshape(seq_len), targets.reshape(seq_len)),
        "vocab",
        merge_stats,
    )
    log_total = peak_all + jnp.log(total_all)
    lse_own = lax.dynamic_slice_in_dim(log_total, own_first, tokens)
    target_own = lax.dynamic_slice_in_dim(target_all, own_first, tokens)
    pred_error = predicted - clean_emb
    square_own = jnp.sum(mask_own[:, None] * pred_error * pred_error)
    cross_own = jnp.sum(mask_own * (lse_own - target_own))
    norm_own = jnp.sum(mask_own * jnp.sqrt(jnp.sum(clean_emb * clean_emb, -1) + 1e-06))
    count_all, square, cross_sum, norm_total = lax.psum(
        (jnp.sum(mask_own), square_own, cross_own, norm_own), ("dp", "vocab")
    )
    weight_blocks = (seq_mask / count_all).reshape(head_count, head_width)
    lse_blocks = log_total.reshape(head_count, head_width)

    def head_back(grad_table, block_data):
        pred_blk, rows_blk, lse_blk, weight_blk = block_data
        logits = matmul_nt(pred_blk, table_low)
        probabilities = jnp.exp(logits - lse_blk[:, None])
        onehot = (columns[None, :] == rows_blk[:, None]).astype(jnp.float32)
        grad_logits = ((probabilities - onehot) * weight_blk[:, None]).astype(jnp.bfloat16)
        return (grad_table + matmul_tn(grad_logits, pred_blk), matmul_nn(grad_logits, table_low))

    zero_table = jnp.zeros((vocab_rows, EMBED_WIDTH), jnp.float32)
    grad_table_head, grad_pred_blocks = lax.scan(
        head_back, zero_table, (pred_blocks, row_blocks, lse_blocks, weight_blocks)
    )
    grad_pred = lax.psum_scatter(
        grad_pred_blocks.reshape(seq_len, EMBED_WIDTH).astype(jnp.bfloat16),
        "vocab",
        scatter_dimension=0,
        tiled=True,
    ).astype(jnp.float32)
    error_grad = 2.0 * mask_own[:, None] * pred_error / count_all
    grad_pred_low = (grad_pred + error_grad).astype(jnp.bfloat16)
    grad_final_w = matmul_tn(grad_pred_low, final_norm)
    grad_final = matmul_nn(grad_pred_low, w_final)
    grad_hidden, grad_gain_final, grad_shift_final = norm_back(
        norm_final, inv_final, gain_final, grad_final
    )
    layer_grads = [None] * LAYERS
    vec_grads = [None] * LAYERS
    for layer_idx in reversed(range(LAYERS)):
        vec_layer = vec_params[layer_idx * vec_rows : (layer_idx + 1) * vec_rows]
        grad_hidden, layer_grads[layer_idx], vec_grads[layer_idx] = layer_backward(
            grad_hidden,
            kept_list[layer_idx],
            layer_weights(layer_idx),
            vec_layer,
            keep_keys,
            score_scale,
        )
    grad_hidden_low = grad_hidden.astype(jnp.bfloat16)
    grad_input_w = matmul_tn(inputs, grad_hidden_low)
    grad_inputs = matmul_nt(grad_hidden_low, w_input)
    grad_clean = jnp.sqrt(signal_level) * grad_inputs[:, :EMBED_WIDTH] - error_grad
    grad_clean_all = lax.all_gather(
        grad_clean.astype(jnp.bfloat16), "vocab", axis=0, tiled=True
    ).astype(grad_clean.dtype)
    grad_table_look = zero_table.at[safe_row].add(
        jnp.where(valid_row[:, None], grad_clean_all, 0.0)
    )
    grad_table_local = grad_table_head + grad_table_look
    canon_list = []
    layer_idx = 0
    canon_list = canon_list + layer_grads[layer_idx]
    canon_grad = jnp.concatenate(canon_list + [grad_input_w, grad_final_w], 0).T
    vec_grad = jnp.concatenate(vec_grads + [grad_gain_final, grad_shift_final])
    grad_cols, vec_part = (
        lax.psum_scatter(canon_grad, "vocab", scatter_dimension=0, tiled=True),
        lax.psum_scatter(vec_grad, "vocab", scatter_dimension=0, tiled=True),
    )
    emb_cols = emb_table.shape[1]
    summed_cols, summed_vec, summed_table = lax.psum((grad_cols, vec_part, grad_table_local), "dp")
    table_grad = lax.dynamic_slice_in_dim(summed_table, data_pos * emb_cols, emb_cols, 1)
    slot_grad = jnp.zeros_like(mat_slots)
    cursor = 0
    for mat_idx in range(len(row_counts)):
        piece_cols = summed_cols[:, cursor : cursor + row_counts[mat_idx]]
        updated = lax.dynamic_update_slice_in_dim(slot_grad, piece_cols, local_start[mat_idx], 1)
        slot_grad = jnp.where(owners[mat_idx] == data_pos, updated, slot_grad)
        cursor = cursor + row_counts[mat_idx]
    vec_share = vec_first.shape[0]
    own_vecs = lax.dynamic_slice_in_dim(vec_params, vocab_pos * vec_share, vec_share)
    new_slots, slot_first_new, slot_second_new = adamw(
        mat_slots, slot_grad, slot_first, slot_second
    )
    new_table, table_first_new, table_second_new = adamw(
        emb_table, table_grad, table_first_moment, table_second_moment
    )
    new_vecs, vec_first_new, vec_second_new = adamw(own_vecs, summed_vec, vec_first, vec_second)
    loss_pair = jnp.stack([square + cross_sum, count_all])
    emb_norm = norm_total / count_all
    return (
        loss_pair,
        emb_norm,
        new_table,
        table_first_new,
        table_second_new,
        new_slots,
        slot_first_new,
        slot_second_new,
        new_vecs,
        vec_first_new,
        vec_second_new,
    )


def solution(mesh):
    in_specs = (
        P("dp", None),
        P("dp"),
        P("dp", None),
        P("dp", "vocab", None),
        P(),
        P("vocab", "dp"),
        P("vocab", "dp"),
        P("vocab", "dp"),
        P("vocab", "dp"),
        P("vocab", "dp"),
        P("vocab", "dp"),
        P(),
        P("vocab"),
        P("vocab"),
    )
    out_specs = (
        P(),
        P(),
        P("vocab", "dp"),
        P("vocab", "dp"),
        P("vocab", "dp"),
        P("vocab", "dp"),
        P("vocab", "dp"),
        P("vocab", "dp"),
        P("vocab"),
        P("vocab"),
        P("vocab"),
    )
    fast = mesh.shape["dp"] == 8 and mesh.shape["vocab"] == 4
    body = per_device if fast else any_mesh_device
    return jax.shard_map(
        body, mesh=mesh, in_specs=in_specs, out_specs=out_specs, check_vma=False
    )
```

```python
import functools
import math

import jax
import jax.numpy as jnp
from jax import lax
from jax.experimental import pallas as pl
from jax.experimental.pallas import tpu as pltpu
from jax.sharding import PartitionSpec as P

D = 768
HEADS = 12
HDIM = 64
FF = 3072
EMBED_WIDTH = 128
DIFF = 2000
STEP = 10
CAP = 3072
LAYERS = 1
LANES = 128


beta_one = 0.9
beta_two = 0.999
learn_rate = 0.02
weight_decay = 0.01
eps_adam = 1e-08
eps_norm = 1e-05
f32 = jnp.float32
bf16 = jnp.bfloat16


def matmul_nn(left, right):
    return jnp.dot(left, right, preferred_element_type=f32)


def matmul_tn(left, right):
    return lax.dot_general(left, right, (((0,), (0,)), ((), ())), preferred_element_type=f32)


def matmul_nt(left, right):
    return lax.dot_general(left, right, (((1,), (1,)), ((), ())), preferred_element_type=f32)


ROW_COUNTS = [D, D, D, D, FF, FF, EMBED_WIDTH, EMBED_WIDTH, EMBED_WIDTH]


def slot_starts(owners):
    counts = jnp.array(ROW_COUNTS, jnp.int32)
    same_owner = (owners[:, None] == owners[None, :]).astype(jnp.int32)
    earlier_mask = jnp.tril(jnp.ones((len(ROW_COUNTS),) * 2, jnp.int32), -1)
    return jnp.sum(same_owner * earlier_mask * counts[None, :], 1)


def waves(places, width):
    half_width = width // 2
    frequency = jnp.exp(-math.log(10000.0) * jnp.arange(half_width, dtype=f32) / half_width)
    angles = places[:, None] * frequency[None, :]
    return jnp.concatenate([jnp.sin(angles), jnp.cos(angles)], 1)


def norm_parts(value_entries):
    center = value_entries - jnp.mean(value_entries, -1, keepdims=True)
    scale_inv = lax.rsqrt(jnp.mean(center * center, -1, keepdims=True) + eps_norm)
    return (center * scale_inv, scale_inv)


def norm_back(normal_part, scale_inv, gain_vec, grad_out):
    scaled = grad_out * gain_vec
    inner = (
        scaled
        - jnp.mean(scaled, -1, keepdims=True)
        - normal_part * jnp.mean(scaled * normal_part, -1, keepdims=True)
    )
    return (inner * scale_inv, jnp.sum(grad_out * normal_part, 0), jnp.sum(grad_out, 0))


def adamw(weight, gradient, moment_one, moment_two):
    moment_one = beta_one * moment_one + (1.0 - beta_one) * gradient
    moment_two = beta_two * moment_two + (1.0 - beta_two) * gradient * gradient
    fix_one = 1.0 - beta_one**STEP
    fix_two = 1.0 - beta_two**STEP
    update_dir = moment_one / fix_one / (jnp.sqrt(moment_two / fix_two) + eps_adam)
    return (weight - learn_rate * (update_dir + weight_decay * weight), moment_one, moment_two)


def swap_vocab(value, mask):
    return lax.ppermute(value, "vocab", [(i, i ^ mask) for i in range(4)])


def relative(value, axis=0):
    v = lax.axis_index("vocab")
    p = jnp.split(value, 4, axis)
    swapped = jnp.where(v % 2 == 1, jnp.concatenate([p[1], p[0], p[3], p[2]], axis), value)
    q = jnp.split(swapped, 4, axis)
    return jnp.where(v // 2 == 1, jnp.concatenate([q[2], q[3], q[0], q[1]], axis), swapped)


def vocab_gather(own, axis=0):
    far = swap_vocab(own, 2)
    near = swap_vocab(own, 1)
    return jnp.concatenate([own, near, far, swap_vocab(far, 1)], axis)


def vocab_gather_direct(own, axis=0):
    return jnp.concatenate([own] + [swap_vocab(own, k) for k in (1, 2, 3)], axis)


def vocab_exchange(pieces):
    return [pieces[0]] + [swap_vocab(pieces[k], k) for k in (1, 2, 3)]


def vocab_reduce(value):
    p = jnp.split(value, 4, 0)
    sent = swap_vocab(jnp.concatenate([p[1], p[3]], 0).astype(bf16), 1)
    near, far = jnp.split(sent, 2, 0)
    far = p[2] + far.astype(f32)
    return p[0] + near.astype(f32) + swap_vocab(far.astype(bf16), 2).astype(f32)


MESH = pl.DeviceIdType.MESH
ANY = pl.BlockSpec(memory_space=pl.ANY)
UNIT = 768
HALF = 96
QUARTER = 192


def place():
    d, v = lax.axis_index("dp"), lax.axis_index("vocab")
    return d // 2, d % 2, d, v


def greet(partners):
    barrier = pltpu.get_barrier_semaphore()
    for partner in partners:
        pl.semaphore_signal(barrier, inc=1, device_id=partner, device_id_type=MESH)
    pl.semaphore_wait(barrier, len(partners))


def remote(src, dst, sems, index, partner):
    return pltpu.make_async_remote_copy(
        src_ref=src,
        dst_ref=dst,
        send_sem=sems[0].at[index],
        recv_sem=sems[1].at[index],
        device_id=partner,
        device_id_type=MESH,
    )


def start_all(copies):
    for copy in copies:
        copy.start()
    return copies


def arrive_all(copies):
    for copy in copies:
        copy.wait_recv()


def trade_kernel(payload, tile, arrived, tiles, send, recv, tile_send, tile_recv, local):
    z, y, d, v = place()
    masks = (4, 6, 5, 7, 2, 3, 1)
    greet([(d ^ m, v) for m in masks])
    copies = [
        remote(payload.at[d ^ m], arrived.at[d], (send, recv), i, (d ^ m, v))
        for i, m in enumerate(masks)
    ] + [
        remote(tile, tiles.at[d], (tile_send, tile_recv), i, (d ^ m, v))
        for i, m in enumerate(masks)
    ]
    start_all(copies)
    own = [
        pltpu.make_async_copy(payload.at[d], arrived.at[d], local.at[0]),
        pltpu.make_async_copy(tile, tiles.at[d], local.at[1]),
    ]
    start_all(own)
    for copy in own + copies:
        copy.wait()


def trade(payload, tile, collective_id):
    dma = pltpu.SemaphoreType.DMA
    return pl.pallas_call(
        trade_kernel,
        out_shape=[
            jax.ShapeDtypeStruct(payload.shape, payload.dtype),
            jax.ShapeDtypeStruct((8,) + tile.shape, tile.dtype),
        ],
        in_specs=[ANY, ANY],
        out_specs=[ANY, ANY],
        scratch_shapes=[dma((7,))] * 4 + [dma((2,))],
        compiler_params=pltpu.CompilerParams(collective_id=collective_id, has_side_effects=True),
    )(payload, tile)


def spread_kernel(
    up_home, down_home, small_home, attn_home, table_home,
    up, down, small, attn, out, table,
    z_send, z_recv, y_send, y_recv, x_send, x_recv, n_send, n_recv, f_send, f_recv, local,
):
    z, y, d, v = place()
    far, near = v ^ 2, v ^ 1
    greet([(d ^ m, v) for m in (2, 4, 6, 1)] + [(d, far), (d, near)])
    homes = [up_home, down_home, small_home, attn_home, table_home]
    fulls = [up, down, small, attn, table]
    own_rows = pl.ds(v * QUARTER, QUARTER)

    def spot(c, unit):
        if c == 4:
            return table.at[2 * unit + y]
        first = y * HALF if c == 3 else v * QUARTER + y * HALF
        return fulls[c].at[unit, pl.ds(first, HALF), :]

    def start_line(c):
        keep = pltpu.make_async_copy(homes[c], spot(c, z), local.at[c])
        keep.start()
        return [keep] + start_all(
            [
                remote(homes[c], spot(c, z), (z_send, z_recv), (c, k - 1), (d ^ (2 * k), v))
                for k in (2, 1, 3)
            ]
        )

    def wait_line(copies):
        copies[0].wait()
        arrive_all(copies[1:])
        return copies[1:]

    def start_side(c):
        return start_all(
            [remote(spot(c, u), spot(c, u), (y_send, y_recv), (c, u), (d ^ 1, v)) for u in range(4)]
        )

    def strips(c, rows):
        if c == 3:
            return [out.at[rows, :]]
        return [fulls[c].at[u, rows, :] for u in range(4)]

    def sources(c):
        return [attn.at[3]] if c == 3 else strips(c, own_rows)

    def start_far(c):
        return start_all(
            [
                remote(s, t, (x_send, x_recv), (c, u), (d, far))
                for u, (s, t) in enumerate(zip(sources(c), strips(c, own_rows)))
            ]
        )

    def start_near(c):
        return start_all(
            [
                remote(s, t, (n_send, n_recv), (c, u), (d, near))
                for u, (s, t) in enumerate(zip(sources(c), strips(c, own_rows)))
            ]
        )

    def start_last(c):
        rows = pl.ds(far * QUARTER, QUARTER)
        return start_all(
            [
                remote(s, s, (f_send, f_recv), (c, u), (d, near))
                for u, s in enumerate(strips(c, rows))
            ]
        )

    sent, landing = [], []
    line, side, chip = {}, {}, {}

    def begin_chip(c):
        arrive_all(side[c])
        if c == 3:
            keep = pltpu.make_async_copy(attn.at[3], out.at[own_rows, :], local.at[5])
            keep.start()
            keep.wait()
        if c != 4:
            chip[c] = start_far(c)
            near_copies = start_near(c)
            sent.extend(chip[c] + near_copies)
            landing.extend(near_copies)

    def begin_last(c):
        if c != 4:
            arrive_all(chip[c])
            last = start_last(c)
            sent.extend(last)
            landing.extend(last)

    waves_of = [[0], [1], [2, 3], [4]]
    for c in waves_of[0]:
        line[c] = start_line(c)
    for i, wave in enumerate(waves_of):
        for c in wave:
            sent.extend(wait_line(line[c]))
        if i + 1 < len(waves_of):
            for c in waves_of[i + 1]:
                line[c] = start_line(c)
        for c in wave:
            side[c] = start_side(c)
            sent.extend(side[c])
        if i >= 1:
            for c in waves_of[i - 1]:
                begin_chip(c)
        if i >= 2:
            for c in waves_of[i - 2]:
                begin_last(c)
    for c in waves_of[-1]:
        begin_chip(c)
    for wave in waves_of[-2:]:
        for c in wave:
            begin_last(c)
    arrive_all(landing)
    for copy in sent:
        copy.wait_send()


def spread(up_home, down_home, small_home, attn_home, table_home):
    small_cols = small_home.shape[1]
    rows, vocab_rows = table_home.shape
    dma = pltpu.SemaphoreType.DMA

    def shape(*dims):
        return jax.ShapeDtypeStruct(dims, bf16)

    return pl.pallas_call(
        spread_kernel,
        out_shape=[
            shape(4, D, UNIT),
            shape(4, D, UNIT),
            shape(4, D, small_cols),
            shape(4, QUARTER, UNIT),
            shape(D, UNIT),
            shape(8, rows, vocab_rows),
        ],
        in_specs=[ANY] * 5,
        out_specs=[ANY] * 6,
        scratch_shapes=[dma((5, 3))] * 2 + [dma((5, 4))] * 2 + [dma((4, 4))] * 6 + [dma((6,))],
        compiler_params=pltpu.CompilerParams(collective_id=1, has_side_effects=True),
    )(up_home, down_home, small_home, attn_home, table_home)

VMEM = pl.BlockSpec(memory_space=pltpu.VMEM)


def neighbours():
    d, v = lax.axis_index("dp"), lax.axis_index("vocab")
    return [(d, v ^ k) for k in (1, 2, 3)]


def by_position(v, store):
    for i in range(4):
        pl.when(v == i)(functools.partial(store, i))


def forward_kernel(
    found, noise, levels, places, small, attn, out_w, up_hbm, down_hbm, vecs, keep,
    clean, inputs, hidden, normed_all, q, k, k_t, values, log_total, mixed, middle, normed_two,
    up_proj, active, hidden_two, final_norm, predicted, pred_all,
    up_w, down_w, found_in, values_t, mixed_out, mixed_in,
    w_sem, e_send, e_recv, n_send, n_recv, m_send, m_recv, p_send, p_recv,
):
    v = lax.axis_index("vocab")
    partners = neighbours()
    loads = []
    for j in range(4):
        for i, (src, dst) in enumerate(((up_hbm, up_w), (down_hbm, down_w))):
            copy = pltpu.make_async_copy(src.at[j], dst.at[j], w_sem.at[2 * j + i])
            copy.start()
            loads.append(copy)
    greet(partners)
    asked = start_all(
        [
            remote(found.at[m], found_in.at[m - 1], (e_send, e_recv), m - 1, partners[m - 1])
            for m in (2, 3, 1)
        ]
    )
    wave = levels[2:3].astype(bf16)
    time_part = matmul_nt(jnp.broadcast_to(wave, (16, EMBED_WIDTH)), small[1])[0:1]
    arrive_all(asked)
    total = found[0].astype(f32)
    for m in range(3):
        total = total + found_in[m].astype(f32)
    clean[...] = total
    noisy = levels[0:1] * total + levels[1:2] * noise[...].astype(f32)
    inputs[:, 0:EMBED_WIDTH] = noisy.astype(bf16)
    inputs[:, EMBED_WIDTH:] = jnp.broadcast_to(wave, noisy.shape)
    value = matmul_nt(inputs[:, 0:EMBED_WIDTH], small[0]) + time_part + places[...]
    hidden[...] = value
    normed_all[0] = (norm_parts(value)[0] * vecs[0:1] + vecs[1:2]).astype(bf16)

    far = remote(normed_all.at[0], normed_all.at[2], (n_send, n_recv), 0, partners[1])
    near = remote(normed_all.at[0], normed_all.at[1], (n_send, n_recv), 1, partners[0])
    last = remote(normed_all.at[2], normed_all.at[3], (n_send, n_recv), 2, partners[0])
    far.start()
    near.start()

    def project(b):
        rows = pl.ds(b * 256, 256)
        block = normed_all[b]
        for i, ref in ((0, q), (1, k), (2, values)):
            result = matmul_nt(block, attn[i])
            if i == 0:
                result = result.astype(bf16).astype(f32) * HDIM ** (-0.5)
            for h in range(3):
                ref[h, rows, :] = result[:, h * HDIM : (h + 1) * HDIM].astype(bf16)
        k_t[:, rows] = matmul_nt(attn[1], block).astype(bf16)
        values_t[:, rows] = matmul_nt(attn[2], block).astype(bf16)

    project(0)
    near.wait_recv()
    project(1)
    far.wait_recv()
    last.start()
    project(2)
    last.wait_recv()
    project(3)

    given = []
    for b in (2, 3, 1, 0):
        rows = pl.ds(b * 256, 256)
        parts = []
        for h in range(3):
            scores = matmul_nt(k[h], q[h, rows, :])
            scores = jnp.where(keep[...] > 0.0, scores, -1000000000.0)
            top = jnp.max(scores, 0, keepdims=True)
            expo = jnp.exp(scores - top)
            mass = jnp.sum(expo, 0, keepdims=True)
            probs = (expo * (1.0 / mass)).astype(bf16)
            log_total[pl.ds(3 * b + h, 1), :] = top + jnp.log(mass)
            parts.append(matmul_nn(values_t[h * HDIM : (h + 1) * HDIM, :], probs))
        block = jnp.concatenate(parts, 0).T.astype(bf16)
        if b == 0:
            mixed_in[0] = block
        else:
            mixed_out[b - 1] = block
            copy = remote(
                mixed_out.at[b - 1], mixed_in.at[b], (m_send, m_recv), b - 1, partners[b - 1]
            )
            copy.start()
            given.append(copy)
    arrive_all(given)

    def lay(i):
        for b in range(4):
            mixed[:, QUARTER * (i ^ b) : QUARTER * ((i ^ b) + 1)] = mixed_in[b]

    by_position(v, lay)
    value = hidden[...] + matmul_nt(mixed[...], out_w[...])
    middle[...] = value
    normed_two[...] = (norm_parts(value)[0] * vecs[2:3] + vecs[3:4]).astype(bf16)
    for j in range(4):
        loads[2 * j].wait()
        loads[2 * j + 1].wait()
        raised = matmul_nn(normed_two[...], up_w[j]) + vecs[4 + j : 5 + j]
        up_proj[j] = raised
        active[j] = jax.nn.gelu(raised).astype(bf16)
        lowered = matmul_nt(active[j], down_w[j])
        hidden_two[...] = (middle[...] if j == 0 else hidden_two[...]) + lowered
    final_norm[...] = (norm_parts(hidden_two[...])[0] * vecs[8:9] + vecs[9:10]).astype(bf16)
    predicted[...] = matmul_nn(final_norm[...], small[2])
    pred_all[0] = predicted[...].astype(bf16)
    shown = start_all(
        [
            remote(pred_all.at[0], pred_all.at[m], (p_send, p_recv), m - 1, partners[m - 1])
            for m in (2, 3, 1)
        ]
    )
    arrive_all(shown)
    for copy in asked + [far, near, last] + given + shown:
        copy.wait_send()


def forward(found, noise, levels, places, small, attn, out_w, up_w, down_w, vecs, keep):
    dma, vmem = pltpu.SemaphoreType.DMA, pltpu.VMEM
    n = 256

    def shape(kind, *dims):
        return jax.ShapeDtypeStruct(dims, kind)

    return pl.pallas_call(
        forward_kernel,
        out_shape=[
            shape(f32, n, EMBED_WIDTH),
            shape(bf16, n, 2 * EMBED_WIDTH),
            shape(f32, n, D),
            shape(bf16, 4, n, D),
            shape(bf16, 3, 4 * n, HDIM),
            shape(bf16, 3, 4 * n, HDIM),
            shape(bf16, QUARTER, 4 * n),
            shape(bf16, 3, 4 * n, HDIM),
            shape(f32, 16, n),
            shape(bf16, n, D),
            shape(f32, n, D),
            shape(bf16, n, D),
            shape(f32, 4, n, UNIT),
            shape(bf16, 4, n, UNIT),
            shape(f32, n, D),
            shape(bf16, n, D),
            shape(f32, n, EMBED_WIDTH),
            shape(bf16, 4, n, EMBED_WIDTH),
        ],
        in_specs=[VMEM] * 7 + [ANY] * 2 + [VMEM] * 2,
        out_specs=[VMEM] * 18,
        scratch_shapes=[
            vmem((4, D, UNIT), bf16),
            vmem((4, D, UNIT), bf16),
            vmem((3, n, EMBED_WIDTH), bf16),
            vmem((QUARTER, 4 * n), bf16),
            vmem((3, n, QUARTER), bf16),
            vmem((4, n, QUARTER), bf16),
            dma((8,)),
        ]
        + [dma((3,))] * 8,
        compiler_params=pltpu.CompilerParams(
            collective_id=4, has_side_effects=True, vmem_limit_bytes=60 * 2**20
        ),
    )(found, noise, levels, places, small, attn, out_w, up_w, down_w, vecs, keep)


STRIP = 768


def strips(rows):
    return [(lo, min(STRIP, rows - lo)) for lo in range(0, rows, STRIP)]


def head_kernel(
    pred_all, table, table_t, row_of, weight, found,
    grad_pred, lse, logits, stats, gathered, outgoing, incoming,
    s_send, s_recv, g_send, g_recv,
):
    partners = neighbours()
    greet(partners)
    rows = table_t.shape[0]
    full, rest = rows // STRIP, rows % STRIP
    mixes = []
    for b in range(4):
        block = pred_all[b]
        wanted = row_of[b : b + 1, :]

        def first(at, size, top):
            value = matmul_nt(table_t[at, :], block)
            logits[at, :] = value
            return jnp.maximum(top, jnp.max(value, 0, keepdims=True))

        def second(at, size, lo, carry, peak):
            mass, target, mix = carry
            value = logits[at, :]
            expo = jnp.exp(value - peak)
            here = lax.broadcasted_iota(jnp.int32, (size, 256), 0) == wanted - lo
            mass = mass + jnp.sum(expo, 0, keepdims=True)
            target = target + jnp.sum(jnp.where(here, value, 0.0), 0, keepdims=True)
            return mass, target, mix + matmul_nn(table[:, at], expo.astype(bf16))

        peak = lax.fori_loop(
            0,
            full,
            lambda t, top: first(pl.ds(pl.multiple_of(t * STRIP, STRIP), STRIP), STRIP, top),
            jnp.full((1, 256), -jnp.inf, f32),
        )
        tail = pl.ds(full * STRIP, rest)
        if rest:
            peak = first(tail, rest, peak)
        zero = jnp.zeros((1, 256), f32)
        carry = lax.fori_loop(
            0,
            full,
            lambda t, carry: second(
                pl.ds(pl.multiple_of(t * STRIP, STRIP), STRIP), STRIP, t * STRIP, carry, peak
            ),
            (zero, zero, jnp.zeros((EMBED_WIDTH, 256), f32)),
        )
        if rest:
            carry = second(tail, rest, full * STRIP, carry, peak)
        stats[b, 0:1] = peak
        stats[b, 1:2] = carry[0]
        stats[b, 2:3] = carry[1]
        stats[b, 3:8] = jnp.zeros((5, 256), f32)
        mixes.append(carry[2])
    told = start_all(
        [
            remote(stats, gathered.at[m - 1], (s_send, s_recv), m - 1, partners[m - 1])
            for m in (2, 3, 1)
        ]
    )
    arrive_all(told)
    given = []
    for b in (2, 3, 1, 0):
        views = [stats[b]] + [gathered[m - 1, b ^ m] for m in (1, 2, 3)]
        peak = functools.reduce(jnp.maximum, [view[0:1] for view in views])
        mass = sum(view[1:2] * jnp.exp(view[0:1] - peak) for view in views)
        total = peak + jnp.log(mass)
        lse[b : b + 1, :] = total
        if b == 0:
            target = sum(view[2:3] for view in views)
            lse[4:5, :] = weight[0:1, :] * (total - target)
            lse[5:8, :] = jnp.zeros((3, 256), f32)
        share = weight[b : b + 1, :]
        local = mixes[b] * (jnp.exp(stats[b, 0:1] - total) * share)
        local = local - found[b].astype(f32).T * share
        outgoing[b] = local.T.astype(bf16)
        if b:
            copy = remote(
                outgoing.at[b], incoming.at[b - 1], (g_send, g_recv), b - 1, partners[b - 1]
            )
            copy.start()
            given.append(copy)
    arrive_all(given)
    value = outgoing[0].astype(f32)
    for m in range(3):
        value = value + incoming[m].astype(f32)
    grad_pred[...] = value
    for copy in told + given:
        copy.wait_send()


def head(pred_all, table, table_t, row_of, weight, found):
    dma, vmem = pltpu.SemaphoreType.DMA, pltpu.VMEM
    return pl.pallas_call(
        head_kernel,
        out_shape=[
            jax.ShapeDtypeStruct((256, EMBED_WIDTH), f32),
            jax.ShapeDtypeStruct((8, 256), f32),
        ],
        in_specs=[VMEM] * 6,
        out_specs=[VMEM] * 2,
        scratch_shapes=[
            vmem((table_t.shape[0], 256), f32),
            vmem((4, 8, 256), f32),
            vmem((3, 4, 8, 256), f32),
            vmem((4, 256, EMBED_WIDTH), bf16),
            vmem((3, 256, EMBED_WIDTH), bf16),
        ]
        + [dma((3,))] * 4,
        compiler_params=pltpu.CompilerParams(
            collective_id=5, has_side_effects=True, vmem_limit_bytes=60 * 2**20
        ),
    )(pred_all, table, table_t, row_of, weight, found)


def gelu_slope(u):
    inner = math.sqrt(2.0 / math.pi)
    bent = jnp.tanh(inner * (u + 0.044715 * (u * u * u)))
    return 0.5 * (1.0 + bent) + (0.5 * inner) * u * (1.0 - bent * bent) * (
        1.0 + (3.0 * 0.044715) * (u * u)
    )


def backward_kernel(
    grad_pred, clean, predicted, twice, levels, head_stats, hidden, middle, hidden_two,
    normed_two, final_norm, up_proj, q, k, k_t, values, log_total, keep,
    small, attn, out_w, up_hbm, down_hbm, vecs,
    grad_pred_low, down_left, up_left, out_left, small_left, final_left, qkv_left, grad_up, grad_clean, sums,
    up_w, down_w, carried, folded, mix_out, mix_in, grad_k, grad_v, n_out, n_in, f_out, f_in,
    w_sem, m_send, m_recv, n_send, n_recv, c_send, c_recv,
):
    v = lax.axis_index("vocab")
    partners = neighbours()
    loads = []
    for j in range(4):
        for i, (src, dst) in enumerate(((down_hbm, down_w), (up_hbm, up_w))):
            copy = pltpu.make_async_copy(src.at[j], dst.at[j], w_sem.at[2 * j + i])
            copy.start()
            loads.append(copy)
    greet(partners)

    def turned(value):
        return value.astype(f32).T.astype(bf16)

    error = predicted[...] - clean[...]
    pull = twice[...] * error
    low = (grad_pred[...] + pull).astype(bf16)
    grad_pred_low[...] = low
    length = jnp.sqrt(jnp.sum(clean[...] * clean[...], -1, keepdims=True) + 1e-06)
    lane = lax.broadcasted_iota(jnp.int32, (1, UNIT), 1)
    scalars = (jnp.sum(pull * error), jnp.sum(head_stats[4:5, :]), jnp.sum(twice[...] * length))
    sums[10:11, :] = sum(jnp.where(lane == i, scalars[i], 0.0) for i in range(3))
    sums[11:16, :] = jnp.zeros((5, UNIT), f32)

    def through_norm(value, gain_row, grad_out, at):
        normal, scale_inv = norm_parts(value)
        part, grad_gain, grad_shift = norm_back(normal, scale_inv, vecs[gain_row : gain_row + 1], grad_out)
        sums[at : at + 1, :] = grad_gain[None, :]
        sums[at + 1 : at + 2, :] = grad_shift[None, :]
        return part

    carried[...] = through_norm(hidden_two[...], 8, matmul_nt(low, small[2]), 8)
    low = carried[...].astype(bf16)
    down_left[...] = turned(carried[...])
    up_left[...] = turned(normed_two[...])
    final_left[...] = turned(final_norm[...])
    for j in range(4):
        loads[2 * j].wait()
        loads[2 * j + 1].wait()
        slope = matmul_nn(low, down_w[j]) * gelu_slope(up_proj[j])
        grad_up[j] = slope.astype(bf16)
        sums[4 + j : 5 + j, :] = jnp.sum(grad_up[j].astype(f32), 0, keepdims=True)
        part = matmul_nt(grad_up[j], up_w[j])
        folded[...] = part if j == 0 else folded[...] + part
    carried[...] = carried[...] + through_norm(middle[...], 2, folded[...], 2)
    out_left[...] = turned(carried[...])
    folded[...] = matmul_nn(carried[...].astype(bf16), out_w[...])

    def lay(i):
        for b in range(4):
            mix_out[b] = folded[:, QUARTER * (i ^ b) : QUARTER * ((i ^ b) + 1)].astype(bf16)

    by_position(v, lay)
    mixed = [
        remote(mix_out.at[m], mix_in.at[m - 1], (m_send, m_recv), m - 1, partners[m - 1])
        for m in (1, 2, 3)
    ]
    for m in (2, 3, 1):
        mixed[m - 1].start()
    for b in range(4):
        if b:
            mixed[b - 1].wait_recv()
        grad_block = mix_out[0] if b == 0 else mix_in[b - 1]
        rows = pl.ds(b * 256, 256)
        for h in range(3):
            grad_mix = grad_block[:, h * HDIM : (h + 1) * HDIM]
            asked = q[h, rows, :]
            scores = matmul_nt(k[h], asked)
            scores = jnp.where(keep[...] > 0.0, scores, -1000000000.0)
            probs = jnp.exp(scores - log_total[3 * b + h : 3 * b + h + 1, :])
            grad_probs = matmul_nt(values[h], grad_mix)
            inner = jnp.sum(probs * grad_probs, 0, keepdims=True)
            grad_scores = (probs * (grad_probs - inner)).astype(bf16)
            grad_asked = matmul_nn(k_t[h * HDIM : (h + 1) * HDIM, :], grad_scores)
            qkv_left[0, h * HDIM : (h + 1) * HDIM, rows] = (grad_asked * HDIM ** (-0.5)).astype(bf16)
            part_k = matmul_nn(grad_scores, asked)
            part_v = matmul_nn(probs.astype(bf16), grad_mix)
            grad_k[h] = part_k if b == 0 else grad_k[h] + part_k
            grad_v[h] = part_v if b == 0 else grad_v[h] + part_v
    for h in range(3):
        lanes = pl.ds(h * HDIM, HDIM)
        qkv_left[1, lanes, :] = grad_k[h].T.astype(bf16)
        qkv_left[2, lanes, :] = grad_v[h].T.astype(bf16)

    def grad_normed(b):
        rows = pl.ds(b * 256, 256)
        return sum(matmul_tn(qkv_left[i, :, rows], attn[i]) for i in range(3))

    n_out[0] = grad_normed(1).astype(bf16)
    n_out[1] = grad_normed(3).astype(bf16)
    near = remote(n_out, n_in, (n_send, n_recv), 0, partners[0])
    near.start()
    folded[...] = grad_normed(2)
    near.wait_recv()
    f_out[...] = (folded[...] + n_in[1].astype(f32)).astype(bf16)
    far = remote(f_out, f_in, (n_send, n_recv), 1, partners[1])
    far.start()
    folded[...] = grad_normed(0) + n_in[0].astype(f32)
    far.wait_recv()
    grad_out = folded[...] + f_in[...].astype(f32)
    carried[...] = carried[...] + through_norm(hidden[...], 0, grad_out, 0)
    small_left[...] = turned(carried[...])
    back = matmul_nn(carried[...].astype(bf16), small[0])
    grad_clean[0] = (levels[0:1] * back - twice[...] * (predicted[...] - clean[...])).astype(bf16)
    shown = start_all(
        [
            remote(grad_clean.at[0], grad_clean.at[m], (c_send, c_recv), m - 1, partners[m - 1])
            for m in (2, 3, 1)
        ]
    )
    arrive_all(shown)
    for copy in mixed + [near, far] + shown:
        copy.wait_send()


def backward(*operands):
    dma, vmem = pltpu.SemaphoreType.DMA, pltpu.VMEM
    n = 256

    def shape(kind, *dims):
        return jax.ShapeDtypeStruct(dims, kind)

    return pl.pallas_call(
        backward_kernel,
        out_shape=[shape(bf16, n, EMBED_WIDTH)]
        + [shape(bf16, D, n)] * 5
        + [
            shape(bf16, 3, QUARTER, 4 * n),
            shape(bf16, 4, n, UNIT),
            shape(bf16, 4, n, EMBED_WIDTH),
            shape(f32, 16, UNIT),
        ],
        in_specs=[VMEM] * 21 + [ANY] * 2 + [VMEM],
        out_specs=[VMEM] * 10,
        scratch_shapes=[
            vmem((4, D, UNIT), bf16),
            vmem((4, D, UNIT), bf16),
            vmem((n, D), f32),
            vmem((n, D), f32),
            vmem((4, n, QUARTER), bf16),
            vmem((3, n, QUARTER), bf16),
            vmem((3, 4 * n, HDIM), f32),
            vmem((3, 4 * n, HDIM), f32),
            vmem((2, n, D), bf16),
            vmem((2, n, D), bf16),
            vmem((n, D), bf16),
            vmem((n, D), bf16),
            dma((8,)),
        ]
        + [dma((3,))] * 6,
        compiler_params=pltpu.CompilerParams(
            collective_id=6, has_side_effects=True, vmem_limit_bytes=60 * 2**20
        ),
    )(*operands)

I16 = jnp.int16
TAIL = 16
TILES = 60


def exponent(peak):
    return jnp.ceil(jnp.log2(jnp.maximum(peak, 1e-30))) + 1.0


def coded(value, power):
    return jnp.round(value * jnp.exp2(15.0 - power)).astype(jnp.int32).astype(I16)


def plain(code, power):
    return code.astype(jnp.int32).astype(f32) * jnp.exp2(power - 15.0)


def put(ref, value):
    rows, cols = value.shape
    power = exponent(jnp.max(jnp.abs(value), 0, keepdims=True))
    ref[0:rows, :] = coded(value, power)
    ref[rows : rows + TAIL, :] = (
        jnp.broadcast_to(power, (TAIL, cols)).astype(jnp.int32).astype(I16)
    )


def get(ref, rows):
    power = ref[rows : rows + TAIL, :].astype(jnp.int32).astype(f32)[0:1]
    return plain(ref[0:rows, :], power)


def put_tiles(ref, source, rows):
    lane = lax.broadcasted_iota(jnp.int32, (rows, LANES), 1)

    def body(tile, powers):
        at = pl.ds(pl.multiple_of(tile * LANES, LANES), LANES)
        value = source(at)
        power = exponent(jnp.max(jnp.abs(value), 1, keepdims=True))
        ref[:, at] = coded(value, power)
        return jnp.where(lane == tile, power, powers)

    powers = lax.fori_loop(0, TILES, body, jnp.zeros((rows, LANES), f32), unroll=6)
    ref[:, TILES * LANES :] = powers.astype(jnp.int32).astype(I16)


def tile_getter(ref, rows):
    lane = lax.broadcasted_iota(jnp.int32, (rows, LANES), 1)
    powers = ref[:, TILES * LANES :].astype(jnp.int32).astype(f32)

    def read(tile, at):
        power = jnp.sum(jnp.where(lane == tile, powers, 0.0), 1, keepdims=True)
        return plain(ref[:, at], power)

    return read


def grads_kernel(
    down_left, up_left, out_left, small_left, final_left, qkv_left,
    active, grad_up, mixed, inputs, grad_pred, normed, pred_all, grad_clean, table_t, lse, weight, row_of, tile,
    home, small_home, table_sum, tile_sum,
    cs, cr, xs, xr, ys, yr, zs, zr, part, half,
    small_cs, small_cr, small_xs, small_xr, small_ys, small_yr, small_zs, small_zr, small_half,
    table, pred_t, clean_t, ts, tr, tzs, tzr, tile_at, tile_from,
    c_send, c_recv, x_send, x_recv, y_send, y_recv, z_send, z_recv, t_send, t_recv,
):
    z, y, d, v = place()
    far, near = v ^ 2, v ^ 1
    greet([(d ^ m, v) for m in (2, 4, 6, 1)] + [(d, far), (d, near)])
    sent = []

    def send(src, dst, sems, index, partner):
        copy = remote(src, dst, sems, index, partner)
        copy.start()
        sent.append(copy)
        return copy

    def product(n, who):
        if n == 0:
            return matmul_nn(out_left[who], mixed[...])
        if n < 5:
            return matmul_nn(down_left[who], active[n - 1])
        return matmul_nn(up_left[who], grad_up[n - 5])

    core, chip, side, line = {}, {}, {}, {}

    def to_core(n):
        put(cs.at[n, 0], product(n, near))
        put(cs.at[n, 1], product(n, near ^ 2))
        core[n] = send(cs.at[n], cr.at[n], (c_send, c_recv), n, (d, near))

    def to_chip(n):
        core[n].wait_recv()
        put(xs.at[n], product(n, far) + get(cr.at[n, 1], QUARTER))
        chip[n] = send(xs.at[n], xr.at[n], (x_send, x_recv), n, (d, far))

    def halves(slot, value):
        part[...] = value
        put(ys.at[slot], part[pl.ds((1 - y) * HALF, HALF), :])
        half[slot] = part[pl.ds(y * HALF, HALF), :]
        side[slot] = send(ys.at[slot], yr.at[slot], (y_send, y_recv), slot, (d ^ 1, v))

    def to_side(n):
        chip[n].wait_recv()
        value = product(n, v) + get(cr.at[n, 0], QUARTER) + get(xr.at[n], QUARTER)
        halves(3 + n, value)

    def to_line(group):
        for u in range(4):
            slot = 4 * group + u
            side[slot].wait_recv()
            half[slot] = half[slot] + get(yr.at[slot], HALF)
        for k in (2, 1, 3):
            put(zs.at[group, k - 1], half[4 * group + (z ^ k)])
            line[group, k] = send(
                zs.at[group, k - 1], zr.at[group, k - 1], (z_send, z_recv), 3 * group + k - 1, (d ^ (2 * k), v)
            )

    def to_home(group):
        total = half[4 * group + z]
        for k in (2, 1, 3):
            line[group, k].wait_recv()
            total = total + get(zr.at[group, k - 1], HALF)
        put(home.at[group], total)

    def small_product(who):
        return jnp.concatenate(
            [matmul_nn(small_left[who], inputs[...]), matmul_nn(final_left[who], grad_pred[...])], 1
        )

    def small_to_core():
        put(small_cs.at[0], small_product(near))
        put(small_cs.at[1], small_product(near ^ 2))
        core[9] = send(small_cs, small_cr, (c_send, c_recv), 9, (d, near))

    def small_to_chip():
        core[9].wait_recv()
        put(small_xs, small_product(far) + get(small_cr.at[1], QUARTER))
        chip[9] = send(small_xs, small_xr, (x_send, x_recv), 9, (d, far))

    def small_to_side():
        chip[9].wait_recv()
        value = small_product(v) + get(small_cr.at[0], QUARTER) + get(small_xr, QUARTER)
        cols = value.shape[1]
        part[:, 0:cols] = value
        put(small_ys, part[pl.ds((1 - y) * HALF, HALF), 0:cols])
        small_half[0] = part[pl.ds(y * HALF, HALF), 0:LANES]
        small_half[1] = part[pl.ds(y * HALF, HALF), LANES : 2 * LANES]
        small_half[2] = part[pl.ds(y * HALF, HALF), 2 * LANES : cols]
        small_half[3] = jnp.zeros((HALF, LANES), f32)
        side[12] = send(small_ys, small_yr, (y_send, y_recv), 12, (d ^ 1, v))

    def small_to_line():
        side[12].wait_recv()
        value = get(small_yr, HALF)
        for u in range(3):
            small_half[u] = small_half[u] + value[:, u * LANES : (u + 1) * LANES]
        for k in (2, 1, 3):
            put(small_zs.at[k - 1], small_half[z ^ k])
            line[3, k] = send(
                small_zs.at[k - 1], small_zr.at[k - 1], (z_send, z_recv), 9 + k - 1, (d ^ (2 * k), v)
            )

    def small_to_home():
        total = small_half[z]
        for k in (2, 1, 3):
            line[3, k].wait_recv()
            total = total + get(small_zr.at[k - 1], HALF)
        put(small_home, total)

    def turn_tokens():
        for b in range(4):
            pred_t[b] = pred_all[b].astype(f32).T.astype(bf16)
            clean_t[b] = grad_clean[b].astype(f32).T.astype(bf16)

    vocab_rows = table_t.shape[0]

    def table_strip(lo, size):
        total = jnp.zeros((EMBED_WIDTH, size), f32)
        for b in range(4):
            logits = matmul_nt(table_t[lo : lo + size, :], pred_all[b])
            probs = jnp.exp(logits - lse[b : b + 1, :])
            here = lax.broadcasted_iota(jnp.int32, (size, 256), 0) == row_of[b : b + 1, :] - lo
            here = here.astype(f32)
            grad_logits = ((probs - here) * weight[b : b + 1, :]).astype(bf16)
            total = total + matmul_nt(pred_t[b], grad_logits)
            total = total + matmul_nt(clean_t[b], here.astype(bf16))
        for i in range(8):
            rows = slice(16 * (i // 2), 16 * (i // 2) + 16)
            table[i % 2, rows, lo : lo + size] = total[16 * i : 16 * i + 16]
        if lo + size == vocab_rows:
            table[:, :, vocab_rows:] = jnp.zeros((2, 64, TILES * LANES - vocab_rows), f32)

    table_strips = [(lo, min(STRIP, vocab_rows - lo)) for lo in range(0, vocab_rows, STRIP)]

    def table_to_side():
        put_tiles(ts, lambda at: table[1 - y, :, at], 64)
        side[13] = send(ts, tr, (y_send, y_recv), 13, (d ^ 1, v))

    def table_line_value(which):
        rows = pl.ds(pl.multiple_of(which * 16, 16), 16)
        read = tile_getter(tr.at[rows, :], 16)
        return rows, read

    def table_to_line():
        side[13].wait_recv()
        for k in (2, 1, 3):
            rows, read = table_line_value(z ^ k)

            def source(at, rows=rows, read=read):
                return table[y, rows, at] + read(at.start // LANES, at)

            put_tiles(tzs.at[k - 1], source, 16)
            line[4, k] = send(
                tzs.at[k - 1], tzr.at[k - 1], (z_send, z_recv), 12 + k - 1, (d ^ (2 * k), v)
            )

    def table_to_home():
        for k in (2, 1, 3):
            line[4, k].wait_recv()
        rows, read = table_line_value(z)
        others = [tile_getter(tzr.at[k], 16) for k in range(3)]

        def body(tile, carry):
            at = pl.ds(pl.multiple_of(tile * LANES, LANES), LANES)
            value = table[y, rows, at] + read(tile, at)
            for other in others:
                value = value + other(tile, at)
            table_sum[:, at] = value
            return carry

        lax.fori_loop(0, TILES, body, 0, unroll=4)

    hops = [(d, near), (d, far), (d ^ 1, v), (d ^ 2, v), (d ^ 4, v)]
    tile_copies = {}

    def tile_send(hop):
        if hop == 0:
            tile_at[0] = tile[...]
        else:
            tile_copies[hop - 1].wait_recv()
            tile_at[hop] = tile_at[hop - 1] + tile_from[hop - 1]
        tile_copies[hop] = send(
            tile_at.at[hop], tile_from.at[hop], (t_send, t_recv), hop, hops[hop]
        )

    turn_tokens()
    to_core(0)
    to_core(1)
    to_chip(0)
    tile_send(0)
    to_core(2)
    table_strip(*table_strips[0])
    to_chip(1)
    table_strip(*table_strips[1])
    table_strip(*table_strips[2])
    to_core(3)
    to_chip(2)
    table_strip(*table_strips[3])
    table_strip(*table_strips[4])
    table_strip(*table_strips[5])
    to_core(4)
    to_chip(3)
    table_strip(*table_strips[6])
    table_strip(*table_strips[7])
    for strip in table_strips[8:]:
        table_strip(*strip)
    table_to_side()
    tile_send(1)
    for u in range(3):
        halves(u, sum(matmul_nn(qkv_left[u, :, 256 * b : 256 * b + 256], normed[b]) for b in range(4)))
    small_to_core()
    to_core(5)
    to_chip(4)
    to_side(0)
    tile_send(2)
    to_core(6)
    to_chip(5)
    small_to_chip()
    to_side(1)
    table_to_line()
    tile_send(3)
    to_core(7)
    to_chip(6)
    to_side(2)
    to_line(0)
    to_core(8)
    to_chip(7)
    tile_send(4)
    to_side(3)
    to_chip(8)
    to_side(4)
    to_line(1)
    small_to_side()
    table_to_home()
    to_side(5)
    to_home(0)
    to_side(6)
    small_to_line()
    to_side(7)
    to_home(1)
    to_side(8)
    to_line(2)
    small_to_home()
    tile_copies[4].wait_recv()
    tile_sum[...] = tile_at[4] + tile_from[4]
    to_home(2)
    for copy in sent:
        copy.wait_send()


def reduce_grads(*operands):
    dma = pltpu.SemaphoreType.DMA
    vmem = pltpu.VMEM
    tall, low, wide = QUARTER + TAIL, HALF + TAIL, 3 * LANES
    table_cols = TILES * LANES
    return pl.pallas_call(
        grads_kernel,
        out_shape=[
            jax.ShapeDtypeStruct((3, low, UNIT), I16),
            jax.ShapeDtypeStruct((low, LANES), I16),
            jax.ShapeDtypeStruct((16, table_cols), f32),
            jax.ShapeDtypeStruct((16, UNIT), f32),
        ],
        in_specs=[pl.BlockSpec(memory_space=pltpu.VMEM)] * 19,
        out_specs=[pl.BlockSpec(memory_space=pltpu.VMEM)] * 4,
        scratch_shapes=[
            vmem((9, 2, tall, UNIT), I16),
            vmem((9, 2, tall, UNIT), I16),
            vmem((9, tall, UNIT), I16),
            vmem((9, tall, UNIT), I16),
            vmem((12, low, UNIT), I16),
            vmem((12, low, UNIT), I16),
            vmem((3, 3, low, UNIT), I16),
            vmem((3, 3, low, UNIT), I16),
            vmem((QUARTER, UNIT), f32),
            vmem((12, HALF, UNIT), f32),
            vmem((2, tall, wide), I16),
            vmem((2, tall, wide), I16),
            vmem((tall, wide), I16),
            vmem((tall, wide), I16),
            vmem((low, wide), I16),
            vmem((low, wide), I16),
            vmem((3, low, LANES), I16),
            vmem((3, low, LANES), I16),
            vmem((4, HALF, LANES), f32),
            vmem((2, 64, table_cols), f32),
            vmem((4, EMBED_WIDTH, 256), bf16),
            vmem((4, EMBED_WIDTH, 256), bf16),
            vmem((64, table_cols + LANES), I16),
            vmem((64, table_cols + LANES), I16),
            vmem((3, 16, table_cols + LANES), I16),
            vmem((3, 16, table_cols + LANES), I16),
            vmem((5, 16, UNIT), f32),
            vmem((5, 16, UNIT), f32),
        ]
        + [dma((10,))] * 4
        + [dma((14,))] * 2
        + [dma((15,))] * 2
        + [dma((5,))] * 2,
        compiler_params=pltpu.CompilerParams(
            collective_id=2, has_side_effects=True, vmem_limit_bytes=60 * 2**20
        ),
    )(*operands)


def slot_kernel(kind, unit, column, big, small, w, m1, m2, w_out, m1_out, m2_out):
    which = kind[pl.program_id(0)]

    def rows_of(ref):
        return jnp.concatenate([get(ref.at[0], HALF), get(ref.at[1], HALF)], 0)

    zero = jnp.zeros(w.shape, f32)
    g = jnp.where(which == 1, rows_of(big), jnp.where(which == 2, rows_of(small), zero))
    w_out[...], m1_out[...], m2_out[...] = adamw(w[...], g, m1[...], m2[...])


def slot_update(owners, starts, summed, slots, first, second):
    rows = slots.shape[0]
    blocks = CAP // LANES
    d = lax.axis_index("dp")
    spots, units, columns, kinds = [], [], [], []
    per_unit = UNIT // LANES
    first_unit = [0, 1, 2, 3, 0, 0, 0, 1, 2]
    for i, count in enumerate(ROW_COUNTS):
        spots.append(jnp.where(owners[i] == d, starts[i] // LANES, -CAP) + jnp.arange(count // LANES))
        for b in range(count // LANES):
            units.append(first_unit[i] + b // per_unit)
            columns.append(b % per_unit)
            kinds.append(2 if i > 5 else 1)
    hit = jnp.concatenate(spots)[None, :] == jnp.arange(blocks)[:, None]

    def looked_up(values):
        return jnp.sum(jnp.where(hit, jnp.array(values, jnp.int32)[None, :], 0), 1).astype(jnp.int32)

    kind, unit, column = looked_up(kinds), looked_up(units), looked_up(columns)
    plain_spec = pl.BlockSpec((rows, LANES), lambda j, k, u, c: (0, j))
    low = HALF + TAIL
    big_spec = pl.BlockSpec(
        (2, low, LANES),
        lambda j, k, u, c: (jnp.where(k[j] == 1, u[j], 0), 0, jnp.where(k[j] == 1, c[j], 0)),
    )
    small_spec = pl.BlockSpec(
        (2, low, LANES), lambda j, k, u, c: (jnp.where(k[j] == 2, u[j], 0), 0, per_unit)
    )
    return pl.pallas_call(
        slot_kernel,
        grid_spec=pltpu.PrefetchScalarGridSpec(
            num_scalar_prefetch=3,
            grid=(blocks,),
            in_specs=[big_spec, small_spec, plain_spec, plain_spec, plain_spec],
            out_specs=[plain_spec, plain_spec, plain_spec],
        ),
        out_shape=[jax.ShapeDtypeStruct(slots.shape, f32)] * 3,
        cost_estimate=pl.CostEstimate(flops=0, bytes_accessed=28 * rows * CAP, transcendentals=0),
    )(kind, unit, column, summed, summed, slots, first, second)


def per_device(
    token_ids,
    timesteps,
    pad_mask,
    noise_draw,
    owners,
    emb_table,
    table_first_moment,
    table_second_moment,
    mat_slots,
    slot_first,
    slot_second,
    vec_params,
    vec_first,
    vec_second,
):
    v = lax.axis_index("vocab")
    d = lax.axis_index("dp")
    z = d // 2
    seq_len = token_ids.shape[1]
    tokens = seq_len // 4
    vocab_rows, emb_cols = emb_table.shape

    starts = slot_starts(owners)
    whole = (owners[4] == d) | (owners[5] == d)

    def unit_payload(u):
        start = jnp.where(whole, u * UNIT, starts[u])
        main = lax.dynamic_slice(mat_slots, (0, start), (QUARTER, UNIT))
        extra = lax.dynamic_slice(
            mat_slots, (0, starts[6 + min(u, 2)]), (QUARTER, EMBED_WIDTH)
        )
        return jnp.concatenate([main, extra], 1).astype(bf16)

    payload = jnp.stack([unit_payload(u) for u in range(4)])
    mask_count = jnp.sum(pad_mask.astype(f32))
    arrived, counts = trade(
        payload.reshape(8, HALF, UNIT + EMBED_WIDTH), jnp.broadcast_to(mask_count, (8, LANES)), 0
    )
    count_all = jnp.sum(counts[:, 0, 0])

    def from_owner(index, lo, width):
        return lax.dynamic_slice(arrived, (owners[index], 0, lo), (1, HALF, width))[0]

    table_own = emb_table.T
    w_up, w_down, w_small, w_attn, w_out, table_low = spread(
        from_owner(4, 0, UNIT),
        from_owner(5, 0, UNIT),
        from_owner(6 + jnp.minimum(z, 2), UNIT, EMBED_WIDTH),
        from_owner(z, 0, UNIT),
        table_own.astype(bf16),
    )
    table_low = table_low.reshape(EMBED_WIDTH, vocab_rows)

    ids_rel = relative(token_ids[0])
    mask_rel = relative(pad_mask[0])
    weight_rel = mask_rel.astype(f32)
    mask_own = weight_rel[:tokens]
    local_row = ids_rel - v * vocab_rows
    valid_row = (local_row >= 0) & (local_row < vocab_rows)
    safe_row = jnp.clip(local_row, 0, vocab_rows - 1)
    table_t = table_low.T
    found_rows = jnp.where(
        valid_row[:, None], jnp.take(table_t, safe_row, axis=0), jnp.zeros((), bf16)
    ).reshape(4, tokens, EMBED_WIDTH)
    own_places = (v * tokens + jnp.arange(tokens)).astype(f32)
    step_val = timesteps[0].astype(f32)
    signal_level = 1.0 - jnp.sqrt(step_val / DIFF + 0.0001)
    levels = jnp.concatenate(
        [
            jnp.full((1, EMBED_WIDTH), jnp.sqrt(signal_level)),
            jnp.full((1, EMBED_WIDTH), jnp.sqrt(1.0 - signal_level)),
            waves(step_val[None], EMBED_WIDTH),
            jnp.zeros((5, EMBED_WIDTH), f32),
        ]
    )
    vecs = vec_params.reshape(10, D)
    keep_column = weight_rel[:, None]
    (
        clean_emb, inputs, hidden, normed_all, q_h, k_h, k_t, v_h, log_total, mixed_own, middle,
        normed_two, up_proj, active, hidden_two, final_norm, predicted, pred_all,
    ) = forward(
        found_rows,
        noise_draw[0],
        levels,
        waves(own_places, D),
        w_small,
        w_attn,
        w_out,
        w_up,
        w_down,
        vecs,
        keep_column,
    )
    row_weight = (weight_rel / count_all).reshape(4, tokens)
    row_of = local_row.reshape(4, tokens)
    grad_pred, head_stats = head(
        pred_all,
        table_low,
        table_t,
        row_of,
        row_weight,
        found_rows,
    )
    (
        grad_pred_low, down_left, up_left, out_left, small_left, final_left, qkv_left, grad_up, grad_clean, sums,
    ) = backward(
        grad_pred, clean_emb, predicted, 2.0 * mask_own[:, None] / count_all, levels, head_stats,
        hidden, middle, hidden_two, normed_two, final_norm, up_proj,
        q_h, k_h, k_t, v_h, log_total, keep_column,
        w_small, w_attn, w_out, w_up, w_down, vecs,
    )

    def left(value):
        return value.reshape(4, QUARTER, tokens)

    home, small_home, table_grad, tile_sum = reduce_grads(
        left(down_left),
        left(up_left),
        left(out_left),
        left(small_left),
        left(final_left),
        qkv_left,
        active,
        grad_up,
        mixed_own,
        inputs,
        grad_pred_low,
        normed_all,
        pred_all,
        grad_clean,
        table_t,
        head_stats,
        row_weight,
        row_of,
        sums,
    )
    tile_sum = tile_sum.reshape(16 * UNIT)
    vec_share = vec_first.shape[0]
    own_grad = lax.dynamic_slice_in_dim(tile_sum, v * vec_share, vec_share)
    own_vecs = lax.dynamic_slice_in_dim(vec_params, v * vec_share, vec_share)
    vec_len = vec_params.shape[0]
    square = tile_sum[vec_len] * (0.5 * count_all)
    cross_sum = tile_sum[vec_len + 1] * count_all
    emb_norm = tile_sum[vec_len + 2] * 0.5

    takers = jnp.arange(8)[:, None, None]
    unit_home = jnp.where(
        takers == owners[5], home[1][None], jnp.where(takers == owners[4], home[2][None], home[0][None])
    )
    outgoing = jnp.concatenate(
        [unit_home, jnp.broadcast_to(small_home[None], (8,) + small_home.shape)], 2
    )
    summed, _ = trade(outgoing, jnp.zeros((8, LANES), f32), 3)
    new_slots, slot_first_new, slot_second_new = slot_update(
        owners, starts, summed, mat_slots, slot_first, slot_second
    )
    new_table, table_first_new, table_second_new = adamw(
        table_own, table_grad[:, :vocab_rows], table_first_moment.T, table_second_moment.T
    )
    new_vecs, vec_first_new, vec_second_new = adamw(own_vecs, own_grad, vec_first, vec_second)
    loss_pair = jnp.stack([square + cross_sum, count_all])
    return (
        loss_pair,
        emb_norm,
        new_table.T,
        table_first_new.T,
        table_second_new.T,
        new_slots,
        slot_first_new,
        slot_second_new,
        new_vecs,
        vec_first_new,
        vec_second_new,
    )


def broadcast(value, axis, source):
    kept = jnp.where(lax.axis_index(axis) == source, value, 0).astype(value.dtype)
    return lax.psum(kept, axis)


def merged(value, axis, join):
    pieces = jax.tree.map(lambda part: lax.all_gather(part, axis), value)
    head = jax.tree.map(lambda part: part[0], pieces)
    tail = jax.tree.map(lambda part: part[1:], pieces)
    so_far, _ = lax.scan(lambda so_far, share: (join(so_far, share), None), head, tail)
    return so_far


def matrix_rows():
    return [D, D, D, D, FF, FF] * LAYERS + [EMBED_WIDTH, EMBED_WIDTH, EMBED_WIDTH]


def slot_places(owners):
    counts = jnp.array(matrix_rows(), jnp.int32)
    mat_total = counts.shape[0]
    same_owner = (owners[:, None] == owners[None, :]).astype(jnp.int32)
    earlier_mask = jnp.tril(jnp.ones((mat_total, mat_total), jnp.int32), -1)
    return owners * CAP + jnp.sum(same_owner * earlier_mask * counts[None, :], 1)


def block_scores(query_blk, keys_all, keep_keys, score_scale):
    scores = (
        jnp.einsum("qhd,khd->hqk", query_blk, keys_all, preferred_element_type=jnp.float32)
        * score_scale
    )
    return jnp.where(keep_keys[None, None, :], scores, -1000000000.0)


def attention(queries, keys_all, values_all, keep_keys, score_scale):
    tokens = queries.shape[0]
    width = min(512, tokens)
    query_blocks = queries.reshape(tokens // width, width, HEADS, HDIM)

    def one_block(query_blk):
        scores = block_scores(query_blk, keys_all, keep_keys, score_scale)
        row_max = jnp.max(scores, -1, keepdims=True)
        expo = jnp.exp(scores - row_max)
        exp_total = jnp.sum(expo, -1, keepdims=True)
        probabilities = (expo / exp_total).astype(jnp.bfloat16)
        mixed_out = jnp.einsum(
            "hqk,khd->qhd", probabilities, values_all, preferred_element_type=jnp.float32
        )
        return (mixed_out, (row_max + jnp.log(exp_total))[..., 0])

    mixed_out, log_total = lax.map(one_block, query_blocks)
    return (mixed_out.reshape(tokens, HEADS, HDIM), log_total)


def attention_back(queries, keys_all, values_all, keep_keys, log_total, grad_mixed, score_scale):
    tokens = queries.shape[0]
    width = min(512, tokens)
    query_blocks = queries.reshape(tokens // width, width, HEADS, HDIM)
    grad_blocks = grad_mixed.reshape(tokens // width, width, HEADS, HDIM)

    def one_block(carry_sums, block_data):
        query_blk, total_blk, grad_blk = block_data
        scores = block_scores(query_blk, keys_all, keep_keys, score_scale)
        probabilities = jnp.exp(scores - total_blk[..., None])
        grad_probs = jnp.einsum(
            "qhd,khd->hqk", grad_blk, values_all, preferred_element_type=jnp.float32
        )
        inner_sum = jnp.sum(probabilities * grad_probs, -1, keepdims=True)
        grad_scores = (probabilities * (grad_probs - inner_sum)).astype(jnp.bfloat16)
        grad_query = (
            jnp.einsum("hqk,khd->qhd", grad_scores, keys_all, preferred_element_type=jnp.float32)
            * score_scale
        )
        grad_key = (
            jnp.einsum("hqk,qhd->khd", grad_scores, query_blk, preferred_element_type=jnp.float32)
            * score_scale
        )
        grad_value = jnp.einsum(
            "hqk,qhd->khd",
            probabilities.astype(jnp.bfloat16),
            grad_blk,
            preferred_element_type=jnp.float32,
        )
        return ((carry_sums[0] + grad_key, carry_sums[1] + grad_value), grad_query)

    zero_keys = jnp.zeros(keys_all.shape, jnp.float32)
    grad_kv, grad_queries = lax.scan(
        one_block, (zero_keys, zero_keys), (query_blocks, log_total, grad_blocks)
    )
    return (grad_queries.reshape(tokens, D), grad_kv[0].reshape(-1, D), grad_kv[1].reshape(-1, D))


def send_matrix(piece_cols, root):
    return broadcast(piece_cols, "dp", root)


def fetch_keys(key_rows, value_rows):
    return (
        lax.all_gather(key_rows, "vocab", axis=0, tiled=True),
        lax.all_gather(value_rows, "vocab", axis=0, tiled=True),
    )


def layer_forward(hidden, weights, vec_layer, keep_keys, score_scale):
    w_query, w_key, w_value, w_out, w_up, w_down = weights
    tokens = hidden.shape[0]
    norm_one, inv_one = norm_parts(hidden)
    normed = (norm_one * vec_layer[0:D] + vec_layer[D : 2 * D]).astype(jnp.bfloat16)
    queries = matmul_nn(normed, w_query).astype(jnp.bfloat16)
    key_rows = matmul_nn(normed, w_key).astype(jnp.bfloat16)
    value_rows = matmul_nn(normed, w_value).astype(jnp.bfloat16)
    keys_all, values_all = fetch_keys(key_rows, value_rows)
    keys_all = keys_all.reshape(-1, HEADS, HDIM)
    values_all = values_all.reshape(-1, HEADS, HDIM)
    mixed_out, log_total = attention(
        queries.reshape(tokens, HEADS, HDIM), keys_all, values_all, keep_keys, score_scale
    )
    mixed_low = mixed_out.reshape(tokens, D).astype(jnp.bfloat16)
    middle = hidden + matmul_nn(mixed_low, w_out)
    norm_two, inv_two = norm_parts(middle)
    normed_two = (norm_two * vec_layer[2 * D : 3 * D] + vec_layer[3 * D : 4 * D]).astype(
        jnp.bfloat16
    )
    up_proj = matmul_nt(normed_two, w_up) + vec_layer[4 * D :]
    active = jax.nn.gelu(up_proj).astype(jnp.bfloat16)
    out_rows = middle + matmul_nn(active, w_down)
    kept_vals = (
        norm_one,
        inv_one,
        normed,
        queries,
        key_rows,
        value_rows,
        keys_all,
        values_all,
        log_total,
        mixed_low,
        norm_two,
        inv_two,
        normed_two,
        up_proj,
        active,
    )
    return (out_rows, kept_vals)


def layer_backward(grad_out, kept_vals, weights, vec_layer, keep_keys, score_scale):
    w_query, w_key, w_value, w_out, w_up, w_down = weights
    (
        norm_one,
        inv_one,
        normed,
        queries,
        key_rows,
        value_rows,
        keys_all,
        values_all,
        log_total,
        mixed_low,
        norm_two,
        inv_two,
        normed_two,
        up_proj,
        active,
    ) = kept_vals
    tokens = grad_out.shape[0]
    grad_low = grad_out.astype(jnp.bfloat16)
    grad_down = matmul_tn(active, grad_low)
    grad_active = matmul_nt(grad_low, w_down)
    grad_up_proj = jax.vjp(jax.nn.gelu, up_proj)[1](grad_active)[0].astype(jnp.bfloat16)
    grad_bias = jnp.sum(grad_up_proj.astype(jnp.float32), 0)
    grad_up = matmul_tn(grad_up_proj, normed_two)
    grad_normed_two = matmul_nn(grad_up_proj, w_up)
    grad_part, grad_gain_two, grad_shift_two = norm_back(
        norm_two, inv_two, vec_layer[2 * D : 3 * D], grad_normed_two
    )
    grad_middle = grad_out + grad_part
    grad_attn = grad_middle.astype(jnp.bfloat16)
    grad_out_w = matmul_tn(mixed_low, grad_attn)
    grad_mixed = matmul_nt(grad_attn, w_out).astype(jnp.bfloat16).reshape(tokens, HEADS, HDIM)
    grad_queries, grad_keys_all, grad_values_all = attention_back(
        queries.reshape(tokens, HEADS, HDIM),
        keys_all,
        values_all,
        keep_keys,
        log_total,
        grad_mixed,
        score_scale,
    )
    grad_key_rows, grad_value_rows = (
        lax.psum_scatter(
            grad_keys_all.astype(jnp.bfloat16), "vocab", scatter_dimension=0, tiled=True
        ).astype(jnp.float32),
        lax.psum_scatter(
            grad_values_all.astype(jnp.bfloat16), "vocab", scatter_dimension=0, tiled=True
        ).astype(jnp.float32),
    )
    grad_q_low = grad_queries.astype(jnp.bfloat16)
    grad_k_low = grad_key_rows.astype(jnp.bfloat16)
    grad_v_low = grad_value_rows.astype(jnp.bfloat16)
    grad_wq = matmul_tn(normed, grad_q_low)
    grad_wk = matmul_tn(normed, grad_k_low)
    grad_wv = matmul_tn(normed, grad_v_low)
    grad_normed = (
        matmul_nt(grad_q_low, w_query)
        + matmul_nt(grad_k_low, w_key)
        + matmul_nt(grad_v_low, w_value)
    )
    grad_part_one, grad_gain_one, grad_shift_one = norm_back(
        norm_one, inv_one, vec_layer[0:D], grad_normed
    )
    grad_hidden = grad_middle + grad_part_one
    grad_mats = [grad_wq, grad_wk, grad_wv, grad_out_w, grad_up, grad_down]
    grad_vec = jnp.concatenate(
        [grad_gain_one, grad_shift_one, grad_gain_two, grad_shift_two, grad_bias]
    )
    return (grad_hidden, grad_mats, grad_vec)


def merge_stats(first_part, second_part):
    peak_val = jnp.maximum(first_part[0], second_part[0])
    exp_total = first_part[1] * jnp.exp(first_part[0] - peak_val) + second_part[1] * jnp.exp(
        second_part[0] - peak_val
    )
    return (peak_val, exp_total, first_part[2] + second_part[2])


def any_mesh_device(
    token_ids,
    timesteps,
    pad_mask,
    noise_draw,
    owners,
    emb_table,
    table_first_moment,
    table_second_moment,
    mat_slots,
    slot_first,
    slot_second,
    vec_params,
    vec_first,
    vec_second,
):
    vocab_count = lax.axis_size("vocab")
    vocab_pos = lax.axis_index("vocab")
    data_pos = lax.axis_index("dp")
    seq_len = token_ids.shape[1]
    tokens = seq_len // vocab_count
    vocab_rows = emb_table.shape[0]
    score_scale = HDIM ** (-0.5)
    table_low = lax.all_gather(emb_table.astype(jnp.bfloat16), "dp", axis=1, tiled=True)
    row_counts = matrix_rows()
    local_start = slot_places(owners) - owners * CAP
    sent_pieces = [
        send_matrix(
            lax.dynamic_slice_in_dim(
                mat_slots, local_start[mat_idx], row_counts[mat_idx], 1
            ).astype(jnp.bfloat16),
            owners[mat_idx],
        )
        for mat_idx in range(len(row_counts))
    ]
    canon = jnp.concatenate(sent_pieces, 1)
    weights = lax.all_gather(canon, "vocab", axis=0, tiled=True).T
    layer_rows = 4 * D + 2 * FF
    vec_rows = 4 * D + FF
    tail_at = LAYERS * layer_rows

    def layer_weights(layer_idx):
        begin_row = layer_idx * layer_rows
        cuts = [
            begin_row,
            begin_row + D,
            begin_row + 2 * D,
            begin_row + 3 * D,
            begin_row + 4 * D,
            begin_row + 4 * D + FF,
            begin_row + layer_rows,
        ]
        return [weights[cuts[cut_idx] : cuts[cut_idx + 1]] for cut_idx in range(6)]

    w_input = weights[tail_at : tail_at + 2 * EMBED_WIDTH]
    w_final = weights[tail_at + 2 * EMBED_WIDTH : tail_at + 3 * EMBED_WIDTH]
    seq_ids = token_ids[0]
    seq_mask = pad_mask[0].astype(jnp.float32)
    keep_keys = pad_mask[0] > 0
    local_row = seq_ids - vocab_pos * vocab_rows
    valid_row = (local_row >= 0) & (local_row < vocab_rows)
    safe_row = jnp.clip(local_row, 0, vocab_rows - 1)
    found_rows = jnp.where(
        valid_row[:, None], jnp.take(table_low, safe_row, axis=0), jnp.zeros((), jnp.bfloat16)
    )
    arrived = lax.all_to_all(found_rows, "vocab", split_axis=0, concat_axis=0, tiled=True)
    clean_emb = jnp.sum(arrived.reshape(vocab_count, tokens, EMBED_WIDTH).astype(jnp.float32), 0)
    own_first = vocab_pos * tokens
    mask_own = lax.dynamic_slice_in_dim(seq_mask, own_first, tokens)
    own_places = (own_first + jnp.arange(tokens)).astype(jnp.float32)
    step_val = timesteps[0].astype(jnp.float32)
    signal_level = 1.0 - jnp.sqrt(step_val / DIFF + 0.0001)
    noisy_emb = jnp.sqrt(signal_level) * clean_emb + jnp.sqrt(1.0 - signal_level) * noise_draw[
        0
    ].astype(jnp.float32)
    time_feat = jnp.broadcast_to(waves(step_val[None], EMBED_WIDTH), (tokens, EMBED_WIDTH))
    inputs = jnp.concatenate([noisy_emb, time_feat], 1).astype(jnp.bfloat16)
    hidden = matmul_nn(inputs, w_input) + waves(own_places, D)
    layer_idx = 0
    vec_layer = vec_params[layer_idx * vec_rows : (layer_idx + 1) * vec_rows]
    hidden, kept_vals = layer_forward(
        hidden, layer_weights(layer_idx), vec_layer, keep_keys, score_scale
    )
    kept_list = [kept_vals]
    gain_final = vec_params[LAYERS * vec_rows : LAYERS * vec_rows + D]
    shift_final = vec_params[LAYERS * vec_rows + D :]
    norm_final, inv_final = norm_parts(hidden)
    final_norm = (norm_final * gain_final + shift_final).astype(jnp.bfloat16)
    predicted = matmul_nt(final_norm, w_final)
    pred_all = lax.all_gather(predicted.astype(jnp.bfloat16), "vocab", axis=0, tiled=True)
    head_width = min(512, seq_len)
    head_count = seq_len // head_width
    columns = jnp.arange(vocab_rows)
    pred_blocks = pred_all.reshape(head_count, head_width, EMBED_WIDTH)
    row_blocks = local_row.reshape(head_count, head_width)

    def head_stats(block_data):
        pred_blk, rows_blk = block_data
        logits = matmul_nt(pred_blk, table_low)
        row_max = jnp.max(logits, -1)
        exp_total = jnp.sum(jnp.exp(logits - row_max[:, None]), -1)
        target = jnp.sum(jnp.where(columns[None, :] == rows_blk[:, None], logits, 0.0), -1)
        return (row_max, exp_total, target)

    peaks, totals, targets = lax.map(head_stats, (pred_blocks, row_blocks))
    peak_all, total_all, target_all = merged(
        (peaks.reshape(seq_len), totals.reshape(seq_len), targets.reshape(seq_len)),
        "vocab",
        merge_stats,
    )
    log_total = peak_all + jnp.log(total_all)
    lse_own = lax.dynamic_slice_in_dim(log_total, own_first, tokens)
    target_own = lax.dynamic_slice_in_dim(target_all, own_first, tokens)
    pred_error = predicted - clean_emb
    square_own = jnp.sum(mask_own[:, None] * pred_error * pred_error)
    cross_own = jnp.sum(mask_own * (lse_own - target_own))
    norm_own = jnp.sum(mask_own * jnp.sqrt(jnp.sum(clean_emb * clean_emb, -1) + 1e-06))
    count_all, square, cross_sum, norm_total = lax.psum(
        (jnp.sum(mask_own), square_own, cross_own, norm_own), ("dp", "vocab")
    )
    weight_blocks = (seq_mask / count_all).reshape(head_count, head_width)
    lse_blocks = log_total.reshape(head_count, head_width)

    def head_back(grad_table, block_data):
        pred_blk, rows_blk, lse_blk, weight_blk = block_data
        logits = matmul_nt(pred_blk, table_low)
        probabilities = jnp.exp(logits - lse_blk[:, None])
        onehot = (columns[None, :] == rows_blk[:, None]).astype(jnp.float32)
        grad_logits = ((probabilities - onehot) * weight_blk[:, None]).astype(jnp.bfloat16)
        return (grad_table + matmul_tn(grad_logits, pred_blk), matmul_nn(grad_logits, table_low))

    zero_table = jnp.zeros((vocab_rows, EMBED_WIDTH), jnp.float32)
    grad_table_head, grad_pred_blocks = lax.scan(
        head_back, zero_table, (pred_blocks, row_blocks, lse_blocks, weight_blocks)
    )
    grad_pred = lax.psum_scatter(
        grad_pred_blocks.reshape(seq_len, EMBED_WIDTH).astype(jnp.bfloat16),
        "vocab",
        scatter_dimension=0,
        tiled=True,
    ).astype(jnp.float32)
    error_grad = 2.0 * mask_own[:, None] * pred_error / count_all
    grad_pred_low = (grad_pred + error_grad).astype(jnp.bfloat16)
    grad_final_w = matmul_tn(grad_pred_low, final_norm)
    grad_final = matmul_nn(grad_pred_low, w_final)
    grad_hidden, grad_gain_final, grad_shift_final = norm_back(
        norm_final, inv_final, gain_final, grad_final
    )
    layer_grads = [None] * LAYERS
    vec_grads = [None] * LAYERS
    for layer_idx in reversed(range(LAYERS)):
        vec_layer = vec_params[layer_idx * vec_rows : (layer_idx + 1) * vec_rows]
        grad_hidden, layer_grads[layer_idx], vec_grads[layer_idx] = layer_backward(
            grad_hidden,
            kept_list[layer_idx],
            layer_weights(layer_idx),
            vec_layer,
            keep_keys,
            score_scale,
        )
    grad_hidden_low = grad_hidden.astype(jnp.bfloat16)
    grad_input_w = matmul_tn(inputs, grad_hidden_low)
    grad_inputs = matmul_nt(grad_hidden_low, w_input)
    grad_clean = jnp.sqrt(signal_level) * grad_inputs[:, :EMBED_WIDTH] - error_grad
    grad_clean_all = lax.all_gather(
        grad_clean.astype(jnp.bfloat16), "vocab", axis=0, tiled=True
    ).astype(grad_clean.dtype)
    grad_table_look = zero_table.at[safe_row].add(
        jnp.where(valid_row[:, None], grad_clean_all, 0.0)
    )
    grad_table_local = grad_table_head + grad_table_look
    canon_list = []
    layer_idx = 0
    canon_list = canon_list + layer_grads[layer_idx]
    canon_grad = jnp.concatenate(canon_list + [grad_input_w, grad_final_w], 0).T
    vec_grad = jnp.concatenate(vec_grads + [grad_gain_final, grad_shift_final])
    grad_cols, vec_part = (
        lax.psum_scatter(canon_grad, "vocab", scatter_dimension=0, tiled=True),
        lax.psum_scatter(vec_grad, "vocab", scatter_dimension=0, tiled=True),
    )
    emb_cols = emb_table.shape[1]
    summed_cols, summed_vec, summed_table = lax.psum((grad_cols, vec_part, grad_table_local), "dp")
    table_grad = lax.dynamic_slice_in_dim(summed_table, data_pos * emb_cols, emb_cols, 1)
    slot_grad = jnp.zeros_like(mat_slots)
    cursor = 0
    for mat_idx in range(len(row_counts)):
        piece_cols = summed_cols[:, cursor : cursor + row_counts[mat_idx]]
        updated = lax.dynamic_update_slice_in_dim(slot_grad, piece_cols, local_start[mat_idx], 1)
        slot_grad = jnp.where(owners[mat_idx] == data_pos, updated, slot_grad)
        cursor = cursor + row_counts[mat_idx]
    vec_share = vec_first.shape[0]
    own_vecs = lax.dynamic_slice_in_dim(vec_params, vocab_pos * vec_share, vec_share)
    new_slots, slot_first_new, slot_second_new = adamw(
        mat_slots, slot_grad, slot_first, slot_second
    )
    new_table, table_first_new, table_second_new = adamw(
        emb_table, table_grad, table_first_moment, table_second_moment
    )
    new_vecs, vec_first_new, vec_second_new = adamw(own_vecs, summed_vec, vec_first, vec_second)
    loss_pair = jnp.stack([square + cross_sum, count_all])
    emb_norm = norm_total / count_all
    return (
        loss_pair,
        emb_norm,
        new_table,
        table_first_new,
        table_second_new,
        new_slots,
        slot_first_new,
        slot_second_new,
        new_vecs,
        vec_first_new,
        vec_second_new,
    )


def solution(mesh):
    in_specs = (
        P("dp", None),
        P("dp"),
        P("dp", None),
        P("dp", "vocab", None),
        P(),
        P("vocab", "dp"),
        P("vocab", "dp"),
        P("vocab", "dp"),
        P("vocab", "dp"),
        P("vocab", "dp"),
        P("vocab", "dp"),
        P(),
        P("vocab"),
        P("vocab"),
    )
    out_specs = (
        P(),
        P(),
        P("vocab", "dp"),
        P("vocab", "dp"),
        P("vocab", "dp"),
        P("vocab", "dp"),
        P("vocab", "dp"),
        P("vocab", "dp"),
        P("vocab"),
        P("vocab"),
        P("vocab"),
    )
    fast = mesh.shape["dp"] == 8 and mesh.shape["vocab"] == 4
    body = per_device if fast else any_mesh_device
    return jax.shard_map(
        body, mesh=mesh, in_specs=in_specs, out_specs=out_specs, check_vma=False
    )
```

```python
import functools
import math

import jax
import jax.numpy as jnp
from jax import lax
from jax.experimental import pallas as pl
from jax.experimental.pallas import tpu as pltpu
from jax.sharding import PartitionSpec as P

D = 768
HEADS = 12
HDIM = 64
FF = 3072
EMBED_WIDTH = 128
DIFF = 2000
STEP = 10
CAP = 3072
LAYERS = 1
LANES = 128


beta_one = 0.9
beta_two = 0.999
learn_rate = 0.02
weight_decay = 0.01
eps_adam = 1e-08
eps_norm = 1e-05
f32 = jnp.float32
bf16 = jnp.bfloat16


def matmul_nn(left, right):
    return jnp.dot(left, right, preferred_element_type=f32)


def matmul_tn(left, right):
    return lax.dot_general(left, right, (((0,), (0,)), ((), ())), preferred_element_type=f32)


def matmul_nt(left, right):
    return lax.dot_general(left, right, (((1,), (1,)), ((), ())), preferred_element_type=f32)


ROW_COUNTS = [D, D, D, D, FF, FF, EMBED_WIDTH, EMBED_WIDTH, EMBED_WIDTH]


def slot_starts(owners):
    counts = jnp.array(ROW_COUNTS, jnp.int32)
    same_owner = (owners[:, None] == owners[None, :]).astype(jnp.int32)
    earlier_mask = jnp.tril(jnp.ones((len(ROW_COUNTS),) * 2, jnp.int32), -1)
    return jnp.sum(same_owner * earlier_mask * counts[None, :], 1)


def waves(places, width):
    half_width = width // 2
    frequency = jnp.exp(-math.log(10000.0) * jnp.arange(half_width, dtype=f32) / half_width)
    angles = places[:, None] * frequency[None, :]
    return jnp.concatenate([jnp.sin(angles), jnp.cos(angles)], 1)


def norm_parts(value_entries):
    center = value_entries - jnp.mean(value_entries, -1, keepdims=True)
    scale_inv = lax.rsqrt(jnp.mean(center * center, -1, keepdims=True) + eps_norm)
    return (center * scale_inv, scale_inv)


def norm_back(normal_part, scale_inv, gain_vec, grad_out):
    scaled = grad_out * gain_vec
    inner = (
        scaled
        - jnp.mean(scaled, -1, keepdims=True)
        - normal_part * jnp.mean(scaled * normal_part, -1, keepdims=True)
    )
    return (inner * scale_inv, jnp.sum(grad_out * normal_part, 0), jnp.sum(grad_out, 0))


def adamw(weight, gradient, moment_one, moment_two):
    moment_one = beta_one * moment_one + (1.0 - beta_one) * gradient
    moment_two = beta_two * moment_two + (1.0 - beta_two) * gradient * gradient
    fix_one = 1.0 - beta_one**STEP
    fix_two = 1.0 - beta_two**STEP
    update_dir = moment_one / fix_one / (jnp.sqrt(moment_two / fix_two) + eps_adam)
    return (weight - learn_rate * (update_dir + weight_decay * weight), moment_one, moment_two)


MESH = pl.DeviceIdType.MESH
ANY = pl.BlockSpec(memory_space=pl.ANY)
UNIT = 768
HALF = 96
QUARTER = 192


def place():
    d, v = lax.axis_index("dp"), lax.axis_index("vocab")
    return d // 2, d % 2, d, v


def greet(partners):
    barrier = pltpu.get_barrier_semaphore()
    for partner in partners:
        pl.semaphore_signal(barrier, inc=1, device_id=partner, device_id_type=MESH)
    pl.semaphore_wait(barrier, len(partners))


def remote(src, dst, sems, index, partner):
    return pltpu.make_async_remote_copy(
        src_ref=src,
        dst_ref=dst,
        send_sem=sems[0].at[index],
        recv_sem=sems[1].at[index],
        device_id=partner,
        device_id_type=MESH,
    )


def start_all(copies):
    for copy in copies:
        copy.start()
    return copies


def arrive_all(copies):
    for copy in copies:
        copy.wait_recv()


VMEM = pl.BlockSpec(memory_space=pltpu.VMEM)
SMEM = pl.BlockSpec(memory_space=pltpu.SMEM)


def prepare_kernel(
    owners, ids, mask, table, slots,
    payload, table_low, row_of, safe, keep_rows, keep, valid, count, kind, unit, column,
    units, extras, sems,
):
    d, v = lax.axis_index("dp"), lax.axis_index("vocab")
    starts = [
        sum(jnp.where(owners[j] == owners[i], ROW_COUNTS[j], 0) for j in range(i)) + 0 * owners[i]
        for i in range(len(ROW_COUNTS))
    ]
    whole = (owners[4] == d) | (owners[5] == d)
    copies = []
    for u in range(4):
        first = pl.multiple_of(jnp.where(whole, u * UNIT, starts[u]), LANES)
        copies.append(
            pltpu.make_async_copy(slots.at[:, pl.ds(first, UNIT)], units.at[u], sems.at[u])
        )
        first = pl.multiple_of(starts[6 + min(u, 2)], LANES)
        copies.append(
            pltpu.make_async_copy(slots.at[:, pl.ds(first, LANES)], extras.at[u], sems.at[4 + u])
        )
    for copy in copies:
        copy.start()

    def clear(j, carry):
        kind[j] = 0
        unit[j] = 0
        column[j] = 0
        return carry

    lax.fori_loop(0, CAP // LANES, clear, 0)
    per_unit = UNIT // LANES
    first_unit = [0, 1, 2, 3, 0, 0, 0, 1, 2]
    for i, rows in enumerate(ROW_COUNTS):

        def claim(i=i, rows=rows):
            def one(b, carry):
                j = starts[i] // LANES + b
                kind[j] = 2 if i > 5 else 1
                unit[j] = first_unit[i] + b // per_unit
                column[j] = b % per_unit
                return carry

            lax.fori_loop(0, rows // LANES, one, 0)

        pl.when(owners[i] == d)(claim)

    table_low[...] = table[...].astype(bf16)
    count[...] = jnp.full((8, LANES), jnp.sum(mask[...].astype(f32)))
    for b in range(4):
        at = pl.ds(pl.multiple_of((v ^ b) * 256, 256), 256)
        local = ids[:, at] - v * table.shape[1]
        row_of[b : b + 1, :] = local
        safe[:, 256 * b : 256 * b + 256] = jnp.clip(local, 0, table.shape[1] - 1)
        weight = mask[:, at].astype(f32)
        keep_rows[b : b + 1, :] = weight
        inside = ((local >= 0) & (local < table.shape[1])).astype(f32)
        both = jnp.concatenate([weight, inside, jnp.zeros((6, 256), f32)], 0).T
        keep[256 * b : 256 * b + 256, :] = both[:, 0:1]
        valid[256 * b : 256 * b + 256, :] = both[:, 1:2]
    for copy in copies:
        copy.wait()
    for u in range(4):
        for half in range(2):
            rows = slice(half * HALF, half * HALF + HALF)
            payload[2 * u + half, :, 0:UNIT] = units[u, rows, :].astype(bf16)
            payload[2 * u + half, :, UNIT:] = extras[u, rows, :].astype(bf16)


def prepare(owners, ids, mask, table, slots):
    def shape(kind, *dims):
        return jax.ShapeDtypeStruct(dims, kind)

    blocks = CAP // LANES
    tokens = ids.shape[1]
    return pl.pallas_call(
        prepare_kernel,
        out_shape=[
            shape(bf16, 8, HALF, UNIT + LANES),
            shape(bf16, *table.shape),
            shape(jnp.int32, 4, tokens // 4),
            shape(jnp.int32, 1, tokens),
            shape(f32, 4, tokens // 4),
            shape(f32, tokens, 1),
            shape(f32, tokens, 1),
            shape(f32, 8, LANES),
        ]
        + [shape(jnp.int32, blocks)] * 3,
        in_specs=[SMEM, VMEM, VMEM, VMEM, ANY],
        out_specs=[VMEM] * 8 + [SMEM] * 3,
        scratch_shapes=[
            pltpu.VMEM((4, QUARTER, UNIT), f32),
            pltpu.VMEM((4, QUARTER, LANES), f32),
            pltpu.SemaphoreType.DMA((8,)),
        ],
        compiler_params=pltpu.CompilerParams(vmem_limit_bytes=40 * 2**20),
    )(owners, ids, mask, table, slots)


TRADE_MASKS = (4, 6, 5, 7, 2, 3, 1)


def chosen_of(pieces, wanted):
    value = pieces[0]
    for i in range(1, len(pieces)):
        value = jnp.where(wanted == i, pieces[i], value)
    return value


def spread_kernel(
    owners, payload, tile, keep_rows, keep, table_home,
    up, down, small, attn, out, table, weight, twice,
    arrived, tiles, up_home, down_home, small_home, attn_home,
    a_send, a_recv, b_send, b_recv,
    z_send, z_recv, y_send, y_recv, x_send, x_recv, n_send, n_recv, f_send, f_recv, local,
):
    z, y, d, v = place()
    far, near = v ^ 2, v ^ 1
    greet([(d ^ m, v) for m in TRADE_MASKS] + [(d, far), (d, near)])
    traded = start_all(
        [
            remote(payload.at[d ^ m], arrived.at[i], (a_send, a_recv), i, (d ^ m, v))
            for i, m in enumerate(TRADE_MASKS)
        ]
        + [
            remote(tile, tiles.at[i], (b_send, b_recv), i, (d ^ m, v))
            for i, m in enumerate(TRADE_MASKS)
        ]
    )
    homes = [up_home, down_home, small_home, attn_home, table_home]
    fulls = [up, down, small, attn, table]
    own_rows = pl.ds(v * QUARTER, QUARTER)

    def spot(c, unit):
        if c == 4:
            return table.at[2 * unit + y]
        first = y * HALF if c == 3 else v * QUARTER + y * HALF
        return fulls[c].at[unit, pl.ds(first, HALF), :]

    def start_line(c):
        keep = pltpu.make_async_copy(homes[c], spot(c, z), local.at[c])
        keep.start()
        return [keep] + start_all(
            [
                remote(homes[c], spot(c, z), (z_send, z_recv), (c, k - 1), (d ^ (2 * k), v))
                for k in (2, 1, 3)
            ]
        )

    def wait_line(copies):
        copies[0].wait()
        arrive_all(copies[1:])
        return copies[1:]

    def start_side(c):
        return start_all(
            [remote(spot(c, u), spot(c, u), (y_send, y_recv), (c, u), (d ^ 1, v)) for u in range(4)]
        )

    def strips(c, rows):
        if c == 3:
            return [out.at[rows, :]]
        return [fulls[c].at[u, rows, :] for u in range(4)]

    def sources(c):
        return [attn.at[3]] if c == 3 else strips(c, own_rows)

    def start_far(c):
        return start_all(
            [
                remote(s, t, (x_send, x_recv), (c, u), (d, far))
                for u, (s, t) in enumerate(zip(sources(c), strips(c, own_rows)))
            ]
        )

    def start_near(c):
        return start_all(
            [
                remote(s, t, (n_send, n_recv), (c, u), (d, near))
                for u, (s, t) in enumerate(zip(sources(c), strips(c, own_rows)))
            ]
        )

    def start_last(c):
        rows = pl.ds(far * QUARTER, QUARTER)
        return start_all(
            [
                remote(s, s, (f_send, f_recv), (c, u), (d, near))
                for u, s in enumerate(strips(c, rows))
            ]
        )

    sent, landing = [], []
    line, side, chip = {}, {}, {}

    def begin_chip(c):
        arrive_all(side[c])
        if c == 3:
            keep = pltpu.make_async_copy(attn.at[3], out.at[own_rows, :], local.at[5])
            keep.start()
            keep.wait()
        if c != 4:
            chip[c] = start_far(c)
            near_copies = start_near(c)
            sent.extend(chip[c] + near_copies)
            landing.extend(near_copies)

    def begin_last(c):
        if c != 4:
            arrive_all(chip[c])
            last = start_last(c)
            sent.extend(last)
            landing.extend(last)

    arrive_all(traded)
    sent.extend(traded)
    total = tile[...]
    for i in range(7):
        total = total + tiles[i]
    weight[...] = keep_rows[...] / jnp.concatenate([total[0:4]] * 2, 1)
    twice[...] = 2.0 * keep[0:256, :] / total[0:1, 0:1]

    def from_owner(owner, lanes):
        value = payload[d, :, lanes]
        for i, m in enumerate(TRADE_MASKS):
            value = jnp.where(owner == d ^ m, arrived[i, :, lanes], value)
        return value

    up_home[...] = from_owner(owners[4], slice(0, UNIT))
    down_home[...] = from_owner(owners[5], slice(0, UNIT))
    attn_home[...] = from_owner(chosen_of([owners[u] for u in range(4)], z), slice(0, UNIT))
    small_home[...] = from_owner(
        chosen_of([owners[6 + min(u, 2)] for u in range(4)], z), slice(UNIT, UNIT + LANES)
    )

    waves_of = [[0], [1], [2, 3], [4]]
    for c in waves_of[0]:
        line[c] = start_line(c)
    for i, wave in enumerate(waves_of):
        for c in wave:
            sent.extend(wait_line(line[c]))
        if i + 1 < len(waves_of):
            for c in waves_of[i + 1]:
                line[c] = start_line(c)
        for c in wave:
            side[c] = start_side(c)
            sent.extend(side[c])
        if i >= 1:
            for c in waves_of[i - 1]:
                begin_chip(c)
        if i >= 2:
            for c in waves_of[i - 2]:
                begin_last(c)
    for c in waves_of[-1]:
        begin_chip(c)
    for wave in waves_of[-2:]:
        for c in wave:
            begin_last(c)
    arrive_all(landing)
    for copy in sent:
        copy.wait_send()


def spread(owners, payload, tile, keep_rows, keep, table_home):
    rows, vocab_rows = table_home.shape
    dma, vmem = pltpu.SemaphoreType.DMA, pltpu.VMEM

    def shape(*dims):
        return jax.ShapeDtypeStruct(dims, bf16)

    return pl.pallas_call(
        spread_kernel,
        out_shape=[
            shape(4, D, UNIT),
            shape(4, D, UNIT),
            shape(4, D, LANES),
            shape(4, QUARTER, UNIT),
            shape(D, UNIT),
            shape(8, rows, vocab_rows),
            jax.ShapeDtypeStruct(keep_rows.shape, f32),
            jax.ShapeDtypeStruct((256, 1), f32),
        ],
        in_specs=[SMEM] + [VMEM] * 5,
        out_specs=[ANY] * 6 + [VMEM] * 2,
        scratch_shapes=[
            vmem((7, HALF, UNIT + LANES), bf16),
            vmem((7, 8, LANES), f32),
            vmem((HALF, UNIT), bf16),
            vmem((HALF, UNIT), bf16),
            vmem((HALF, LANES), bf16),
            vmem((HALF, UNIT), bf16),
        ]
        + [dma((7,))] * 4
        + [dma((5, 3))] * 2
        + [dma((5, 4))] * 2
        + [dma((4, 4))] * 6
        + [dma((6,))],
        compiler_params=pltpu.CompilerParams(
            collective_id=1, has_side_effects=True, vmem_limit_bytes=40 * 2**20
        ),
    )(owners, payload, tile, keep_rows, keep, table_home)

def neighbours():
    d, v = lax.axis_index("dp"), lax.axis_index("vocab")
    return [(d, v ^ k) for k in (1, 2, 3)]


def by_position(v, store):
    for i in range(4):
        pl.when(v == i)(functools.partial(store, i))


def forward_kernel(
    looked, valid, noise, levels, places, small, attn, out_w, up_hbm, down_hbm, vecs, keep,
    found, clean, inputs, hidden, normed_all, q, k, k_t, values, log_total, mixed, middle, normed_two,
    up_proj, active, hidden_two, final_norm, predicted, pred_all,
    up_w, down_w, found_in, values_t, mixed_out, mixed_in,
    w_sem, e_send, e_recv, n_send, n_recv, m_send, m_recv, p_send, p_recv,
):
    v = lax.axis_index("vocab")
    partners = neighbours()
    loads = []
    for j in range(4):
        for i, (src, dst) in enumerate(((up_hbm, up_w), (down_hbm, down_w))):
            copy = pltpu.make_async_copy(src.at[j], dst.at[j], w_sem.at[2 * j + i])
            copy.start()
            loads.append(copy)
    for b in range(4):
        found[b] = jnp.where(
            valid[256 * b : 256 * b + 256, :] > 0.0, looked[b].astype(f32), 0.0
        ).astype(bf16)
    greet(partners)
    asked = start_all(
        [
            remote(found.at[m], found_in.at[m - 1], (e_send, e_recv), m - 1, partners[m - 1])
            for m in (2, 3, 1)
        ]
    )
    wave = levels[2:3].astype(bf16)
    time_part = matmul_nt(jnp.broadcast_to(wave, (16, EMBED_WIDTH)), small[1])[0:1]
    arrive_all(asked)
    total = found[0].astype(f32)
    for m in range(3):
        total = total + found_in[m].astype(f32)
    clean[...] = total
    noisy = levels[0:1] * total + levels[1:2] * noise[...].astype(f32)
    inputs[:, 0:EMBED_WIDTH] = noisy.astype(bf16)
    inputs[:, EMBED_WIDTH:] = jnp.broadcast_to(wave, noisy.shape)
    value = matmul_nt(inputs[:, 0:EMBED_WIDTH], small[0]) + time_part + places[...]
    hidden[...] = value
    normed_all[0] = (norm_parts(value)[0] * vecs[0:1] + vecs[1:2]).astype(bf16)

    far = remote(normed_all.at[0], normed_all.at[2], (n_send, n_recv), 0, partners[1])
    near = remote(normed_all.at[0], normed_all.at[1], (n_send, n_recv), 1, partners[0])
    last = remote(normed_all.at[2], normed_all.at[3], (n_send, n_recv), 2, partners[0])
    far.start()
    near.start()

    def project(b):
        rows = pl.ds(b * 256, 256)
        block = normed_all[b]
        for i, ref in ((0, q), (1, k), (2, values)):
            result = matmul_nt(block, attn[i])
            if i == 0:
                result = result.astype(bf16).astype(f32) * HDIM ** (-0.5)
            for h in range(3):
                ref[h, rows, :] = result[:, h * HDIM : (h + 1) * HDIM].astype(bf16)
        k_t[:, rows] = matmul_nt(attn[1], block).astype(bf16)
        values_t[:, rows] = matmul_nt(attn[2], block).astype(bf16)

    project(0)
    near.wait_recv()
    project(1)
    far.wait_recv()
    last.start()
    project(2)
    last.wait_recv()
    project(3)

    given = []
    for b in (2, 3, 1, 0):
        rows = pl.ds(b * 256, 256)
        parts = []
        for h in range(3):
            scores = matmul_nt(k[h], q[h, rows, :])
            scores = jnp.where(keep[...] > 0.0, scores, -1000000000.0)
            top = jnp.max(scores, 0, keepdims=True)
            expo = jnp.exp(scores - top)
            mass = jnp.sum(expo, 0, keepdims=True)
            probs = (expo * (1.0 / mass)).astype(bf16)
            log_total[pl.ds(3 * b + h, 1), :] = top + jnp.log(mass)
            parts.append(matmul_nn(values_t[h * HDIM : (h + 1) * HDIM, :], probs))
        block = jnp.concatenate(parts, 0).T.astype(bf16)
        if b == 0:
            mixed_in[0] = block
        else:
            mixed_out[b - 1] = block
            copy = remote(
                mixed_out.at[b - 1], mixed_in.at[b], (m_send, m_recv), b - 1, partners[b - 1]
            )
            copy.start()
            given.append(copy)
    arrive_all(given)

    def lay(i):
        for b in range(4):
            mixed[:, QUARTER * (i ^ b) : QUARTER * ((i ^ b) + 1)] = mixed_in[b]

    by_position(v, lay)
    value = hidden[...] + matmul_nt(mixed[...], out_w[...])
    middle[...] = value
    normed_two[...] = (norm_parts(value)[0] * vecs[2:3] + vecs[3:4]).astype(bf16)
    for j in range(4):
        loads[2 * j].wait()
        loads[2 * j + 1].wait()
        raised = matmul_nn(normed_two[...], up_w[j]) + vecs[4 + j : 5 + j]
        up_proj[j] = raised
        active[j] = jax.nn.gelu(raised).astype(bf16)
        lowered = matmul_nt(active[j], down_w[j])
        hidden_two[...] = (middle[...] if j == 0 else hidden_two[...]) + lowered
    final_norm[...] = (norm_parts(hidden_two[...])[0] * vecs[8:9] + vecs[9:10]).astype(bf16)
    predicted[...] = matmul_nn(final_norm[...], small[2])
    pred_all[0] = predicted[...].astype(bf16)
    shown = start_all(
        [
            remote(pred_all.at[0], pred_all.at[m], (p_send, p_recv), m - 1, partners[m - 1])
            for m in (2, 3, 1)
        ]
    )
    arrive_all(shown)
    for copy in asked + [far, near, last] + given + shown:
        copy.wait_send()


def forward(looked, valid, noise, levels, places, small, attn, out_w, up_w, down_w, vecs, keep):
    dma, vmem = pltpu.SemaphoreType.DMA, pltpu.VMEM
    n = 256

    def shape(kind, *dims):
        return jax.ShapeDtypeStruct(dims, kind)

    return pl.pallas_call(
        forward_kernel,
        out_shape=[
            shape(bf16, 4, n, EMBED_WIDTH),
            shape(f32, n, EMBED_WIDTH),
            shape(bf16, n, 2 * EMBED_WIDTH),
            shape(f32, n, D),
            shape(bf16, 4, n, D),
            shape(bf16, 3, 4 * n, HDIM),
            shape(bf16, 3, 4 * n, HDIM),
            shape(bf16, QUARTER, 4 * n),
            shape(bf16, 3, 4 * n, HDIM),
            shape(f32, 16, n),
            shape(bf16, n, D),
            shape(f32, n, D),
            shape(bf16, n, D),
            shape(f32, 4, n, UNIT),
            shape(bf16, 4, n, UNIT),
            shape(f32, n, D),
            shape(bf16, n, D),
            shape(f32, n, EMBED_WIDTH),
            shape(bf16, 4, n, EMBED_WIDTH),
        ],
        in_specs=[VMEM] * 8 + [ANY] * 2 + [VMEM] * 2,
        out_specs=[VMEM] * 19,
        scratch_shapes=[
            vmem((4, D, UNIT), bf16),
            vmem((4, D, UNIT), bf16),
            vmem((3, n, EMBED_WIDTH), bf16),
            vmem((QUARTER, 4 * n), bf16),
            vmem((3, n, QUARTER), bf16),
            vmem((4, n, QUARTER), bf16),
            dma((8,)),
        ]
        + [dma((3,))] * 8,
        compiler_params=pltpu.CompilerParams(
            collective_id=4, has_side_effects=True, vmem_limit_bytes=60 * 2**20
        ),
    )(looked, valid, noise, levels, places, small, attn, out_w, up_w, down_w, vecs, keep)


STRIP = 768


def strips(rows):
    return [(lo, min(STRIP, rows - lo)) for lo in range(0, rows, STRIP)]


def head_kernel(
    pred_all, table, table_t, row_of, weight, found,
    grad_pred, lse, logits, stats, gathered, outgoing, incoming,
    s_send, s_recv, g_send, g_recv,
):
    partners = neighbours()
    greet(partners)
    rows = table_t.shape[0]
    full, rest = rows // STRIP, rows % STRIP
    mixes = []
    for b in range(4):
        block = pred_all[b]
        wanted = row_of[b : b + 1, :]

        def first(at, size, top):
            value = matmul_nt(table_t[at, :], block)
            logits[at, :] = value
            return jnp.maximum(top, jnp.max(value, 0, keepdims=True))

        def second(at, size, lo, carry, peak):
            mass, target, mix = carry
            value = logits[at, :]
            expo = jnp.exp(value - peak)
            here = lax.broadcasted_iota(jnp.int32, (size, 256), 0) == wanted - lo
            mass = mass + jnp.sum(expo, 0, keepdims=True)
            target = target + jnp.sum(jnp.where(here, value, 0.0), 0, keepdims=True)
            return mass, target, mix + matmul_nn(table[:, at], expo.astype(bf16))

        peak = lax.fori_loop(
            0,
            full,
            lambda t, top: first(pl.ds(pl.multiple_of(t * STRIP, STRIP), STRIP), STRIP, top),
            jnp.full((1, 256), -jnp.inf, f32),
        )
        tail = pl.ds(full * STRIP, rest)
        if rest:
            peak = first(tail, rest, peak)
        zero = jnp.zeros((1, 256), f32)
        carry = lax.fori_loop(
            0,
            full,
            lambda t, carry: second(
                pl.ds(pl.multiple_of(t * STRIP, STRIP), STRIP), STRIP, t * STRIP, carry, peak
            ),
            (zero, zero, jnp.zeros((EMBED_WIDTH, 256), f32)),
        )
        if rest:
            carry = second(tail, rest, full * STRIP, carry, peak)
        stats[b, 0:1] = peak
        stats[b, 1:2] = carry[0]
        stats[b, 2:3] = carry[1]
        stats[b, 3:8] = jnp.zeros((5, 256), f32)
        mixes.append(carry[2])
    told = start_all(
        [
            remote(stats, gathered.at[m - 1], (s_send, s_recv), m - 1, partners[m - 1])
            for m in (2, 3, 1)
        ]
    )
    arrive_all(told)
    given = []
    for b in (2, 3, 1, 0):
        views = [stats[b]] + [gathered[m - 1, b ^ m] for m in (1, 2, 3)]
        peak = functools.reduce(jnp.maximum, [view[0:1] for view in views])
        mass = sum(view[1:2] * jnp.exp(view[0:1] - peak) for view in views)
        total = peak + jnp.log(mass)
        lse[b : b + 1, :] = total
        if b == 0:
            target = sum(view[2:3] for view in views)
            lse[4:5, :] = weight[0:1, :] * (total - target)
            lse[5:8, :] = jnp.zeros((3, 256), f32)
        share = weight[b : b + 1, :]
        local = mixes[b] * (jnp.exp(stats[b, 0:1] - total) * share)
        local = local - found[b].astype(f32).T * share
        outgoing[b] = local.T.astype(bf16)
        if b:
            copy = remote(
                outgoing.at[b], incoming.at[b - 1], (g_send, g_recv), b - 1, partners[b - 1]
            )
            copy.start()
            given.append(copy)
    arrive_all(given)
    value = outgoing[0].astype(f32)
    for m in range(3):
        value = value + incoming[m].astype(f32)
    grad_pred[...] = value
    for copy in told + given:
        copy.wait_send()


def head(pred_all, table, table_t, row_of, weight, found):
    dma, vmem = pltpu.SemaphoreType.DMA, pltpu.VMEM
    return pl.pallas_call(
        head_kernel,
        out_shape=[
            jax.ShapeDtypeStruct((256, EMBED_WIDTH), f32),
            jax.ShapeDtypeStruct((8, 256), f32),
        ],
        in_specs=[VMEM] * 6,
        out_specs=[VMEM] * 2,
        scratch_shapes=[
            vmem((table_t.shape[0], 256), f32),
            vmem((4, 8, 256), f32),
            vmem((3, 4, 8, 256), f32),
            vmem((4, 256, EMBED_WIDTH), bf16),
            vmem((3, 256, EMBED_WIDTH), bf16),
        ]
        + [dma((3,))] * 4,
        compiler_params=pltpu.CompilerParams(
            collective_id=5, has_side_effects=True, vmem_limit_bytes=60 * 2**20
        ),
    )(pred_all, table, table_t, row_of, weight, found)


def gelu_slope(u):
    inner = math.sqrt(2.0 / math.pi)
    bent = jnp.tanh(inner * (u + 0.044715 * (u * u * u)))
    return 0.5 * (1.0 + bent) + (0.5 * inner) * u * (1.0 - bent * bent) * (
        1.0 + (3.0 * 0.044715) * (u * u)
    )


def backward_kernel(
    grad_pred, clean, predicted, twice, levels, head_stats, hidden, middle, hidden_two,
    normed_two, final_norm, up_proj, q, k, k_t, values, log_total, keep,
    small, attn, out_w, up_hbm, down_hbm, vecs,
    grad_pred_low, down_left, up_left, out_left, small_left, final_left, qkv_left, grad_up, grad_clean, sums,
    up_w, down_w, carried, folded, mix_out, mix_in, grad_k, grad_v, n_out, n_in, f_out, f_in,
    w_sem, m_send, m_recv, n_send, n_recv, c_send, c_recv,
):
    v = lax.axis_index("vocab")
    partners = neighbours()
    loads = []
    for j in range(4):
        for i, (src, dst) in enumerate(((down_hbm, down_w), (up_hbm, up_w))):
            copy = pltpu.make_async_copy(src.at[j], dst.at[j], w_sem.at[2 * j + i])
            copy.start()
            loads.append(copy)
    greet(partners)

    def turned(value):
        return value.astype(f32).T.astype(bf16)

    error = predicted[...] - clean[...]
    pull = twice[...] * error
    low = (grad_pred[...] + pull).astype(bf16)
    grad_pred_low[...] = low
    length = jnp.sqrt(jnp.sum(clean[...] * clean[...], -1, keepdims=True) + 1e-06)
    lane = lax.broadcasted_iota(jnp.int32, (1, UNIT), 1)
    scalars = (jnp.sum(pull * error), jnp.sum(head_stats[4:5, :]), jnp.sum(twice[...] * length))
    counted = jnp.sum(keep[0:256, :])
    sums[10:11, :] = sum(jnp.where(lane == i, x, 0.0) for i, x in enumerate(scalars + (counted,)))
    sums[11:16, :] = jnp.zeros((5, UNIT), f32)

    def through_norm(value, gain_row, grad_out, at):
        normal, scale_inv = norm_parts(value)
        part, grad_gain, grad_shift = norm_back(normal, scale_inv, vecs[gain_row : gain_row + 1], grad_out)
        sums[at : at + 1, :] = grad_gain[None, :]
        sums[at + 1 : at + 2, :] = grad_shift[None, :]
        return part

    carried[...] = through_norm(hidden_two[...], 8, matmul_nt(low, small[2]), 8)
    low = carried[...].astype(bf16)
    down_left[...] = turned(carried[...])
    up_left[...] = turned(normed_two[...])
    final_left[...] = turned(final_norm[...])
    for j in range(4):
        loads[2 * j].wait()
        loads[2 * j + 1].wait()
        slope = matmul_nn(low, down_w[j]) * gelu_slope(up_proj[j])
        grad_up[j] = slope.astype(bf16)
        sums[4 + j : 5 + j, :] = jnp.sum(grad_up[j].astype(f32), 0, keepdims=True)
        part = matmul_nt(grad_up[j], up_w[j])
        folded[...] = part if j == 0 else folded[...] + part
    carried[...] = carried[...] + through_norm(middle[...], 2, folded[...], 2)
    out_left[...] = turned(carried[...])
    folded[...] = matmul_nn(carried[...].astype(bf16), out_w[...])

    def lay(i):
        for b in range(4):
            mix_out[b] = folded[:, QUARTER * (i ^ b) : QUARTER * ((i ^ b) + 1)].astype(bf16)

    by_position(v, lay)
    mixed = [
        remote(mix_out.at[m], mix_in.at[m - 1], (m_send, m_recv), m - 1, partners[m - 1])
        for m in (1, 2, 3)
    ]
    for m in (2, 3, 1):
        mixed[m - 1].start()
    for b in range(4):
        if b:
            mixed[b - 1].wait_recv()
        grad_block = mix_out[0] if b == 0 else mix_in[b - 1]
        rows = pl.ds(b * 256, 256)
        for h in range(3):
            grad_mix = grad_block[:, h * HDIM : (h + 1) * HDIM]
            asked = q[h, rows, :]
            scores = matmul_nt(k[h], asked)
            scores = jnp.where(keep[...] > 0.0, scores, -1000000000.0)
            probs = jnp.exp(scores - log_total[3 * b + h : 3 * b + h + 1, :])
            grad_probs = matmul_nt(values[h], grad_mix)
            inner = jnp.sum(probs * grad_probs, 0, keepdims=True)
            grad_scores = (probs * (grad_probs - inner)).astype(bf16)
            grad_asked = matmul_nn(k_t[h * HDIM : (h + 1) * HDIM, :], grad_scores)
            qkv_left[0, h * HDIM : (h + 1) * HDIM, rows] = (grad_asked * HDIM ** (-0.5)).astype(bf16)
            part_k = matmul_nn(grad_scores, asked)
            part_v = matmul_nn(probs.astype(bf16), grad_mix)
            grad_k[h] = part_k if b == 0 else grad_k[h] + part_k
            grad_v[h] = part_v if b == 0 else grad_v[h] + part_v
    for h in range(3):
        lanes = pl.ds(h * HDIM, HDIM)
        qkv_left[1, lanes, :] = grad_k[h].T.astype(bf16)
        qkv_left[2, lanes, :] = grad_v[h].T.astype(bf16)

    def grad_normed(b):
        rows = pl.ds(b * 256, 256)
        return sum(matmul_tn(qkv_left[i, :, rows], attn[i]) for i in range(3))

    n_out[0] = grad_normed(1).astype(bf16)
    n_out[1] = grad_normed(3).astype(bf16)
    near = remote(n_out, n_in, (n_send, n_recv), 0, partners[0])
    near.start()
    folded[...] = grad_normed(2)
    near.wait_recv()
    f_out[...] = (folded[...] + n_in[1].astype(f32)).astype(bf16)
    far = remote(f_out, f_in, (n_send, n_recv), 1, partners[1])
    far.start()
    folded[...] = grad_normed(0) + n_in[0].astype(f32)
    far.wait_recv()
    grad_out = folded[...] + f_in[...].astype(f32)
    carried[...] = carried[...] + through_norm(hidden[...], 0, grad_out, 0)
    small_left[...] = turned(carried[...])
    back = matmul_nn(carried[...].astype(bf16), small[0])
    grad_clean[0] = (levels[0:1] * back - twice[...] * (predicted[...] - clean[...])).astype(bf16)
    shown = start_all(
        [
            remote(grad_clean.at[0], grad_clean.at[m], (c_send, c_recv), m - 1, partners[m - 1])
            for m in (2, 3, 1)
        ]
    )
    arrive_all(shown)
    for copy in mixed + [near, far] + shown:
        copy.wait_send()


def backward(*operands):
    dma, vmem = pltpu.SemaphoreType.DMA, pltpu.VMEM
    n = 256

    def shape(kind, *dims):
        return jax.ShapeDtypeStruct(dims, kind)

    return pl.pallas_call(
        backward_kernel,
        out_shape=[shape(bf16, n, EMBED_WIDTH)]
        + [shape(bf16, D, n)] * 5
        + [
            shape(bf16, 3, QUARTER, 4 * n),
            shape(bf16, 4, n, UNIT),
            shape(bf16, 4, n, EMBED_WIDTH),
            shape(f32, 16, UNIT),
        ],
        in_specs=[VMEM] * 21 + [ANY] * 2 + [VMEM],
        out_specs=[VMEM] * 10,
        scratch_shapes=[
            vmem((4, D, UNIT), bf16),
            vmem((4, D, UNIT), bf16),
            vmem((n, D), f32),
            vmem((n, D), f32),
            vmem((4, n, QUARTER), bf16),
            vmem((3, n, QUARTER), bf16),
            vmem((3, 4 * n, HDIM), f32),
            vmem((3, 4 * n, HDIM), f32),
            vmem((2, n, D), bf16),
            vmem((2, n, D), bf16),
            vmem((n, D), bf16),
            vmem((n, D), bf16),
            dma((8,)),
        ]
        + [dma((3,))] * 6,
        compiler_params=pltpu.CompilerParams(
            collective_id=6, has_side_effects=True, vmem_limit_bytes=60 * 2**20
        ),
    )(*operands)

I16 = jnp.int16
TAIL = 16
TILES = 60


def exponent(peak):
    return jnp.ceil(jnp.log2(jnp.maximum(peak, 1e-30))) + 1.0


def coded(value, power):
    return jnp.round(value * jnp.exp2(15.0 - power)).astype(jnp.int32).astype(I16)


def plain(code, power):
    return code.astype(jnp.int32).astype(f32) * jnp.exp2(power - 15.0)


def put(ref, value):
    rows, cols = value.shape
    power = exponent(jnp.max(jnp.abs(value), 0, keepdims=True))
    ref[0:rows, :] = coded(value, power)
    ref[rows : rows + TAIL, :] = (
        jnp.broadcast_to(power, (TAIL, cols)).astype(jnp.int32).astype(I16)
    )


def get(ref, rows):
    power = ref[rows : rows + TAIL, :].astype(jnp.int32).astype(f32)[0:1]
    return plain(ref[0:rows, :], power)


def put_tiles(ref, source, rows):
    lane = lax.broadcasted_iota(jnp.int32, (rows, LANES), 1)

    def body(tile, powers):
        at = pl.ds(pl.multiple_of(tile * LANES, LANES), LANES)
        value = source(at)
        power = exponent(jnp.max(jnp.abs(value), 1, keepdims=True))
        ref[:, at] = coded(value, power)
        return jnp.where(lane == tile, power, powers)

    powers = lax.fori_loop(0, TILES, body, jnp.zeros((rows, LANES), f32), unroll=6)
    ref[:, TILES * LANES :] = powers.astype(jnp.int32).astype(I16)


def tile_getter(ref, rows):
    lane = lax.broadcasted_iota(jnp.int32, (rows, LANES), 1)
    powers = ref[:, TILES * LANES :].astype(jnp.int32).astype(f32)

    def read(tile, at):
        power = jnp.sum(jnp.where(lane == tile, powers, 0.0), 1, keepdims=True)
        return plain(ref[:, at], power)

    return read


def grads_kernel(
    owners, down_left, up_left, out_left, small_left, final_left, qkv_left,
    active, grad_up, mixed, inputs, grad_pred, normed, pred_all, grad_clean, table_t, lse, weight, row_of, tile,
    summed, table_sum, tile_sum,
    home, small_home, outgoing, cs, cr, xs, xr, ys, yr, zs, zr, part, half,
    small_cs, small_cr, small_xs, small_xr, small_ys, small_yr, small_zs, small_zr, small_half,
    table, pred_t, clean_t, ts, tr, tzs, tzr, tile_at, tile_from,
    c_send, c_recv, x_send, x_recv, y_send, y_recv, z_send, z_recv, t_send, t_recv, a_send, a_recv, local,
):
    z, y, d, v = place()
    far, near = v ^ 2, v ^ 1
    greet([(d ^ m, v) for m in TRADE_MASKS] + [(d, far), (d, near)])
    sent = []

    def send(src, dst, sems, index, partner):
        copy = remote(src, dst, sems, index, partner)
        copy.start()
        sent.append(copy)
        return copy

    def product(n, who):
        if n == 0:
            return matmul_nn(out_left[who], mixed[...])
        if n < 5:
            return matmul_nn(down_left[who], active[n - 1])
        return matmul_nn(up_left[who], grad_up[n - 5])

    core, chip, side, line = {}, {}, {}, {}

    def to_core(n):
        put(cs.at[n, 0], product(n, near))
        put(cs.at[n, 1], product(n, near ^ 2))
        core[n] = send(cs.at[n], cr.at[n], (c_send, c_recv), n, (d, near))

    def to_chip(n):
        core[n].wait_recv()
        put(xs.at[n], product(n, far) + get(cr.at[n, 1], QUARTER))
        chip[n] = send(xs.at[n], xr.at[n], (x_send, x_recv), n, (d, far))

    def halves(slot, value):
        part[...] = value
        put(ys.at[slot], part[pl.ds((1 - y) * HALF, HALF), :])
        half[slot] = part[pl.ds(y * HALF, HALF), :]
        side[slot] = send(ys.at[slot], yr.at[slot], (y_send, y_recv), slot, (d ^ 1, v))

    def to_side(n):
        chip[n].wait_recv()
        value = product(n, v) + get(cr.at[n, 0], QUARTER) + get(xr.at[n], QUARTER)
        halves(3 + n, value)

    def to_line(group):
        for u in range(4):
            slot = 4 * group + u
            side[slot].wait_recv()
            half[slot] = half[slot] + get(yr.at[slot], HALF)
        for k in (2, 1, 3):
            put(zs.at[group, k - 1], half[4 * group + (z ^ k)])
            line[group, k] = send(
                zs.at[group, k - 1], zr.at[group, k - 1], (z_send, z_recv), 3 * group + k - 1, (d ^ (2 * k), v)
            )

    def to_home(group):
        total = half[4 * group + z]
        for k in (2, 1, 3):
            line[group, k].wait_recv()
            total = total + get(zr.at[group, k - 1], HALF)
        put(home.at[group], total)

    def small_product(who):
        return jnp.concatenate(
            [matmul_nn(small_left[who], inputs[...]), matmul_nn(final_left[who], grad_pred[...])], 1
        )

    def small_to_core():
        put(small_cs.at[0], small_product(near))
        put(small_cs.at[1], small_product(near ^ 2))
        core[9] = send(small_cs, small_cr, (c_send, c_recv), 9, (d, near))

    def small_to_chip():
        core[9].wait_recv()
        put(small_xs, small_product(far) + get(small_cr.at[1], QUARTER))
        chip[9] = send(small_xs, small_xr, (x_send, x_recv), 9, (d, far))

    def small_to_side():
        chip[9].wait_recv()
        value = small_product(v) + get(small_cr.at[0], QUARTER) + get(small_xr, QUARTER)
        cols = value.shape[1]
        part[:, 0:cols] = value
        put(small_ys, part[pl.ds((1 - y) * HALF, HALF), 0:cols])
        small_half[0] = part[pl.ds(y * HALF, HALF), 0:LANES]
        small_half[1] = part[pl.ds(y * HALF, HALF), LANES : 2 * LANES]
        small_half[2] = part[pl.ds(y * HALF, HALF), 2 * LANES : cols]
        small_half[3] = jnp.zeros((HALF, LANES), f32)
        side[12] = send(small_ys, small_yr, (y_send, y_recv), 12, (d ^ 1, v))

    def small_to_line():
        side[12].wait_recv()
        value = get(small_yr, HALF)
        for u in range(3):
            small_half[u] = small_half[u] + value[:, u * LANES : (u + 1) * LANES]
        for k in (2, 1, 3):
            put(small_zs.at[k - 1], small_half[z ^ k])
            line[3, k] = send(
                small_zs.at[k - 1], small_zr.at[k - 1], (z_send, z_recv), 9 + k - 1, (d ^ (2 * k), v)
            )

    def small_to_home():
        total = small_half[z]
        for k in (2, 1, 3):
            line[3, k].wait_recv()
            total = total + get(small_zr.at[k - 1], HALF)
        put(small_home, total)

    def turn_tokens():
        for b in range(4):
            pred_t[b] = pred_all[b].astype(f32).T.astype(bf16)
            clean_t[b] = grad_clean[b].astype(f32).T.astype(bf16)

    vocab_rows = table_t.shape[0]

    def table_strip(lo, size):
        total = jnp.zeros((EMBED_WIDTH, size), f32)
        for b in range(4):
            logits = matmul_nt(table_t[lo : lo + size, :], pred_all[b])
            probs = jnp.exp(logits - lse[b : b + 1, :])
            here = lax.broadcasted_iota(jnp.int32, (size, 256), 0) == row_of[b : b + 1, :] - lo
            here = here.astype(f32)
            grad_logits = ((probs - here) * weight[b : b + 1, :]).astype(bf16)
            total = total + matmul_nt(pred_t[b], grad_logits)
            total = total + matmul_nt(clean_t[b], here.astype(bf16))
        for i in range(8):
            rows = slice(16 * (i // 2), 16 * (i // 2) + 16)
            table[i % 2, rows, lo : lo + size] = total[16 * i : 16 * i + 16]
        if lo + size == vocab_rows:
            table[:, :, vocab_rows:] = jnp.zeros((2, 64, TILES * LANES - vocab_rows), f32)

    table_strips = [(lo, min(STRIP, vocab_rows - lo)) for lo in range(0, vocab_rows, STRIP)]

    def table_to_side():
        put_tiles(ts, lambda at: table[1 - y, :, at], 64)
        side[13] = send(ts, tr, (y_send, y_recv), 13, (d ^ 1, v))

    def table_line_value(which):
        rows = pl.ds(pl.multiple_of(which * 16, 16), 16)
        read = tile_getter(tr.at[rows, :], 16)
        return rows, read

    def table_to_line():
        side[13].wait_recv()
        for k in (2, 1, 3):
            rows, read = table_line_value(z ^ k)

            def source(at, rows=rows, read=read):
                return table[y, rows, at] + read(at.start // LANES, at)

            put_tiles(tzs.at[k - 1], source, 16)
            line[4, k] = send(
                tzs.at[k - 1], tzr.at[k - 1], (z_send, z_recv), 12 + k - 1, (d ^ (2 * k), v)
            )

    def table_to_home():
        for k in (2, 1, 3):
            line[4, k].wait_recv()
        rows, read = table_line_value(z)
        others = [tile_getter(tzr.at[k], 16) for k in range(3)]

        def body(tile, carry):
            at = pl.ds(pl.multiple_of(tile * LANES, LANES), LANES)
            value = table[y, rows, at] + read(tile, at)
            for other in others:
                value = value + other(tile, at)
            table_sum[:, at] = value
            return carry

        lax.fori_loop(0, TILES, body, 0, unroll=4)

    hops = [(d, near), (d, far), (d ^ 1, v), (d ^ 2, v), (d ^ 4, v)]
    tile_copies = {}

    def tile_send(hop):
        if hop == 0:
            tile_at[0] = tile[...]
        else:
            tile_copies[hop - 1].wait_recv()
            tile_at[hop] = tile_at[hop - 1] + tile_from[hop - 1]
        tile_copies[hop] = send(
            tile_at.at[hop], tile_from.at[hop], (t_send, t_recv), hop, hops[hop]
        )

    turn_tokens()
    to_core(0)
    to_core(1)
    to_chip(0)
    tile_send(0)
    to_core(2)
    table_strip(*table_strips[0])
    to_chip(1)
    table_strip(*table_strips[1])
    table_strip(*table_strips[2])
    to_core(3)
    to_chip(2)
    table_strip(*table_strips[3])
    table_strip(*table_strips[4])
    table_strip(*table_strips[5])
    to_core(4)
    to_chip(3)
    table_strip(*table_strips[6])
    table_strip(*table_strips[7])
    for strip in table_strips[8:]:
        table_strip(*strip)
    table_to_side()
    tile_send(1)
    for u in range(3):
        halves(u, sum(matmul_nn(qkv_left[u, :, 256 * b : 256 * b + 256], normed[b]) for b in range(4)))
    small_to_core()
    to_core(5)
    to_chip(4)
    to_side(0)
    tile_send(2)
    to_core(6)
    to_chip(5)
    small_to_chip()
    to_side(1)
    table_to_line()
    tile_send(3)
    to_core(7)
    to_chip(6)
    to_side(2)
    to_line(0)
    to_core(8)
    to_chip(7)
    tile_send(4)
    to_side(3)
    to_chip(8)
    to_side(4)
    to_line(1)
    small_to_side()
    table_to_home()
    to_side(5)
    to_home(0)
    to_side(6)
    small_to_line()
    to_side(7)
    to_home(1)
    to_side(8)
    to_line(2)
    small_to_home()
    tile_copies[4].wait_recv()
    tile_sum[...] = tile_at[4] + tile_from[4]
    to_home(2)

    def offer(m):
        taker = d ^ m
        unit = jnp.where(owners[4] == taker, home[2], home[0])
        outgoing[m, :, 0:UNIT] = jnp.where(owners[5] == taker, home[1], unit)
        outgoing[m, :, UNIT:] = small_home[...]

    offered = []
    for i, m in enumerate(TRADE_MASKS):
        offer(m)
        offered.append(send(outgoing.at[m], summed.at[d], (a_send, a_recv), i, (d ^ m, v)))
    offer(0)
    keep = pltpu.make_async_copy(outgoing.at[0], summed.at[d], local)
    keep.start()
    keep.wait()
    arrive_all(offered)
    for copy in sent:
        copy.wait_send()


def reduce_grads(*operands):
    dma = pltpu.SemaphoreType.DMA
    vmem = pltpu.VMEM
    tall, low, wide = QUARTER + TAIL, HALF + TAIL, 3 * LANES
    table_cols = TILES * LANES
    return pl.pallas_call(
        grads_kernel,
        out_shape=[
            jax.ShapeDtypeStruct((8, low, UNIT + LANES), I16),
            jax.ShapeDtypeStruct((16, table_cols), f32),
            jax.ShapeDtypeStruct((16, UNIT), f32),
        ],
        in_specs=[SMEM] + [VMEM] * 19,
        out_specs=[VMEM] * 3,
        scratch_shapes=[
            vmem((3, low, UNIT), I16),
            vmem((low, LANES), I16),
            vmem((8, low, UNIT + LANES), I16),
            vmem((9, 2, tall, UNIT), I16),
            vmem((9, 2, tall, UNIT), I16),
            vmem((9, tall, UNIT), I16),
            vmem((9, tall, UNIT), I16),
            vmem((12, low, UNIT), I16),
            vmem((12, low, UNIT), I16),
            vmem((3, 3, low, UNIT), I16),
            vmem((3, 3, low, UNIT), I16),
            vmem((QUARTER, UNIT), f32),
            vmem((12, HALF, UNIT), f32),
            vmem((2, tall, wide), I16),
            vmem((2, tall, wide), I16),
            vmem((tall, wide), I16),
            vmem((tall, wide), I16),
            vmem((low, wide), I16),
            vmem((low, wide), I16),
            vmem((3, low, LANES), I16),
            vmem((3, low, LANES), I16),
            vmem((4, HALF, LANES), f32),
            vmem((2, 64, table_cols), f32),
            vmem((4, EMBED_WIDTH, 256), bf16),
            vmem((4, EMBED_WIDTH, 256), bf16),
            vmem((64, table_cols + LANES), I16),
            vmem((64, table_cols + LANES), I16),
            vmem((3, 16, table_cols + LANES), I16),
            vmem((3, 16, table_cols + LANES), I16),
            vmem((5, 16, UNIT), f32),
            vmem((5, 16, UNIT), f32),
        ]
        + [dma((10,))] * 4
        + [dma((14,))] * 2
        + [dma((15,))] * 2
        + [dma((5,))] * 2
        + [dma((7,))] * 2
        + [dma],
        compiler_params=pltpu.CompilerParams(
            collective_id=2, has_side_effects=True, vmem_limit_bytes=60 * 2**20
        ),
    )(*operands)


def slot_kernel(kind, unit, column, big, small, w, m1, m2, w_out, m1_out, m2_out):
    which = kind[pl.program_id(0)]

    def rows_of(ref):
        return jnp.concatenate([get(ref.at[0], HALF), get(ref.at[1], HALF)], 0)

    zero = jnp.zeros(w.shape, f32)
    g = jnp.where(which == 1, rows_of(big), jnp.where(which == 2, rows_of(small), zero))
    w_out[...], m1_out[...], m2_out[...] = adamw(w[...], g, m1[...], m2[...])


def slot_update(kind, unit, column, summed, slots, first, second):
    rows = slots.shape[0]
    blocks = CAP // LANES
    per_unit = UNIT // LANES
    plain_spec = pl.BlockSpec((rows, LANES), lambda j, k, u, c: (0, j))
    low = HALF + TAIL
    big_spec = pl.BlockSpec(
        (2, low, LANES),
        lambda j, k, u, c: (jnp.where(k[j] == 1, u[j], 0), 0, jnp.where(k[j] == 1, c[j], 0)),
    )
    small_spec = pl.BlockSpec(
        (2, low, LANES), lambda j, k, u, c: (jnp.where(k[j] == 2, u[j], 0), 0, per_unit)
    )
    return pl.pallas_call(
        slot_kernel,
        grid_spec=pltpu.PrefetchScalarGridSpec(
            num_scalar_prefetch=3,
            grid=(blocks,),
            in_specs=[big_spec, small_spec, plain_spec, plain_spec, plain_spec],
            out_specs=[plain_spec, plain_spec, plain_spec],
        ),
        out_shape=[jax.ShapeDtypeStruct(slots.shape, f32)] * 3,
        cost_estimate=pl.CostEstimate(flops=0, bytes_accessed=28 * rows * CAP, transcendentals=0),
    )(kind, unit, column, summed, summed, slots, first, second)


def per_device(
    token_ids,
    timesteps,
    pad_mask,
    noise_draw,
    owners,
    emb_table,
    table_first_moment,
    table_second_moment,
    mat_slots,
    slot_first,
    slot_second,
    vec_params,
    vec_first,
    vec_second,
):
    v = lax.axis_index("vocab")
    seq_len = token_ids.shape[1]
    tokens = seq_len // 4
    vocab_rows, emb_cols = emb_table.shape
    table_own = emb_table.T
    (
        payload, table_home, row_of, safe_row, keep_rows, keep_column, valid_column, count_tile,
        kind, unit, column,
    ) = prepare(owners, token_ids, pad_mask, table_own, mat_slots)
    w_up, w_down, w_small, w_attn, w_out, table_low, row_weight, twice = spread(
        owners, payload, count_tile, keep_rows, keep_column, table_home
    )
    table_low = table_low.reshape(EMBED_WIDTH, vocab_rows)
    table_t = table_low.T
    looked = table_t.at[safe_row[0]].get(mode="promise_in_bounds").reshape(4, tokens, EMBED_WIDTH)
    own_places = (v * tokens + jnp.arange(tokens)).astype(f32)
    step_val = timesteps[0].astype(f32)
    signal_level = 1.0 - jnp.sqrt(step_val / DIFF + 0.0001)
    levels = jnp.concatenate(
        [
            jnp.full((1, EMBED_WIDTH), jnp.sqrt(signal_level)),
            jnp.full((1, EMBED_WIDTH), jnp.sqrt(1.0 - signal_level)),
            waves(step_val[None], EMBED_WIDTH),
            jnp.zeros((5, EMBED_WIDTH), f32),
        ]
    )
    vecs = vec_params.reshape(10, D)
    (
        found_rows, clean_emb, inputs, hidden, normed_all, q_h, k_h, k_t, v_h, log_total, mixed_own, middle,
        normed_two, up_proj, active, hidden_two, final_norm, predicted, pred_all,
    ) = forward(
        looked,
        valid_column,
        noise_draw[0],
        levels,
        waves(own_places, D),
        w_small,
        w_attn,
        w_out,
        w_up,
        w_down,
        vecs,
        keep_column,
    )
    grad_pred, head_stats = head(
        pred_all,
        table_low,
        table_t,
        row_of,
        row_weight,
        found_rows,
    )
    (
        grad_pred_low, down_left, up_left, out_left, small_left, final_left, qkv_left, grad_up, grad_clean, sums,
    ) = backward(
        grad_pred, clean_emb, predicted, twice, levels, head_stats,
        hidden, middle, hidden_two, normed_two, final_norm, up_proj,
        q_h, k_h, k_t, v_h, log_total, keep_column,
        w_small, w_attn, w_out, w_up, w_down, vecs,
    )

    def left(value):
        return value.reshape(4, QUARTER, tokens)

    summed, table_grad, tile_sum = reduce_grads(
        owners,
        left(down_left),
        left(up_left),
        left(out_left),
        left(small_left),
        left(final_left),
        qkv_left,
        active,
        grad_up,
        mixed_own,
        inputs,
        grad_pred_low,
        normed_all,
        pred_all,
        grad_clean,
        table_t,
        head_stats,
        row_weight,
        row_of,
        sums,
    )
    tile_sum = tile_sum.reshape(16 * UNIT)
    vec_share = vec_first.shape[0]
    own_grad = lax.dynamic_slice_in_dim(tile_sum, v * vec_share, vec_share)
    own_vecs = lax.dynamic_slice_in_dim(vec_params, v * vec_share, vec_share)
    vec_len = vec_params.shape[0]
    count_all = tile_sum[vec_len + 3]
    square = tile_sum[vec_len] * (0.5 * count_all)
    cross_sum = tile_sum[vec_len + 1] * count_all
    emb_norm = tile_sum[vec_len + 2] * 0.5

    new_slots, slot_first_new, slot_second_new = slot_update(
        kind, unit, column, summed, mat_slots, slot_first, slot_second
    )
    new_table, table_first_new, table_second_new = adamw(
        table_own, table_grad[:, :vocab_rows], table_first_moment.T, table_second_moment.T
    )
    new_vecs, vec_first_new, vec_second_new = adamw(own_vecs, own_grad, vec_first, vec_second)
    loss_pair = jnp.stack([square + cross_sum, count_all])
    return (
        loss_pair,
        emb_norm,
        new_table.T,
        table_first_new.T,
        table_second_new.T,
        new_slots,
        slot_first_new,
        slot_second_new,
        new_vecs,
        vec_first_new,
        vec_second_new,
    )


def broadcast(value, axis, source):
    kept = jnp.where(lax.axis_index(axis) == source, value, 0).astype(value.dtype)
    return lax.psum(kept, axis)


def merged(value, axis, join):
    pieces = jax.tree.map(lambda part: lax.all_gather(part, axis), value)
    head = jax.tree.map(lambda part: part[0], pieces)
    tail = jax.tree.map(lambda part: part[1:], pieces)
    so_far, _ = lax.scan(lambda so_far, share: (join(so_far, share), None), head, tail)
    return so_far


def matrix_rows():
    return [D, D, D, D, FF, FF] * LAYERS + [EMBED_WIDTH, EMBED_WIDTH, EMBED_WIDTH]


def slot_places(owners):
    counts = jnp.array(matrix_rows(), jnp.int32)
    mat_total = counts.shape[0]
    same_owner = (owners[:, None] == owners[None, :]).astype(jnp.int32)
    earlier_mask = jnp.tril(jnp.ones((mat_total, mat_total), jnp.int32), -1)
    return owners * CAP + jnp.sum(same_owner * earlier_mask * counts[None, :], 1)


def block_scores(query_blk, keys_all, keep_keys, score_scale):
    scores = (
        jnp.einsum("qhd,khd->hqk", query_blk, keys_all, preferred_element_type=jnp.float32)
        * score_scale
    )
    return jnp.where(keep_keys[None, None, :], scores, -1000000000.0)


def attention(queries, keys_all, values_all, keep_keys, score_scale):
    tokens = queries.shape[0]
    width = min(512, tokens)
    query_blocks = queries.reshape(tokens // width, width, HEADS, HDIM)

    def one_block(query_blk):
        scores = block_scores(query_blk, keys_all, keep_keys, score_scale)
        row_max = jnp.max(scores, -1, keepdims=True)
        expo = jnp.exp(scores - row_max)
        exp_total = jnp.sum(expo, -1, keepdims=True)
        probabilities = (expo / exp_total).astype(jnp.bfloat16)
        mixed_out = jnp.einsum(
            "hqk,khd->qhd", probabilities, values_all, preferred_element_type=jnp.float32
        )
        return (mixed_out, (row_max + jnp.log(exp_total))[..., 0])

    mixed_out, log_total = lax.map(one_block, query_blocks)
    return (mixed_out.reshape(tokens, HEADS, HDIM), log_total)


def attention_back(queries, keys_all, values_all, keep_keys, log_total, grad_mixed, score_scale):
    tokens = queries.shape[0]
    width = min(512, tokens)
    query_blocks = queries.reshape(tokens // width, width, HEADS, HDIM)
    grad_blocks = grad_mixed.reshape(tokens // width, width, HEADS, HDIM)

    def one_block(carry_sums, block_data):
        query_blk, total_blk, grad_blk = block_data
        scores = block_scores(query_blk, keys_all, keep_keys, score_scale)
        probabilities = jnp.exp(scores - total_blk[..., None])
        grad_probs = jnp.einsum(
            "qhd,khd->hqk", grad_blk, values_all, preferred_element_type=jnp.float32
        )
        inner_sum = jnp.sum(probabilities * grad_probs, -1, keepdims=True)
        grad_scores = (probabilities * (grad_probs - inner_sum)).astype(jnp.bfloat16)
        grad_query = (
            jnp.einsum("hqk,khd->qhd", grad_scores, keys_all, preferred_element_type=jnp.float32)
            * score_scale
        )
        grad_key = (
            jnp.einsum("hqk,qhd->khd", grad_scores, query_blk, preferred_element_type=jnp.float32)
            * score_scale
        )
        grad_value = jnp.einsum(
            "hqk,qhd->khd",
            probabilities.astype(jnp.bfloat16),
            grad_blk,
            preferred_element_type=jnp.float32,
        )
        return ((carry_sums[0] + grad_key, carry_sums[1] + grad_value), grad_query)

    zero_keys = jnp.zeros(keys_all.shape, jnp.float32)
    grad_kv, grad_queries = lax.scan(
        one_block, (zero_keys, zero_keys), (query_blocks, log_total, grad_blocks)
    )
    return (grad_queries.reshape(tokens, D), grad_kv[0].reshape(-1, D), grad_kv[1].reshape(-1, D))


def send_matrix(piece_cols, root):
    return broadcast(piece_cols, "dp", root)


def fetch_keys(key_rows, value_rows):
    return (
        lax.all_gather(key_rows, "vocab", axis=0, tiled=True),
        lax.all_gather(value_rows, "vocab", axis=0, tiled=True),
    )


def layer_forward(hidden, weights, vec_layer, keep_keys, score_scale):
    w_query, w_key, w_value, w_out, w_up, w_down = weights
    tokens = hidden.shape[0]
    norm_one, inv_one = norm_parts(hidden)
    normed = (norm_one * vec_layer[0:D] + vec_layer[D : 2 * D]).astype(jnp.bfloat16)
    queries = matmul_nn(normed, w_query).astype(jnp.bfloat16)
    key_rows = matmul_nn(normed, w_key).astype(jnp.bfloat16)
    value_rows = matmul_nn(normed, w_value).astype(jnp.bfloat16)
    keys_all, values_all = fetch_keys(key_rows, value_rows)
    keys_all = keys_all.reshape(-1, HEADS, HDIM)
    values_all = values_all.reshape(-1, HEADS, HDIM)
    mixed_out, log_total = attention(
        queries.reshape(tokens, HEADS, HDIM), keys_all, values_all, keep_keys, score_scale
    )
    mixed_low = mixed_out.reshape(tokens, D).astype(jnp.bfloat16)
    middle = hidden + matmul_nn(mixed_low, w_out)
    norm_two, inv_two = norm_parts(middle)
    normed_two = (norm_two * vec_layer[2 * D : 3 * D] + vec_layer[3 * D : 4 * D]).astype(
        jnp.bfloat16
    )
    up_proj = matmul_nt(normed_two, w_up) + vec_layer[4 * D :]
    active = jax.nn.gelu(up_proj).astype(jnp.bfloat16)
    out_rows = middle + matmul_nn(active, w_down)
    kept_vals = (
        norm_one,
        inv_one,
        normed,
        queries,
        key_rows,
        value_rows,
        keys_all,
        values_all,
        log_total,
        mixed_low,
        norm_two,
        inv_two,
        normed_two,
        up_proj,
        active,
    )
    return (out_rows, kept_vals)


def layer_backward(grad_out, kept_vals, weights, vec_layer, keep_keys, score_scale):
    w_query, w_key, w_value, w_out, w_up, w_down = weights
    (
        norm_one,
        inv_one,
        normed,
        queries,
        key_rows,
        value_rows,
        keys_all,
        values_all,
        log_total,
        mixed_low,
        norm_two,
        inv_two,
        normed_two,
        up_proj,
        active,
    ) = kept_vals
    tokens = grad_out.shape[0]
    grad_low = grad_out.astype(jnp.bfloat16)
    grad_down = matmul_tn(active, grad_low)
    grad_active = matmul_nt(grad_low, w_down)
    grad_up_proj = jax.vjp(jax.nn.gelu, up_proj)[1](grad_active)[0].astype(jnp.bfloat16)
    grad_bias = jnp.sum(grad_up_proj.astype(jnp.float32), 0)
    grad_up = matmul_tn(grad_up_proj, normed_two)
    grad_normed_two = matmul_nn(grad_up_proj, w_up)
    grad_part, grad_gain_two, grad_shift_two = norm_back(
        norm_two, inv_two, vec_layer[2 * D : 3 * D], grad_normed_two
    )
    grad_middle = grad_out + grad_part
    grad_attn = grad_middle.astype(jnp.bfloat16)
    grad_out_w = matmul_tn(mixed_low, grad_attn)
    grad_mixed = matmul_nt(grad_attn, w_out).astype(jnp.bfloat16).reshape(tokens, HEADS, HDIM)
    grad_queries, grad_keys_all, grad_values_all = attention_back(
        queries.reshape(tokens, HEADS, HDIM),
        keys_all,
        values_all,
        keep_keys,
        log_total,
        grad_mixed,
        score_scale,
    )
    grad_key_rows, grad_value_rows = (
        lax.psum_scatter(
            grad_keys_all.astype(jnp.bfloat16), "vocab", scatter_dimension=0, tiled=True
        ).astype(jnp.float32),
        lax.psum_scatter(
            grad_values_all.astype(jnp.bfloat16), "vocab", scatter_dimension=0, tiled=True
        ).astype(jnp.float32),
    )
    grad_q_low = grad_queries.astype(jnp.bfloat16)
    grad_k_low = grad_key_rows.astype(jnp.bfloat16)
    grad_v_low = grad_value_rows.astype(jnp.bfloat16)
    grad_wq = matmul_tn(normed, grad_q_low)
    grad_wk = matmul_tn(normed, grad_k_low)
    grad_wv = matmul_tn(normed, grad_v_low)
    grad_normed = (
        matmul_nt(grad_q_low, w_query)
        + matmul_nt(grad_k_low, w_key)
        + matmul_nt(grad_v_low, w_value)
    )
    grad_part_one, grad_gain_one, grad_shift_one = norm_back(
        norm_one, inv_one, vec_layer[0:D], grad_normed
    )
    grad_hidden = grad_middle + grad_part_one
    grad_mats = [grad_wq, grad_wk, grad_wv, grad_out_w, grad_up, grad_down]
    grad_vec = jnp.concatenate(
        [grad_gain_one, grad_shift_one, grad_gain_two, grad_shift_two, grad_bias]
    )
    return (grad_hidden, grad_mats, grad_vec)


def merge_stats(first_part, second_part):
    peak_val = jnp.maximum(first_part[0], second_part[0])
    exp_total = first_part[1] * jnp.exp(first_part[0] - peak_val) + second_part[1] * jnp.exp(
        second_part[0] - peak_val
    )
    return (peak_val, exp_total, first_part[2] + second_part[2])


def any_mesh_device(
    token_ids,
    timesteps,
    pad_mask,
    noise_draw,
    owners,
    emb_table,
    table_first_moment,
    table_second_moment,
    mat_slots,
    slot_first,
    slot_second,
    vec_params,
    vec_first,
    vec_second,
):
    vocab_count = lax.axis_size("vocab")
    vocab_pos = lax.axis_index("vocab")
    data_pos = lax.axis_index("dp")
    seq_len = token_ids.shape[1]
    tokens = seq_len // vocab_count
    vocab_rows = emb_table.shape[0]
    score_scale = HDIM ** (-0.5)
    table_low = lax.all_gather(emb_table.astype(jnp.bfloat16), "dp", axis=1, tiled=True)
    row_counts = matrix_rows()
    local_start = slot_places(owners) - owners * CAP
    sent_pieces = [
        send_matrix(
            lax.dynamic_slice_in_dim(
                mat_slots, local_start[mat_idx], row_counts[mat_idx], 1
            ).astype(jnp.bfloat16),
            owners[mat_idx],
        )
        for mat_idx in range(len(row_counts))
    ]
    canon = jnp.concatenate(sent_pieces, 1)
    weights = lax.all_gather(canon, "vocab", axis=0, tiled=True).T
    layer_rows = 4 * D + 2 * FF
    vec_rows = 4 * D + FF
    tail_at = LAYERS * layer_rows

    def layer_weights(layer_idx):
        begin_row = layer_idx * layer_rows
        cuts = [
            begin_row,
            begin_row + D,
            begin_row + 2 * D,
            begin_row + 3 * D,
            begin_row + 4 * D,
            begin_row + 4 * D + FF,
            begin_row + layer_rows,
        ]
        return [weights[cuts[cut_idx] : cuts[cut_idx + 1]] for cut_idx in range(6)]

    w_input = weights[tail_at : tail_at + 2 * EMBED_WIDTH]
    w_final = weights[tail_at + 2 * EMBED_WIDTH : tail_at + 3 * EMBED_WIDTH]
    seq_ids = token_ids[0]
    seq_mask = pad_mask[0].astype(jnp.float32)
    keep_keys = pad_mask[0] > 0
    local_row = seq_ids - vocab_pos * vocab_rows
    valid_row = (local_row >= 0) & (local_row < vocab_rows)
    safe_row = jnp.clip(local_row, 0, vocab_rows - 1)
    found_rows = jnp.where(
        valid_row[:, None], jnp.take(table_low, safe_row, axis=0), jnp.zeros((), jnp.bfloat16)
    )
    arrived = lax.all_to_all(found_rows, "vocab", split_axis=0, concat_axis=0, tiled=True)
    clean_emb = jnp.sum(arrived.reshape(vocab_count, tokens, EMBED_WIDTH).astype(jnp.float32), 0)
    own_first = vocab_pos * tokens
    mask_own = lax.dynamic_slice_in_dim(seq_mask, own_first, tokens)
    own_places = (own_first + jnp.arange(tokens)).astype(jnp.float32)
    step_val = timesteps[0].astype(jnp.float32)
    signal_level = 1.0 - jnp.sqrt(step_val / DIFF + 0.0001)
    noisy_emb = jnp.sqrt(signal_level) * clean_emb + jnp.sqrt(1.0 - signal_level) * noise_draw[
        0
    ].astype(jnp.float32)
    time_feat = jnp.broadcast_to(waves(step_val[None], EMBED_WIDTH), (tokens, EMBED_WIDTH))
    inputs = jnp.concatenate([noisy_emb, time_feat], 1).astype(jnp.bfloat16)
    hidden = matmul_nn(inputs, w_input) + waves(own_places, D)
    layer_idx = 0
    vec_layer = vec_params[layer_idx * vec_rows : (layer_idx + 1) * vec_rows]
    hidden, kept_vals = layer_forward(
        hidden, layer_weights(layer_idx), vec_layer, keep_keys, score_scale
    )
    kept_list = [kept_vals]
    gain_final = vec_params[LAYERS * vec_rows : LAYERS * vec_rows + D]
    shift_final = vec_params[LAYERS * vec_rows + D :]
    norm_final, inv_final = norm_parts(hidden)
    final_norm = (norm_final * gain_final + shift_final).astype(jnp.bfloat16)
    predicted = matmul_nt(final_norm, w_final)
    pred_all = lax.all_gather(predicted.astype(jnp.bfloat16), "vocab", axis=0, tiled=True)
    head_width = min(512, seq_len)
    head_count = seq_len // head_width
    columns = jnp.arange(vocab_rows)
    pred_blocks = pred_all.reshape(head_count, head_width, EMBED_WIDTH)
    row_blocks = local_row.reshape(head_count, head_width)

    def head_stats(block_data):
        pred_blk, rows_blk = block_data
        logits = matmul_nt(pred_blk, table_low)
        row_max = jnp.max(logits, -1)
        exp_total = jnp.sum(jnp.exp(logits - row_max[:, None]), -1)
        target = jnp.sum(jnp.where(columns[None, :] == rows_blk[:, None], logits, 0.0), -1)
        return (row_max, exp_total, target)

    peaks, totals, targets = lax.map(head_stats, (pred_blocks, row_blocks))
    peak_all, total_all, target_all = merged(
        (peaks.reshape(seq_len), totals.reshape(seq_len), targets.reshape(seq_len)),
        "vocab",
        merge_stats,
    )
    log_total = peak_all + jnp.log(total_all)
    lse_own = lax.dynamic_slice_in_dim(log_total, own_first, tokens)
    target_own = lax.dynamic_slice_in_dim(target_all, own_first, tokens)
    pred_error = predicted - clean_emb
    square_own = jnp.sum(mask_own[:, None] * pred_error * pred_error)
    cross_own = jnp.sum(mask_own * (lse_own - target_own))
    norm_own = jnp.sum(mask_own * jnp.sqrt(jnp.sum(clean_emb * clean_emb, -1) + 1e-06))
    count_all, square, cross_sum, norm_total = lax.psum(
        (jnp.sum(mask_own), square_own, cross_own, norm_own), ("dp", "vocab")
    )
    weight_blocks = (seq_mask / count_all).reshape(head_count, head_width)
    lse_blocks = log_total.reshape(head_count, head_width)

    def head_back(grad_table, block_data):
        pred_blk, rows_blk, lse_blk, weight_blk = block_data
        logits = matmul_nt(pred_blk, table_low)
        probabilities = jnp.exp(logits - lse_blk[:, None])
        onehot = (columns[None, :] == rows_blk[:, None]).astype(jnp.float32)
        grad_logits = ((probabilities - onehot) * weight_blk[:, None]).astype(jnp.bfloat16)
        return (grad_table + matmul_tn(grad_logits, pred_blk), matmul_nn(grad_logits, table_low))

    zero_table = jnp.zeros((vocab_rows, EMBED_WIDTH), jnp.float32)
    grad_table_head, grad_pred_blocks = lax.scan(
        head_back, zero_table, (pred_blocks, row_blocks, lse_blocks, weight_blocks)
    )
    grad_pred = lax.psum_scatter(
        grad_pred_blocks.reshape(seq_len, EMBED_WIDTH).astype(jnp.bfloat16),
        "vocab",
        scatter_dimension=0,
        tiled=True,
    ).astype(jnp.float32)
    error_grad = 2.0 * mask_own[:, None] * pred_error / count_all
    grad_pred_low = (grad_pred + error_grad).astype(jnp.bfloat16)
    grad_final_w = matmul_tn(grad_pred_low, final_norm)
    grad_final = matmul_nn(grad_pred_low, w_final)
    grad_hidden, grad_gain_final, grad_shift_final = norm_back(
        norm_final, inv_final, gain_final, grad_final
    )
    layer_grads = [None] * LAYERS
    vec_grads = [None] * LAYERS
    for layer_idx in reversed(range(LAYERS)):
        vec_layer = vec_params[layer_idx * vec_rows : (layer_idx + 1) * vec_rows]
        grad_hidden, layer_grads[layer_idx], vec_grads[layer_idx] = layer_backward(
            grad_hidden,
            kept_list[layer_idx],
            layer_weights(layer_idx),
            vec_layer,
            keep_keys,
            score_scale,
        )
    grad_hidden_low = grad_hidden.astype(jnp.bfloat16)
    grad_input_w = matmul_tn(inputs, grad_hidden_low)
    grad_inputs = matmul_nt(grad_hidden_low, w_input)
    grad_clean = jnp.sqrt(signal_level) * grad_inputs[:, :EMBED_WIDTH] - error_grad
    grad_clean_all = lax.all_gather(
        grad_clean.astype(jnp.bfloat16), "vocab", axis=0, tiled=True
    ).astype(grad_clean.dtype)
    grad_table_look = zero_table.at[safe_row].add(
        jnp.where(valid_row[:, None], grad_clean_all, 0.0)
    )
    grad_table_local = grad_table_head + grad_table_look
    canon_list = []
    layer_idx = 0
    canon_list = canon_list + layer_grads[layer_idx]
    canon_grad = jnp.concatenate(canon_list + [grad_input_w, grad_final_w], 0).T
    vec_grad = jnp.concatenate(vec_grads + [grad_gain_final, grad_shift_final])
    grad_cols, vec_part = (
        lax.psum_scatter(canon_grad, "vocab", scatter_dimension=0, tiled=True),
        lax.psum_scatter(vec_grad, "vocab", scatter_dimension=0, tiled=True),
    )
    emb_cols = emb_table.shape[1]
    summed_cols, summed_vec, summed_table = lax.psum((grad_cols, vec_part, grad_table_local), "dp")
    table_grad = lax.dynamic_slice_in_dim(summed_table, data_pos * emb_cols, emb_cols, 1)
    slot_grad = jnp.zeros_like(mat_slots)
    cursor = 0
    for mat_idx in range(len(row_counts)):
        piece_cols = summed_cols[:, cursor : cursor + row_counts[mat_idx]]
        updated = lax.dynamic_update_slice_in_dim(slot_grad, piece_cols, local_start[mat_idx], 1)
        slot_grad = jnp.where(owners[mat_idx] == data_pos, updated, slot_grad)
        cursor = cursor + row_counts[mat_idx]
    vec_share = vec_first.shape[0]
    own_vecs = lax.dynamic_slice_in_dim(vec_params, vocab_pos * vec_share, vec_share)
    new_slots, slot_first_new, slot_second_new = adamw(
        mat_slots, slot_grad, slot_first, slot_second
    )
    new_table, table_first_new, table_second_new = adamw(
        emb_table, table_grad, table_first_moment, table_second_moment
    )
    new_vecs, vec_first_new, vec_second_new = adamw(own_vecs, summed_vec, vec_first, vec_second)
    loss_pair = jnp.stack([square + cross_sum, count_all])
    emb_norm = norm_total / count_all
    return (
        loss_pair,
        emb_norm,
        new_table,
        table_first_new,
        table_second_new,
        new_slots,
        slot_first_new,
        slot_second_new,
        new_vecs,
        vec_first_new,
        vec_second_new,
    )


def solution(mesh):
    in_specs = (
        P("dp", None),
        P("dp"),
        P("dp", None),
        P("dp", "vocab", None),
        P(),
        P("vocab", "dp"),
        P("vocab", "dp"),
        P("vocab", "dp"),
        P("vocab", "dp"),
        P("vocab", "dp"),
        P("vocab", "dp"),
        P(),
        P("vocab"),
        P("vocab"),
    )
    out_specs = (
        P(),
        P(),
        P("vocab", "dp"),
        P("vocab", "dp"),
        P("vocab", "dp"),
        P("vocab", "dp"),
        P("vocab", "dp"),
        P("vocab", "dp"),
        P("vocab"),
        P("vocab"),
        P("vocab"),
    )
    fast = mesh.shape["dp"] == 8 and mesh.shape["vocab"] == 4
    body = per_device if fast else any_mesh_device
    return jax.shard_map(
        body, mesh=mesh, in_specs=in_specs, out_specs=out_specs, check_vma=False
    )
```

```python
import functools
import math

import jax
import jax.numpy as jnp
from jax import lax
from jax.experimental import pallas as pl
from jax.experimental.pallas import tpu as pltpu
from jax.sharding import PartitionSpec as P

D = 768
HEADS = 12
HDIM = 64
FF = 3072
EMBED_WIDTH = 128
DIFF = 2000
STEP = 10
CAP = 3072
LAYERS = 1
LANES = 128


beta_one = 0.9
beta_two = 0.999
learn_rate = 0.02
weight_decay = 0.01
eps_adam = 1e-08
eps_norm = 1e-05
f32 = jnp.float32
bf16 = jnp.bfloat16


def matmul_nn(left, right):
    return jnp.dot(left, right, preferred_element_type=f32)


def matmul_tn(left, right):
    return lax.dot_general(left, right, (((0,), (0,)), ((), ())), preferred_element_type=f32)


def matmul_nt(left, right):
    return lax.dot_general(left, right, (((1,), (1,)), ((), ())), preferred_element_type=f32)


ROW_COUNTS = [D, D, D, D, FF, FF, EMBED_WIDTH, EMBED_WIDTH, EMBED_WIDTH]


def slot_starts(owners):
    counts = jnp.array(ROW_COUNTS, jnp.int32)
    same_owner = (owners[:, None] == owners[None, :]).astype(jnp.int32)
    earlier_mask = jnp.tril(jnp.ones((len(ROW_COUNTS),) * 2, jnp.int32), -1)
    return jnp.sum(same_owner * earlier_mask * counts[None, :], 1)


def waves(places, width):
    half_width = width // 2
    frequency = jnp.exp(-math.log(10000.0) * jnp.arange(half_width, dtype=f32) / half_width)
    angles = places[:, None] * frequency[None, :]
    return jnp.concatenate([jnp.sin(angles), jnp.cos(angles)], 1)


def norm_parts(value_entries):
    center = value_entries - jnp.mean(value_entries, -1, keepdims=True)
    scale_inv = lax.rsqrt(jnp.mean(center * center, -1, keepdims=True) + eps_norm)
    return (center * scale_inv, scale_inv)


def norm_back(normal_part, scale_inv, gain_vec, grad_out):
    scaled = grad_out * gain_vec
    inner = (
        scaled
        - jnp.mean(scaled, -1, keepdims=True)
        - normal_part * jnp.mean(scaled * normal_part, -1, keepdims=True)
    )
    return (inner * scale_inv, jnp.sum(grad_out * normal_part, 0), jnp.sum(grad_out, 0))


def adamw(weight, gradient, moment_one, moment_two):
    moment_one = beta_one * moment_one + (1.0 - beta_one) * gradient
    moment_two = beta_two * moment_two + (1.0 - beta_two) * gradient * gradient
    fix_one = 1.0 - beta_one**STEP
    fix_two = 1.0 - beta_two**STEP
    update_dir = moment_one / fix_one / (jnp.sqrt(moment_two / fix_two) + eps_adam)
    return (weight - learn_rate * (update_dir + weight_decay * weight), moment_one, moment_two)


MESH = pl.DeviceIdType.MESH
ANY = pl.BlockSpec(memory_space=pl.ANY)
UNIT = 768
HALF = 96
QUARTER = 192


def place():
    d, v = lax.axis_index("dp"), lax.axis_index("vocab")
    return d // 2, d % 2, d, v


def greet(partners):
    barrier = pltpu.get_barrier_semaphore()
    for partner in partners:
        pl.semaphore_signal(barrier, inc=1, device_id=partner, device_id_type=MESH)
    pl.semaphore_wait(barrier, len(partners))


def remote(src, dst, sems, index, partner):
    return pltpu.make_async_remote_copy(
        src_ref=src,
        dst_ref=dst,
        send_sem=sems[0].at[index],
        recv_sem=sems[1].at[index],
        device_id=partner,
        device_id_type=MESH,
    )


def start_all(copies):
    for copy in copies:
        copy.start()
    return copies


def arrive_all(copies):
    for copy in copies:
        copy.wait_recv()


VMEM = pl.BlockSpec(memory_space=pltpu.VMEM)
SMEM = pl.BlockSpec(memory_space=pltpu.SMEM)


def prepare_kernel(
    owners, ids, mask, table, slots,
    payload, table_low, row_of, safe, keep_rows, keep, valid, count, kind, unit, column,
    units, extras, sems,
):
    d, v = lax.axis_index("dp"), lax.axis_index("vocab")
    starts = [
        sum(jnp.where(owners[j] == owners[i], ROW_COUNTS[j], 0) for j in range(i)) + 0 * owners[i]
        for i in range(len(ROW_COUNTS))
    ]
    whole = (owners[4] == d) | (owners[5] == d)
    copies = []
    for u in range(4):
        first = pl.multiple_of(jnp.where(whole, u * UNIT, starts[u]), LANES)
        copies.append(
            pltpu.make_async_copy(slots.at[:, pl.ds(first, UNIT)], units.at[u], sems.at[u])
        )
        first = pl.multiple_of(starts[6 + min(u, 2)], LANES)
        copies.append(
            pltpu.make_async_copy(slots.at[:, pl.ds(first, LANES)], extras.at[u], sems.at[4 + u])
        )
    for copy in copies:
        copy.start()

    def clear(j, carry):
        kind[j] = 0
        unit[j] = 0
        column[j] = 0
        return carry

    lax.fori_loop(0, CAP // LANES, clear, 0)
    per_unit = UNIT // LANES
    first_unit = [0, 1, 2, 3, 0, 0, 0, 1, 2]
    for i, rows in enumerate(ROW_COUNTS):

        def claim(i=i, rows=rows):
            def one(b, carry):
                j = starts[i] // LANES + b
                kind[j] = 2 if i > 5 else 1
                unit[j] = first_unit[i] + b // per_unit
                column[j] = b % per_unit
                return carry

            lax.fori_loop(0, rows // LANES, one, 0)

        pl.when(owners[i] == d)(claim)

    table_low[...] = table[...].astype(bf16)
    count[...] = jnp.full((8, LANES), jnp.sum(mask[...].astype(f32)))
    for b in range(4):
        at = pl.ds(pl.multiple_of((v ^ b) * 256, 256), 256)
        local = ids[:, at] - v * table.shape[1]
        row_of[b : b + 1, :] = local
        safe[:, 256 * b : 256 * b + 256] = jnp.clip(local, 0, table.shape[1] - 1)
        weight = mask[:, at].astype(f32)
        keep_rows[b : b + 1, :] = weight
        inside = ((local >= 0) & (local < table.shape[1])).astype(f32)
        both = jnp.concatenate([weight, inside, jnp.zeros((6, 256), f32)], 0).T
        keep[256 * b : 256 * b + 256, :] = both[:, 0:1]
        valid[256 * b : 256 * b + 256, :] = both[:, 1:2]
    for copy in copies:
        copy.wait()
    for u in range(4):
        for half in range(2):
            rows = slice(half * HALF, half * HALF + HALF)
            payload[2 * u + half, :, 0:UNIT] = units[u, rows, :].astype(bf16)
            payload[2 * u + half, :, UNIT:] = extras[u, rows, :].astype(bf16)


def prepare(owners, ids, mask, table, slots):
    def shape(kind, *dims):
        return jax.ShapeDtypeStruct(dims, kind)

    blocks = CAP // LANES
    tokens = ids.shape[1]
    return pl.pallas_call(
        prepare_kernel,
        out_shape=[
            shape(bf16, 8, HALF, UNIT + LANES),
            shape(bf16, *table.shape),
            shape(jnp.int32, 4, tokens // 4),
            shape(jnp.int32, 1, tokens),
            shape(f32, 4, tokens // 4),
            shape(f32, tokens, 1),
            shape(f32, tokens, 1),
            shape(f32, 8, LANES),
        ]
        + [shape(jnp.int32, blocks)] * 3,
        in_specs=[SMEM, VMEM, VMEM, VMEM, ANY],
        out_specs=[VMEM] * 8 + [SMEM] * 3,
        scratch_shapes=[
            pltpu.VMEM((4, QUARTER, UNIT), f32),
            pltpu.VMEM((4, QUARTER, LANES), f32),
            pltpu.SemaphoreType.DMA((8,)),
        ],
        compiler_params=pltpu.CompilerParams(vmem_limit_bytes=40 * 2**20),
    )(owners, ids, mask, table, slots)


TRADE_MASKS = (4, 6, 5, 7, 2, 3, 1)


def chosen_of(pieces, wanted):
    value = pieces[0]
    for i in range(1, len(pieces)):
        value = jnp.where(wanted == i, pieces[i], value)
    return value


def spread_kernel(
    owners, payload, tile, keep_rows, keep, table_home,
    up, down, small, attn, out, table, weight, twice,
    arrived, tiles, up_home, down_home, small_home, attn_home,
    a_send, a_recv, b_send, b_recv,
    z_send, z_recv, y_send, y_recv, x_send, x_recv, n_send, n_recv, f_send, f_recv, local,
):
    z, y, d, v = place()
    far, near = v ^ 2, v ^ 1
    greet([(d ^ m, v) for m in TRADE_MASKS] + [(d, far), (d, near)])
    traded = start_all(
        [
            remote(payload.at[d ^ m], arrived.at[i], (a_send, a_recv), i, (d ^ m, v))
            for i, m in enumerate(TRADE_MASKS)
        ]
        + [
            remote(tile, tiles.at[i], (b_send, b_recv), i, (d ^ m, v))
            for i, m in enumerate(TRADE_MASKS)
        ]
    )
    homes = [up_home, down_home, small_home, attn_home, table_home]
    fulls = [up, down, small, attn, table]
    own_rows = pl.ds(v * QUARTER, QUARTER)

    def spot(c, unit):
        if c == 4:
            return table.at[2 * unit + y]
        first = y * HALF if c == 3 else v * QUARTER + y * HALF
        return fulls[c].at[unit, pl.ds(first, HALF), :]

    keeps, line, side, chip = {}, {}, {}, {}
    sent, landing = [], []

    def note(copy, store=None, at=None):
        copy.start()
        sent.append(copy)
        if store is not None:
            store[at] = copy
        return copy

    def start_class(c):
        keeps[c] = pltpu.make_async_copy(homes[c], spot(c, z), local.at[c])
        keeps[c].start()
        for k in (2, 1, 3):
            note(
                remote(homes[c], spot(c, z), (z_send, z_recv), (c, k - 1), (d ^ (2 * k), v)),
                line,
                (c, k),
            )
        note(remote(homes[c], spot(c, z), (y_send, y_recv), (c, 0), (d ^ 1, v)), side, (c, 0))

    def relay(c, then=()):
        for k in (2, 1, 3):
            if k == 3:
                for other in then:
                    start_class(other)
            line[c, k].wait_recv()
            slab = spot(c, z ^ k)
            note(remote(slab, slab, (y_send, y_recv), (c, k), (d ^ 1, v)), side, (c, k))

    def chip_slab(c, k, source, target):
        note(remote(source, target, (x_send, x_recv), (c, k), (d, far)), chip, (c, k))
        landing.append(note(remote(source, target, (n_send, n_recv), (c, k), (d, near))))

    def to_chip(c):
        for k in (0, 2, 1, 3):
            side[c, k].wait_recv()
            if k == 0:
                keeps[c].wait()
            if c < 3:
                slab = fulls[c].at[z ^ k, own_rows, :]
                chip_slab(c, k, slab, slab)
        if c == 3:
            keep = pltpu.make_async_copy(attn.at[3], out.at[own_rows, :], local.at[5])
            keep.start()
            chip_slab(c, 0, attn.at[3], out.at[own_rows, :])
            keep.wait()

    def to_last(c):
        rows = pl.ds(far * QUARTER, QUARTER)
        for k in (0,) if c == 3 else (0, 2, 1, 3):
            chip[c, k].wait_recv()
            slab = out.at[rows, :] if c == 3 else fulls[c].at[z ^ k, rows, :]
            landing.append(note(remote(slab, slab, (f_send, f_recv), (c, k), (d, near))))

    arrive_all(traded)
    sent.extend(traded)
    total = tile[...]
    for i in range(7):
        total = total + tiles[i]
    weight[...] = keep_rows[...] / jnp.concatenate([total[0:4]] * 2, 1)
    twice[...] = 2.0 * keep[0:256, :] / total[0:1, 0:1]

    def from_owner(owner, lanes):
        value = payload[d, :, lanes]
        for i, m in enumerate(TRADE_MASKS):
            value = jnp.where(owner == d ^ m, arrived[i, :, lanes], value)
        return value

    up_home[...] = from_owner(owners[4], slice(0, UNIT))
    down_home[...] = from_owner(owners[5], slice(0, UNIT))
    attn_home[...] = from_owner(chosen_of([owners[u] for u in range(4)], z), slice(0, UNIT))
    small_home[...] = from_owner(
        chosen_of([owners[6 + min(u, 2)] for u in range(4)], z), slice(UNIT, UNIT + LANES)
    )

    start_class(0)
    relay(0, (1,))
    to_chip(0)
    relay(1, (2, 3))
    to_chip(1)
    relay(2)
    relay(3, (4,))
    to_chip(2)
    to_chip(3)
    to_last(0)
    relay(4)
    to_last(1)
    to_last(2)
    to_last(3)
    to_chip(4)
    arrive_all(landing)
    for copy in sent:
        copy.wait_send()


def spread(owners, payload, tile, keep_rows, keep, table_home):
    rows, vocab_rows = table_home.shape
    dma, vmem = pltpu.SemaphoreType.DMA, pltpu.VMEM

    def shape(*dims):
        return jax.ShapeDtypeStruct(dims, bf16)

    return pl.pallas_call(
        spread_kernel,
        out_shape=[
            shape(4, D, UNIT),
            shape(4, D, UNIT),
            shape(4, D, LANES),
            shape(4, QUARTER, UNIT),
            shape(D, UNIT),
            shape(8, rows, vocab_rows),
            jax.ShapeDtypeStruct(keep_rows.shape, f32),
            jax.ShapeDtypeStruct((256, 1), f32),
        ],
        in_specs=[SMEM] + [VMEM] * 5,
        out_specs=[ANY] * 6 + [VMEM] * 2,
        scratch_shapes=[
            vmem((7, HALF, UNIT + LANES), bf16),
            vmem((7, 8, LANES), f32),
            vmem((HALF, UNIT), bf16),
            vmem((HALF, UNIT), bf16),
            vmem((HALF, LANES), bf16),
            vmem((HALF, UNIT), bf16),
        ]
        + [dma((7,))] * 4
        + [dma((5, 3))] * 2
        + [dma((5, 4))] * 2
        + [dma((4, 4))] * 6
        + [dma((6,))],
        compiler_params=pltpu.CompilerParams(
            collective_id=1, has_side_effects=True, vmem_limit_bytes=40 * 2**20
        ),
    )(owners, payload, tile, keep_rows, keep, table_home)

def neighbours():
    d, v = lax.axis_index("dp"), lax.axis_index("vocab")
    return [(d, v ^ k) for k in (1, 2, 3)]


def by_position(v, store):
    for i in range(4):
        pl.when(v == i)(functools.partial(store, i))


def forward_kernel(
    looked, valid, noise, levels, places, small, attn, out_w, up_hbm, down_hbm, vecs, keep,
    found, clean, inputs, hidden, normed_all, q, k, k_t, values, log_total, mixed, middle, normed_two,
    up_proj, active, hidden_two, final_norm, predicted, pred_all,
    up_w, down_w, found_in, values_t, mixed_out, mixed_in,
    w_sem, e_send, e_recv, n_send, n_recv, m_send, m_recv, p_send, p_recv,
):
    v = lax.axis_index("vocab")
    partners = neighbours()
    loads = []
    for j in range(4):
        for i, (src, dst) in enumerate(((up_hbm, up_w), (down_hbm, down_w))):
            copy = pltpu.make_async_copy(src.at[j], dst.at[j], w_sem.at[2 * j + i])
            copy.start()
            loads.append(copy)
    for b in range(4):
        found[b] = jnp.where(
            valid[256 * b : 256 * b + 256, :] > 0.0, looked[b].astype(f32), 0.0
        ).astype(bf16)
    greet(partners)
    asked = start_all(
        [
            remote(found.at[m], found_in.at[m - 1], (e_send, e_recv), m - 1, partners[m - 1])
            for m in (2, 3, 1)
        ]
    )
    wave = levels[2:3].astype(bf16)
    time_part = matmul_nt(jnp.broadcast_to(wave, (16, EMBED_WIDTH)), small[1])[0:1]
    arrive_all(asked)
    total = found[0].astype(f32)
    for m in range(3):
        total = total + found_in[m].astype(f32)
    clean[...] = total
    noisy = levels[0:1] * total + levels[1:2] * noise[...].astype(f32)
    inputs[:, 0:EMBED_WIDTH] = noisy.astype(bf16)
    inputs[:, EMBED_WIDTH:] = jnp.broadcast_to(wave, noisy.shape)
    value = matmul_nt(inputs[:, 0:EMBED_WIDTH], small[0]) + time_part + places[...]
    hidden[...] = value
    normed_all[0] = (norm_parts(value)[0] * vecs[0:1] + vecs[1:2]).astype(bf16)

    far = remote(normed_all.at[0], normed_all.at[2], (n_send, n_recv), 0, partners[1])
    near = remote(normed_all.at[0], normed_all.at[1], (n_send, n_recv), 1, partners[0])
    last = remote(normed_all.at[2], normed_all.at[3], (n_send, n_recv), 2, partners[0])
    far.start()
    near.start()

    def project(b):
        rows = pl.ds(b * 256, 256)
        block = normed_all[b]
        for i, ref in ((0, q), (1, k), (2, values)):
            result = matmul_nt(block, attn[i])
            if i == 0:
                result = result.astype(bf16).astype(f32) * HDIM ** (-0.5)
            for h in range(3):
                ref[h, rows, :] = result[:, h * HDIM : (h + 1) * HDIM].astype(bf16)
        k_t[:, rows] = matmul_nt(attn[1], block).astype(bf16)
        values_t[:, rows] = matmul_nt(attn[2], block).astype(bf16)

    project(0)
    near.wait_recv()
    project(1)
    far.wait_recv()
    last.start()
    project(2)
    last.wait_recv()
    project(3)

    given = []
    for b in (2, 3, 1, 0):
        rows = pl.ds(b * 256, 256)
        parts = []
        for h in range(3):
            scores = matmul_nt(k[h], q[h, rows, :])
            scores = jnp.where(keep[...] > 0.0, scores, -1000000000.0)
            top = jnp.max(scores, 0, keepdims=True)
            expo = jnp.exp(scores - top)
            mass = jnp.sum(expo, 0, keepdims=True)
            probs = (expo * (1.0 / mass)).astype(bf16)
            log_total[pl.ds(3 * b + h, 1), :] = top + jnp.log(mass)
            parts.append(matmul_nn(values_t[h * HDIM : (h + 1) * HDIM, :], probs))
        block = jnp.concatenate(parts, 0).T.astype(bf16)
        if b == 0:
            mixed_in[0] = block
        else:
            mixed_out[b - 1] = block
            copy = remote(
                mixed_out.at[b - 1], mixed_in.at[b], (m_send, m_recv), b - 1, partners[b - 1]
            )
            copy.start()
            given.append(copy)
    arrive_all(given)

    def lay(i):
        for b in range(4):
            mixed[:, QUARTER * (i ^ b) : QUARTER * ((i ^ b) + 1)] = mixed_in[b]

    by_position(v, lay)
    value = hidden[...] + matmul_nt(mixed[...], out_w[...])
    middle[...] = value
    normed_two[...] = (norm_parts(value)[0] * vecs[2:3] + vecs[3:4]).astype(bf16)
    for j in range(4):
        loads[2 * j].wait()
        loads[2 * j + 1].wait()
        raised = matmul_nn(normed_two[...], up_w[j]) + vecs[4 + j : 5 + j]
        up_proj[j] = raised
        active[j] = jax.nn.gelu(raised).astype(bf16)
        lowered = matmul_nt(active[j], down_w[j])
        hidden_two[...] = (middle[...] if j == 0 else hidden_two[...]) + lowered
    final_norm[...] = (norm_parts(hidden_two[...])[0] * vecs[8:9] + vecs[9:10]).astype(bf16)
    predicted[...] = matmul_nn(final_norm[...], small[2])
    pred_all[0] = predicted[...].astype(bf16)
    shown = start_all(
        [
            remote(pred_all.at[0], pred_all.at[m], (p_send, p_recv), m - 1, partners[m - 1])
            for m in (2, 3, 1)
        ]
    )
    arrive_all(shown)
    for copy in asked + [far, near, last] + given + shown:
        copy.wait_send()


def forward(looked, valid, noise, levels, places, small, attn, out_w, up_w, down_w, vecs, keep):
    dma, vmem = pltpu.SemaphoreType.DMA, pltpu.VMEM
    n = 256

    def shape(kind, *dims):
        return jax.ShapeDtypeStruct(dims, kind)

    return pl.pallas_call(
        forward_kernel,
        out_shape=[
            shape(bf16, 4, n, EMBED_WIDTH),
            shape(f32, n, EMBED_WIDTH),
            shape(bf16, n, 2 * EMBED_WIDTH),
            shape(f32, n, D),
            shape(bf16, 4, n, D),
            shape(bf16, 3, 4 * n, HDIM),
            shape(bf16, 3, 4 * n, HDIM),
            shape(bf16, QUARTER, 4 * n),
            shape(bf16, 3, 4 * n, HDIM),
            shape(f32, 16, n),
            shape(bf16, n, D),
            shape(f32, n, D),
            shape(bf16, n, D),
            shape(f32, 4, n, UNIT),
            shape(bf16, 4, n, UNIT),
            shape(f32, n, D),
            shape(bf16, n, D),
            shape(f32, n, EMBED_WIDTH),
            shape(bf16, 4, n, EMBED_WIDTH),
        ],
        in_specs=[VMEM] * 8 + [ANY] * 2 + [VMEM] * 2,
        out_specs=[VMEM] * 19,
        scratch_shapes=[
            vmem((4, D, UNIT), bf16),
            vmem((4, D, UNIT), bf16),
            vmem((3, n, EMBED_WIDTH), bf16),
            vmem((QUARTER, 4 * n), bf16),
            vmem((3, n, QUARTER), bf16),
            vmem((4, n, QUARTER), bf16),
            dma((8,)),
        ]
        + [dma((3,))] * 8,
        compiler_params=pltpu.CompilerParams(
            collective_id=4, has_side_effects=True, vmem_limit_bytes=60 * 2**20
        ),
    )(looked, valid, noise, levels, places, small, attn, out_w, up_w, down_w, vecs, keep)


STRIP = 768


def strips(rows):
    return [(lo, min(STRIP, rows - lo)) for lo in range(0, rows, STRIP)]


def head_kernel(
    pred_all, table, table_t, row_of, weight, found,
    grad_pred, lse, logits, stats, gathered, outgoing, incoming,
    s_send, s_recv, g_send, g_recv,
):
    partners = neighbours()
    greet(partners)
    rows = table_t.shape[0]
    full, rest = rows // STRIP, rows % STRIP
    mixes = []
    for b in range(4):
        block = pred_all[b]
        wanted = row_of[b : b + 1, :]

        def first(at, size, top):
            value = matmul_nt(table_t[at, :], block)
            logits[at, :] = value
            return jnp.maximum(top, jnp.max(value, 0, keepdims=True))

        def second(at, size, lo, carry, peak):
            mass, target, mix = carry
            value = logits[at, :]
            expo = jnp.exp(value - peak)
            here = lax.broadcasted_iota(jnp.int32, (size, 256), 0) == wanted - lo
            mass = mass + jnp.sum(expo, 0, keepdims=True)
            target = target + jnp.sum(jnp.where(here, value, 0.0), 0, keepdims=True)
            return mass, target, mix + matmul_nn(table[:, at], expo.astype(bf16))

        peak = lax.fori_loop(
            0,
            full,
            lambda t, top: first(pl.ds(pl.multiple_of(t * STRIP, STRIP), STRIP), STRIP, top),
            jnp.full((1, 256), -jnp.inf, f32),
        )
        tail = pl.ds(full * STRIP, rest)
        if rest:
            peak = first(tail, rest, peak)
        zero = jnp.zeros((1, 256), f32)
        carry = lax.fori_loop(
            0,
            full,
            lambda t, carry: second(
                pl.ds(pl.multiple_of(t * STRIP, STRIP), STRIP), STRIP, t * STRIP, carry, peak
            ),
            (zero, zero, jnp.zeros((EMBED_WIDTH, 256), f32)),
        )
        if rest:
            carry = second(tail, rest, full * STRIP, carry, peak)
        stats[b, 0:1] = peak
        stats[b, 1:2] = carry[0]
        stats[b, 2:3] = carry[1]
        stats[b, 3:8] = jnp.zeros((5, 256), f32)
        mixes.append(carry[2])
    told = start_all(
        [
            remote(stats, gathered.at[m - 1], (s_send, s_recv), m - 1, partners[m - 1])
            for m in (2, 3, 1)
        ]
    )
    arrive_all(told)
    given = []
    for b in (2, 3, 1, 0):
        views = [stats[b]] + [gathered[m - 1, b ^ m] for m in (1, 2, 3)]
        peak = functools.reduce(jnp.maximum, [view[0:1] for view in views])
        mass = sum(view[1:2] * jnp.exp(view[0:1] - peak) for view in views)
        total = peak + jnp.log(mass)
        lse[b : b + 1, :] = total
        if b == 0:
            target = sum(view[2:3] for view in views)
            lse[4:5, :] = weight[0:1, :] * (total - target)
            lse[5:8, :] = jnp.zeros((3, 256), f32)
        share = weight[b : b + 1, :]
        local = mixes[b] * (jnp.exp(stats[b, 0:1] - total) * share)
        local = local - found[b].astype(f32).T * share
        outgoing[b] = local.T.astype(bf16)
        if b:
            copy = remote(
                outgoing.at[b], incoming.at[b - 1], (g_send, g_recv), b - 1, partners[b - 1]
            )
            copy.start()
            given.append(copy)
    arrive_all(given)
    value = outgoing[0].astype(f32)
    for m in range(3):
        value = value + incoming[m].astype(f32)
    grad_pred[...] = value
    for copy in told + given:
        copy.wait_send()


def head(pred_all, table, table_t, row_of, weight, found):
    dma, vmem = pltpu.SemaphoreType.DMA, pltpu.VMEM
    return pl.pallas_call(
        head_kernel,
        out_shape=[
            jax.ShapeDtypeStruct((256, EMBED_WIDTH), f32),
            jax.ShapeDtypeStruct((8, 256), f32),
        ],
        in_specs=[VMEM] * 6,
        out_specs=[VMEM] * 2,
        scratch_shapes=[
            vmem((table_t.shape[0], 256), f32),
            vmem((4, 8, 256), f32),
            vmem((3, 4, 8, 256), f32),
            vmem((4, 256, EMBED_WIDTH), bf16),
            vmem((3, 256, EMBED_WIDTH), bf16),
        ]
        + [dma((3,))] * 4,
        compiler_params=pltpu.CompilerParams(
            collective_id=5, has_side_effects=True, vmem_limit_bytes=60 * 2**20
        ),
    )(pred_all, table, table_t, row_of, weight, found)


def gelu_slope(u):
    inner = math.sqrt(2.0 / math.pi)
    bent = jnp.tanh(inner * (u + 0.044715 * (u * u * u)))
    return 0.5 * (1.0 + bent) + (0.5 * inner) * u * (1.0 - bent * bent) * (
        1.0 + (3.0 * 0.044715) * (u * u)
    )


def backward_kernel(
    grad_pred, clean, predicted, twice, levels, head_stats, hidden, middle, hidden_two,
    normed_two, final_norm, up_proj, q, k, k_t, values, log_total, keep,
    small, attn, out_w, up_hbm, down_hbm, vecs,
    grad_pred_low, down_left, up_left, out_left, small_left, final_left, qkv_left, grad_up, grad_clean, sums,
    up_w, down_w, carried, folded, mix_out, mix_in, grad_k, grad_v, n_out, n_in, f_out, f_in,
    w_sem, m_send, m_recv, n_send, n_recv, c_send, c_recv,
):
    v = lax.axis_index("vocab")
    partners = neighbours()
    loads = []
    for j in range(4):
        for i, (src, dst) in enumerate(((down_hbm, down_w), (up_hbm, up_w))):
            copy = pltpu.make_async_copy(src.at[j], dst.at[j], w_sem.at[2 * j + i])
            copy.start()
            loads.append(copy)
    greet(partners)

    def turned(value):
        return value.astype(f32).T.astype(bf16)

    error = predicted[...] - clean[...]
    pull = twice[...] * error
    low = (grad_pred[...] + pull).astype(bf16)
    grad_pred_low[...] = low
    length = jnp.sqrt(jnp.sum(clean[...] * clean[...], -1, keepdims=True) + 1e-06)
    lane = lax.broadcasted_iota(jnp.int32, (1, UNIT), 1)
    scalars = (jnp.sum(pull * error), jnp.sum(head_stats[4:5, :]), jnp.sum(twice[...] * length))
    counted = jnp.sum(keep[0:256, :])
    sums[10:11, :] = sum(jnp.where(lane == i, x, 0.0) for i, x in enumerate(scalars + (counted,)))
    sums[11:16, :] = jnp.zeros((5, UNIT), f32)

    def through_norm(value, gain_row, grad_out, at):
        normal, scale_inv = norm_parts(value)
        part, grad_gain, grad_shift = norm_back(normal, scale_inv, vecs[gain_row : gain_row + 1], grad_out)
        sums[at : at + 1, :] = grad_gain[None, :]
        sums[at + 1 : at + 2, :] = grad_shift[None, :]
        return part

    carried[...] = through_norm(hidden_two[...], 8, matmul_nt(low, small[2]), 8)
    low = carried[...].astype(bf16)
    down_left[...] = turned(carried[...])
    up_left[...] = turned(normed_two[...])
    final_left[...] = turned(final_norm[...])
    for j in range(4):
        loads[2 * j].wait()
        loads[2 * j + 1].wait()
        slope = matmul_nn(low, down_w[j]) * gelu_slope(up_proj[j])
        grad_up[j] = slope.astype(bf16)
        sums[4 + j : 5 + j, :] = jnp.sum(grad_up[j].astype(f32), 0, keepdims=True)
        part = matmul_nt(grad_up[j], up_w[j])
        folded[...] = part if j == 0 else folded[...] + part
    carried[...] = carried[...] + through_norm(middle[...], 2, folded[...], 2)
    out_left[...] = turned(carried[...])
    folded[...] = matmul_nn(carried[...].astype(bf16), out_w[...])

    def lay(i):
        for b in range(4):
            mix_out[b] = folded[:, QUARTER * (i ^ b) : QUARTER * ((i ^ b) + 1)].astype(bf16)

    by_position(v, lay)
    mixed = [
        remote(mix_out.at[m], mix_in.at[m - 1], (m_send, m_recv), m - 1, partners[m - 1])
        for m in (1, 2, 3)
    ]
    for m in (2, 3, 1):
        mixed[m - 1].start()
    for b in range(4):
        if b:
            mixed[b - 1].wait_recv()
        grad_block = mix_out[0] if b == 0 else mix_in[b - 1]
        rows = pl.ds(b * 256, 256)
        for h in range(3):
            grad_mix = grad_block[:, h * HDIM : (h + 1) * HDIM]
            asked = q[h, rows, :]
            scores = matmul_nt(k[h], asked)
            scores = jnp.where(keep[...] > 0.0, scores, -1000000000.0)
            probs = jnp.exp(scores - log_total[3 * b + h : 3 * b + h + 1, :])
            grad_probs = matmul_nt(values[h], grad_mix)
            inner = jnp.sum(probs * grad_probs, 0, keepdims=True)
            grad_scores = (probs * (grad_probs - inner)).astype(bf16)
            grad_asked = matmul_nn(k_t[h * HDIM : (h + 1) * HDIM, :], grad_scores)
            qkv_left[0, h * HDIM : (h + 1) * HDIM, rows] = (grad_asked * HDIM ** (-0.5)).astype(bf16)
            part_k = matmul_nn(grad_scores, asked)
            part_v = matmul_nn(probs.astype(bf16), grad_mix)
            grad_k[h] = part_k if b == 0 else grad_k[h] + part_k
            grad_v[h] = part_v if b == 0 else grad_v[h] + part_v
    for h in range(3):
        lanes = pl.ds(h * HDIM, HDIM)
        qkv_left[1, lanes, :] = grad_k[h].T.astype(bf16)
        qkv_left[2, lanes, :] = grad_v[h].T.astype(bf16)

    def grad_normed(b):
        rows = pl.ds(b * 256, 256)
        return sum(matmul_tn(qkv_left[i, :, rows], attn[i]) for i in range(3))

    n_out[0] = grad_normed(1).astype(bf16)
    n_out[1] = grad_normed(3).astype(bf16)
    near = remote(n_out, n_in, (n_send, n_recv), 0, partners[0])
    near.start()
    folded[...] = grad_normed(2)
    near.wait_recv()
    f_out[...] = (folded[...] + n_in[1].astype(f32)).astype(bf16)
    far = remote(f_out, f_in, (n_send, n_recv), 1, partners[1])
    far.start()
    folded[...] = grad_normed(0) + n_in[0].astype(f32)
    far.wait_recv()
    grad_out = folded[...] + f_in[...].astype(f32)
    carried[...] = carried[...] + through_norm(hidden[...], 0, grad_out, 0)
    small_left[...] = turned(carried[...])
    back = matmul_nn(carried[...].astype(bf16), small[0])
    grad_clean[0] = (levels[0:1] * back - twice[...] * (predicted[...] - clean[...])).astype(bf16)
    shown = start_all(
        [
            remote(grad_clean.at[0], grad_clean.at[m], (c_send, c_recv), m - 1, partners[m - 1])
            for m in (2, 3, 1)
        ]
    )
    arrive_all(shown)
    for copy in mixed + [near, far] + shown:
        copy.wait_send()


def backward(*operands):
    dma, vmem = pltpu.SemaphoreType.DMA, pltpu.VMEM
    n = 256

    def shape(kind, *dims):
        return jax.ShapeDtypeStruct(dims, kind)

    return pl.pallas_call(
        backward_kernel,
        out_shape=[shape(bf16, n, EMBED_WIDTH)]
        + [shape(bf16, D, n)] * 5
        + [
            shape(bf16, 3, QUARTER, 4 * n),
            shape(bf16, 4, n, UNIT),
            shape(bf16, 4, n, EMBED_WIDTH),
            shape(f32, 16, UNIT),
        ],
        in_specs=[VMEM] * 21 + [ANY] * 2 + [VMEM],
        out_specs=[VMEM] * 10,
        scratch_shapes=[
            vmem((4, D, UNIT), bf16),
            vmem((4, D, UNIT), bf16),
            vmem((n, D), f32),
            vmem((n, D), f32),
            vmem((4, n, QUARTER), bf16),
            vmem((3, n, QUARTER), bf16),
            vmem((3, 4 * n, HDIM), f32),
            vmem((3, 4 * n, HDIM), f32),
            vmem((2, n, D), bf16),
            vmem((2, n, D), bf16),
            vmem((n, D), bf16),
            vmem((n, D), bf16),
            dma((8,)),
        ]
        + [dma((3,))] * 6,
        compiler_params=pltpu.CompilerParams(
            collective_id=6, has_side_effects=True, vmem_limit_bytes=60 * 2**20
        ),
    )(*operands)

I16 = jnp.int16
TAIL = 16
TILES = 60
PART_TILES = 30
PART = 3840


def exponent(peak):
    return jnp.ceil(jnp.log2(jnp.maximum(peak, 1e-30))) + 1.0


def coded(value, power):
    return jnp.round(value * jnp.exp2(15.0 - power)).astype(jnp.int32).astype(I16)


def plain(code, power):
    return code.astype(jnp.int32).astype(f32) * jnp.exp2(power - 15.0)


def put(ref, value):
    rows, cols = value.shape
    power = exponent(jnp.max(jnp.abs(value), 0, keepdims=True))
    ref[0:rows, :] = coded(value, power)
    ref[rows : rows + TAIL, :] = (
        jnp.broadcast_to(power, (TAIL, cols)).astype(jnp.int32).astype(I16)
    )


def get(ref, rows):
    power = ref[rows : rows + TAIL, :].astype(jnp.int32).astype(f32)[0:1]
    return plain(ref[0:rows, :], power)


def put_tiles(ref, source, rows):
    lane = lax.broadcasted_iota(jnp.int32, (rows, LANES), 1)

    def body(tile, powers):
        at = pl.ds(pl.multiple_of(tile * LANES, LANES), LANES)
        value = source(at)
        power = exponent(jnp.max(jnp.abs(value), 1, keepdims=True))
        ref[:, at] = coded(value, power)
        return jnp.where(lane == tile, power, powers)

    powers = lax.fori_loop(0, PART_TILES, body, jnp.zeros((rows, LANES), f32), unroll=6)
    ref[:, PART:] = powers.astype(jnp.int32).astype(I16)


def tile_getter(ref, rows):
    lane = lax.broadcasted_iota(jnp.int32, (rows, LANES), 1)
    powers = ref[:, PART:].astype(jnp.int32).astype(f32)

    def read(tile, at):
        power = jnp.sum(jnp.where(lane == tile, powers, 0.0), 1, keepdims=True)
        return plain(ref[:, at], power)

    return read


def grads_kernel(
    owners, down_left, up_left, out_left, small_left, final_left, qkv_left,
    active, grad_up, mixed, inputs, grad_pred, normed, pred_all, grad_clean, table_t, lse, weight, row_of, tile,
    summed, table_sum, tile_sum,
    home, small_home, outgoing, cs, cr, xs, xr, ys, yr, zs, zr, part, half,
    small_cs, small_cr, small_xs, small_xr, small_ys, small_yr, small_zs, small_zr, small_half,
    table, pred_t, clean_t, ts, tr, tzs, tzr, tile_at, tile_from,
    c_send, c_recv, x_send, x_recv, y_send, y_recv, z_send, z_recv, t_send, t_recv, a_send, a_recv, local,
):
    z, y, d, v = place()
    far, near = v ^ 2, v ^ 1
    greet([(d ^ m, v) for m in TRADE_MASKS] + [(d, far), (d, near)])
    sent = []

    def send(src, dst, sems, index, partner):
        copy = remote(src, dst, sems, index, partner)
        copy.start()
        sent.append(copy)
        return copy

    def product(n, who):
        if n == 0:
            return matmul_nn(out_left[who], mixed[...])
        if n < 5:
            return matmul_nn(down_left[who], active[n - 1])
        return matmul_nn(up_left[who], grad_up[n - 5])

    core, chip, side, line = {}, {}, {}, {}

    def to_core(n):
        put(cs.at[n, 0], product(n, near))
        put(cs.at[n, 1], product(n, near ^ 2))
        core[n] = send(cs.at[n], cr.at[n], (c_send, c_recv), n, (d, near))

    def to_chip(n):
        core[n].wait_recv()
        put(xs.at[n], product(n, far) + get(cr.at[n, 1], QUARTER))
        chip[n] = send(xs.at[n], xr.at[n], (x_send, x_recv), n, (d, far))

    def halves(slot, value):
        part[...] = value
        put(ys.at[slot], part[pl.ds((1 - y) * HALF, HALF), :])
        half[slot] = part[pl.ds(y * HALF, HALF), :]
        side[slot] = send(ys.at[slot], yr.at[slot], (y_send, y_recv), slot, (d ^ 1, v))

    def to_side(n):
        chip[n].wait_recv()
        value = product(n, v) + get(cr.at[n, 0], QUARTER) + get(xr.at[n], QUARTER)
        halves(3 + n, value)

    def to_line(group):
        for u in range(4):
            slot = 4 * group + u
            side[slot].wait_recv()
            half[slot] = half[slot] + get(yr.at[slot], HALF)
        for k in (2, 1, 3):
            put(zs.at[group, k - 1], half[4 * group + (z ^ k)])
            line[group, k] = send(
                zs.at[group, k - 1], zr.at[group, k - 1], (z_send, z_recv), 3 * group + k - 1, (d ^ (2 * k), v)
            )

    def to_home(group):
        total = half[4 * group + z]
        for k in (2, 1, 3):
            line[group, k].wait_recv()
            total = total + get(zr.at[group, k - 1], HALF)
        put(home.at[group], total)

    def small_product(who):
        return jnp.concatenate(
            [matmul_nn(small_left[who], inputs[...]), matmul_nn(final_left[who], grad_pred[...])], 1
        )

    def small_to_core():
        put(small_cs.at[0], small_product(near))
        put(small_cs.at[1], small_product(near ^ 2))
        core[9] = send(small_cs, small_cr, (c_send, c_recv), 9, (d, near))

    def small_to_chip():
        core[9].wait_recv()
        put(small_xs, small_product(far) + get(small_cr.at[1], QUARTER))
        chip[9] = send(small_xs, small_xr, (x_send, x_recv), 9, (d, far))

    def small_to_side():
        chip[9].wait_recv()
        value = small_product(v) + get(small_cr.at[0], QUARTER) + get(small_xr, QUARTER)
        cols = value.shape[1]
        part[:, 0:cols] = value
        put(small_ys, part[pl.ds((1 - y) * HALF, HALF), 0:cols])
        small_half[0] = part[pl.ds(y * HALF, HALF), 0:LANES]
        small_half[1] = part[pl.ds(y * HALF, HALF), LANES : 2 * LANES]
        small_half[2] = part[pl.ds(y * HALF, HALF), 2 * LANES : cols]
        small_half[3] = jnp.zeros((HALF, LANES), f32)
        side[12] = send(small_ys, small_yr, (y_send, y_recv), 12, (d ^ 1, v))

    def small_to_line():
        side[12].wait_recv()
        value = get(small_yr, HALF)
        for u in range(3):
            small_half[u] = small_half[u] + value[:, u * LANES : (u + 1) * LANES]
        for k in (2, 1, 3):
            put(small_zs.at[k - 1], small_half[z ^ k])
            line[3, k] = send(
                small_zs.at[k - 1], small_zr.at[k - 1], (z_send, z_recv), 9 + k - 1, (d ^ (2 * k), v)
            )

    def small_to_home():
        total = small_half[z]
        for k in (2, 1, 3):
            line[3, k].wait_recv()
            total = total + get(small_zr.at[k - 1], HALF)
        put(small_home, total)

    def turn_tokens():
        for b in range(4):
            pred_t[b] = pred_all[b].astype(f32).T.astype(bf16)
            clean_t[b] = grad_clean[b].astype(f32).T.astype(bf16)

    vocab_rows = table_t.shape[0]

    def table_strip(lo, size):
        total = jnp.zeros((EMBED_WIDTH, size), f32)
        for b in range(4):
            logits = matmul_nt(table_t[lo : lo + size, :], pred_all[b])
            probs = jnp.exp(logits - lse[b : b + 1, :])
            here = lax.broadcasted_iota(jnp.int32, (size, 256), 0) == row_of[b : b + 1, :] - lo
            here = here.astype(f32)
            grad_logits = ((probs - here) * weight[b : b + 1, :]).astype(bf16)
            total = total + matmul_nt(pred_t[b], grad_logits)
            total = total + matmul_nt(clean_t[b], here.astype(bf16))
        for i in range(8):
            rows = slice(16 * (i // 2), 16 * (i // 2) + 16)
            table[i % 2, rows, lo : lo + size] = total[16 * i : 16 * i + 16]
        if lo + size == vocab_rows:
            table[:, :, vocab_rows:] = jnp.zeros((2, 64, TILES * LANES - vocab_rows), f32)

    table_strips = [(lo, min(STRIP, vocab_rows - lo)) for lo in range(0, vocab_rows, STRIP)]

    def shifted(at, p):
        return pl.ds(pl.multiple_of(at.start + p * PART, LANES), LANES)

    def table_to_side(p):
        put_tiles(ts.at[p], lambda at: table[1 - y, :, shifted(at, p)], 64)
        side[13 + p] = send(ts.at[p], tr.at[p], (y_send, y_recv), 13 + p, (d ^ 1, v))

    def table_line_value(which, p):
        rows = pl.ds(pl.multiple_of(which * 16, 16), 16)
        read = tile_getter(tr.at[p, rows, :], 16)
        return rows, read

    def table_to_line(p):
        side[13 + p].wait_recv()
        for k in (2, 1, 3):
            rows, read = table_line_value(z ^ k, p)

            def source(at, rows=rows, read=read):
                return table[y, rows, shifted(at, p)] + read(at.start // LANES, at)

            put_tiles(tzs.at[p, k - 1], source, 16)
            line[4 + p, k] = send(
                tzs.at[p, k - 1],
                tzr.at[p, k - 1],
                (z_send, z_recv),
                12 + 3 * p + k - 1,
                (d ^ (2 * k), v),
            )

    def table_to_home(p):
        for k in (2, 1, 3):
            line[4 + p, k].wait_recv()
        rows, read = table_line_value(z, p)
        others = [tile_getter(tzr.at[p, k], 16) for k in range(3)]

        def body(tile, carry):
            at = pl.ds(pl.multiple_of(tile * LANES, LANES), LANES)
            value = table[y, rows, shifted(at, p)] + read(tile, at)
            for other in others:
                value = value + other(tile, at)
            table_sum[:, shifted(at, p)] = value
            return carry

        lax.fori_loop(0, PART_TILES, body, 0, unroll=5)

    hops = [(d, near), (d, far), (d ^ 1, v), (d ^ 2, v), (d ^ 4, v)]
    tile_copies = {}

    def tile_send(hop):
        if hop == 0:
            tile_at[0] = tile[...]
        else:
            tile_copies[hop - 1].wait_recv()
            tile_at[hop] = tile_at[hop - 1] + tile_from[hop - 1]
        tile_copies[hop] = send(
            tile_at.at[hop], tile_from.at[hop], (t_send, t_recv), hop, hops[hop]
        )

    def token_products():
        for u in range(3):
            halves(
                u,
                sum(matmul_nn(qkv_left[u, :, 256 * b : 256 * b + 256], normed[b]) for b in range(4)),
            )

    turn_tokens()
    token_products()
    to_core(0)
    to_core(1)
    to_chip(0)
    tile_send(0)
    table_strip(*table_strips[0])
    table_strip(*table_strips[1])
    to_core(2)
    to_chip(1)
    to_side(0)
    table_strip(*table_strips[2])
    table_strip(*table_strips[3])
    to_core(3)
    to_chip(2)
    table_strip(*table_strips[4])
    table_to_side(0)
    to_line(0)
    to_side(1)
    table_strip(*table_strips[5])
    table_strip(*table_strips[6])
    to_core(4)
    to_chip(3)
    table_strip(*table_strips[7])
    table_strip(*table_strips[8])
    for strip in table_strips[9:]:
        table_strip(*strip)
    table_to_side(1)
    to_side(2)
    to_core(5)
    to_chip(4)
    tile_send(1)
    table_to_line(0)
    to_core(6)
    to_chip(5)
    to_side(3)
    to_core(7)
    to_chip(6)
    small_to_core()
    to_core(8)
    to_chip(7)
    small_to_chip()
    to_chip(8)
    to_side(4)
    tile_send(2)
    table_to_line(1)
    to_line(1)
    to_side(5)
    to_home(0)
    tile_send(3)
    small_to_side()
    to_side(6)
    table_to_home(0)
    small_to_line()
    tile_send(4)
    to_side(7)
    to_home(1)
    to_side(8)
    to_line(2)
    table_to_home(1)
    small_to_home()
    tile_copies[4].wait_recv()
    tile_sum[...] = tile_at[4] + tile_from[4]
    to_home(2)

    def offer(m):
        taker = d ^ m
        unit = jnp.where(owners[4] == taker, home[2], home[0])
        outgoing[m, :, 0:UNIT] = jnp.where(owners[5] == taker, home[1], unit)
        outgoing[m, :, UNIT:] = small_home[...]

    offered = []
    for i, m in enumerate(TRADE_MASKS):
        offer(m)
        offered.append(send(outgoing.at[m], summed.at[d], (a_send, a_recv), i, (d ^ m, v)))
    offer(0)
    keep = pltpu.make_async_copy(outgoing.at[0], summed.at[d], local)
    keep.start()
    keep.wait()
    arrive_all(offered)
    for copy in sent:
        copy.wait_send()


def reduce_grads(*operands):
    dma = pltpu.SemaphoreType.DMA
    vmem = pltpu.VMEM
    tall, low, wide = QUARTER + TAIL, HALF + TAIL, 3 * LANES
    table_cols = TILES * LANES
    return pl.pallas_call(
        grads_kernel,
        out_shape=[
            jax.ShapeDtypeStruct((8, low, UNIT + LANES), I16),
            jax.ShapeDtypeStruct((16, table_cols), f32),
            jax.ShapeDtypeStruct((16, UNIT), f32),
        ],
        in_specs=[SMEM] + [VMEM] * 19,
        out_specs=[VMEM] * 3,
        scratch_shapes=[
            vmem((3, low, UNIT), I16),
            vmem((low, LANES), I16),
            vmem((8, low, UNIT + LANES), I16),
            vmem((9, 2, tall, UNIT), I16),
            vmem((9, 2, tall, UNIT), I16),
            vmem((9, tall, UNIT), I16),
            vmem((9, tall, UNIT), I16),
            vmem((12, low, UNIT), I16),
            vmem((12, low, UNIT), I16),
            vmem((3, 3, low, UNIT), I16),
            vmem((3, 3, low, UNIT), I16),
            vmem((QUARTER, UNIT), f32),
            vmem((12, HALF, UNIT), f32),
            vmem((2, tall, wide), I16),
            vmem((2, tall, wide), I16),
            vmem((tall, wide), I16),
            vmem((tall, wide), I16),
            vmem((low, wide), I16),
            vmem((low, wide), I16),
            vmem((3, low, LANES), I16),
            vmem((3, low, LANES), I16),
            vmem((4, HALF, LANES), f32),
            vmem((2, 64, table_cols), f32),
            vmem((4, EMBED_WIDTH, 256), bf16),
            vmem((4, EMBED_WIDTH, 256), bf16),
            vmem((2, 64, PART + LANES), I16),
            vmem((2, 64, PART + LANES), I16),
            vmem((2, 3, 16, PART + LANES), I16),
            vmem((2, 3, 16, PART + LANES), I16),
            vmem((5, 16, UNIT), f32),
            vmem((5, 16, UNIT), f32),
        ]
        + [dma((10,))] * 4
        + [dma((15,))] * 2
        + [dma((18,))] * 2
        + [dma((5,))] * 2
        + [dma((7,))] * 2
        + [dma],
        compiler_params=pltpu.CompilerParams(
            collective_id=2, has_side_effects=True, vmem_limit_bytes=60 * 2**20
        ),
    )(*operands)


def slot_kernel(kind, unit, column, summed, w, m1, m2, w_out, m1_out, m2_out):
    per_unit = UNIT // LANES
    for b in range(per_unit):
        j = pl.program_id(0) * per_unit + b
        first = jnp.where(kind[j] == 2, per_unit, column[j])
        at = pl.ds(pl.multiple_of(first * LANES, LANES), LANES)
        lanes = slice(b * LANES, b * LANES + LANES)
        for half in range(2):
            rows = slice(half * HALF, half * HALF + HALF)
            g = get(summed.at[2 * unit[j] + half, :, at], HALF)
            g = jnp.where(kind[j] > 0, g, jnp.zeros_like(g))
            w_out[rows, lanes], m1_out[rows, lanes], m2_out[rows, lanes] = adamw(
                w[rows, lanes], g, m1[rows, lanes], m2[rows, lanes]
            )


def slot_update(kind, unit, column, summed, slots, first, second):
    rows = slots.shape[0]
    plain_spec = pl.BlockSpec((rows, UNIT), lambda j, k, u, c: (0, j))
    return pl.pallas_call(
        slot_kernel,
        grid_spec=pltpu.PrefetchScalarGridSpec(
            num_scalar_prefetch=3,
            grid=(CAP // UNIT,),
            in_specs=[pl.BlockSpec(summed.shape, lambda j, k, u, c: (0, 0, 0))] + [plain_spec] * 3,
            out_specs=[plain_spec] * 3,
        ),
        out_shape=[jax.ShapeDtypeStruct(slots.shape, f32)] * 3,
        cost_estimate=pl.CostEstimate(flops=0, bytes_accessed=28 * rows * CAP, transcendentals=0),
        compiler_params=pltpu.CompilerParams(vmem_limit_bytes=40 * 2**20),
    )(kind, unit, column, summed, slots, first, second)


def per_device(
    token_ids,
    timesteps,
    pad_mask,
    noise_draw,
    owners,
    emb_table,
    table_first_moment,
    table_second_moment,
    mat_slots,
    slot_first,
    slot_second,
    vec_params,
    vec_first,
    vec_second,
):
    v = lax.axis_index("vocab")
    seq_len = token_ids.shape[1]
    tokens = seq_len // 4
    vocab_rows, emb_cols = emb_table.shape
    table_own = emb_table.T
    (
        payload, table_home, row_of, safe_row, keep_rows, keep_column, valid_column, count_tile,
        kind, unit, column,
    ) = prepare(owners, token_ids, pad_mask, table_own, mat_slots)
    w_up, w_down, w_small, w_attn, w_out, table_low, row_weight, twice = spread(
        owners, payload, count_tile, keep_rows, keep_column, table_home
    )
    table_low = table_low.reshape(EMBED_WIDTH, vocab_rows)
    table_t = table_low.T
    looked = table_t.at[safe_row[0]].get(mode="promise_in_bounds").reshape(4, tokens, EMBED_WIDTH)
    own_places = (v * tokens + jnp.arange(tokens)).astype(f32)
    step_val = timesteps[0].astype(f32)
    signal_level = 1.0 - jnp.sqrt(step_val / DIFF + 0.0001)
    levels = jnp.concatenate(
        [
            jnp.full((1, EMBED_WIDTH), jnp.sqrt(signal_level)),
            jnp.full((1, EMBED_WIDTH), jnp.sqrt(1.0 - signal_level)),
            waves(step_val[None], EMBED_WIDTH),
            jnp.zeros((5, EMBED_WIDTH), f32),
        ]
    )
    vecs = vec_params.reshape(10, D)
    (
        found_rows, clean_emb, inputs, hidden, normed_all, q_h, k_h, k_t, v_h, log_total, mixed_own, middle,
        normed_two, up_proj, active, hidden_two, final_norm, predicted, pred_all,
    ) = forward(
        looked,
        valid_column,
        noise_draw[0],
        levels,
        waves(own_places, D),
        w_small,
        w_attn,
        w_out,
        w_up,
        w_down,
        vecs,
        keep_column,
    )
    grad_pred, head_stats = head(
        pred_all,
        table_low,
        table_t,
        row_of,
        row_weight,
        found_rows,
    )
    (
        grad_pred_low, down_left, up_left, out_left, small_left, final_left, qkv_left, grad_up, grad_clean, sums,
    ) = backward(
        grad_pred, clean_emb, predicted, twice, levels, head_stats,
        hidden, middle, hidden_two, normed_two, final_norm, up_proj,
        q_h, k_h, k_t, v_h, log_total, keep_column,
        w_small, w_attn, w_out, w_up, w_down, vecs,
    )

    def left(value):
        return value.reshape(4, QUARTER, tokens)

    summed, table_grad, tile_sum = reduce_grads(
        owners,
        left(down_left),
        left(up_left),
        left(out_left),
        left(small_left),
        left(final_left),
        qkv_left,
        active,
        grad_up,
        mixed_own,
        inputs,
        grad_pred_low,
        normed_all,
        pred_all,
        grad_clean,
        table_t,
        head_stats,
        row_weight,
        row_of,
        sums,
    )
    tile_sum = tile_sum.reshape(16 * UNIT)
    vec_share = vec_first.shape[0]
    own_grad = lax.dynamic_slice_in_dim(tile_sum, v * vec_share, vec_share)
    own_vecs = lax.dynamic_slice_in_dim(vec_params, v * vec_share, vec_share)
    vec_len = vec_params.shape[0]
    count_all = tile_sum[vec_len + 3]
    square = tile_sum[vec_len] * (0.5 * count_all)
    cross_sum = tile_sum[vec_len + 1] * count_all
    emb_norm = tile_sum[vec_len + 2] * 0.5

    new_slots, slot_first_new, slot_second_new = slot_update(
        kind, unit, column, summed, mat_slots, slot_first, slot_second
    )
    new_table, table_first_new, table_second_new = adamw(
        table_own, table_grad[:, :vocab_rows], table_first_moment.T, table_second_moment.T
    )
    new_vecs, vec_first_new, vec_second_new = adamw(own_vecs, own_grad, vec_first, vec_second)
    loss_pair = jnp.stack([square + cross_sum, count_all])
    return (
        loss_pair,
        emb_norm,
        new_table.T,
        table_first_new.T,
        table_second_new.T,
        new_slots,
        slot_first_new,
        slot_second_new,
        new_vecs,
        vec_first_new,
        vec_second_new,
    )


def broadcast(value, axis, source):
    kept = jnp.where(lax.axis_index(axis) == source, value, 0).astype(value.dtype)
    return lax.psum(kept, axis)


def merged(value, axis, join):
    pieces = jax.tree.map(lambda part: lax.all_gather(part, axis), value)
    head = jax.tree.map(lambda part: part[0], pieces)
    tail = jax.tree.map(lambda part: part[1:], pieces)
    so_far, _ = lax.scan(lambda so_far, share: (join(so_far, share), None), head, tail)
    return so_far


def matrix_rows():
    return [D, D, D, D, FF, FF] * LAYERS + [EMBED_WIDTH, EMBED_WIDTH, EMBED_WIDTH]


def slot_places(owners):
    counts = jnp.array(matrix_rows(), jnp.int32)
    mat_total = counts.shape[0]
    same_owner = (owners[:, None] == owners[None, :]).astype(jnp.int32)
    earlier_mask = jnp.tril(jnp.ones((mat_total, mat_total), jnp.int32), -1)
    return owners * CAP + jnp.sum(same_owner * earlier_mask * counts[None, :], 1)


def block_scores(query_blk, keys_all, keep_keys, score_scale):
    scores = (
        jnp.einsum("qhd,khd->hqk", query_blk, keys_all, preferred_element_type=jnp.float32)
        * score_scale
    )
    return jnp.where(keep_keys[None, None, :], scores, -1000000000.0)


def attention(queries, keys_all, values_all, keep_keys, score_scale):
    tokens = queries.shape[0]
    width = min(512, tokens)
    query_blocks = queries.reshape(tokens // width, width, HEADS, HDIM)

    def one_block(query_blk):
        scores = block_scores(query_blk, keys_all, keep_keys, score_scale)
        row_max = jnp.max(scores, -1, keepdims=True)
        expo = jnp.exp(scores - row_max)
        exp_total = jnp.sum(expo, -1, keepdims=True)
        probabilities = (expo / exp_total).astype(jnp.bfloat16)
        mixed_out = jnp.einsum(
            "hqk,khd->qhd", probabilities, values_all, preferred_element_type=jnp.float32
        )
        return (mixed_out, (row_max + jnp.log(exp_total))[..., 0])

    mixed_out, log_total = lax.map(one_block, query_blocks)
    return (mixed_out.reshape(tokens, HEADS, HDIM), log_total)


def attention_back(queries, keys_all, values_all, keep_keys, log_total, grad_mixed, score_scale):
    tokens = queries.shape[0]
    width = min(512, tokens)
    query_blocks = queries.reshape(tokens // width, width, HEADS, HDIM)
    grad_blocks = grad_mixed.reshape(tokens // width, width, HEADS, HDIM)

    def one_block(carry_sums, block_data):
        query_blk, total_blk, grad_blk = block_data
        scores = block_scores(query_blk, keys_all, keep_keys, score_scale)
        probabilities = jnp.exp(scores - total_blk[..., None])
        grad_probs = jnp.einsum(
            "qhd,khd->hqk", grad_blk, values_all, preferred_element_type=jnp.float32
        )
        inner_sum = jnp.sum(probabilities * grad_probs, -1, keepdims=True)
        grad_scores = (probabilities * (grad_probs - inner_sum)).astype(jnp.bfloat16)
        grad_query = (
            jnp.einsum("hqk,khd->qhd", grad_scores, keys_all, preferred_element_type=jnp.float32)
            * score_scale
        )
        grad_key = (
            jnp.einsum("hqk,qhd->khd", grad_scores, query_blk, preferred_element_type=jnp.float32)
            * score_scale
        )
        grad_value = jnp.einsum(
            "hqk,qhd->khd",
            probabilities.astype(jnp.bfloat16),
            grad_blk,
            preferred_element_type=jnp.float32,
        )
        return ((carry_sums[0] + grad_key, carry_sums[1] + grad_value), grad_query)

    zero_keys = jnp.zeros(keys_all.shape, jnp.float32)
    grad_kv, grad_queries = lax.scan(
        one_block, (zero_keys, zero_keys), (query_blocks, log_total, grad_blocks)
    )
    return (grad_queries.reshape(tokens, D), grad_kv[0].reshape(-1, D), grad_kv[1].reshape(-1, D))


def send_matrix(piece_cols, root):
    return broadcast(piece_cols, "dp", root)


def fetch_keys(key_rows, value_rows):
    return (
        lax.all_gather(key_rows, "vocab", axis=0, tiled=True),
        lax.all_gather(value_rows, "vocab", axis=0, tiled=True),
    )


def layer_forward(hidden, weights, vec_layer, keep_keys, score_scale):
    w_query, w_key, w_value, w_out, w_up, w_down = weights
    tokens = hidden.shape[0]
    norm_one, inv_one = norm_parts(hidden)
    normed = (norm_one * vec_layer[0:D] + vec_layer[D : 2 * D]).astype(jnp.bfloat16)
    queries = matmul_nn(normed, w_query).astype(jnp.bfloat16)
    key_rows = matmul_nn(normed, w_key).astype(jnp.bfloat16)
    value_rows = matmul_nn(normed, w_value).astype(jnp.bfloat16)
    keys_all, values_all = fetch_keys(key_rows, value_rows)
    keys_all = keys_all.reshape(-1, HEADS, HDIM)
    values_all = values_all.reshape(-1, HEADS, HDIM)
    mixed_out, log_total = attention(
        queries.reshape(tokens, HEADS, HDIM), keys_all, values_all, keep_keys, score_scale
    )
    mixed_low = mixed_out.reshape(tokens, D).astype(jnp.bfloat16)
    middle = hidden + matmul_nn(mixed_low, w_out)
    norm_two, inv_two = norm_parts(middle)
    normed_two = (norm_two * vec_layer[2 * D : 3 * D] + vec_layer[3 * D : 4 * D]).astype(
        jnp.bfloat16
    )
    up_proj = matmul_nt(normed_two, w_up) + vec_layer[4 * D :]
    active = jax.nn.gelu(up_proj).astype(jnp.bfloat16)
    out_rows = middle + matmul_nn(active, w_down)
    kept_vals = (
        norm_one,
        inv_one,
        normed,
        queries,
        key_rows,
        value_rows,
        keys_all,
        values_all,
        log_total,
        mixed_low,
        norm_two,
        inv_two,
        normed_two,
        up_proj,
        active,
    )
    return (out_rows, kept_vals)


def layer_backward(grad_out, kept_vals, weights, vec_layer, keep_keys, score_scale):
    w_query, w_key, w_value, w_out, w_up, w_down = weights
    (
        norm_one,
        inv_one,
        normed,
        queries,
        key_rows,
        value_rows,
        keys_all,
        values_all,
        log_total,
        mixed_low,
        norm_two,
        inv_two,
        normed_two,
        up_proj,
        active,
    ) = kept_vals
    tokens = grad_out.shape[0]
    grad_low = grad_out.astype(jnp.bfloat16)
    grad_down = matmul_tn(active, grad_low)
    grad_active = matmul_nt(grad_low, w_down)
    grad_up_proj = jax.vjp(jax.nn.gelu, up_proj)[1](grad_active)[0].astype(jnp.bfloat16)
    grad_bias = jnp.sum(grad_up_proj.astype(jnp.float32), 0)
    grad_up = matmul_tn(grad_up_proj, normed_two)
    grad_normed_two = matmul_nn(grad_up_proj, w_up)
    grad_part, grad_gain_two, grad_shift_two = norm_back(
        norm_two, inv_two, vec_layer[2 * D : 3 * D], grad_normed_two
    )
    grad_middle = grad_out + grad_part
    grad_attn = grad_middle.astype(jnp.bfloat16)
    grad_out_w = matmul_tn(mixed_low, grad_attn)
    grad_mixed = matmul_nt(grad_attn, w_out).astype(jnp.bfloat16).reshape(tokens, HEADS, HDIM)
    grad_queries, grad_keys_all, grad_values_all = attention_back(
        queries.reshape(tokens, HEADS, HDIM),
        keys_all,
        values_all,
        keep_keys,
        log_total,
        grad_mixed,
        score_scale,
    )
    grad_key_rows, grad_value_rows = (
        lax.psum_scatter(
            grad_keys_all.astype(jnp.bfloat16), "vocab", scatter_dimension=0, tiled=True
        ).astype(jnp.float32),
        lax.psum_scatter(
            grad_values_all.astype(jnp.bfloat16), "vocab", scatter_dimension=0, tiled=True
        ).astype(jnp.float32),
    )
    grad_q_low = grad_queries.astype(jnp.bfloat16)
    grad_k_low = grad_key_rows.astype(jnp.bfloat16)
    grad_v_low = grad_value_rows.astype(jnp.bfloat16)
    grad_wq = matmul_tn(normed, grad_q_low)
    grad_wk = matmul_tn(normed, grad_k_low)
    grad_wv = matmul_tn(normed, grad_v_low)
    grad_normed = (
        matmul_nt(grad_q_low, w_query)
        + matmul_nt(grad_k_low, w_key)
        + matmul_nt(grad_v_low, w_value)
    )
    grad_part_one, grad_gain_one, grad_shift_one = norm_back(
        norm_one, inv_one, vec_layer[0:D], grad_normed
    )
    grad_hidden = grad_middle + grad_part_one
    grad_mats = [grad_wq, grad_wk, grad_wv, grad_out_w, grad_up, grad_down]
    grad_vec = jnp.concatenate(
        [grad_gain_one, grad_shift_one, grad_gain_two, grad_shift_two, grad_bias]
    )
    return (grad_hidden, grad_mats, grad_vec)


def merge_stats(first_part, second_part):
    peak_val = jnp.maximum(first_part[0], second_part[0])
    exp_total = first_part[1] * jnp.exp(first_part[0] - peak_val) + second_part[1] * jnp.exp(
        second_part[0] - peak_val
    )
    return (peak_val, exp_total, first_part[2] + second_part[2])


def any_mesh_device(
    token_ids,
    timesteps,
    pad_mask,
    noise_draw,
    owners,
    emb_table,
    table_first_moment,
    table_second_moment,
    mat_slots,
    slot_first,
    slot_second,
    vec_params,
    vec_first,
    vec_second,
):
    vocab_count = lax.axis_size("vocab")
    vocab_pos = lax.axis_index("vocab")
    data_pos = lax.axis_index("dp")
    seq_len = token_ids.shape[1]
    tokens = seq_len // vocab_count
    vocab_rows = emb_table.shape[0]
    score_scale = HDIM ** (-0.5)
    table_low = lax.all_gather(emb_table.astype(jnp.bfloat16), "dp", axis=1, tiled=True)
    row_counts = matrix_rows()
    local_start = slot_places(owners) - owners * CAP
    sent_pieces = [
        send_matrix(
            lax.dynamic_slice_in_dim(
                mat_slots, local_start[mat_idx], row_counts[mat_idx], 1
            ).astype(jnp.bfloat16),
            owners[mat_idx],
        )
        for mat_idx in range(len(row_counts))
    ]
    canon = jnp.concatenate(sent_pieces, 1)
    weights = lax.all_gather(canon, "vocab", axis=0, tiled=True).T
    layer_rows = 4 * D + 2 * FF
    vec_rows = 4 * D + FF
    tail_at = LAYERS * layer_rows

    def layer_weights(layer_idx):
        begin_row = layer_idx * layer_rows
        cuts = [
            begin_row,
            begin_row + D,
            begin_row + 2 * D,
            begin_row + 3 * D,
            begin_row + 4 * D,
            begin_row + 4 * D + FF,
            begin_row + layer_rows,
        ]
        return [weights[cuts[cut_idx] : cuts[cut_idx + 1]] for cut_idx in range(6)]

    w_input = weights[tail_at : tail_at + 2 * EMBED_WIDTH]
    w_final = weights[tail_at + 2 * EMBED_WIDTH : tail_at + 3 * EMBED_WIDTH]
    seq_ids = token_ids[0]
    seq_mask = pad_mask[0].astype(jnp.float32)
    keep_keys = pad_mask[0] > 0
    local_row = seq_ids - vocab_pos * vocab_rows
    valid_row = (local_row >= 0) & (local_row < vocab_rows)
    safe_row = jnp.clip(local_row, 0, vocab_rows - 1)
    found_rows = jnp.where(
        valid_row[:, None], jnp.take(table_low, safe_row, axis=0), jnp.zeros((), jnp.bfloat16)
    )
    arrived = lax.all_to_all(found_rows, "vocab", split_axis=0, concat_axis=0, tiled=True)
    clean_emb = jnp.sum(arrived.reshape(vocab_count, tokens, EMBED_WIDTH).astype(jnp.float32), 0)
    own_first = vocab_pos * tokens
    mask_own = lax.dynamic_slice_in_dim(seq_mask, own_first, tokens)
    own_places = (own_first + jnp.arange(tokens)).astype(jnp.float32)
    step_val = timesteps[0].astype(jnp.float32)
    signal_level = 1.0 - jnp.sqrt(step_val / DIFF + 0.0001)
    noisy_emb = jnp.sqrt(signal_level) * clean_emb + jnp.sqrt(1.0 - signal_level) * noise_draw[
        0
    ].astype(jnp.float32)
    time_feat = jnp.broadcast_to(waves(step_val[None], EMBED_WIDTH), (tokens, EMBED_WIDTH))
    inputs = jnp.concatenate([noisy_emb, time_feat], 1).astype(jnp.bfloat16)
    hidden = matmul_nn(inputs, w_input) + waves(own_places, D)
    layer_idx = 0
    vec_layer = vec_params[layer_idx * vec_rows : (layer_idx + 1) * vec_rows]
    hidden, kept_vals = layer_forward(
        hidden, layer_weights(layer_idx), vec_layer, keep_keys, score_scale
    )
    kept_list = [kept_vals]
    gain_final = vec_params[LAYERS * vec_rows : LAYERS * vec_rows + D]
    shift_final = vec_params[LAYERS * vec_rows + D :]
    norm_final, inv_final = norm_parts(hidden)
    final_norm = (norm_final * gain_final + shift_final).astype(jnp.bfloat16)
    predicted = matmul_nt(final_norm, w_final)
    pred_all = lax.all_gather(predicted.astype(jnp.bfloat16), "vocab", axis=0, tiled=True)
    head_width = min(512, seq_len)
    head_count = seq_len // head_width
    columns = jnp.arange(vocab_rows)
    pred_blocks = pred_all.reshape(head_count, head_width, EMBED_WIDTH)
    row_blocks = local_row.reshape(head_count, head_width)

    def head_stats(block_data):
        pred_blk, rows_blk = block_data
        logits = matmul_nt(pred_blk, table_low)
        row_max = jnp.max(logits, -1)
        exp_total = jnp.sum(jnp.exp(logits - row_max[:, None]), -1)
        target = jnp.sum(jnp.where(columns[None, :] == rows_blk[:, None], logits, 0.0), -1)
        return (row_max, exp_total, target)

    peaks, totals, targets = lax.map(head_stats, (pred_blocks, row_blocks))
    peak_all, total_all, target_all = merged(
        (peaks.reshape(seq_len), totals.reshape(seq_len), targets.reshape(seq_len)),
        "vocab",
        merge_stats,
    )
    log_total = peak_all + jnp.log(total_all)
    lse_own = lax.dynamic_slice_in_dim(log_total, own_first, tokens)
    target_own = lax.dynamic_slice_in_dim(target_all, own_first, tokens)
    pred_error = predicted - clean_emb
    square_own = jnp.sum(mask_own[:, None] * pred_error * pred_error)
    cross_own = jnp.sum(mask_own * (lse_own - target_own))
    norm_own = jnp.sum(mask_own * jnp.sqrt(jnp.sum(clean_emb * clean_emb, -1) + 1e-06))
    count_all, square, cross_sum, norm_total = lax.psum(
        (jnp.sum(mask_own), square_own, cross_own, norm_own), ("dp", "vocab")
    )
    weight_blocks = (seq_mask / count_all).reshape(head_count, head_width)
    lse_blocks = log_total.reshape(head_count, head_width)

    def head_back(grad_table, block_data):
        pred_blk, rows_blk, lse_blk, weight_blk = block_data
        logits = matmul_nt(pred_blk, table_low)
        probabilities = jnp.exp(logits - lse_blk[:, None])
        onehot = (columns[None, :] == rows_blk[:, None]).astype(jnp.float32)
        grad_logits = ((probabilities - onehot) * weight_blk[:, None]).astype(jnp.bfloat16)
        return (grad_table + matmul_tn(grad_logits, pred_blk), matmul_nn(grad_logits, table_low))

    zero_table = jnp.zeros((vocab_rows, EMBED_WIDTH), jnp.float32)
    grad_table_head, grad_pred_blocks = lax.scan(
        head_back, zero_table, (pred_blocks, row_blocks, lse_blocks, weight_blocks)
    )
    grad_pred = lax.psum_scatter(
        grad_pred_blocks.reshape(seq_len, EMBED_WIDTH).astype(jnp.bfloat16),
        "vocab",
        scatter_dimension=0,
        tiled=True,
    ).astype(jnp.float32)
    error_grad = 2.0 * mask_own[:, None] * pred_error / count_all
    grad_pred_low = (grad_pred + error_grad).astype(jnp.bfloat16)
    grad_final_w = matmul_tn(grad_pred_low, final_norm)
    grad_final = matmul_nn(grad_pred_low, w_final)
    grad_hidden, grad_gain_final, grad_shift_final = norm_back(
        norm_final, inv_final, gain_final, grad_final
    )
    layer_grads = [None] * LAYERS
    vec_grads = [None] * LAYERS
    for layer_idx in reversed(range(LAYERS)):
        vec_layer = vec_params[layer_idx * vec_rows : (layer_idx + 1) * vec_rows]
        grad_hidden, layer_grads[layer_idx], vec_grads[layer_idx] = layer_backward(
            grad_hidden,
            kept_list[layer_idx],
            layer_weights(layer_idx),
            vec_layer,
            keep_keys,
            score_scale,
        )
    grad_hidden_low = grad_hidden.astype(jnp.bfloat16)
    grad_input_w = matmul_tn(inputs, grad_hidden_low)
    grad_inputs = matmul_nt(grad_hidden_low, w_input)
    grad_clean = jnp.sqrt(signal_level) * grad_inputs[:, :EMBED_WIDTH] - error_grad
    grad_clean_all = lax.all_gather(
        grad_clean.astype(jnp.bfloat16), "vocab", axis=0, tiled=True
    ).astype(grad_clean.dtype)
    grad_table_look = zero_table.at[safe_row].add(
        jnp.where(valid_row[:, None], grad_clean_all, 0.0)
    )
    grad_table_local = grad_table_head + grad_table_look
    canon_list = []
    layer_idx = 0
    canon_list = canon_list + layer_grads[layer_idx]
    canon_grad = jnp.concatenate(canon_list + [grad_input_w, grad_final_w], 0).T
    vec_grad = jnp.concatenate(vec_grads + [grad_gain_final, grad_shift_final])
    grad_cols, vec_part = (
        lax.psum_scatter(canon_grad, "vocab", scatter_dimension=0, tiled=True),
        lax.psum_scatter(vec_grad, "vocab", scatter_dimension=0, tiled=True),
    )
    emb_cols = emb_table.shape[1]
    summed_cols, summed_vec, summed_table = lax.psum((grad_cols, vec_part, grad_table_local), "dp")
    table_grad = lax.dynamic_slice_in_dim(summed_table, data_pos * emb_cols, emb_cols, 1)
    slot_grad = jnp.zeros_like(mat_slots)
    cursor = 0
    for mat_idx in range(len(row_counts)):
        piece_cols = summed_cols[:, cursor : cursor + row_counts[mat_idx]]
        updated = lax.dynamic_update_slice_in_dim(slot_grad, piece_cols, local_start[mat_idx], 1)
        slot_grad = jnp.where(owners[mat_idx] == data_pos, updated, slot_grad)
        cursor = cursor + row_counts[mat_idx]
    vec_share = vec_first.shape[0]
    own_vecs = lax.dynamic_slice_in_dim(vec_params, vocab_pos * vec_share, vec_share)
    new_slots, slot_first_new, slot_second_new = adamw(
        mat_slots, slot_grad, slot_first, slot_second
    )
    new_table, table_first_new, table_second_new = adamw(
        emb_table, table_grad, table_first_moment, table_second_moment
    )
    new_vecs, vec_first_new, vec_second_new = adamw(own_vecs, summed_vec, vec_first, vec_second)
    loss_pair = jnp.stack([square + cross_sum, count_all])
    emb_norm = norm_total / count_all
    return (
        loss_pair,
        emb_norm,
        new_table,
        table_first_new,
        table_second_new,
        new_slots,
        slot_first_new,
        slot_second_new,
        new_vecs,
        vec_first_new,
        vec_second_new,
    )


def solution(mesh):
    in_specs = (
        P("dp", None),
        P("dp"),
        P("dp", None),
        P("dp", "vocab", None),
        P(),
        P("vocab", "dp"),
        P("vocab", "dp"),
        P("vocab", "dp"),
        P("vocab", "dp"),
        P("vocab", "dp"),
        P("vocab", "dp"),
        P(),
        P("vocab"),
        P("vocab"),
    )
    out_specs = (
        P(),
        P(),
        P("vocab", "dp"),
        P("vocab", "dp"),
        P("vocab", "dp"),
        P("vocab", "dp"),
        P("vocab", "dp"),
        P("vocab", "dp"),
        P("vocab"),
        P("vocab"),
        P("vocab"),
    )
    fast = mesh.shape["dp"] == 8 and mesh.shape["vocab"] == 4
    body = per_device if fast else any_mesh_device
    return jax.shard_map(
        body, mesh=mesh, in_specs=in_specs, out_specs=out_specs, check_vma=False
    )
```

```python
import functools
import math

import jax
import jax.numpy as jnp
from jax import lax
from jax.experimental import pallas as pl
from jax.experimental.pallas import tpu as pltpu
from jax.sharding import PartitionSpec as P

D = 768
HEADS = 12
HDIM = 64
FF = 3072
EMBED_WIDTH = 128
DIFF = 2000
STEP = 10
CAP = 3072
LAYERS = 1
LANES = 128


beta_one = 0.9
beta_two = 0.999
learn_rate = 0.02
weight_decay = 0.01
eps_adam = 1e-08
eps_norm = 1e-05
f32 = jnp.float32
bf16 = jnp.bfloat16


def matmul_nn(left, right):
    return jnp.dot(left, right, preferred_element_type=f32)


def matmul_tn(left, right):
    return lax.dot_general(left, right, (((0,), (0,)), ((), ())), preferred_element_type=f32)


def matmul_nt(left, right):
    return lax.dot_general(left, right, (((1,), (1,)), ((), ())), preferred_element_type=f32)


ROW_COUNTS = [D, D, D, D, FF, FF, EMBED_WIDTH, EMBED_WIDTH, EMBED_WIDTH]


def slot_starts(owners):
    counts = jnp.array(ROW_COUNTS, jnp.int32)
    same_owner = (owners[:, None] == owners[None, :]).astype(jnp.int32)
    earlier_mask = jnp.tril(jnp.ones((len(ROW_COUNTS),) * 2, jnp.int32), -1)
    return jnp.sum(same_owner * earlier_mask * counts[None, :], 1)


def waves(places, width):
    half_width = width // 2
    frequency = jnp.exp(-math.log(10000.0) * jnp.arange(half_width, dtype=f32) / half_width)
    angles = places[:, None] * frequency[None, :]
    return jnp.concatenate([jnp.sin(angles), jnp.cos(angles)], 1)


def norm_parts(value_entries):
    center = value_entries - jnp.mean(value_entries, -1, keepdims=True)
    scale_inv = lax.rsqrt(jnp.mean(center * center, -1, keepdims=True) + eps_norm)
    return (center * scale_inv, scale_inv)


def norm_back(normal_part, scale_inv, gain_vec, grad_out):
    scaled = grad_out * gain_vec
    inner = (
        scaled
        - jnp.mean(scaled, -1, keepdims=True)
        - normal_part * jnp.mean(scaled * normal_part, -1, keepdims=True)
    )
    return (inner * scale_inv, jnp.sum(grad_out * normal_part, 0), jnp.sum(grad_out, 0))


def adamw(weight, gradient, moment_one, moment_two):
    moment_one = beta_one * moment_one + (1.0 - beta_one) * gradient
    moment_two = beta_two * moment_two + (1.0 - beta_two) * gradient * gradient
    fix_one = 1.0 - beta_one**STEP
    fix_two = 1.0 - beta_two**STEP
    update_dir = moment_one / fix_one / (jnp.sqrt(moment_two / fix_two) + eps_adam)
    return (weight - learn_rate * (update_dir + weight_decay * weight), moment_one, moment_two)


MESH = pl.DeviceIdType.MESH
ANY = pl.BlockSpec(memory_space=pl.ANY)
UNIT = 768
HALF = 96
QUARTER = 192


def place():
    d, v = lax.axis_index("dp"), lax.axis_index("vocab")
    return d // 2, d % 2, d, v


def greet(partners):
    barrier = pltpu.get_barrier_semaphore()
    for partner in partners:
        pl.semaphore_signal(barrier, inc=1, device_id=partner, device_id_type=MESH)
    pl.semaphore_wait(barrier, len(partners))


def remote(src, dst, sems, index, partner):
    return pltpu.make_async_remote_copy(
        src_ref=src,
        dst_ref=dst,
        send_sem=sems[0].at[index],
        recv_sem=sems[1].at[index],
        device_id=partner,
        device_id_type=MESH,
    )


def start_all(copies):
    for copy in copies:
        copy.start()
    return copies


def arrive_all(copies):
    for copy in copies:
        copy.wait_recv()


VMEM = pl.BlockSpec(memory_space=pltpu.VMEM)
SMEM = pl.BlockSpec(memory_space=pltpu.SMEM)


def prepare_kernel(
    owners, ids_from, mask_from, table_from, slots,
    payload, table_low, row_of, safe, keep_rows, keep, valid, count, kind, unit, column,
    units, extras, ids, mask, table, sems, own_sems,
):
    d, v = lax.axis_index("dp"), lax.axis_index("vocab")
    starts = [
        sum(jnp.where(owners[j] == owners[i], ROW_COUNTS[j], 0) for j in range(i)) + 0 * owners[i]
        for i in range(len(ROW_COUNTS))
    ]
    whole = (owners[4] == d) | (owners[5] == d)
    fetched = [
        pltpu.make_async_copy(src, dst, own_sems.at[i])
        for i, (src, dst) in enumerate(((ids_from, ids), (mask_from, mask), (table_from, table)))
    ]
    for copy in fetched:
        copy.start()
    copies = []
    for u in range(4):
        first = pl.multiple_of(jnp.where(whole, u * UNIT, starts[u]), LANES)
        copies.append(
            pltpu.make_async_copy(slots.at[:, pl.ds(first, UNIT)], units.at[u], sems.at[u])
        )
        first = pl.multiple_of(starts[6 + min(u, 2)], LANES)
        copies.append(
            pltpu.make_async_copy(slots.at[:, pl.ds(first, LANES)], extras.at[u], sems.at[4 + u])
        )
    for copy in copies:
        copy.start()

    def clear(j, carry):
        kind[j] = 0
        unit[j] = 0
        column[j] = 0
        return carry

    lax.fori_loop(0, CAP // LANES, clear, 0)
    per_unit = UNIT // LANES
    first_unit = [0, 1, 2, 3, 0, 0, 0, 1, 2]
    for i, rows in enumerate(ROW_COUNTS):

        def claim(i=i, rows=rows):
            def one(b, carry):
                j = starts[i] // LANES + b
                kind[j] = 2 if i > 5 else 1
                unit[j] = first_unit[i] + b // per_unit
                column[j] = b % per_unit
                return carry

            lax.fori_loop(0, rows // LANES, one, 0)

        pl.when(owners[i] == d)(claim)

    for copy in fetched:
        copy.wait()
    table_low[...] = table[...].astype(bf16)
    count[...] = jnp.full((8, LANES), jnp.sum(mask[...].astype(f32)))
    for b in range(4):
        at = pl.ds(pl.multiple_of((v ^ b) * 256, 256), 256)
        local = ids[:, at] - v * table.shape[1]
        row_of[b : b + 1, :] = local
        safe[:, 256 * b : 256 * b + 256] = jnp.clip(local, 0, table.shape[1] - 1)
        weight = mask[:, at].astype(f32)
        keep_rows[b : b + 1, :] = weight
        inside = ((local >= 0) & (local < table.shape[1])).astype(f32)
        both = jnp.concatenate([weight, inside, jnp.zeros((6, 256), f32)], 0).T
        keep[256 * b : 256 * b + 256, :] = both[:, 0:1]
        valid[256 * b : 256 * b + 256, :] = both[:, 1:2]
    for copy in copies:
        copy.wait()
    for u in range(4):
        for half in range(2):
            rows = slice(half * HALF, half * HALF + HALF)
            payload[2 * u + half, :, 0:UNIT] = units[u, rows, :].astype(bf16)
            payload[2 * u + half, :, UNIT:] = extras[u, rows, :].astype(bf16)


def prepare(owners, ids, mask, table, slots):
    def shape(kind, *dims):
        return jax.ShapeDtypeStruct(dims, kind)

    blocks = CAP // LANES
    tokens = ids.shape[1]
    return pl.pallas_call(
        prepare_kernel,
        out_shape=[
            shape(bf16, 8, HALF, UNIT + LANES),
            shape(bf16, *table.shape),
            shape(jnp.int32, 4, tokens // 4),
            shape(jnp.int32, 1, tokens),
            shape(f32, 4, tokens // 4),
            shape(f32, tokens, 1),
            shape(f32, tokens, 1),
            shape(f32, 8, LANES),
        ]
        + [shape(jnp.int32, blocks)] * 3,
        in_specs=[SMEM, ANY, ANY, ANY, ANY],
        out_specs=[VMEM] * 8 + [SMEM] * 3,
        scratch_shapes=[
            pltpu.VMEM((4, QUARTER, UNIT), f32),
            pltpu.VMEM((4, QUARTER, LANES), f32),
            pltpu.VMEM(ids.shape, jnp.int32),
            pltpu.VMEM(mask.shape, jnp.int32),
            pltpu.VMEM(table.shape, f32),
            pltpu.SemaphoreType.DMA((8,)),
            pltpu.SemaphoreType.DMA((3,)),
        ],
        compiler_params=pltpu.CompilerParams(vmem_limit_bytes=60 * 2**20),
    )(owners, ids, mask, table, slots)


TRADE_MASKS = (4, 6, 5, 7, 2, 3, 1)


def chosen_of(pieces, wanted):
    value = pieces[0]
    for i in range(1, len(pieces)):
        value = jnp.where(wanted == i, pieces[i], value)
    return value


def spread_kernel(
    owners, steps, payload, tile, keep_rows, keep, table_home,
    up_to, down_to, small_to, attn_to, out_to, table_to, weight, twice, places, levels,
    up, down, small, attn, out, table, arrived, tiles, up_home, down_home, small_home, attn_home,
    a_send, a_recv, b_send, b_recv,
    z_send, z_recv, y_send, y_recv, x_send, x_recv, n_send, n_recv, f_send, f_recv, local, o_sem,
):
    z, y, d, v = place()
    far, near = v ^ 2, v ^ 1
    greet([(d ^ m, v) for m in TRADE_MASKS] + [(d, far), (d, near)])
    traded = start_all(
        [
            remote(payload.at[d ^ m], arrived.at[i], (a_send, a_recv), i, (d ^ m, v))
            for i, m in enumerate(TRADE_MASKS)
        ]
        + [
            remote(tile, tiles.at[i], (b_send, b_recv), i, (d ^ m, v))
            for i, m in enumerate(TRADE_MASKS)
        ]
    )
    homes = [up_home, down_home, small_home, attn_home, table_home]
    fulls = [up, down, small, attn, table]
    own_rows = pl.ds(v * QUARTER, QUARTER)

    def spot(c, unit):
        if c == 4:
            return table.at[2 * unit + y]
        first = y * HALF if c == 3 else v * QUARTER + y * HALF
        return fulls[c].at[unit, pl.ds(first, HALF), :]

    keeps, line, side, chip = {}, {}, {}, {}
    sent, landing, stores = [], {c: [] for c in range(4)}, []

    def note(copy, store=None, at=None):
        copy.start()
        sent.append(copy)
        if store is not None:
            store[at] = copy
        return copy

    def start_class(c):
        keeps[c] = pltpu.make_async_copy(homes[c], spot(c, z), local.at[c])
        keeps[c].start()
        for k in (2, 1, 3):
            note(
                remote(homes[c], spot(c, z), (z_send, z_recv), (c, k - 1), (d ^ (2 * k), v)),
                line,
                (c, k),
            )
        note(remote(homes[c], spot(c, z), (y_send, y_recv), (c, 0), (d ^ 1, v)), side, (c, 0))

    def relay(c, then=()):
        for k in (2, 1, 3):
            if k == 3:
                for other in then:
                    start_class(other)
            line[c, k].wait_recv()
            slab = spot(c, z ^ k)
            note(remote(slab, slab, (y_send, y_recv), (c, k), (d ^ 1, v)), side, (c, k))

    def chip_slab(c, k, source, target):
        note(remote(source, target, (x_send, x_recv), (c, k), (d, far)), chip, (c, k))
        landing[c].append(note(remote(source, target, (n_send, n_recv), (c, k), (d, near))))

    def to_chip(c):
        for k in (0, 2, 1, 3):
            side[c, k].wait_recv()
            if k == 0:
                keeps[c].wait()
            if c < 3:
                slab = fulls[c].at[z ^ k, own_rows, :]
                chip_slab(c, k, slab, slab)
        if c == 3:
            keep = pltpu.make_async_copy(attn.at[3], out.at[own_rows, :], local.at[5])
            keep.start()
            chip_slab(c, 0, attn.at[3], out.at[own_rows, :])
            keep.wait()

    def to_last(c):
        rows = pl.ds(far * QUARTER, QUARTER)
        for k in (0,) if c == 3 else (0, 2, 1, 3):
            chip[c, k].wait_recv()
            slab = out.at[rows, :] if c == 3 else fulls[c].at[z ^ k, rows, :]
            landing[c].append(note(remote(slab, slab, (f_send, f_recv), (c, k), (d, near))))

    def angles(position, width, count):
        lane = lax.broadcasted_iota(jnp.int32, (count, width), 1).astype(f32)
        return position * jnp.exp(-math.log(10000.0) * lane / width)

    position = v * 256 + lax.broadcasted_iota(jnp.int32, (256, D // 2), 0)
    angle = angles(position.astype(f32), D // 2, 256)
    places[:, 0 : D // 2] = jnp.sin(angle)
    places[:, D // 2 :] = jnp.cos(angle)
    step = jnp.full((8, EMBED_WIDTH), steps[0], jnp.int32).astype(f32)
    signal = 1.0 - jnp.sqrt(step / DIFF + 0.0001)
    angle = angles(step[:, 0 : EMBED_WIDTH // 2], EMBED_WIDTH // 2, 8)
    levels[0:1] = jnp.sqrt(signal[0:1])
    levels[1:2] = jnp.sqrt(1.0 - signal[0:1])
    levels[2:3] = jnp.concatenate([jnp.sin(angle), jnp.cos(angle)], 1)[0:1]
    levels[3:8] = jnp.zeros((5, EMBED_WIDTH), f32)
    arrive_all(traded)
    sent.extend(traded)
    total = tile[...]
    for i in range(7):
        total = total + tiles[i]
    weight[...] = keep_rows[...] / jnp.concatenate([total[0:4]] * 2, 1)
    twice[...] = 2.0 * keep[0:256, :] / total[0:1, 0:1]

    def from_owner(owner, lanes):
        value = payload[d, :, lanes]
        for i, m in enumerate(TRADE_MASKS):
            value = jnp.where(owner == d ^ m, arrived[i, :, lanes], value)
        return value

    up_home[...] = from_owner(owners[4], slice(0, UNIT))
    down_home[...] = from_owner(owners[5], slice(0, UNIT))
    attn_home[...] = from_owner(chosen_of([owners[u] for u in range(4)], z), slice(0, UNIT))
    small_home[...] = from_owner(
        chosen_of([owners[6 + min(u, 2)] for u in range(4)], z), slice(UNIT, UNIT + LANES)
    )

    def store(src, dst, index):
        copy = pltpu.make_async_copy(src, dst, o_sem.at[index])
        copy.start()
        stores.append(copy)

    def finish(c):
        arrive_all(landing[c])
        if c == 3:
            store(out, out_to, 3)
        else:
            store(fulls[c], (up_to, down_to, small_to)[c], c)

    start_class(0)
    relay(0, (1,))
    to_chip(0)
    relay(1, (2, 3))
    to_chip(1)
    relay(2)
    relay(3, (4,))
    to_chip(2)
    to_chip(3)
    store(attn, attn_to, 4)
    to_last(0)
    relay(4)
    finish(0)
    to_last(1)
    to_last(2)
    to_last(3)
    to_chip(4)
    store(table, table_to, 5)
    finish(1)
    finish(2)
    finish(3)
    for copy in stores:
        copy.wait()
    for copy in sent:
        copy.wait_send()


def spread(owners, steps, payload, tile, keep_rows, keep, table_home):
    rows, vocab_rows = table_home.shape
    dma, vmem = pltpu.SemaphoreType.DMA, pltpu.VMEM

    def shape(*dims):
        return jax.ShapeDtypeStruct(dims, bf16)

    return pl.pallas_call(
        spread_kernel,
        out_shape=[
            shape(4, D, UNIT),
            shape(4, D, UNIT),
            shape(4, D, LANES),
            shape(4, QUARTER, UNIT),
            shape(D, UNIT),
            shape(8, rows, vocab_rows),
            jax.ShapeDtypeStruct(keep_rows.shape, f32),
            jax.ShapeDtypeStruct((256, 1), f32),
            jax.ShapeDtypeStruct((256, D), f32),
            jax.ShapeDtypeStruct((8, EMBED_WIDTH), f32),
        ],
        in_specs=[SMEM] * 2 + [VMEM] * 5,
        out_specs=[ANY] * 6 + [VMEM] * 4,
        scratch_shapes=[
            vmem((4, D, UNIT), bf16),
            vmem((4, D, UNIT), bf16),
            vmem((4, D, LANES), bf16),
            vmem((4, QUARTER, UNIT), bf16),
            vmem((D, UNIT), bf16),
            vmem((8, rows, vocab_rows), bf16),
            vmem((7, HALF, UNIT + LANES), bf16),
            vmem((7, 8, LANES), f32),
            vmem((HALF, UNIT), bf16),
            vmem((HALF, UNIT), bf16),
            vmem((HALF, LANES), bf16),
            vmem((HALF, UNIT), bf16),
        ]
        + [dma((7,))] * 4
        + [dma((5, 3))] * 2
        + [dma((5, 4))] * 2
        + [dma((4, 4))] * 6
        + [dma((6,))] * 2,
        compiler_params=pltpu.CompilerParams(
            collective_id=1, has_side_effects=True, vmem_limit_bytes=60 * 2**20
        ),
    )(owners, steps, payload, tile, keep_rows, keep, table_home)

def neighbours():
    d, v = lax.axis_index("dp"), lax.axis_index("vocab")
    return [(d, v ^ k) for k in (1, 2, 3)]


def by_position(v, store):
    for i in range(4):
        pl.when(v == i)(functools.partial(store, i))


def forward_kernel(
    looked, valid, levels, places, vecs, keep, noise_hbm, small_hbm, attn_hbm, out_hbm, up_hbm, down_hbm,
    found, clean, inputs, hidden, normed_all, q, k, k_t, values, log_total, mixed, middle, normed_two,
    up_proj, active, hidden_two, final_norm, predicted, pred_all,
    noise, small, attn, out_w, up_w, down_w, found_in, values_t, mixed_out, mixed_in, seen,
    w_sem, s_sem, e_send, e_recv, n_send, n_recv, m_send, m_recv, p_send, p_recv,
):
    v = lax.axis_index("vocab")
    partners = neighbours()
    sources = ((noise_hbm, noise), (small_hbm, small), (attn_hbm, attn), (out_hbm, out_w))
    first = [
        pltpu.make_async_copy(src, dst, s_sem.at[i]) for i, (src, dst) in enumerate(sources)
    ]
    for copy in first:
        copy.start()
    loads = []
    for j in range(4):
        for i, (src, dst) in enumerate(((up_hbm, up_w), (down_hbm, down_w))):
            copy = pltpu.make_async_copy(src.at[j], dst.at[j], w_sem.at[2 * j + i])
            copy.start()
            loads.append(copy)
    for b in range(4):
        found[b] = jnp.where(
            valid[256 * b : 256 * b + 256, :] > 0.0, looked[b].astype(f32), 0.0
        ).astype(bf16)
    greet(partners)
    asked = start_all(
        [
            remote(found.at[m], found_in.at[m - 1], (e_send, e_recv), m - 1, partners[m - 1])
            for m in (2, 3, 1)
        ]
    )
    seen[...] = jnp.broadcast_to(keep[...], seen.shape)
    for copy in first:
        copy.wait()
    wave = levels[2:3].astype(bf16)
    time_part = matmul_nt(jnp.broadcast_to(wave, (16, EMBED_WIDTH)), small[1])[0:1]
    arrive_all(asked)
    total = found[0].astype(f32)
    for m in range(3):
        total = total + found_in[m].astype(f32)
    clean[...] = total
    noisy = levels[0:1] * total + levels[1:2] * noise[...].astype(f32)
    inputs[:, 0:EMBED_WIDTH] = noisy.astype(bf16)
    inputs[:, EMBED_WIDTH:] = jnp.broadcast_to(wave, noisy.shape)
    value = matmul_nt(inputs[:, 0:EMBED_WIDTH], small[0]) + time_part + places[...]
    hidden[...] = value
    normed_all[0] = (norm_parts(value)[0] * vecs[0:1] + vecs[1:2]).astype(bf16)

    far = remote(normed_all.at[0], normed_all.at[2], (n_send, n_recv), 0, partners[1])
    near = remote(normed_all.at[0], normed_all.at[1], (n_send, n_recv), 1, partners[0])
    last = remote(normed_all.at[2], normed_all.at[3], (n_send, n_recv), 2, partners[0])
    far.start()
    near.start()

    def project(b):
        rows = pl.ds(b * 256, 256)
        block = normed_all[b]
        for i, ref in ((0, q), (1, k), (2, values)):
            result = matmul_nt(block, attn[i])
            if i == 0:
                result = result.astype(bf16).astype(f32) * HDIM ** (-0.5)
            for h in range(3):
                ref[h, rows, :] = result[:, h * HDIM : (h + 1) * HDIM].astype(bf16)
        k_t[:, rows] = matmul_nt(attn[1], block).astype(bf16)
        values_t[:, rows] = matmul_nt(attn[2], block).astype(bf16)

    project(0)
    near.wait_recv()
    project(1)
    far.wait_recv()
    last.start()
    project(2)
    last.wait_recv()
    project(3)

    given = []
    for b in (2, 3, 1, 0):
        rows = pl.ds(b * 256, 256)
        parts = []
        for h in range(3):
            scores = matmul_nt(k[h], q[h, rows, :])
            scores = jnp.where(seen[...] > 0.0, scores, -1000000000.0)
            top = jnp.max(scores, 0, keepdims=True)
            expo = jnp.exp(scores - top)
            mass = jnp.sum(expo, 0, keepdims=True)
            probs = (expo * (1.0 / mass)).astype(bf16)
            log_total[pl.ds(3 * b + h, 1), :] = top + jnp.log(mass)
            parts.append(matmul_nn(values_t[h * HDIM : (h + 1) * HDIM, :], probs))
        block = jnp.concatenate(parts, 0).T.astype(bf16)
        if b == 0:
            mixed_in[0] = block
        else:
            mixed_out[b - 1] = block
            copy = remote(
                mixed_out.at[b - 1], mixed_in.at[b], (m_send, m_recv), b - 1, partners[b - 1]
            )
            copy.start()
            given.append(copy)
    arrive_all(given)

    def lay(i):
        for b in range(4):
            mixed[:, QUARTER * (i ^ b) : QUARTER * ((i ^ b) + 1)] = mixed_in[b]

    by_position(v, lay)
    value = hidden[...] + matmul_nt(mixed[...], out_w[...])
    middle[...] = value
    normed_two[...] = (norm_parts(value)[0] * vecs[2:3] + vecs[3:4]).astype(bf16)
    for j in range(4):
        loads[2 * j].wait()
        loads[2 * j + 1].wait()
        raised = matmul_nn(normed_two[...], up_w[j]) + vecs[4 + j : 5 + j]
        up_proj[j] = raised
        active[j] = jax.nn.gelu(raised).astype(bf16)
        lowered = matmul_nt(active[j], down_w[j])
        hidden_two[...] = (middle[...] if j == 0 else hidden_two[...]) + lowered
    final_norm[...] = (norm_parts(hidden_two[...])[0] * vecs[8:9] + vecs[9:10]).astype(bf16)
    predicted[...] = matmul_nn(final_norm[...], small[2])
    pred_all[0] = predicted[...].astype(bf16)
    shown = start_all(
        [
            remote(pred_all.at[0], pred_all.at[m], (p_send, p_recv), m - 1, partners[m - 1])
            for m in (2, 3, 1)
        ]
    )
    arrive_all(shown)
    for copy in asked + [far, near, last] + given + shown:
        copy.wait_send()


def forward(*operands):
    dma, vmem = pltpu.SemaphoreType.DMA, pltpu.VMEM
    n = 256

    def shape(kind, *dims):
        return jax.ShapeDtypeStruct(dims, kind)

    return pl.pallas_call(
        forward_kernel,
        out_shape=[
            shape(bf16, 4, n, EMBED_WIDTH),
            shape(f32, n, EMBED_WIDTH),
            shape(bf16, n, 2 * EMBED_WIDTH),
            shape(f32, n, D),
            shape(bf16, 4, n, D),
            shape(bf16, 3, 4 * n, HDIM),
            shape(bf16, 3, 4 * n, HDIM),
            shape(bf16, QUARTER, 4 * n),
            shape(bf16, 3, 4 * n, HDIM),
            shape(f32, 16, n),
            shape(bf16, n, D),
            shape(f32, n, D),
            shape(bf16, n, D),
            shape(f32, 4, n, UNIT),
            shape(bf16, 4, n, UNIT),
            shape(f32, n, D),
            shape(bf16, n, D),
            shape(f32, n, EMBED_WIDTH),
            shape(bf16, 4, n, EMBED_WIDTH),
        ],
        in_specs=[VMEM] * 6 + [ANY] * 6,
        out_specs=[VMEM] * 19,
        scratch_shapes=[
            vmem((n, EMBED_WIDTH), bf16),
            vmem((4, D, LANES), bf16),
            vmem((4, QUARTER, UNIT), bf16),
            vmem((D, UNIT), bf16),
            vmem((4, D, UNIT), bf16),
            vmem((4, D, UNIT), bf16),
            vmem((3, n, EMBED_WIDTH), bf16),
            vmem((QUARTER, 4 * n), bf16),
            vmem((3, n, QUARTER), bf16),
            vmem((4, n, QUARTER), bf16),
            vmem((4 * n, n), f32),
            dma((8,)),
            dma((4,)),
        ]
        + [dma((3,))] * 8,
        compiler_params=pltpu.CompilerParams(
            collective_id=4, has_side_effects=True, vmem_limit_bytes=60 * 2**20
        ),
    )(*operands)


STRIP = 768


def strips(rows):
    return [(lo, min(STRIP, rows - lo)) for lo in range(0, rows, STRIP)]


def head_kernel(
    pred_all, table, table_t, weight, found,
    grad_pred, lse, found_t, stats, gathered, outgoing, incoming,
    s_send, s_recv, g_send, g_recv,
):
    partners = neighbours()
    greet(partners)
    rows = table_t.shape[0]
    full, rest = rows // STRIP, rows % STRIP
    mixes = []
    for b in range(4):
        block = pred_all[b]

        def strip(at, carry):
            peak, mass, mix = carry
            value = matmul_nt(table_t[at, :], block)
            top = jnp.maximum(peak, jnp.max(value, 0, keepdims=True))
            expo = jnp.exp(value - top)
            fade = jnp.exp(peak - top)
            mass = mass * fade + jnp.sum(expo, 0, keepdims=True)
            return top, mass, mix * fade + matmul_nn(table[:, at], expo.astype(bf16))

        carry = lax.fori_loop(
            0,
            full,
            lambda t, carry: strip(pl.ds(pl.multiple_of(t * STRIP, STRIP), STRIP), carry),
            (
                jnp.full((1, 256), -jnp.inf, f32),
                jnp.zeros((1, 256), f32),
                jnp.zeros((EMBED_WIDTH, 256), f32),
            ),
            unroll=3,
        )
        if rest:
            carry = strip(pl.ds(full * STRIP, rest), carry)
        found_t[b] = found[b].astype(f32).T
        stats[b, 2:3] = jnp.sum(block.astype(f32).T * found_t[b], 0, keepdims=True)
        stats[b, 0:1] = carry[0]
        stats[b, 1:2] = carry[1]
        stats[b, 3:8] = jnp.zeros((5, 256), f32)
        mixes.append(carry[2])
    told = start_all(
        [
            remote(stats, gathered.at[m - 1], (s_send, s_recv), m - 1, partners[m - 1])
            for m in (2, 3, 1)
        ]
    )
    arrive_all(told)
    given = []
    for b in (2, 3, 1, 0):
        views = [stats[b]] + [gathered[m - 1, b ^ m] for m in (1, 2, 3)]
        peak = functools.reduce(jnp.maximum, [view[0:1] for view in views])
        mass = sum(view[1:2] * jnp.exp(view[0:1] - peak) for view in views)
        total = peak + jnp.log(mass)
        lse[b : b + 1, :] = total
        if b == 0:
            target = sum(view[2:3] for view in views)
            lse[4:5, :] = weight[0:1, :] * (total - target)
            lse[5:8, :] = jnp.zeros((3, 256), f32)
        share = weight[b : b + 1, :]
        local = mixes[b] * (jnp.exp(stats[b, 0:1] - total) * share)
        local = local - found_t[b] * share
        outgoing[b] = local.T.astype(bf16)
        if b:
            copy = remote(
                outgoing.at[b], incoming.at[b - 1], (g_send, g_recv), b - 1, partners[b - 1]
            )
            copy.start()
            given.append(copy)
    arrive_all(given)
    value = outgoing[0].astype(f32)
    for m in range(3):
        value = value + incoming[m].astype(f32)
    grad_pred[...] = value
    for copy in told + given:
        copy.wait_send()


def head(pred_all, table, table_t, weight, found):
    dma, vmem = pltpu.SemaphoreType.DMA, pltpu.VMEM
    return pl.pallas_call(
        head_kernel,
        out_shape=[
            jax.ShapeDtypeStruct((256, EMBED_WIDTH), f32),
            jax.ShapeDtypeStruct((8, 256), f32),
        ],
        in_specs=[VMEM] * 5,
        out_specs=[VMEM] * 2,
        scratch_shapes=[
            vmem((4, EMBED_WIDTH, 256), f32),
            vmem((4, 8, 256), f32),
            vmem((3, 4, 8, 256), f32),
            vmem((4, 256, EMBED_WIDTH), bf16),
            vmem((3, 256, EMBED_WIDTH), bf16),
        ]
        + [dma((3,))] * 4,
        compiler_params=pltpu.CompilerParams(
            collective_id=5, has_side_effects=True, vmem_limit_bytes=60 * 2**20
        ),
    )(pred_all, table, table_t, weight, found)


def gelu_slope(u):
    inner = math.sqrt(2.0 / math.pi)
    bent = jnp.tanh(inner * (u + 0.044715 * (u * u * u)))
    return 0.5 * (1.0 + bent) + (0.5 * inner) * u * (1.0 - bent * bent) * (
        1.0 + (3.0 * 0.044715) * (u * u)
    )


def backward_kernel(
    grad_pred, clean, predicted, twice, levels, head_stats, hidden, middle, hidden_two,
    normed_two, final_norm, up_proj, q, k, k_t, values, log_total, keep,
    small, attn, out_w, up_hbm, down_hbm, vecs,
    grad_pred_low, down_left, up_left, out_left, small_left, final_left, qkv_left, grad_up, grad_clean, sums,
    up_w, down_w, carried, folded, mix_out, mix_in, grad_k, grad_v, n_out, n_in, f_out, f_in, seen,
    w_sem, m_send, m_recv, n_send, n_recv, c_send, c_recv,
):
    v = lax.axis_index("vocab")
    partners = neighbours()
    loads = []
    for j in range(4):
        for i, (src, dst) in enumerate(((down_hbm, down_w), (up_hbm, up_w))):
            copy = pltpu.make_async_copy(src.at[j], dst.at[j], w_sem.at[2 * j + i])
            copy.start()
            loads.append(copy)
    seen[...] = jnp.broadcast_to(keep[...], seen.shape)
    greet(partners)

    def turned(value):
        return value.astype(f32).T.astype(bf16)

    error = predicted[...] - clean[...]
    pull = twice[...] * error
    low = (grad_pred[...] + pull).astype(bf16)
    grad_pred_low[...] = low
    length = jnp.sqrt(jnp.sum(clean[...] * clean[...], -1, keepdims=True) + 1e-06)
    lane = lax.broadcasted_iota(jnp.int32, (1, UNIT), 1)
    scalars = (jnp.sum(pull * error), jnp.sum(head_stats[4:5, :]), jnp.sum(twice[...] * length))
    counted = jnp.sum(keep[0:256, :])
    sums[10:11, :] = sum(jnp.where(lane == i, x, 0.0) for i, x in enumerate(scalars + (counted,)))
    sums[11:16, :] = jnp.zeros((5, UNIT), f32)

    def through_norm(value, gain_row, grad_out, at):
        normal, scale_inv = norm_parts(value)
        part, grad_gain, grad_shift = norm_back(normal, scale_inv, vecs[gain_row : gain_row + 1], grad_out)
        sums[at : at + 1, :] = grad_gain[None, :]
        sums[at + 1 : at + 2, :] = grad_shift[None, :]
        return part

    carried[...] = through_norm(hidden_two[...], 8, matmul_nt(low, small[2]), 8)
    low = carried[...].astype(bf16)
    down_left[...] = turned(carried[...])
    up_left[...] = turned(normed_two[...])
    final_left[...] = turned(final_norm[...])
    for j in range(4):
        loads[2 * j].wait()
        loads[2 * j + 1].wait()
        slope = matmul_nn(low, down_w[j]) * gelu_slope(up_proj[j])
        grad_up[j] = slope.astype(bf16)
        sums[4 + j : 5 + j, :] = jnp.sum(grad_up[j].astype(f32), 0, keepdims=True)
        part = matmul_nt(grad_up[j], up_w[j])
        folded[...] = part if j == 0 else folded[...] + part
    carried[...] = carried[...] + through_norm(middle[...], 2, folded[...], 2)
    out_left[...] = turned(carried[...])
    folded[...] = matmul_nn(carried[...].astype(bf16), out_w[...])

    def lay(i):
        for b in range(4):
            mix_out[b] = folded[:, QUARTER * (i ^ b) : QUARTER * ((i ^ b) + 1)].astype(bf16)

    by_position(v, lay)
    mixed = [
        remote(mix_out.at[m], mix_in.at[m - 1], (m_send, m_recv), m - 1, partners[m - 1])
        for m in (1, 2, 3)
    ]
    for m in (2, 3, 1):
        mixed[m - 1].start()
    for b in range(4):
        if b:
            mixed[b - 1].wait_recv()
        grad_block = mix_out[0] if b == 0 else mix_in[b - 1]
        rows = pl.ds(b * 256, 256)
        for h in range(3):
            grad_mix = grad_block[:, h * HDIM : (h + 1) * HDIM]
            asked = q[h, rows, :]
            scores = matmul_nt(k[h], asked)
            scores = jnp.where(seen[...] > 0.0, scores, -1000000000.0)
            probs = jnp.exp(scores - log_total[3 * b + h : 3 * b + h + 1, :])
            grad_probs = matmul_nt(values[h], grad_mix)
            inner = jnp.sum(probs * grad_probs, 0, keepdims=True)
            grad_scores = (probs * (grad_probs - inner)).astype(bf16)
            grad_asked = matmul_nn(k_t[h * HDIM : (h + 1) * HDIM, :], grad_scores)
            qkv_left[0, h * HDIM : (h + 1) * HDIM, rows] = (grad_asked * HDIM ** (-0.5)).astype(bf16)
            part_k = matmul_nn(grad_scores, asked)
            part_v = matmul_nn(probs.astype(bf16), grad_mix)
            grad_k[h] = part_k if b == 0 else grad_k[h] + part_k
            grad_v[h] = part_v if b == 0 else grad_v[h] + part_v
    for h in range(3):
        lanes = pl.ds(h * HDIM, HDIM)
        qkv_left[1, lanes, :] = grad_k[h].T.astype(bf16)
        qkv_left[2, lanes, :] = grad_v[h].T.astype(bf16)

    def grad_normed(b):
        rows = pl.ds(b * 256, 256)
        return sum(matmul_tn(qkv_left[i, :, rows], attn[i]) for i in range(3))

    n_out[0] = grad_normed(1).astype(bf16)
    n_out[1] = grad_normed(3).astype(bf16)
    near = remote(n_out, n_in, (n_send, n_recv), 0, partners[0])
    near.start()
    folded[...] = grad_normed(2)
    near.wait_recv()
    f_out[...] = (folded[...] + n_in[1].astype(f32)).astype(bf16)
    far = remote(f_out, f_in, (n_send, n_recv), 1, partners[1])
    far.start()
    folded[...] = grad_normed(0) + n_in[0].astype(f32)
    far.wait_recv()
    grad_out = folded[...] + f_in[...].astype(f32)
    carried[...] = carried[...] + through_norm(hidden[...], 0, grad_out, 0)
    small_left[...] = turned(carried[...])
    back = matmul_nn(carried[...].astype(bf16), small[0])
    grad_clean[0] = (levels[0:1] * back - twice[...] * (predicted[...] - clean[...])).astype(bf16)
    shown = start_all(
        [
            remote(grad_clean.at[0], grad_clean.at[m], (c_send, c_recv), m - 1, partners[m - 1])
            for m in (2, 3, 1)
        ]
    )
    arrive_all(shown)
    for copy in mixed + [near, far] + shown:
        copy.wait_send()


def backward(*operands):
    dma, vmem = pltpu.SemaphoreType.DMA, pltpu.VMEM
    n = 256

    def shape(kind, *dims):
        return jax.ShapeDtypeStruct(dims, kind)

    return pl.pallas_call(
        backward_kernel,
        out_shape=[shape(bf16, n, EMBED_WIDTH)]
        + [shape(bf16, D, n)] * 5
        + [
            shape(bf16, 3, QUARTER, 4 * n),
            shape(bf16, 4, n, UNIT),
            shape(bf16, 4, n, EMBED_WIDTH),
            shape(f32, 16, UNIT),
        ],
        in_specs=[VMEM] * 21 + [ANY] * 2 + [VMEM],
        out_specs=[VMEM] * 10,
        scratch_shapes=[
            vmem((4, D, UNIT), bf16),
            vmem((4, D, UNIT), bf16),
            vmem((n, D), f32),
            vmem((n, D), f32),
            vmem((4, n, QUARTER), bf16),
            vmem((3, n, QUARTER), bf16),
            vmem((3, 4 * n, HDIM), f32),
            vmem((3, 4 * n, HDIM), f32),
            vmem((2, n, D), bf16),
            vmem((2, n, D), bf16),
            vmem((n, D), bf16),
            vmem((n, D), bf16),
            vmem((4 * n, n), f32),
            dma((8,)),
        ]
        + [dma((3,))] * 6,
        compiler_params=pltpu.CompilerParams(
            collective_id=6, has_side_effects=True, vmem_limit_bytes=60 * 2**20
        ),
    )(*operands)

I16 = jnp.int16
TAIL = 16
TILES = 60
PART_TILES = 30
PART = 3840


def exponent(peak):
    return jnp.ceil(jnp.log2(jnp.maximum(peak, 1e-30))) + 1.0


def coded(value, power):
    return jnp.round(value * jnp.exp2(15.0 - power)).astype(jnp.int32).astype(I16)


def plain(code, power):
    return code.astype(jnp.int32).astype(f32) * jnp.exp2(power - 15.0)


def put(ref, value):
    rows, cols = value.shape
    power = exponent(jnp.max(jnp.abs(value), 0, keepdims=True))
    ref[0:rows, :] = coded(value, power)
    ref[rows : rows + TAIL, :] = (
        jnp.broadcast_to(power, (TAIL, cols)).astype(jnp.int32).astype(I16)
    )


def get(ref, rows):
    power = ref[rows : rows + TAIL, :].astype(jnp.int32).astype(f32)[0:1]
    return plain(ref[0:rows, :], power)


def put_tiles(ref, source, rows):
    lane = lax.broadcasted_iota(jnp.int32, (rows, LANES), 1)

    def body(tile, powers):
        at = pl.ds(pl.multiple_of(tile * LANES, LANES), LANES)
        value = source(at)
        power = exponent(jnp.max(jnp.abs(value), 1, keepdims=True))
        ref[:, at] = coded(value, power)
        return jnp.where(lane == tile, power, powers)

    powers = lax.fori_loop(0, PART_TILES, body, jnp.zeros((rows, LANES), f32), unroll=6)
    ref[:, PART:] = powers.astype(jnp.int32).astype(I16)


def tile_getter(ref, rows):
    lane = lax.broadcasted_iota(jnp.int32, (rows, LANES), 1)
    powers = ref[:, PART:].astype(jnp.int32).astype(f32)

    def read(tile, at):
        power = jnp.sum(jnp.where(lane == tile, powers, 0.0), 1, keepdims=True)
        return plain(ref[:, at], power)

    return read


def grads_kernel(
    owners, down_left, up_left, out_left, small_left, final_left, qkv_left,
    active, grad_up, mixed, inputs, grad_pred, normed, pred_all, grad_clean, table_t, lse, weight, row_of, tile,
    summed, table_sum, tile_sum,
    home, small_home, outgoing, cs, cr, xs, xr, ys, yr, zs, zr, part, half,
    small_cs, small_cr, small_xs, small_xr, small_ys, small_yr, small_zs, small_zr, small_half,
    table, pred_t, clean_t, ts, tr, tzs, tzr, tile_at, tile_from,
    c_send, c_recv, x_send, x_recv, y_send, y_recv, z_send, z_recv, t_send, t_recv, a_send, a_recv, local,
):
    z, y, d, v = place()
    far, near = v ^ 2, v ^ 1
    greet([(d ^ m, v) for m in TRADE_MASKS] + [(d, far), (d, near)])
    sent = []

    def send(src, dst, sems, index, partner):
        copy = remote(src, dst, sems, index, partner)
        copy.start()
        sent.append(copy)
        return copy

    def product(n, who):
        if n == 0:
            return matmul_nn(out_left[who], mixed[...])
        if n < 5:
            return matmul_nn(down_left[who], active[n - 1])
        return matmul_nn(up_left[who], grad_up[n - 5])

    core, chip, side, line = {}, {}, {}, {}

    def to_core(n):
        put(cs.at[n, 0], product(n, near))
        put(cs.at[n, 1], product(n, near ^ 2))
        core[n] = send(cs.at[n], cr.at[n], (c_send, c_recv), n, (d, near))

    def to_chip(n):
        core[n].wait_recv()
        put(xs.at[n], product(n, far) + get(cr.at[n, 1], QUARTER))
        chip[n] = send(xs.at[n], xr.at[n], (x_send, x_recv), n, (d, far))

    def halves(slot, value):
        part[...] = value
        put(ys.at[slot], part[pl.ds((1 - y) * HALF, HALF), :])
        half[slot] = part[pl.ds(y * HALF, HALF), :]
        side[slot] = send(ys.at[slot], yr.at[slot], (y_send, y_recv), slot, (d ^ 1, v))

    def to_side(n):
        chip[n].wait_recv()
        value = product(n, v) + get(cr.at[n, 0], QUARTER) + get(xr.at[n], QUARTER)
        halves(3 + n, value)

    def to_line(group):
        for u in range(4):
            slot = 4 * group + u
            side[slot].wait_recv()
            half[slot] = half[slot] + get(yr.at[slot], HALF)
        for k in (2, 1, 3):
            put(zs.at[group, k - 1], half[4 * group + (z ^ k)])
            line[group, k] = send(
                zs.at[group, k - 1], zr.at[group, k - 1], (z_send, z_recv), 3 * group + k - 1, (d ^ (2 * k), v)
            )

    def to_home(group):
        total = half[4 * group + z]
        for k in (2, 1, 3):
            line[group, k].wait_recv()
            total = total + get(zr.at[group, k - 1], HALF)
        put(home.at[group], total)

    def small_product(who):
        return jnp.concatenate(
            [matmul_nn(small_left[who], inputs[...]), matmul_nn(final_left[who], grad_pred[...])], 1
        )

    def small_to_core():
        put(small_cs.at[0], small_product(near))
        put(small_cs.at[1], small_product(near ^ 2))
        core[9] = send(small_cs, small_cr, (c_send, c_recv), 9, (d, near))

    def small_to_chip():
        core[9].wait_recv()
        put(small_xs, small_product(far) + get(small_cr.at[1], QUARTER))
        chip[9] = send(small_xs, small_xr, (x_send, x_recv), 9, (d, far))

    def small_to_side():
        chip[9].wait_recv()
        value = small_product(v) + get(small_cr.at[0], QUARTER) + get(small_xr, QUARTER)
        cols = value.shape[1]
        part[:, 0:cols] = value
        put(small_ys, part[pl.ds((1 - y) * HALF, HALF), 0:cols])
        small_half[0] = part[pl.ds(y * HALF, HALF), 0:LANES]
        small_half[1] = part[pl.ds(y * HALF, HALF), LANES : 2 * LANES]
        small_half[2] = part[pl.ds(y * HALF, HALF), 2 * LANES : cols]
        small_half[3] = jnp.zeros((HALF, LANES), f32)
        side[12] = send(small_ys, small_yr, (y_send, y_recv), 12, (d ^ 1, v))

    def small_to_line():
        side[12].wait_recv()
        value = get(small_yr, HALF)
        for u in range(3):
            small_half[u] = small_half[u] + value[:, u * LANES : (u + 1) * LANES]
        for k in (2, 1, 3):
            put(small_zs.at[k - 1], small_half[z ^ k])
            line[3, k] = send(
                small_zs.at[k - 1], small_zr.at[k - 1], (z_send, z_recv), 9 + k - 1, (d ^ (2 * k), v)
            )

    def small_to_home():
        total = small_half[z]
        for k in (2, 1, 3):
            line[3, k].wait_recv()
            total = total + get(small_zr.at[k - 1], HALF)
        put(small_home, total)

    def turn_tokens():
        for b in range(4):
            pred_t[b] = pred_all[b].astype(f32).T.astype(bf16)
            clean_t[b] = grad_clean[b].astype(f32).T.astype(bf16)

    vocab_rows = table_t.shape[0]

    def table_strip(lo, size):
        total = jnp.zeros((EMBED_WIDTH, size), f32)
        for b in range(4):
            logits = matmul_nt(table_t[lo : lo + size, :], pred_all[b])
            probs = jnp.exp(logits - lse[b : b + 1, :])
            here = lax.broadcasted_iota(jnp.int32, (size, 256), 0) == row_of[b : b + 1, :] - lo
            here = here.astype(f32)
            grad_logits = ((probs - here) * weight[b : b + 1, :]).astype(bf16)
            total = total + matmul_nt(pred_t[b], grad_logits)
            total = total + matmul_nt(clean_t[b], here.astype(bf16))
        for i in range(8):
            rows = slice(16 * (i // 2), 16 * (i // 2) + 16)
            table[i % 2, rows, lo : lo + size] = total[16 * i : 16 * i + 16]
        if lo + size == vocab_rows:
            table[:, :, vocab_rows:] = jnp.zeros((2, 64, TILES * LANES - vocab_rows), f32)

    table_strips = [(lo, min(STRIP, vocab_rows - lo)) for lo in range(0, vocab_rows, STRIP)]

    def shifted(at, p):
        return pl.ds(pl.multiple_of(at.start + p * PART, LANES), LANES)

    def table_to_side(p):
        put_tiles(ts.at[p], lambda at: table[1 - y, :, shifted(at, p)], 64)
        side[13 + p] = send(ts.at[p], tr.at[p], (y_send, y_recv), 13 + p, (d ^ 1, v))

    def table_line_value(which, p):
        rows = pl.ds(pl.multiple_of(which * 16, 16), 16)
        read = tile_getter(tr.at[p, rows, :], 16)
        return rows, read

    def table_to_line(p):
        side[13 + p].wait_recv()
        for k in (2, 1, 3):
            rows, read = table_line_value(z ^ k, p)

            def source(at, rows=rows, read=read):
                return table[y, rows, shifted(at, p)] + read(at.start // LANES, at)

            put_tiles(tzs.at[p, k - 1], source, 16)
            line[4 + p, k] = send(
                tzs.at[p, k - 1],
                tzr.at[p, k - 1],
                (z_send, z_recv),
                12 + 3 * p + k - 1,
                (d ^ (2 * k), v),
            )

    def table_to_home(p):
        for k in (2, 1, 3):
            line[4 + p, k].wait_recv()
        rows, read = table_line_value(z, p)
        others = [tile_getter(tzr.at[p, k], 16) for k in range(3)]

        def body(tile, carry):
            at = pl.ds(pl.multiple_of(tile * LANES, LANES), LANES)
            value = table[y, rows, shifted(at, p)] + read(tile, at)
            for other in others:
                value = value + other(tile, at)
            table_sum[:, shifted(at, p)] = value
            return carry

        lax.fori_loop(0, PART_TILES, body, 0, unroll=5)

    hops = [(d, near), (d, far), (d ^ 1, v), (d ^ 2, v), (d ^ 4, v)]
    tile_copies = {}

    def tile_send(hop):
        if hop == 0:
            tile_at[0] = tile[...]
        else:
            tile_copies[hop - 1].wait_recv()
            tile_at[hop] = tile_at[hop - 1] + tile_from[hop - 1]
        tile_copies[hop] = send(
            tile_at.at[hop], tile_from.at[hop], (t_send, t_recv), hop, hops[hop]
        )

    def token_products():
        for u in range(3):
            halves(
                u,
                sum(matmul_nn(qkv_left[u, :, 256 * b : 256 * b + 256], normed[b]) for b in range(4)),
            )

    turn_tokens()
    token_products()
    to_core(0)
    to_core(1)
    to_chip(0)
    tile_send(0)
    table_strip(*table_strips[0])
    table_strip(*table_strips[1])
    to_core(2)
    to_chip(1)
    to_side(0)
    table_strip(*table_strips[2])
    table_strip(*table_strips[3])
    to_core(3)
    to_chip(2)
    table_strip(*table_strips[4])
    table_to_side(0)
    to_line(0)
    to_side(1)
    table_strip(*table_strips[5])
    table_strip(*table_strips[6])
    to_core(4)
    to_chip(3)
    table_strip(*table_strips[7])
    table_strip(*table_strips[8])
    for strip in table_strips[9:]:
        table_strip(*strip)
    table_to_side(1)
    to_side(2)
    to_core(5)
    to_chip(4)
    tile_send(1)
    table_to_line(0)
    to_core(6)
    to_chip(5)
    to_side(3)
    to_core(7)
    to_chip(6)
    small_to_core()
    to_core(8)
    to_chip(7)
    small_to_chip()
    to_chip(8)
    to_side(4)
    tile_send(2)
    table_to_line(1)
    to_line(1)
    to_side(5)
    to_home(0)
    tile_send(3)
    small_to_side()
    to_side(6)
    table_to_home(0)
    small_to_line()
    tile_send(4)
    to_side(7)
    to_home(1)
    to_side(8)
    to_line(2)
    table_to_home(1)
    small_to_home()
    tile_copies[4].wait_recv()
    tile_sum[...] = tile_at[4] + tile_from[4]
    to_home(2)

    def offer(m):
        taker = d ^ m
        unit = jnp.where(owners[4] == taker, home[2], home[0])
        outgoing[m, :, 0:UNIT] = jnp.where(owners[5] == taker, home[1], unit)
        outgoing[m, :, UNIT:] = small_home[...]

    offered = []
    for i, m in enumerate(TRADE_MASKS):
        offer(m)
        offered.append(send(outgoing.at[m], summed.at[d], (a_send, a_recv), i, (d ^ m, v)))
    offer(0)
    keep = pltpu.make_async_copy(outgoing.at[0], summed.at[d], local)
    keep.start()
    keep.wait()
    arrive_all(offered)
    for copy in sent:
        copy.wait_send()


def reduce_grads(*operands):
    dma = pltpu.SemaphoreType.DMA
    vmem = pltpu.VMEM
    tall, low, wide = QUARTER + TAIL, HALF + TAIL, 3 * LANES
    table_cols = TILES * LANES
    return pl.pallas_call(
        grads_kernel,
        out_shape=[
            jax.ShapeDtypeStruct((8, low, UNIT + LANES), I16),
            jax.ShapeDtypeStruct((16, table_cols), f32),
            jax.ShapeDtypeStruct((16, UNIT), f32),
        ],
        in_specs=[SMEM] + [VMEM] * 19,
        out_specs=[VMEM] * 3,
        scratch_shapes=[
            vmem((3, low, UNIT), I16),
            vmem((low, LANES), I16),
            vmem((8, low, UNIT + LANES), I16),
            vmem((9, 2, tall, UNIT), I16),
            vmem((9, 2, tall, UNIT), I16),
            vmem((9, tall, UNIT), I16),
            vmem((9, tall, UNIT), I16),
            vmem((12, low, UNIT), I16),
            vmem((12, low, UNIT), I16),
            vmem((3, 3, low, UNIT), I16),
            vmem((3, 3, low, UNIT), I16),
            vmem((QUARTER, UNIT), f32),
            vmem((12, HALF, UNIT), f32),
            vmem((2, tall, wide), I16),
            vmem((2, tall, wide), I16),
            vmem((tall, wide), I16),
            vmem((tall, wide), I16),
            vmem((low, wide), I16),
            vmem((low, wide), I16),
            vmem((3, low, LANES), I16),
            vmem((3, low, LANES), I16),
            vmem((4, HALF, LANES), f32),
            vmem((2, 64, table_cols), f32),
            vmem((4, EMBED_WIDTH, 256), bf16),
            vmem((4, EMBED_WIDTH, 256), bf16),
            vmem((2, 64, PART + LANES), I16),
            vmem((2, 64, PART + LANES), I16),
            vmem((2, 3, 16, PART + LANES), I16),
            vmem((2, 3, 16, PART + LANES), I16),
            vmem((5, 16, UNIT), f32),
            vmem((5, 16, UNIT), f32),
        ]
        + [dma((10,))] * 4
        + [dma((15,))] * 2
        + [dma((18,))] * 2
        + [dma((5,))] * 2
        + [dma((7,))] * 2
        + [dma],
        compiler_params=pltpu.CompilerParams(
            collective_id=2, has_side_effects=True, vmem_limit_bytes=60 * 2**20
        ),
    )(*operands)


def slot_kernel(
    kind, unit, column, summed, table_grad, sums, w, m1, m2, tw, t1, t2,
    w_out, m1_out, m2_out, tw_out, t1_out, t2_out, loss, norm,
):
    per_unit = UNIT // LANES

    def once():
        g = table_grad[:, 0 : tw.shape[1]]
        tw_out[...], t1_out[...], t2_out[...] = adamw(tw[...], g, t1[...], t2[...])
        row = sums[10:11, :]
        lane = lax.broadcasted_iota(jnp.int32, row.shape, 1)
        square, cross, length, count = [jnp.sum(jnp.where(lane == i, row, 0.0)) for i in range(4)]
        loss[0] = (0.5 * square + cross) * count
        loss[1] = count
        norm[0] = 0.5 * length

    pl.when(pl.program_id(0) == 0)(once)
    for b in range(per_unit):
        j = pl.program_id(0) * per_unit + b
        first = jnp.where(kind[j] == 2, per_unit, column[j])
        at = pl.ds(pl.multiple_of(first * LANES, LANES), LANES)
        lanes = slice(b * LANES, b * LANES + LANES)
        for half in range(2):
            rows = slice(half * HALF, half * HALF + HALF)
            g = get(summed.at[2 * unit[j] + half, :, at], HALF)
            g = jnp.where(kind[j] > 0, g, jnp.zeros_like(g))
            w_out[rows, lanes], m1_out[rows, lanes], m2_out[rows, lanes] = adamw(
                w[rows, lanes], g, m1[rows, lanes], m2[rows, lanes]
            )


def slot_update(kind, unit, column, summed, table_grad, sums, slots, first, second, *table):
    rows = slots.shape[0]
    plain_spec = pl.BlockSpec((rows, UNIT), lambda j, k, u, c: (0, j))

    def whole(value):
        return pl.BlockSpec(value.shape, lambda j, k, u, c: (0,) * len(value.shape))

    return pl.pallas_call(
        slot_kernel,
        grid_spec=pltpu.PrefetchScalarGridSpec(
            num_scalar_prefetch=3,
            grid=(CAP // UNIT,),
            in_specs=[whole(summed), whole(table_grad), whole(sums)]
            + [plain_spec] * 3
            + [whole(value) for value in table],
            out_specs=[plain_spec] * 3 + [whole(value) for value in table] + [SMEM] * 2,
        ),
        out_shape=[jax.ShapeDtypeStruct(slots.shape, f32)] * 3
        + [jax.ShapeDtypeStruct(table[0].shape, f32)] * 3
        + [jax.ShapeDtypeStruct((2,), f32), jax.ShapeDtypeStruct((1,), f32)],
        cost_estimate=pl.CostEstimate(flops=0, bytes_accessed=28 * rows * CAP, transcendentals=0),
        compiler_params=pltpu.CompilerParams(vmem_limit_bytes=60 * 2**20),
    )(kind, unit, column, summed, table_grad, sums, slots, first, second, *table)


def per_device(
    token_ids,
    timesteps,
    pad_mask,
    noise_draw,
    owners,
    emb_table,
    table_first_moment,
    table_second_moment,
    mat_slots,
    slot_first,
    slot_second,
    vec_params,
    vec_first,
    vec_second,
):
    v = lax.axis_index("vocab")
    seq_len = token_ids.shape[1]
    tokens = seq_len // 4
    vocab_rows, emb_cols = emb_table.shape
    table_own = emb_table.T
    (
        payload, table_home, row_of, safe_row, keep_rows, keep_column, valid_column, count_tile,
        kind, unit, column,
    ) = prepare(owners, token_ids, pad_mask, table_own, mat_slots)
    w_up, w_down, w_small, w_attn, w_out, table_low, row_weight, twice, places, levels = spread(
        owners, timesteps, payload, count_tile, keep_rows, keep_column, table_home
    )
    table_low = table_low.reshape(EMBED_WIDTH, vocab_rows)
    table_t = table_low.T
    looked = table_t.at[safe_row[0]].get(mode="promise_in_bounds").reshape(4, tokens, EMBED_WIDTH)
    vecs = vec_params.reshape(10, D)
    (
        found_rows, clean_emb, inputs, hidden, normed_all, q_h, k_h, k_t, v_h, log_total, mixed_own, middle,
        normed_two, up_proj, active, hidden_two, final_norm, predicted, pred_all,
    ) = forward(
        looked, valid_column, levels, places, vecs, keep_column,
        noise_draw[0], w_small, w_attn, w_out, w_up, w_down,
    )
    grad_pred, head_stats = head(
        pred_all,
        table_low,
        table_t,
        row_weight,
        found_rows,
    )
    (
        grad_pred_low, down_left, up_left, out_left, small_left, final_left, qkv_left, grad_up, grad_clean, sums,
    ) = backward(
        grad_pred, clean_emb, predicted, twice, levels, head_stats,
        hidden, middle, hidden_two, normed_two, final_norm, up_proj,
        q_h, k_h, k_t, v_h, log_total, keep_column,
        w_small, w_attn, w_out, w_up, w_down, vecs,
    )

    def left(value):
        return value.reshape(4, QUARTER, tokens)

    summed, table_grad, tile_sum = reduce_grads(
        owners,
        left(down_left),
        left(up_left),
        left(out_left),
        left(small_left),
        left(final_left),
        qkv_left,
        active,
        grad_up,
        mixed_own,
        inputs,
        grad_pred_low,
        normed_all,
        pred_all,
        grad_clean,
        table_t,
        head_stats,
        row_weight,
        row_of,
        sums,
    )
    (
        new_slots, slot_first_new, slot_second_new, new_table, table_first_new, table_second_new, loss_pair, emb_norm,
    ) = slot_update(
        kind, unit, column, summed, table_grad, tile_sum, mat_slots, slot_first, slot_second,
        table_own, table_first_moment.T, table_second_moment.T,
    )
    tile_sum = tile_sum.reshape(16 * UNIT)
    vec_share = vec_first.shape[0]
    own_grad = lax.dynamic_slice_in_dim(tile_sum, v * vec_share, vec_share)
    own_vecs = lax.dynamic_slice_in_dim(vec_params, v * vec_share, vec_share)
    new_vecs, vec_first_new, vec_second_new = adamw(own_vecs, own_grad, vec_first, vec_second)
    return (
        loss_pair,
        emb_norm[0],
        new_table.T,
        table_first_new.T,
        table_second_new.T,
        new_slots,
        slot_first_new,
        slot_second_new,
        new_vecs,
        vec_first_new,
        vec_second_new,
    )


def broadcast(value, axis, source):
    kept = jnp.where(lax.axis_index(axis) == source, value, 0).astype(value.dtype)
    return lax.psum(kept, axis)


def merged(value, axis, join):
    pieces = jax.tree.map(lambda part: lax.all_gather(part, axis), value)
    head = jax.tree.map(lambda part: part[0], pieces)
    tail = jax.tree.map(lambda part: part[1:], pieces)
    so_far, _ = lax.scan(lambda so_far, share: (join(so_far, share), None), head, tail)
    return so_far


def matrix_rows():
    return [D, D, D, D, FF, FF] * LAYERS + [EMBED_WIDTH, EMBED_WIDTH, EMBED_WIDTH]


def slot_places(owners):
    counts = jnp.array(matrix_rows(), jnp.int32)
    mat_total = counts.shape[0]
    same_owner = (owners[:, None] == owners[None, :]).astype(jnp.int32)
    earlier_mask = jnp.tril(jnp.ones((mat_total, mat_total), jnp.int32), -1)
    return owners * CAP + jnp.sum(same_owner * earlier_mask * counts[None, :], 1)


def block_scores(query_blk, keys_all, keep_keys, score_scale):
    scores = (
        jnp.einsum("qhd,khd->hqk", query_blk, keys_all, preferred_element_type=jnp.float32)
        * score_scale
    )
    return jnp.where(keep_keys[None, None, :], scores, -1000000000.0)


def attention(queries, keys_all, values_all, keep_keys, score_scale):
    tokens = queries.shape[0]
    width = min(512, tokens)
    query_blocks = queries.reshape(tokens // width, width, HEADS, HDIM)

    def one_block(query_blk):
        scores = block_scores(query_blk, keys_all, keep_keys, score_scale)
        row_max = jnp.max(scores, -1, keepdims=True)
        expo = jnp.exp(scores - row_max)
        exp_total = jnp.sum(expo, -1, keepdims=True)
        probabilities = (expo / exp_total).astype(jnp.bfloat16)
        mixed_out = jnp.einsum(
            "hqk,khd->qhd", probabilities, values_all, preferred_element_type=jnp.float32
        )
        return (mixed_out, (row_max + jnp.log(exp_total))[..., 0])

    mixed_out, log_total = lax.map(one_block, query_blocks)
    return (mixed_out.reshape(tokens, HEADS, HDIM), log_total)


def attention_back(queries, keys_all, values_all, keep_keys, log_total, grad_mixed, score_scale):
    tokens = queries.shape[0]
    width = min(512, tokens)
    query_blocks = queries.reshape(tokens // width, width, HEADS, HDIM)
    grad_blocks = grad_mixed.reshape(tokens // width, width, HEADS, HDIM)

    def one_block(carry_sums, block_data):
        query_blk, total_blk, grad_blk = block_data
        scores = block_scores(query_blk, keys_all, keep_keys, score_scale)
        probabilities = jnp.exp(scores - total_blk[..., None])
        grad_probs = jnp.einsum(
            "qhd,khd->hqk", grad_blk, values_all, preferred_element_type=jnp.float32
        )
        inner_sum = jnp.sum(probabilities * grad_probs, -1, keepdims=True)
        grad_scores = (probabilities * (grad_probs - inner_sum)).astype(jnp.bfloat16)
        grad_query = (
            jnp.einsum("hqk,khd->qhd", grad_scores, keys_all, preferred_element_type=jnp.float32)
            * score_scale
        )
        grad_key = (
            jnp.einsum("hqk,qhd->khd", grad_scores, query_blk, preferred_element_type=jnp.float32)
            * score_scale
        )
        grad_value = jnp.einsum(
            "hqk,qhd->khd",
            probabilities.astype(jnp.bfloat16),
            grad_blk,
            preferred_element_type=jnp.float32,
        )
        return ((carry_sums[0] + grad_key, carry_sums[1] + grad_value), grad_query)

    zero_keys = jnp.zeros(keys_all.shape, jnp.float32)
    grad_kv, grad_queries = lax.scan(
        one_block, (zero_keys, zero_keys), (query_blocks, log_total, grad_blocks)
    )
    return (grad_queries.reshape(tokens, D), grad_kv[0].reshape(-1, D), grad_kv[1].reshape(-1, D))


def send_matrix(piece_cols, root):
    return broadcast(piece_cols, "dp", root)


def fetch_keys(key_rows, value_rows):
    return (
        lax.all_gather(key_rows, "vocab", axis=0, tiled=True),
        lax.all_gather(value_rows, "vocab", axis=0, tiled=True),
    )


def layer_forward(hidden, weights, vec_layer, keep_keys, score_scale):
    w_query, w_key, w_value, w_out, w_up, w_down = weights
    tokens = hidden.shape[0]
    norm_one, inv_one = norm_parts(hidden)
    normed = (norm_one * vec_layer[0:D] + vec_layer[D : 2 * D]).astype(jnp.bfloat16)
    queries = matmul_nn(normed, w_query).astype(jnp.bfloat16)
    key_rows = matmul_nn(normed, w_key).astype(jnp.bfloat16)
    value_rows = matmul_nn(normed, w_value).astype(jnp.bfloat16)
    keys_all, values_all = fetch_keys(key_rows, value_rows)
    keys_all = keys_all.reshape(-1, HEADS, HDIM)
    values_all = values_all.reshape(-1, HEADS, HDIM)
    mixed_out, log_total = attention(
        queries.reshape(tokens, HEADS, HDIM), keys_all, values_all, keep_keys, score_scale
    )
    mixed_low = mixed_out.reshape(tokens, D).astype(jnp.bfloat16)
    middle = hidden + matmul_nn(mixed_low, w_out)
    norm_two, inv_two = norm_parts(middle)
    normed_two = (norm_two * vec_layer[2 * D : 3 * D] + vec_layer[3 * D : 4 * D]).astype(
        jnp.bfloat16
    )
    up_proj = matmul_nt(normed_two, w_up) + vec_layer[4 * D :]
    active = jax.nn.gelu(up_proj).astype(jnp.bfloat16)
    out_rows = middle + matmul_nn(active, w_down)
    kept_vals = (
        norm_one,
        inv_one,
        normed,
        queries,
        key_rows,
        value_rows,
        keys_all,
        values_all,
        log_total,
        mixed_low,
        norm_two,
        inv_two,
        normed_two,
        up_proj,
        active,
    )
    return (out_rows, kept_vals)


def layer_backward(grad_out, kept_vals, weights, vec_layer, keep_keys, score_scale):
    w_query, w_key, w_value, w_out, w_up, w_down = weights
    (
        norm_one,
        inv_one,
        normed,
        queries,
        key_rows,
        value_rows,
        keys_all,
        values_all,
        log_total,
        mixed_low,
        norm_two,
        inv_two,
        normed_two,
        up_proj,
        active,
    ) = kept_vals
    tokens = grad_out.shape[0]
    grad_low = grad_out.astype(jnp.bfloat16)
    grad_down = matmul_tn(active, grad_low)
    grad_active = matmul_nt(grad_low, w_down)
    grad_up_proj = jax.vjp(jax.nn.gelu, up_proj)[1](grad_active)[0].astype(jnp.bfloat16)
    grad_bias = jnp.sum(grad_up_proj.astype(jnp.float32), 0)
    grad_up = matmul_tn(grad_up_proj, normed_two)
    grad_normed_two = matmul_nn(grad_up_proj, w_up)
    grad_part, grad_gain_two, grad_shift_two = norm_back(
        norm_two, inv_two, vec_layer[2 * D : 3 * D], grad_normed_two
    )
    grad_middle = grad_out + grad_part
    grad_attn = grad_middle.astype(jnp.bfloat16)
    grad_out_w = matmul_tn(mixed_low, grad_attn)
    grad_mixed = matmul_nt(grad_attn, w_out).astype(jnp.bfloat16).reshape(tokens, HEADS, HDIM)
    grad_queries, grad_keys_all, grad_values_all = attention_back(
        queries.reshape(tokens, HEADS, HDIM),
        keys_all,
        values_all,
        keep_keys,
        log_total,
        grad_mixed,
        score_scale,
    )
    grad_key_rows, grad_value_rows = (
        lax.psum_scatter(
            grad_keys_all.astype(jnp.bfloat16), "vocab", scatter_dimension=0, tiled=True
        ).astype(jnp.float32),
        lax.psum_scatter(
            grad_values_all.astype(jnp.bfloat16), "vocab", scatter_dimension=0, tiled=True
        ).astype(jnp.float32),
    )
    grad_q_low = grad_queries.astype(jnp.bfloat16)
    grad_k_low = grad_key_rows.astype(jnp.bfloat16)
    grad_v_low = grad_value_rows.astype(jnp.bfloat16)
    grad_wq = matmul_tn(normed, grad_q_low)
    grad_wk = matmul_tn(normed, grad_k_low)
    grad_wv = matmul_tn(normed, grad_v_low)
    grad_normed = (
        matmul_nt(grad_q_low, w_query)
        + matmul_nt(grad_k_low, w_key)
        + matmul_nt(grad_v_low, w_value)
    )
    grad_part_one, grad_gain_one, grad_shift_one = norm_back(
        norm_one, inv_one, vec_layer[0:D], grad_normed
    )
    grad_hidden = grad_middle + grad_part_one
    grad_mats = [grad_wq, grad_wk, grad_wv, grad_out_w, grad_up, grad_down]
    grad_vec = jnp.concatenate(
        [grad_gain_one, grad_shift_one, grad_gain_two, grad_shift_two, grad_bias]
    )
    return (grad_hidden, grad_mats, grad_vec)


def merge_stats(first_part, second_part):
    peak_val = jnp.maximum(first_part[0], second_part[0])
    exp_total = first_part[1] * jnp.exp(first_part[0] - peak_val) + second_part[1] * jnp.exp(
        second_part[0] - peak_val
    )
    return (peak_val, exp_total, first_part[2] + second_part[2])


def any_mesh_device(
    token_ids,
    timesteps,
    pad_mask,
    noise_draw,
    owners,
    emb_table,
    table_first_moment,
    table_second_moment,
    mat_slots,
    slot_first,
    slot_second,
    vec_params,
    vec_first,
    vec_second,
):
    vocab_count = lax.axis_size("vocab")
    vocab_pos = lax.axis_index("vocab")
    data_pos = lax.axis_index("dp")
    seq_len = token_ids.shape[1]
    tokens = seq_len // vocab_count
    vocab_rows = emb_table.shape[0]
    score_scale = HDIM ** (-0.5)
    table_low = lax.all_gather(emb_table.astype(jnp.bfloat16), "dp", axis=1, tiled=True)
    row_counts = matrix_rows()
    local_start = slot_places(owners) - owners * CAP
    sent_pieces = [
        send_matrix(
            lax.dynamic_slice_in_dim(
                mat_slots, local_start[mat_idx], row_counts[mat_idx], 1
            ).astype(jnp.bfloat16),
            owners[mat_idx],
        )
        for mat_idx in range(len(row_counts))
    ]
    canon = jnp.concatenate(sent_pieces, 1)
    weights = lax.all_gather(canon, "vocab", axis=0, tiled=True).T
    layer_rows = 4 * D + 2 * FF
    vec_rows = 4 * D + FF
    tail_at = LAYERS * layer_rows

    def layer_weights(layer_idx):
        begin_row = layer_idx * layer_rows
        cuts = [
            begin_row,
            begin_row + D,
            begin_row + 2 * D,
            begin_row + 3 * D,
            begin_row + 4 * D,
            begin_row + 4 * D + FF,
            begin_row + layer_rows,
        ]
        return [weights[cuts[cut_idx] : cuts[cut_idx + 1]] for cut_idx in range(6)]

    w_input = weights[tail_at : tail_at + 2 * EMBED_WIDTH]
    w_final = weights[tail_at + 2 * EMBED_WIDTH : tail_at + 3 * EMBED_WIDTH]
    seq_ids = token_ids[0]
    seq_mask = pad_mask[0].astype(jnp.float32)
    keep_keys = pad_mask[0] > 0
    local_row = seq_ids - vocab_pos * vocab_rows
    valid_row = (local_row >= 0) & (local_row < vocab_rows)
    safe_row = jnp.clip(local_row, 0, vocab_rows - 1)
    found_rows = jnp.where(
        valid_row[:, None], jnp.take(table_low, safe_row, axis=0), jnp.zeros((), jnp.bfloat16)
    )
    arrived = lax.all_to_all(found_rows, "vocab", split_axis=0, concat_axis=0, tiled=True)
    clean_emb = jnp.sum(arrived.reshape(vocab_count, tokens, EMBED_WIDTH).astype(jnp.float32), 0)
    own_first = vocab_pos * tokens
    mask_own = lax.dynamic_slice_in_dim(seq_mask, own_first, tokens)
    own_places = (own_first + jnp.arange(tokens)).astype(jnp.float32)
    step_val = timesteps[0].astype(jnp.float32)
    signal_level = 1.0 - jnp.sqrt(step_val / DIFF + 0.0001)
    noisy_emb = jnp.sqrt(signal_level) * clean_emb + jnp.sqrt(1.0 - signal_level) * noise_draw[
        0
    ].astype(jnp.float32)
    time_feat = jnp.broadcast_to(waves(step_val[None], EMBED_WIDTH), (tokens, EMBED_WIDTH))
    inputs = jnp.concatenate([noisy_emb, time_feat], 1).astype(jnp.bfloat16)
    hidden = matmul_nn(inputs, w_input) + waves(own_places, D)
    layer_idx = 0
    vec_layer = vec_params[layer_idx * vec_rows : (layer_idx + 1) * vec_rows]
    hidden, kept_vals = layer_forward(
        hidden, layer_weights(layer_idx), vec_layer, keep_keys, score_scale
    )
    kept_list = [kept_vals]
    gain_final = vec_params[LAYERS * vec_rows : LAYERS * vec_rows + D]
    shift_final = vec_params[LAYERS * vec_rows + D :]
    norm_final, inv_final = norm_parts(hidden)
    final_norm = (norm_final * gain_final + shift_final).astype(jnp.bfloat16)
    predicted = matmul_nt(final_norm, w_final)
    pred_all = lax.all_gather(predicted.astype(jnp.bfloat16), "vocab", axis=0, tiled=True)
    head_width = min(512, seq_len)
    head_count = seq_len // head_width
    columns = jnp.arange(vocab_rows)
    pred_blocks = pred_all.reshape(head_count, head_width, EMBED_WIDTH)
    row_blocks = local_row.reshape(head_count, head_width)

    def head_stats(block_data):
        pred_blk, rows_blk = block_data
        logits = matmul_nt(pred_blk, table_low)
        row_max = jnp.max(logits, -1)
        exp_total = jnp.sum(jnp.exp(logits - row_max[:, None]), -1)
        target = jnp.sum(jnp.where(columns[None, :] == rows_blk[:, None], logits, 0.0), -1)
        return (row_max, exp_total, target)

    peaks, totals, targets = lax.map(head_stats, (pred_blocks, row_blocks))
    peak_all, total_all, target_all = merged(
        (peaks.reshape(seq_len), totals.reshape(seq_len), targets.reshape(seq_len)),
        "vocab",
        merge_stats,
    )
    log_total = peak_all + jnp.log(total_all)
    lse_own = lax.dynamic_slice_in_dim(log_total, own_first, tokens)
    target_own = lax.dynamic_slice_in_dim(target_all, own_first, tokens)
    pred_error = predicted - clean_emb
    square_own = jnp.sum(mask_own[:, None] * pred_error * pred_error)
    cross_own = jnp.sum(mask_own * (lse_own - target_own))
    norm_own = jnp.sum(mask_own * jnp.sqrt(jnp.sum(clean_emb * clean_emb, -1) + 1e-06))
    count_all, square, cross_sum, norm_total = lax.psum(
        (jnp.sum(mask_own), square_own, cross_own, norm_own), ("dp", "vocab")
    )
    weight_blocks = (seq_mask / count_all).reshape(head_count, head_width)
    lse_blocks = log_total.reshape(head_count, head_width)

    def head_back(grad_table, block_data):
        pred_blk, rows_blk, lse_blk, weight_blk = block_data
        logits = matmul_nt(pred_blk, table_low)
        probabilities = jnp.exp(logits - lse_blk[:, None])
        onehot = (columns[None, :] == rows_blk[:, None]).astype(jnp.float32)
        grad_logits = ((probabilities - onehot) * weight_blk[:, None]).astype(jnp.bfloat16)
        return (grad_table + matmul_tn(grad_logits, pred_blk), matmul_nn(grad_logits, table_low))

    zero_table = jnp.zeros((vocab_rows, EMBED_WIDTH), jnp.float32)
    grad_table_head, grad_pred_blocks = lax.scan(
        head_back, zero_table, (pred_blocks, row_blocks, lse_blocks, weight_blocks)
    )
    grad_pred = lax.psum_scatter(
        grad_pred_blocks.reshape(seq_len, EMBED_WIDTH).astype(jnp.bfloat16),
        "vocab",
        scatter_dimension=0,
        tiled=True,
    ).astype(jnp.float32)
    error_grad = 2.0 * mask_own[:, None] * pred_error / count_all
    grad_pred_low = (grad_pred + error_grad).astype(jnp.bfloat16)
    grad_final_w = matmul_tn(grad_pred_low, final_norm)
    grad_final = matmul_nn(grad_pred_low, w_final)
    grad_hidden, grad_gain_final, grad_shift_final = norm_back(
        norm_final, inv_final, gain_final, grad_final
    )
    layer_grads = [None] * LAYERS
    vec_grads = [None] * LAYERS
    for layer_idx in reversed(range(LAYERS)):
        vec_layer = vec_params[layer_idx * vec_rows : (layer_idx + 1) * vec_rows]
        grad_hidden, layer_grads[layer_idx], vec_grads[layer_idx] = layer_backward(
            grad_hidden,
            kept_list[layer_idx],
            layer_weights(layer_idx),
            vec_layer,
            keep_keys,
            score_scale,
        )
    grad_hidden_low = grad_hidden.astype(jnp.bfloat16)
    grad_input_w = matmul_tn(inputs, grad_hidden_low)
    grad_inputs = matmul_nt(grad_hidden_low, w_input)
    grad_clean = jnp.sqrt(signal_level) * grad_inputs[:, :EMBED_WIDTH] - error_grad
    grad_clean_all = lax.all_gather(
        grad_clean.astype(jnp.bfloat16), "vocab", axis=0, tiled=True
    ).astype(grad_clean.dtype)
    grad_table_look = zero_table.at[safe_row].add(
        jnp.where(valid_row[:, None], grad_clean_all, 0.0)
    )
    grad_table_local = grad_table_head + grad_table_look
    canon_list = []
    layer_idx = 0
    canon_list = canon_list + layer_grads[layer_idx]
    canon_grad = jnp.concatenate(canon_list + [grad_input_w, grad_final_w], 0).T
    vec_grad = jnp.concatenate(vec_grads + [grad_gain_final, grad_shift_final])
    grad_cols, vec_part = (
        lax.psum_scatter(canon_grad, "vocab", scatter_dimension=0, tiled=True),
        lax.psum_scatter(vec_grad, "vocab", scatter_dimension=0, tiled=True),
    )
    emb_cols = emb_table.shape[1]
    summed_cols, summed_vec, summed_table = lax.psum((grad_cols, vec_part, grad_table_local), "dp")
    table_grad = lax.dynamic_slice_in_dim(summed_table, data_pos * emb_cols, emb_cols, 1)
    slot_grad = jnp.zeros_like(mat_slots)
    cursor = 0
    for mat_idx in range(len(row_counts)):
        piece_cols = summed_cols[:, cursor : cursor + row_counts[mat_idx]]
        updated = lax.dynamic_update_slice_in_dim(slot_grad, piece_cols, local_start[mat_idx], 1)
        slot_grad = jnp.where(owners[mat_idx] == data_pos, updated, slot_grad)
        cursor = cursor + row_counts[mat_idx]
    vec_share = vec_first.shape[0]
    own_vecs = lax.dynamic_slice_in_dim(vec_params, vocab_pos * vec_share, vec_share)
    new_slots, slot_first_new, slot_second_new = adamw(
        mat_slots, slot_grad, slot_first, slot_second
    )
    new_table, table_first_new, table_second_new = adamw(
        emb_table, table_grad, table_first_moment, table_second_moment
    )
    new_vecs, vec_first_new, vec_second_new = adamw(own_vecs, summed_vec, vec_first, vec_second)
    loss_pair = jnp.stack([square + cross_sum, count_all])
    emb_norm = norm_total / count_all
    return (
        loss_pair,
        emb_norm,
        new_table,
        table_first_new,
        table_second_new,
        new_slots,
        slot_first_new,
        slot_second_new,
        new_vecs,
        vec_first_new,
        vec_second_new,
    )


def solution(mesh):
    in_specs = (
        P("dp", None),
        P("dp"),
        P("dp", None),
        P("dp", "vocab", None),
        P(),
        P("vocab", "dp"),
        P("vocab", "dp"),
        P("vocab", "dp"),
        P("vocab", "dp"),
        P("vocab", "dp"),
        P("vocab", "dp"),
        P(),
        P("vocab"),
        P("vocab"),
    )
    out_specs = (
        P(),
        P(),
        P("vocab", "dp"),
        P("vocab", "dp"),
        P("vocab", "dp"),
        P("vocab", "dp"),
        P("vocab", "dp"),
        P("vocab", "dp"),
        P("vocab"),
        P("vocab"),
        P("vocab"),
    )
    fast = mesh.shape["dp"] == 8 and mesh.shape["vocab"] == 4
    body = per_device if fast else any_mesh_device
    return jax.shard_map(
        body, mesh=mesh, in_specs=in_specs, out_specs=out_specs, check_vma=False
    )
```

```python
import functools
import math

import jax
import jax.numpy as jnp
from jax import lax
from jax.experimental import pallas as pl
from jax.experimental.pallas import tpu as pltpu
from jax.sharding import PartitionSpec as P

D = 768
HEADS = 12
HDIM = 64
FF = 3072
EMBED_WIDTH = 128
DIFF = 2000
STEP = 10
CAP = 3072
LAYERS = 1
LANES = 128


beta_one = 0.9
beta_two = 0.999
learn_rate = 0.02
weight_decay = 0.01
eps_adam = 1e-08
eps_norm = 1e-05
f32 = jnp.float32
bf16 = jnp.bfloat16


def matmul_nn(left, right):
    return jnp.dot(left, right, preferred_element_type=f32)


def matmul_tn(left, right):
    return lax.dot_general(left, right, (((0,), (0,)), ((), ())), preferred_element_type=f32)


def matmul_nt(left, right):
    return lax.dot_general(left, right, (((1,), (1,)), ((), ())), preferred_element_type=f32)


ROW_COUNTS = [D, D, D, D, FF, FF, EMBED_WIDTH, EMBED_WIDTH, EMBED_WIDTH]


def slot_starts(owners):
    counts = jnp.array(ROW_COUNTS, jnp.int32)
    same_owner = (owners[:, None] == owners[None, :]).astype(jnp.int32)
    earlier_mask = jnp.tril(jnp.ones((len(ROW_COUNTS),) * 2, jnp.int32), -1)
    return jnp.sum(same_owner * earlier_mask * counts[None, :], 1)


def waves(places, width):
    half_width = width // 2
    frequency = jnp.exp(-math.log(10000.0) * jnp.arange(half_width, dtype=f32) / half_width)
    angles = places[:, None] * frequency[None, :]
    return jnp.concatenate([jnp.sin(angles), jnp.cos(angles)], 1)


def norm_parts(value_entries):
    center = value_entries - jnp.mean(value_entries, -1, keepdims=True)
    scale_inv = lax.rsqrt(jnp.mean(center * center, -1, keepdims=True) + eps_norm)
    return (center * scale_inv, scale_inv)


def norm_back(normal_part, scale_inv, gain_vec, grad_out):
    scaled = grad_out * gain_vec
    inner = (
        scaled
        - jnp.mean(scaled, -1, keepdims=True)
        - normal_part * jnp.mean(scaled * normal_part, -1, keepdims=True)
    )
    return (inner * scale_inv, jnp.sum(grad_out * normal_part, 0), jnp.sum(grad_out, 0))


def adamw(weight, gradient, moment_one, moment_two):
    moment_one = beta_one * moment_one + (1.0 - beta_one) * gradient
    moment_two = beta_two * moment_two + (1.0 - beta_two) * gradient * gradient
    fix_one = 1.0 - beta_one**STEP
    fix_two = 1.0 - beta_two**STEP
    update_dir = moment_one / fix_one / (jnp.sqrt(moment_two / fix_two) + eps_adam)
    return (weight - learn_rate * (update_dir + weight_decay * weight), moment_one, moment_two)


MESH = pl.DeviceIdType.MESH
ANY = pl.BlockSpec(memory_space=pl.ANY)
UNIT = 768
HALF = 96
QUARTER = 192


def place():
    d, v = lax.axis_index("dp"), lax.axis_index("vocab")
    return d // 2, d % 2, d, v


def greet(partners):
    barrier = pltpu.get_barrier_semaphore()
    for partner in partners:
        pl.semaphore_signal(barrier, inc=1, device_id=partner, device_id_type=MESH)
    pl.semaphore_wait(barrier, len(partners))


def remote(src, dst, sems, index, partner):
    return pltpu.make_async_remote_copy(
        src_ref=src,
        dst_ref=dst,
        send_sem=sems[0].at[index],
        recv_sem=sems[1].at[index],
        device_id=partner,
        device_id_type=MESH,
    )


def start_all(copies):
    for copy in copies:
        copy.start()
    return copies


def arrive_all(copies):
    for copy in copies:
        copy.wait_recv()


VMEM = pl.BlockSpec(memory_space=pltpu.VMEM)
SMEM = pl.BlockSpec(memory_space=pltpu.SMEM)


def prepare_kernel(
    owners, ids_from, mask_from, table_from, slots,
    payload, table_low, row_of, safe, keep_rows, keep, valid, count, kind, unit, column,
    units, extras, ids, mask, table, sems, own_sems,
):
    d, v = lax.axis_index("dp"), lax.axis_index("vocab")
    starts = [
        sum(jnp.where(owners[j] == owners[i], ROW_COUNTS[j], 0) for j in range(i)) + 0 * owners[i]
        for i in range(len(ROW_COUNTS))
    ]
    whole = (owners[4] == d) | (owners[5] == d)
    fetched = [
        pltpu.make_async_copy(src, dst, own_sems.at[i])
        for i, (src, dst) in enumerate(((ids_from, ids), (mask_from, mask), (table_from, table)))
    ]
    for copy in fetched:
        copy.start()
    copies = []
    for u in range(4):
        first = pl.multiple_of(jnp.where(whole, u * UNIT, starts[u]), LANES)
        copies.append(
            pltpu.make_async_copy(slots.at[:, pl.ds(first, UNIT)], units.at[u], sems.at[u])
        )
        first = pl.multiple_of(starts[6 + min(u, 2)], LANES)
        copies.append(
            pltpu.make_async_copy(slots.at[:, pl.ds(first, LANES)], extras.at[u], sems.at[4 + u])
        )
    for copy in copies:
        copy.start()

    def clear(j, carry):
        kind[j] = 0
        unit[j] = 0
        column[j] = 0
        return carry

    lax.fori_loop(0, CAP // LANES, clear, 0)
    per_unit = UNIT // LANES
    first_unit = [0, 1, 2, 3, 0, 0, 0, 1, 2]
    for i, rows in enumerate(ROW_COUNTS):

        def claim(i=i, rows=rows):
            def one(b, carry):
                j = starts[i] // LANES + b
                kind[j] = 2 if i > 5 else 1
                unit[j] = first_unit[i] + b // per_unit
                column[j] = b % per_unit
                return carry

            lax.fori_loop(0, rows // LANES, one, 0)

        pl.when(owners[i] == d)(claim)

    for copy in fetched:
        copy.wait()
    table_low[...] = table[...].astype(bf16)
    count[...] = jnp.full((8, LANES), jnp.sum(mask[...].astype(f32)))
    for b in range(4):
        at = pl.ds(pl.multiple_of((v ^ b) * 256, 256), 256)
        local = ids[:, at] - v * table.shape[1]
        row_of[b : b + 1, :] = local
        safe[:, 256 * b : 256 * b + 256] = jnp.clip(local, 0, table.shape[1] - 1)
        weight = mask[:, at].astype(f32)
        keep_rows[b : b + 1, :] = weight
        inside = ((local >= 0) & (local < table.shape[1])).astype(f32)
        both = jnp.concatenate([weight, inside, jnp.zeros((6, 256), f32)], 0).T
        keep[256 * b : 256 * b + 256, :] = both[:, 0:1]
        valid[256 * b : 256 * b + 256, :] = both[:, 1:2]
    for copy in copies:
        copy.wait()
    for u in range(4):
        for half in range(2):
            rows = slice(half * HALF, half * HALF + HALF)
            payload[2 * u + half, :, 0:UNIT] = units[u, rows, :].astype(bf16)
            payload[2 * u + half, :, UNIT:] = extras[u, rows, :].astype(bf16)


def prepare(owners, ids, mask, table, slots):
    def shape(kind, *dims):
        return jax.ShapeDtypeStruct(dims, kind)

    blocks = CAP // LANES
    tokens = ids.shape[1]
    return pl.pallas_call(
        prepare_kernel,
        out_shape=[
            shape(bf16, 8, HALF, UNIT + LANES),
            shape(bf16, *table.shape),
            shape(jnp.int32, 4, tokens // 4),
            shape(jnp.int32, 1, tokens),
            shape(f32, 4, tokens // 4),
            shape(f32, tokens, 1),
            shape(f32, tokens, 1),
            shape(f32, 8, LANES),
        ]
        + [shape(jnp.int32, blocks)] * 3,
        in_specs=[SMEM, ANY, ANY, ANY, ANY],
        out_specs=[VMEM] * 8 + [SMEM] * 3,
        scratch_shapes=[
            pltpu.VMEM((4, QUARTER, UNIT), f32),
            pltpu.VMEM((4, QUARTER, LANES), f32),
            pltpu.VMEM(ids.shape, jnp.int32),
            pltpu.VMEM(mask.shape, jnp.int32),
            pltpu.VMEM(table.shape, f32),
            pltpu.SemaphoreType.DMA((8,)),
            pltpu.SemaphoreType.DMA((3,)),
        ],
        compiler_params=pltpu.CompilerParams(vmem_limit_bytes=60 * 2**20),
    )(owners, ids, mask, table, slots)


TRADE_MASKS = (4, 6, 5, 7, 2, 3, 1)


def chosen_of(pieces, wanted):
    value = pieces[0]
    for i in range(1, len(pieces)):
        value = jnp.where(wanted == i, pieces[i], value)
    return value


def spread_kernel(
    owners, steps, payload, tile, keep_rows, keep, table_home,
    up_to, down_to, small_to, attn_to, out_to, table_to, weight, twice, places, levels,
    up, down, small, attn, out, table, arrived, tiles, up_home, down_home, small_home, attn_home,
    a_send, a_recv, b_send, b_recv,
    z_send, z_recv, y_send, y_recv, x_send, x_recv, n_send, n_recv, f_send, f_recv, local, o_sem,
):
    z, y, d, v = place()
    far, near = v ^ 2, v ^ 1
    greet([(d ^ m, v) for m in TRADE_MASKS] + [(d, far), (d, near)])
    traded = start_all(
        [
            remote(payload.at[d ^ m], arrived.at[i], (a_send, a_recv), i, (d ^ m, v))
            for i, m in enumerate(TRADE_MASKS)
        ]
        + [
            remote(tile, tiles.at[i], (b_send, b_recv), i, (d ^ m, v))
            for i, m in enumerate(TRADE_MASKS)
        ]
    )
    homes = [up_home, down_home, small_home, attn_home, table_home]
    fulls = [up, down, small, attn, table]
    own_rows = pl.ds(v * QUARTER, QUARTER)

    def spot(c, unit):
        if c == 4:
            return table.at[2 * unit + y]
        first = y * HALF if c == 3 else v * QUARTER + y * HALF
        return fulls[c].at[unit, pl.ds(first, HALF), :]

    keeps, line, side, chip = {}, {}, {}, {}
    sent, landing, stores = [], {c: [] for c in range(4)}, []

    def note(copy, store=None, at=None):
        copy.start()
        sent.append(copy)
        if store is not None:
            store[at] = copy
        return copy

    def own_slab(c):
        keeps[c] = pltpu.make_async_copy(homes[c], spot(c, z), local.at[c])
        keeps[c].start()
        note(remote(homes[c], spot(c, z), (y_send, y_recv), (c, 0), (d ^ 1, v)), side, (c, 0))

    def start_class(c):
        for k in (2, 1, 3):
            note(
                remote(homes[c], spot(c, z), (z_send, z_recv), (c, k - 1), (d ^ (2 * k), v)),
                line,
                (c, k),
            )

    def relay(c, then=()):
        for k in (2, 1, 3):
            if k == 3:
                for other in then:
                    start_class(other)
            line[c, k].wait_recv()
            slab = spot(c, z ^ k)
            note(remote(slab, slab, (y_send, y_recv), (c, k), (d ^ 1, v)), side, (c, k))

    def chip_slab(c, k, source, target):
        note(remote(source, target, (x_send, x_recv), (c, k), (d, far)), chip, (c, k))
        landing[c].append(note(remote(source, target, (n_send, n_recv), (c, k), (d, near))))

    def to_chip(c, slabs=(2, 1, 3)):
        for k in slabs:
            side[c, k].wait_recv()
            if k == 0:
                keeps[c].wait()
            if c < 3:
                slab = fulls[c].at[z ^ k, own_rows, :]
                chip_slab(c, k, slab, slab)
        if c == 3 and slabs[-1] == 3:
            keep = pltpu.make_async_copy(attn.at[3], out.at[own_rows, :], local.at[5])
            keep.start()
            chip_slab(c, 0, attn.at[3], out.at[own_rows, :])
            keep.wait()

    def to_last(c):
        rows = pl.ds(far * QUARTER, QUARTER)
        for k in (0,) if c == 3 else (0, 2, 1, 3):
            chip[c, k].wait_recv()
            slab = out.at[rows, :] if c == 3 else fulls[c].at[z ^ k, rows, :]
            landing[c].append(note(remote(slab, slab, (f_send, f_recv), (c, k), (d, near))))

    def angles(position, width, count):
        lane = lax.broadcasted_iota(jnp.int32, (count, width), 1).astype(f32)
        return position * jnp.exp(-math.log(10000.0) * lane / width)

    position = v * 256 + lax.broadcasted_iota(jnp.int32, (256, D // 2), 0)
    angle = angles(position.astype(f32), D // 2, 256)
    places[:, 0 : D // 2] = jnp.sin(angle)
    places[:, D // 2 :] = jnp.cos(angle)
    step = jnp.full((8, EMBED_WIDTH), steps[0], jnp.int32).astype(f32)
    signal = 1.0 - jnp.sqrt(step / DIFF + 0.0001)
    angle = angles(step[:, 0 : EMBED_WIDTH // 2], EMBED_WIDTH // 2, 8)
    levels[0:1] = jnp.sqrt(signal[0:1])
    levels[1:2] = jnp.sqrt(1.0 - signal[0:1])
    levels[2:3] = jnp.concatenate([jnp.sin(angle), jnp.cos(angle)], 1)[0:1]
    levels[3:8] = jnp.zeros((5, EMBED_WIDTH), f32)
    arrive_all(traded)
    sent.extend(traded)
    total = tile[...]
    for i in range(7):
        total = total + tiles[i]
    weight[...] = keep_rows[...] / jnp.concatenate([total[0:4]] * 2, 1)
    twice[...] = 2.0 * keep[0:256, :] / total[0:1, 0:1]

    def from_owner(owner, lanes):
        value = payload[d, :, lanes]
        for i, m in enumerate(TRADE_MASKS):
            value = jnp.where(owner == d ^ m, arrived[i, :, lanes], value)
        return value

    up_home[...] = from_owner(owners[4], slice(0, UNIT))
    down_home[...] = from_owner(owners[5], slice(0, UNIT))
    attn_home[...] = from_owner(chosen_of([owners[u] for u in range(4)], z), slice(0, UNIT))
    small_home[...] = from_owner(
        chosen_of([owners[6 + min(u, 2)] for u in range(4)], z), slice(UNIT, UNIT + LANES)
    )

    def store(src, dst, index):
        copy = pltpu.make_async_copy(src, dst, o_sem.at[index])
        copy.start()
        stores.append(copy)

    def finish(c):
        arrive_all(landing[c])
        if c == 3:
            store(out, out_to, 3)
        else:
            store(fulls[c], (up_to, down_to, small_to)[c], c)

    start_class(0)
    for c in range(5):
        own_slab(c)
    for c in range(3):
        to_chip(c, (0,))
    relay(0, (1,))
    to_chip(0)
    relay(1, (2, 3))
    to_chip(1)
    relay(2)
    relay(3, (4,))
    to_chip(2)
    to_chip(3, (0, 2, 1, 3))
    store(attn, attn_to, 4)
    to_last(0)
    relay(4)
    finish(0)
    to_last(1)
    to_last(2)
    to_last(3)
    to_chip(4, (0, 2, 1, 3))
    store(table, table_to, 5)
    finish(1)
    finish(2)
    finish(3)
    for copy in stores:
        copy.wait()
    for copy in sent:
        copy.wait_send()


def spread(owners, steps, payload, tile, keep_rows, keep, table_home):
    rows, vocab_rows = table_home.shape
    dma, vmem = pltpu.SemaphoreType.DMA, pltpu.VMEM

    def shape(*dims):
        return jax.ShapeDtypeStruct(dims, bf16)

    return pl.pallas_call(
        spread_kernel,
        out_shape=[
            shape(4, D, UNIT),
            shape(4, D, UNIT),
            shape(4, D, LANES),
            shape(4, QUARTER, UNIT),
            shape(D, UNIT),
            shape(8, rows, vocab_rows),
            jax.ShapeDtypeStruct(keep_rows.shape, f32),
            jax.ShapeDtypeStruct((256, 1), f32),
            jax.ShapeDtypeStruct((256, D), f32),
            jax.ShapeDtypeStruct((8, EMBED_WIDTH), f32),
        ],
        in_specs=[SMEM] * 2 + [VMEM] * 5,
        out_specs=[ANY] * 6 + [VMEM] * 4,
        scratch_shapes=[
            vmem((4, D, UNIT), bf16),
            vmem((4, D, UNIT), bf16),
            vmem((4, D, LANES), bf16),
            vmem((4, QUARTER, UNIT), bf16),
            vmem((D, UNIT), bf16),
            vmem((8, rows, vocab_rows), bf16),
            vmem((7, HALF, UNIT + LANES), bf16),
            vmem((7, 8, LANES), f32),
            vmem((HALF, UNIT), bf16),
            vmem((HALF, UNIT), bf16),
            vmem((HALF, LANES), bf16),
            vmem((HALF, UNIT), bf16),
        ]
        + [dma((7,))] * 4
        + [dma((5, 3))] * 2
        + [dma((5, 4))] * 2
        + [dma((4, 4))] * 6
        + [dma((6,))] * 2,
        compiler_params=pltpu.CompilerParams(
            collective_id=1, has_side_effects=True, vmem_limit_bytes=60 * 2**20
        ),
    )(owners, steps, payload, tile, keep_rows, keep, table_home)

def neighbours():
    d, v = lax.axis_index("dp"), lax.axis_index("vocab")
    return [(d, v ^ k) for k in (1, 2, 3)]


def by_position(v, store):
    for i in range(4):
        pl.when(v == i)(functools.partial(store, i))


def forward_kernel(
    looked, valid, levels, places, vecs, keep, noise_hbm, small_hbm, attn_hbm, out_hbm, up_hbm, down_hbm,
    found, clean, inputs, hidden, normed_all, q, k, k_t, values, log_total, mixed, middle, normed_two,
    up_proj, active, hidden_two, final_norm, predicted, pred_all,
    noise, small, attn, out_w, up_w, down_w, found_in, values_t, mixed_out, mixed_in, seen,
    w_sem, s_sem, e_send, e_recv, n_send, n_recv, m_send, m_recv, p_send, p_recv, tables,
):
    v = lax.axis_index("vocab")
    partners = neighbours()
    sources = ((noise_hbm, noise), (small_hbm, small), (attn_hbm, attn), (out_hbm, out_w))
    first = [
        pltpu.make_async_copy(src, dst, s_sem.at[i]) for i, (src, dst) in enumerate(sources)
    ]
    for copy in first:
        copy.start()
    loads = []
    for j in range(4):
        for i, (src, dst) in enumerate(((up_hbm, up_w), (down_hbm, down_w))):
            copy = pltpu.make_async_copy(src.at[j], dst.at[j], w_sem.at[2 * j + i])
            copy.start()
            loads.append(copy)
    for copy in tables:
        copy.start()
    for b in range(4):
        found[b] = jnp.where(
            valid[256 * b : 256 * b + 256, :] > 0.0, looked[b].astype(f32), 0.0
        ).astype(bf16)
    greet(partners)
    asked = start_all(
        [
            remote(found.at[m], found_in.at[m - 1], (e_send, e_recv), m - 1, partners[m - 1])
            for m in (2, 3, 1)
        ]
    )
    seen[...] = jnp.broadcast_to(keep[...], seen.shape)
    for copy in first:
        copy.wait()
    wave = levels[2:3].astype(bf16)
    time_part = matmul_nt(jnp.broadcast_to(wave, (16, EMBED_WIDTH)), small[1])[0:1]
    arrive_all(asked)
    total = found[0].astype(f32)
    for m in range(3):
        total = total + found_in[m].astype(f32)
    clean[...] = total
    noisy = levels[0:1] * total + levels[1:2] * noise[...].astype(f32)
    inputs[:, 0:EMBED_WIDTH] = noisy.astype(bf16)
    inputs[:, EMBED_WIDTH:] = jnp.broadcast_to(wave, noisy.shape)
    value = matmul_nt(inputs[:, 0:EMBED_WIDTH], small[0]) + time_part + places[...]
    hidden[...] = value
    normed_all[0] = (norm_parts(value)[0] * vecs[0:1] + vecs[1:2]).astype(bf16)

    far = remote(normed_all.at[0], normed_all.at[2], (n_send, n_recv), 0, partners[1])
    near = remote(normed_all.at[0], normed_all.at[1], (n_send, n_recv), 1, partners[0])
    last = remote(normed_all.at[2], normed_all.at[3], (n_send, n_recv), 2, partners[0])
    far.start()
    near.start()

    def project(b):
        rows = pl.ds(b * 256, 256)
        block = normed_all[b]
        for i, ref in ((0, q), (1, k), (2, values)):
            result = matmul_nt(block, attn[i])
            if i == 0:
                result = result.astype(bf16).astype(f32) * HDIM ** (-0.5)
            for h in range(3):
                ref[h, rows, :] = result[:, h * HDIM : (h + 1) * HDIM].astype(bf16)
        k_t[:, rows] = matmul_nt(attn[1], block).astype(bf16)
        values_t[:, rows] = matmul_nt(attn[2], block).astype(bf16)

    project(0)
    near.wait_recv()
    project(1)
    far.wait_recv()
    last.start()
    project(2)
    last.wait_recv()
    project(3)

    given = []
    for b in (2, 3, 1, 0):
        rows = pl.ds(b * 256, 256)
        parts = []
        for h in range(3):
            scores = matmul_nt(k[h], q[h, rows, :])
            scores = jnp.where(seen[...] > 0.0, scores, -1000000000.0)
            top = jnp.max(scores, 0, keepdims=True)
            expo = jnp.exp(scores - top)
            mass = jnp.sum(expo, 0, keepdims=True)
            probs = (expo * (1.0 / mass)).astype(bf16)
            log_total[pl.ds(3 * b + h, 1), :] = top + jnp.log(mass)
            parts.append(matmul_nn(values_t[h * HDIM : (h + 1) * HDIM, :], probs))
        block = jnp.concatenate(parts, 0).T.astype(bf16)
        if b == 0:
            mixed_in[0] = block
        else:
            mixed_out[b - 1] = block
            copy = remote(
                mixed_out.at[b - 1], mixed_in.at[b], (m_send, m_recv), b - 1, partners[b - 1]
            )
            copy.start()
            given.append(copy)
    arrive_all(given)

    def lay(i):
        for b in range(4):
            mixed[:, QUARTER * (i ^ b) : QUARTER * ((i ^ b) + 1)] = mixed_in[b]

    by_position(v, lay)
    value = hidden[...] + matmul_nt(mixed[...], out_w[...])
    middle[...] = value
    normed_two[...] = (norm_parts(value)[0] * vecs[2:3] + vecs[3:4]).astype(bf16)
    for j in range(4):
        loads[2 * j].wait()
        loads[2 * j + 1].wait()
        raised = matmul_nn(normed_two[...], up_w[j]) + vecs[4 + j : 5 + j]
        up_proj[j] = raised
        active[j] = jax.nn.gelu(raised).astype(bf16)
        lowered = matmul_nt(active[j], down_w[j])
        hidden_two[...] = (middle[...] if j == 0 else hidden_two[...]) + lowered
    final_norm[...] = (norm_parts(hidden_two[...])[0] * vecs[8:9] + vecs[9:10]).astype(bf16)
    predicted[...] = matmul_nn(final_norm[...], small[2])
    pred_all[0] = predicted[...].astype(bf16)
    shown = start_all(
        [
            remote(pred_all.at[0], pred_all.at[m], (p_send, p_recv), m - 1, partners[m - 1])
            for m in (2, 3, 1)
        ]
    )
    arrive_all(shown)
    for copy in asked + [far, near, last] + given + shown:
        copy.wait_send()


STRIP = 768


def strips(rows):
    return [(lo, min(STRIP, rows - lo)) for lo in range(0, rows, STRIP)]


def head_kernel(
    pred_all, table, table_t, weight, found,
    grad_pred, lse, found_t, stats, gathered, outgoing, incoming,
    s_send, s_recv, g_send, g_recv,
):
    partners = neighbours()
    rows = table_t.shape[0]
    full, rest = rows // STRIP, rows % STRIP
    mixes = []
    for b in range(4):
        block = pred_all[b]

        def strip(at, carry):
            peak, mass, mix = carry
            value = matmul_nt(table_t[at, :], block)
            top = jnp.maximum(peak, jnp.max(value, 0, keepdims=True))
            expo = jnp.exp(value - top)
            fade = jnp.exp(peak - top)
            mass = mass * fade + jnp.sum(expo, 0, keepdims=True)
            return top, mass, mix * fade + matmul_nn(table[:, at], expo.astype(bf16))

        carry = lax.fori_loop(
            0,
            full,
            lambda t, carry: strip(pl.ds(pl.multiple_of(t * STRIP, STRIP), STRIP), carry),
            (
                jnp.full((1, 256), -jnp.inf, f32),
                jnp.zeros((1, 256), f32),
                jnp.zeros((EMBED_WIDTH, 256), f32),
            ),
            unroll=3,
        )
        if rest:
            carry = strip(pl.ds(full * STRIP, rest), carry)
        found_t[b] = found[b].astype(f32).T
        stats[b, 2:3] = jnp.sum(block.astype(f32).T * found_t[b], 0, keepdims=True)
        stats[b, 0:1] = carry[0]
        stats[b, 1:2] = carry[1]
        stats[b, 3:8] = jnp.zeros((5, 256), f32)
        mixes.append(carry[2])
    told = start_all(
        [
            remote(stats, gathered.at[m - 1], (s_send, s_recv), m - 1, partners[m - 1])
            for m in (2, 3, 1)
        ]
    )
    arrive_all(told)
    given = []
    for b in (2, 3, 1, 0):
        views = [stats[b]] + [gathered[m - 1, b ^ m] for m in (1, 2, 3)]
        peak = functools.reduce(jnp.maximum, [view[0:1] for view in views])
        mass = sum(view[1:2] * jnp.exp(view[0:1] - peak) for view in views)
        total = peak + jnp.log(mass)
        lse[b : b + 1, :] = total
        if b == 0:
            target = sum(view[2:3] for view in views)
            lse[4:5, :] = weight[0:1, :] * (total - target)
            lse[5:8, :] = jnp.zeros((3, 256), f32)
        share = weight[b : b + 1, :]
        local = mixes[b] * (jnp.exp(stats[b, 0:1] - total) * share)
        local = local - found_t[b] * share
        outgoing[b] = local.T.astype(bf16)
        if b:
            copy = remote(
                outgoing.at[b], incoming.at[b - 1], (g_send, g_recv), b - 1, partners[b - 1]
            )
            copy.start()
            given.append(copy)
    arrive_all(given)
    value = outgoing[0].astype(f32)
    for m in range(3):
        value = value + incoming[m].astype(f32)
    grad_pred[...] = value
    for copy in told + given:
        copy.wait_send()


def gelu_slope(u):
    inner = math.sqrt(2.0 / math.pi)
    bent = jnp.tanh(inner * (u + 0.044715 * (u * u * u)))
    return 0.5 * (1.0 + bent) + (0.5 * inner) * u * (1.0 - bent * bent) * (
        1.0 + (3.0 * 0.044715) * (u * u)
    )


def backward_kernel(
    grad_pred, clean, predicted, twice, levels, head_stats, hidden, middle, hidden_two,
    normed_two, final_norm, up_proj, q, k, k_t, values, log_total, keep,
    small, attn, out_w, up_w, down_w, vecs,
    grad_pred_low, down_left, up_left, out_left, small_left, final_left, qkv_left, grad_up, grad_clean, sums,
    carried, folded, mix_out, mix_in, grad_k, grad_v, n_out, n_in, f_out, f_in, seen,
    m_send, m_recv, n_send, n_recv, c_send, c_recv,
):
    v = lax.axis_index("vocab")
    partners = neighbours()

    def turned(value):
        return value.astype(f32).T.astype(bf16)

    error = predicted[...] - clean[...]
    pull = twice[...] * error
    low = (grad_pred[...] + pull).astype(bf16)
    grad_pred_low[...] = low
    length = jnp.sqrt(jnp.sum(clean[...] * clean[...], -1, keepdims=True) + 1e-06)
    lane = lax.broadcasted_iota(jnp.int32, (1, UNIT), 1)
    scalars = (jnp.sum(pull * error), jnp.sum(head_stats[4:5, :]), jnp.sum(twice[...] * length))
    counted = jnp.sum(keep[0:256, :])
    sums[10:11, :] = sum(jnp.where(lane == i, x, 0.0) for i, x in enumerate(scalars + (counted,)))
    sums[11:16, :] = jnp.zeros((5, UNIT), f32)

    def through_norm(value, gain_row, grad_out, at):
        normal, scale_inv = norm_parts(value)
        part, grad_gain, grad_shift = norm_back(normal, scale_inv, vecs[gain_row : gain_row + 1], grad_out)
        sums[at : at + 1, :] = grad_gain[None, :]
        sums[at + 1 : at + 2, :] = grad_shift[None, :]
        return part

    carried[...] = through_norm(hidden_two[...], 8, matmul_nt(low, small[2]), 8)
    low = carried[...].astype(bf16)
    down_left[...] = turned(carried[...])
    up_left[...] = turned(normed_two[...])
    final_left[...] = turned(final_norm[...])
    for j in range(4):
        slope = matmul_nn(low, down_w[j]) * gelu_slope(up_proj[j])
        grad_up[j] = slope.astype(bf16)
        sums[4 + j : 5 + j, :] = jnp.sum(grad_up[j].astype(f32), 0, keepdims=True)
        part = matmul_nt(grad_up[j], up_w[j])
        folded[...] = part if j == 0 else folded[...] + part
    carried[...] = carried[...] + through_norm(middle[...], 2, folded[...], 2)
    out_left[...] = turned(carried[...])
    folded[...] = matmul_nn(carried[...].astype(bf16), out_w[...])

    def lay(i):
        for b in range(4):
            mix_out[b] = folded[:, QUARTER * (i ^ b) : QUARTER * ((i ^ b) + 1)].astype(bf16)

    by_position(v, lay)
    mixed = [
        remote(mix_out.at[m], mix_in.at[m - 1], (m_send, m_recv), m - 1, partners[m - 1])
        for m in (1, 2, 3)
    ]
    for m in (2, 3, 1):
        mixed[m - 1].start()
    for b in range(4):
        if b:
            mixed[b - 1].wait_recv()
        grad_block = mix_out[0] if b == 0 else mix_in[b - 1]
        rows = pl.ds(b * 256, 256)
        for h in range(3):
            grad_mix = grad_block[:, h * HDIM : (h + 1) * HDIM]
            asked = q[h, rows, :]
            scores = matmul_nt(k[h], asked)
            scores = jnp.where(seen[...] > 0.0, scores, -1000000000.0)
            probs = jnp.exp(scores - log_total[3 * b + h : 3 * b + h + 1, :])
            grad_probs = matmul_nt(values[h], grad_mix)
            inner = jnp.sum(probs * grad_probs, 0, keepdims=True)
            grad_scores = (probs * (grad_probs - inner)).astype(bf16)
            grad_asked = matmul_nn(k_t[h * HDIM : (h + 1) * HDIM, :], grad_scores)
            qkv_left[0, h * HDIM : (h + 1) * HDIM, rows] = (grad_asked * HDIM ** (-0.5)).astype(bf16)
            part_k = matmul_nn(grad_scores, asked)
            part_v = matmul_nn(probs.astype(bf16), grad_mix)
            grad_k[h] = part_k if b == 0 else grad_k[h] + part_k
            grad_v[h] = part_v if b == 0 else grad_v[h] + part_v
    for h in range(3):
        lanes = pl.ds(h * HDIM, HDIM)
        qkv_left[1, lanes, :] = grad_k[h].T.astype(bf16)
        qkv_left[2, lanes, :] = grad_v[h].T.astype(bf16)

    def grad_normed(b):
        rows = pl.ds(b * 256, 256)
        return sum(matmul_tn(qkv_left[i, :, rows], attn[i]) for i in range(3))

    n_out[0] = grad_normed(1).astype(bf16)
    n_out[1] = grad_normed(3).astype(bf16)
    near = remote(n_out, n_in, (n_send, n_recv), 0, partners[0])
    near.start()
    folded[...] = grad_normed(2)
    near.wait_recv()
    f_out[...] = (folded[...] + n_in[1].astype(f32)).astype(bf16)
    far = remote(f_out, f_in, (n_send, n_recv), 1, partners[1])
    far.start()
    folded[...] = grad_normed(0) + n_in[0].astype(f32)
    far.wait_recv()
    grad_out = folded[...] + f_in[...].astype(f32)
    carried[...] = carried[...] + through_norm(hidden[...], 0, grad_out, 0)
    small_left[...] = turned(carried[...])
    back = matmul_nn(carried[...].astype(bf16), small[0])
    grad_clean[0] = (levels[0:1] * back - twice[...] * (predicted[...] - clean[...])).astype(bf16)
    shown = start_all(
        [
            remote(grad_clean.at[0], grad_clean.at[m], (c_send, c_recv), m - 1, partners[m - 1])
            for m in (2, 3, 1)
        ]
    )
    arrive_all(shown)
    for copy in mixed + [near, far] + shown:
        copy.wait_send()


def step_kernel(
    looked, valid, levels, places, vecs, keep, weight, twice,
    noise_hbm, small_hbm, attn_hbm, out_hbm, up_hbm, down_hbm, table_hbm, table_t_hbm,
    inputs, normed_all, mixed, active, pred_all, lse, grad_pred_low, down_left, up_left, out_left, small_left,
    final_left, qkv_left, grad_up, grad_clean, sums,
    found, clean, hidden, q, k, k_t, values, log_total, middle, normed_two, up_proj, hidden_two, final_norm,
    predicted, grad_pred, noise, small, attn, out_w, up_w, down_w, found_in, values_t, mixed_out, mixed_in, seen,
    table, table_t, found_t, stats, gathered, outgoing, incoming,
    carried, folded, mix_out, mix_in, grad_k, grad_v, n_out, n_in, f_out, f_in,
    w_sem, s_sem, t_sem,
    e_send, e_recv, n_send, n_recv, m_send, m_recv, p_send, p_recv, h_send, h_recv, g_send, g_recv,
    i_send, i_recv, j_send, j_recv, c_send, c_recv,
):
    tables = [
        pltpu.make_async_copy(table_hbm, table, t_sem.at[0]),
        pltpu.make_async_copy(table_t_hbm, table_t, t_sem.at[1]),
    ]
    forward_kernel(
        looked, valid, levels, places, vecs, keep, noise_hbm, small_hbm, attn_hbm, out_hbm, up_hbm, down_hbm,
        found, clean, inputs, hidden, normed_all, q, k, k_t, values, log_total, mixed, middle, normed_two,
        up_proj, active, hidden_two, final_norm, predicted, pred_all,
        noise, small, attn, out_w, up_w, down_w, found_in, values_t, mixed_out, mixed_in, seen,
        w_sem, s_sem, e_send, e_recv, n_send, n_recv, m_send, m_recv, p_send, p_recv, tables,
    )
    for copy in tables:
        copy.wait()
    head_kernel(
        pred_all, table, table_t, weight, found,
        grad_pred, lse, found_t, stats, gathered, outgoing, incoming,
        h_send, h_recv, g_send, g_recv,
    )
    backward_kernel(
        grad_pred, clean, predicted, twice, levels, lse, hidden, middle, hidden_two,
        normed_two, final_norm, up_proj, q, k, k_t, values, log_total, keep,
        small, attn, out_w, up_w, down_w, vecs,
        grad_pred_low, down_left, up_left, out_left, small_left, final_left, qkv_left, grad_up, grad_clean, sums,
        carried, folded, mix_out, mix_in, grad_k, grad_v, n_out, n_in, f_out, f_in, seen,
        i_send, i_recv, j_send, j_recv, c_send, c_recv,
    )


def step(*operands):
    dma, vmem = pltpu.SemaphoreType.DMA, pltpu.VMEM
    n = 256
    table, table_t = operands[-2:]

    def shape(kind, *dims):
        return jax.ShapeDtypeStruct(dims, kind)

    return pl.pallas_call(
        step_kernel,
        out_shape=[
            shape(bf16, n, 2 * EMBED_WIDTH),
            shape(bf16, 4, n, D),
            shape(bf16, n, D),
            shape(bf16, 4, n, UNIT),
            shape(bf16, 4, n, EMBED_WIDTH),
            shape(f32, 8, n),
            shape(bf16, n, EMBED_WIDTH),
        ]
        + [shape(bf16, D, n)] * 5
        + [
            shape(bf16, 3, QUARTER, 4 * n),
            shape(bf16, 4, n, UNIT),
            shape(bf16, 4, n, EMBED_WIDTH),
            shape(f32, 16, UNIT),
        ],
        in_specs=[VMEM] * 8 + [ANY] * 8,
        out_specs=[VMEM] * 16,
        scratch_shapes=[
            vmem((4, n, EMBED_WIDTH), bf16),
            vmem((n, EMBED_WIDTH), f32),
            vmem((n, D), f32),
            vmem((3, 4 * n, HDIM), bf16),
            vmem((3, 4 * n, HDIM), bf16),
            vmem((QUARTER, 4 * n), bf16),
            vmem((3, 4 * n, HDIM), bf16),
            vmem((16, n), f32),
            vmem((n, D), f32),
            vmem((n, D), bf16),
            vmem((4, n, UNIT), f32),
            vmem((n, D), f32),
            vmem((n, D), bf16),
            vmem((n, EMBED_WIDTH), f32),
            vmem((n, EMBED_WIDTH), f32),
            vmem((n, EMBED_WIDTH), bf16),
            vmem((4, D, LANES), bf16),
            vmem((4, QUARTER, UNIT), bf16),
            vmem((D, UNIT), bf16),
            vmem((4, D, UNIT), bf16),
            vmem((4, D, UNIT), bf16),
            vmem((3, n, EMBED_WIDTH), bf16),
            vmem((QUARTER, 4 * n), bf16),
            vmem((3, n, QUARTER), bf16),
            vmem((4, n, QUARTER), bf16),
            vmem((4 * n, n), f32),
            vmem(table.shape, bf16),
            vmem(table_t.shape, bf16),
            vmem((4, EMBED_WIDTH, n), f32),
            vmem((4, 8, n), f32),
            vmem((3, 4, 8, n), f32),
            vmem((4, n, EMBED_WIDTH), bf16),
            vmem((3, n, EMBED_WIDTH), bf16),
            vmem((n, D), f32),
            vmem((n, D), f32),
            vmem((4, n, QUARTER), bf16),
            vmem((3, n, QUARTER), bf16),
            vmem((3, 4 * n, HDIM), f32),
            vmem((3, 4 * n, HDIM), f32),
            vmem((2, n, D), bf16),
            vmem((2, n, D), bf16),
            vmem((n, D), bf16),
            vmem((n, D), bf16),
            dma((8,)),
            dma((4,)),
            dma((2,)),
        ]
        + [dma((3,))] * 18,
        compiler_params=pltpu.CompilerParams(
            collective_id=4, has_side_effects=True, vmem_limit_bytes=60 * 2**20
        ),
    )(*operands)

I16 = jnp.int16
TAIL = 16
TILES = 60
PART_TILES = 30
PART = 3840


def exponent(peak):
    return jnp.ceil(jnp.log2(jnp.maximum(peak, 1e-30))) + 1.0


def coded(value, power):
    return jnp.round(value * jnp.exp2(15.0 - power)).astype(jnp.int32).astype(I16)


def plain(code, power):
    return code.astype(jnp.int32).astype(f32) * jnp.exp2(power - 15.0)


def put(ref, value):
    rows, cols = value.shape
    power = exponent(jnp.max(jnp.abs(value), 0, keepdims=True))
    ref[0:rows, :] = coded(value, power)
    ref[rows : rows + TAIL, :] = (
        jnp.broadcast_to(power, (TAIL, cols)).astype(jnp.int32).astype(I16)
    )


def get(ref, rows):
    power = ref[rows : rows + TAIL, :].astype(jnp.int32).astype(f32)[0:1]
    return plain(ref[0:rows, :], power)


def put_tiles(ref, source, rows):
    lane = lax.broadcasted_iota(jnp.int32, (rows, LANES), 1)

    def body(tile, powers):
        at = pl.ds(pl.multiple_of(tile * LANES, LANES), LANES)
        value = source(at)
        power = exponent(jnp.max(jnp.abs(value), 1, keepdims=True))
        ref[:, at] = coded(value, power)
        return jnp.where(lane == tile, power, powers)

    powers = lax.fori_loop(0, PART_TILES, body, jnp.zeros((rows, LANES), f32), unroll=6)
    ref[:, PART:] = powers.astype(jnp.int32).astype(I16)


def tile_getter(ref, rows):
    lane = lax.broadcasted_iota(jnp.int32, (rows, LANES), 1)
    powers = ref[:, PART:].astype(jnp.int32).astype(f32)

    def read(tile, at):
        power = jnp.sum(jnp.where(lane == tile, powers, 0.0), 1, keepdims=True)
        return plain(ref[:, at], power)

    return read


def grads_kernel(
    owners, inputs, grad_pred, pred_all, grad_clean, lse, weight, row_of, tile,
    out_left_hbm, mixed_hbm, down_left_hbm, active_hbm, qkv_left_hbm, normed_hbm, table_t_hbm, up_left_hbm,
    grad_up_hbm, small_left_hbm, final_left_hbm,
    summed, table_sum, tile_sum,
    out_left, mixed, down_left, active, qkv_left, normed, table_t, up_left, grad_up, small_left, final_left,
    home, small_home, outgoing, cs, cr, xs, xr, ys, yr, zs, zr, part, half,
    small_cs, small_cr, small_xs, small_xr, small_ys, small_yr, small_zs, small_zr, small_half,
    table, pred_t, clean_t, ts, tr, tzs, tzr, tile_at, tile_from,
    c_send, c_recv, x_send, x_recv, y_send, y_recv, z_send, z_recv, t_send, t_recv, a_send, a_recv, local, l_sem,
):
    z, y, d, v = place()
    far, near = v ^ 2, v ^ 1
    pairs = (
        (out_left_hbm, out_left), (mixed_hbm, mixed), (down_left_hbm, down_left), (active_hbm, active),
        (qkv_left_hbm, qkv_left), (normed_hbm, normed), (table_t_hbm, table_t), (up_left_hbm, up_left),
        (grad_up_hbm, grad_up), (small_left_hbm, small_left), (final_left_hbm, final_left),
    )
    loads = [pltpu.make_async_copy(src, dst, l_sem.at[i]) for i, (src, dst) in enumerate(pairs)]
    for copy in loads:
        copy.start()
    loaded = set()

    def need(*which):
        for i in which:
            if i not in loaded:
                loads[i].wait()
                loaded.add(i)

    greet([(d ^ m, v) for m in TRADE_MASKS] + [(d, far), (d, near)])
    sent = []

    def send(src, dst, sems, index, partner):
        copy = remote(src, dst, sems, index, partner)
        copy.start()
        sent.append(copy)
        return copy

    def product(n, who):
        need(*((0, 1) if n == 0 else (2, 3) if n < 5 else (7, 8)))
        if n == 0:
            return matmul_nn(out_left[who], mixed[...])
        if n < 5:
            return matmul_nn(down_left[who], active[n - 1])
        return matmul_nn(up_left[who], grad_up[n - 5])

    core, chip, side, line = {}, {}, {}, {}

    def to_core(n):
        put(cs.at[n, 0], product(n, near))
        put(cs.at[n, 1], product(n, near ^ 2))
        core[n] = send(cs.at[n], cr.at[n], (c_send, c_recv), n, (d, near))

    def to_chip(n):
        core[n].wait_recv()
        put(xs.at[n], product(n, far) + get(cr.at[n, 1], QUARTER))
        chip[n] = send(xs.at[n], xr.at[n], (x_send, x_recv), n, (d, far))

    def halves(slot, value):
        part[...] = value
        put(ys.at[slot], part[pl.ds((1 - y) * HALF, HALF), :])
        half[slot] = part[pl.ds(y * HALF, HALF), :]
        side[slot] = send(ys.at[slot], yr.at[slot], (y_send, y_recv), slot, (d ^ 1, v))

    def to_side(n):
        chip[n].wait_recv()
        value = product(n, v) + get(cr.at[n, 0], QUARTER) + get(xr.at[n], QUARTER)
        halves(3 + n, value)

    def to_line(group):
        for u in range(4):
            slot = 4 * group + u
            side[slot].wait_recv()
            half[slot] = half[slot] + get(yr.at[slot], HALF)
        for k in (2, 1, 3):
            put(zs.at[group, k - 1], half[4 * group + (z ^ k)])
            line[group, k] = send(
                zs.at[group, k - 1], zr.at[group, k - 1], (z_send, z_recv), 3 * group + k - 1, (d ^ (2 * k), v)
            )

    def to_home(group):
        total = half[4 * group + z]
        for k in (2, 1, 3):
            line[group, k].wait_recv()
            total = total + get(zr.at[group, k - 1], HALF)
        put(home.at[group], total)

    def small_product(who):
        need(9, 10)
        return jnp.concatenate(
            [matmul_nn(small_left[who], inputs[...]), matmul_nn(final_left[who], grad_pred[...])], 1
        )

    def small_to_core():
        put(small_cs.at[0], small_product(near))
        put(small_cs.at[1], small_product(near ^ 2))
        core[9] = send(small_cs, small_cr, (c_send, c_recv), 9, (d, near))

    def small_to_chip():
        core[9].wait_recv()
        put(small_xs, small_product(far) + get(small_cr.at[1], QUARTER))
        chip[9] = send(small_xs, small_xr, (x_send, x_recv), 9, (d, far))

    def small_to_side():
        chip[9].wait_recv()
        value = small_product(v) + get(small_cr.at[0], QUARTER) + get(small_xr, QUARTER)
        cols = value.shape[1]
        part[:, 0:cols] = value
        put(small_ys, part[pl.ds((1 - y) * HALF, HALF), 0:cols])
        small_half[0] = part[pl.ds(y * HALF, HALF), 0:LANES]
        small_half[1] = part[pl.ds(y * HALF, HALF), LANES : 2 * LANES]
        small_half[2] = part[pl.ds(y * HALF, HALF), 2 * LANES : cols]
        small_half[3] = jnp.zeros((HALF, LANES), f32)
        side[12] = send(small_ys, small_yr, (y_send, y_recv), 12, (d ^ 1, v))

    def small_to_line():
        side[12].wait_recv()
        value = get(small_yr, HALF)
        for u in range(3):
            small_half[u] = small_half[u] + value[:, u * LANES : (u + 1) * LANES]
        for k in (2, 1, 3):
            put(small_zs.at[k - 1], small_half[z ^ k])
            line[3, k] = send(
                small_zs.at[k - 1], small_zr.at[k - 1], (z_send, z_recv), 9 + k - 1, (d ^ (2 * k), v)
            )

    def small_to_home():
        total = small_half[z]
        for k in (2, 1, 3):
            line[3, k].wait_recv()
            total = total + get(small_zr.at[k - 1], HALF)
        put(small_home, total)

    def turn_tokens():
        for b in range(4):
            pred_t[b] = pred_all[b].astype(f32).T.astype(bf16)
            clean_t[b] = grad_clean[b].astype(f32).T.astype(bf16)

    vocab_rows = table_t.shape[0]

    def table_strip(lo, size):
        need(6)
        total = jnp.zeros((EMBED_WIDTH, size), f32)
        for b in range(4):
            logits = matmul_nt(table_t[lo : lo + size, :], pred_all[b])
            probs = jnp.exp(logits - lse[b : b + 1, :])
            here = lax.broadcasted_iota(jnp.int32, (size, 256), 0) == row_of[b : b + 1, :] - lo
            here = here.astype(f32)
            grad_logits = ((probs - here) * weight[b : b + 1, :]).astype(bf16)
            total = total + matmul_nt(pred_t[b], grad_logits)
            total = total + matmul_nt(clean_t[b], here.astype(bf16))
        for i in range(8):
            rows = slice(16 * (i // 2), 16 * (i // 2) + 16)
            table[i % 2, rows, lo : lo + size] = total[16 * i : 16 * i + 16]
        if lo + size == vocab_rows:
            table[:, :, vocab_rows:] = jnp.zeros((2, 64, TILES * LANES - vocab_rows), f32)

    table_strips = [(lo, min(STRIP, vocab_rows - lo)) for lo in range(0, vocab_rows, STRIP)]

    def shifted(at, p):
        return pl.ds(pl.multiple_of(at.start + p * PART, LANES), LANES)

    def table_to_side(p):
        put_tiles(ts.at[p], lambda at: table[1 - y, :, shifted(at, p)], 64)
        side[13 + p] = send(ts.at[p], tr.at[p], (y_send, y_recv), 13 + p, (d ^ 1, v))

    def table_line_value(which, p):
        rows = pl.ds(pl.multiple_of(which * 16, 16), 16)
        read = tile_getter(tr.at[p, rows, :], 16)
        return rows, read

    def table_to_line(p):
        side[13 + p].wait_recv()
        for k in (2, 1, 3):
            rows, read = table_line_value(z ^ k, p)

            def source(at, rows=rows, read=read):
                return table[y, rows, shifted(at, p)] + read(at.start // LANES, at)

            put_tiles(tzs.at[p, k - 1], source, 16)
            line[4 + p, k] = send(
                tzs.at[p, k - 1],
                tzr.at[p, k - 1],
                (z_send, z_recv),
                12 + 3 * p + k - 1,
                (d ^ (2 * k), v),
            )

    def table_to_home(p):
        for k in (2, 1, 3):
            line[4 + p, k].wait_recv()
        rows, read = table_line_value(z, p)
        others = [tile_getter(tzr.at[p, k], 16) for k in range(3)]

        def body(tile, carry):
            at = pl.ds(pl.multiple_of(tile * LANES, LANES), LANES)
            value = table[y, rows, shifted(at, p)] + read(tile, at)
            for other in others:
                value = value + other(tile, at)
            table_sum[:, shifted(at, p)] = value
            return carry

        lax.fori_loop(0, PART_TILES, body, 0, unroll=5)

    hops = [(d, near), (d, far), (d ^ 1, v), (d ^ 2, v), (d ^ 4, v)]
    tile_copies = {}

    def tile_send(hop):
        if hop == 0:
            tile_at[0] = tile[...]
        else:
            tile_copies[hop - 1].wait_recv()
            tile_at[hop] = tile_at[hop - 1] + tile_from[hop - 1]
        tile_copies[hop] = send(
            tile_at.at[hop], tile_from.at[hop], (t_send, t_recv), hop, hops[hop]
        )

    def token_products():
        need(4, 5)
        for u in range(3):
            halves(
                u,
                sum(matmul_nn(qkv_left[u, :, 256 * b : 256 * b + 256], normed[b]) for b in range(4)),
            )

    to_core(0)
    to_core(1)
    to_chip(0)
    token_products()
    tile_send(0)
    turn_tokens()
    table_strip(*table_strips[0])
    table_strip(*table_strips[1])
    to_core(2)
    to_chip(1)
    to_side(0)
    table_strip(*table_strips[2])
    table_strip(*table_strips[3])
    to_core(3)
    to_chip(2)
    table_strip(*table_strips[4])
    table_to_side(0)
    to_line(0)
    to_side(1)
    table_strip(*table_strips[5])
    table_strip(*table_strips[6])
    to_core(4)
    to_chip(3)
    table_strip(*table_strips[7])
    table_strip(*table_strips[8])
    for strip in table_strips[9:]:
        table_strip(*strip)
    table_to_side(1)
    to_side(2)
    to_core(5)
    to_chip(4)
    tile_send(1)
    table_to_line(0)
    to_core(6)
    to_chip(5)
    to_side(3)
    to_core(7)
    to_chip(6)
    small_to_core()
    to_core(8)
    to_chip(7)
    small_to_chip()
    to_chip(8)
    to_side(4)
    tile_send(2)
    table_to_line(1)
    to_line(1)
    to_side(5)
    to_home(0)
    tile_send(3)
    small_to_side()
    to_side(6)
    table_to_home(0)
    small_to_line()
    tile_send(4)
    to_side(7)
    to_home(1)
    to_side(8)
    to_line(2)
    table_to_home(1)
    small_to_home()
    tile_copies[4].wait_recv()
    tile_sum[...] = tile_at[4] + tile_from[4]
    to_home(2)

    def offer(m):
        taker = d ^ m
        unit = jnp.where(owners[4] == taker, home[2], home[0])
        outgoing[m, :, 0:UNIT] = jnp.where(owners[5] == taker, home[1], unit)
        outgoing[m, :, UNIT:] = small_home[...]

    offered = []
    for i, m in enumerate(TRADE_MASKS):
        offer(m)
        offered.append(send(outgoing.at[m], summed.at[d], (a_send, a_recv), i, (d ^ m, v)))
    offer(0)
    keep = pltpu.make_async_copy(outgoing.at[0], summed.at[d], local)
    keep.start()
    keep.wait()
    arrive_all(offered)
    for copy in sent:
        copy.wait_send()


def reduce_grads(*operands):
    dma = pltpu.SemaphoreType.DMA
    vmem = pltpu.VMEM
    tall, low, wide = QUARTER + TAIL, HALF + TAIL, 3 * LANES
    table_cols = TILES * LANES
    return pl.pallas_call(
        grads_kernel,
        out_shape=[
            jax.ShapeDtypeStruct((8, low, UNIT + LANES), I16),
            jax.ShapeDtypeStruct((16, table_cols), f32),
            jax.ShapeDtypeStruct((16, UNIT), f32),
        ],
        in_specs=[SMEM] + [VMEM] * 8 + [ANY] * 11,
        out_specs=[VMEM] * 3,
        scratch_shapes=[vmem(value.shape, bf16) for value in operands[9:]]
        + [
            vmem((3, low, UNIT), I16),
            vmem((low, LANES), I16),
            vmem((8, low, UNIT + LANES), I16),
            vmem((9, 2, tall, UNIT), I16),
            vmem((9, 2, tall, UNIT), I16),
            vmem((9, tall, UNIT), I16),
            vmem((9, tall, UNIT), I16),
            vmem((12, low, UNIT), I16),
            vmem((12, low, UNIT), I16),
            vmem((3, 3, low, UNIT), I16),
            vmem((3, 3, low, UNIT), I16),
            vmem((QUARTER, UNIT), f32),
            vmem((12, HALF, UNIT), f32),
            vmem((2, tall, wide), I16),
            vmem((2, tall, wide), I16),
            vmem((tall, wide), I16),
            vmem((tall, wide), I16),
            vmem((low, wide), I16),
            vmem((low, wide), I16),
            vmem((3, low, LANES), I16),
            vmem((3, low, LANES), I16),
            vmem((4, HALF, LANES), f32),
            vmem((2, 64, table_cols), f32),
            vmem((4, EMBED_WIDTH, 256), bf16),
            vmem((4, EMBED_WIDTH, 256), bf16),
            vmem((2, 64, PART + LANES), I16),
            vmem((2, 64, PART + LANES), I16),
            vmem((2, 3, 16, PART + LANES), I16),
            vmem((2, 3, 16, PART + LANES), I16),
            vmem((5, 16, UNIT), f32),
            vmem((5, 16, UNIT), f32),
        ]
        + [dma((10,))] * 4
        + [dma((15,))] * 2
        + [dma((18,))] * 2
        + [dma((5,))] * 2
        + [dma((7,))] * 2
        + [dma, dma((11,))],
        compiler_params=pltpu.CompilerParams(
            collective_id=2, has_side_effects=True, vmem_limit_bytes=60 * 2**20
        ),
    )(*operands)


def slot_kernel(
    kind, unit, column, summed, table_grad, sums, w, m1, m2, tw, t1, t2,
    w_out, m1_out, m2_out, tw_out, t1_out, t2_out, loss, norm,
):
    per_unit = UNIT // LANES

    def once():
        g = table_grad[:, 0 : tw.shape[1]]
        tw_out[...], t1_out[...], t2_out[...] = adamw(tw[...], g, t1[...], t2[...])
        row = sums[10:11, :]
        lane = lax.broadcasted_iota(jnp.int32, row.shape, 1)
        square, cross, length, count = [jnp.sum(jnp.where(lane == i, row, 0.0)) for i in range(4)]
        loss[0] = (0.5 * square + cross) * count
        loss[1] = count
        norm[0] = 0.5 * length

    pl.when(pl.program_id(0) == 0)(once)
    for b in range(per_unit):
        j = pl.program_id(0) * per_unit + b
        first = jnp.where(kind[j] == 2, per_unit, column[j])
        at = pl.ds(pl.multiple_of(first * LANES, LANES), LANES)
        lanes = slice(b * LANES, b * LANES + LANES)
        for half in range(2):
            rows = slice(half * HALF, half * HALF + HALF)
            g = get(summed.at[2 * unit[j] + half, :, at], HALF)
            g = jnp.where(kind[j] > 0, g, jnp.zeros_like(g))
            w_out[rows, lanes], m1_out[rows, lanes], m2_out[rows, lanes] = adamw(
                w[rows, lanes], g, m1[rows, lanes], m2[rows, lanes]
            )


def slot_update(kind, unit, column, summed, table_grad, sums, slots, first, second, *table):
    rows = slots.shape[0]
    plain_spec = pl.BlockSpec((rows, UNIT), lambda j, k, u, c: (0, j))

    def whole(value):
        return pl.BlockSpec(value.shape, lambda j, k, u, c: (0,) * len(value.shape))

    return pl.pallas_call(
        slot_kernel,
        grid_spec=pltpu.PrefetchScalarGridSpec(
            num_scalar_prefetch=3,
            grid=(CAP // UNIT,),
            in_specs=[whole(summed), whole(table_grad), whole(sums)]
            + [plain_spec] * 3
            + [whole(value) for value in table],
            out_specs=[plain_spec] * 3 + [whole(value) for value in table] + [SMEM] * 2,
        ),
        out_shape=[jax.ShapeDtypeStruct(slots.shape, f32)] * 3
        + [jax.ShapeDtypeStruct(table[0].shape, f32)] * 3
        + [jax.ShapeDtypeStruct((2,), f32), jax.ShapeDtypeStruct((1,), f32)],
        cost_estimate=pl.CostEstimate(flops=0, bytes_accessed=28 * rows * CAP, transcendentals=0),
        compiler_params=pltpu.CompilerParams(vmem_limit_bytes=60 * 2**20),
    )(kind, unit, column, summed, table_grad, sums, slots, first, second, *table)


def per_device(
    token_ids,
    timesteps,
    pad_mask,
    noise_draw,
    owners,
    emb_table,
    table_first_moment,
    table_second_moment,
    mat_slots,
    slot_first,
    slot_second,
    vec_params,
    vec_first,
    vec_second,
):
    v = lax.axis_index("vocab")
    seq_len = token_ids.shape[1]
    tokens = seq_len // 4
    vocab_rows, emb_cols = emb_table.shape
    table_own = emb_table.T
    (
        payload, table_home, row_of, safe_row, keep_rows, keep_column, valid_column, count_tile,
        kind, unit, column,
    ) = prepare(owners, token_ids, pad_mask, table_own, mat_slots)
    w_up, w_down, w_small, w_attn, w_out, table_low, row_weight, twice, places, levels = spread(
        owners, timesteps, payload, count_tile, keep_rows, keep_column, table_home
    )
    table_low = table_low.reshape(EMBED_WIDTH, vocab_rows)
    table_t = table_low.T
    looked = table_t.at[safe_row[0]].get(mode="promise_in_bounds").reshape(4, tokens, EMBED_WIDTH)
    vecs = vec_params.reshape(10, D)
    (
        inputs, normed_all, mixed_own, active, pred_all, head_stats, grad_pred_low, down_left, up_left, out_left,
        small_left, final_left, qkv_left, grad_up, grad_clean, sums,
    ) = step(
        looked, valid_column, levels, places, vecs, keep_column, row_weight, twice,
        noise_draw[0], w_small, w_attn, w_out, w_up, w_down, table_low, table_t,
    )

    def left(value):
        return value.reshape(4, QUARTER, tokens)

    summed, table_grad, tile_sum = reduce_grads(
        owners, inputs, grad_pred_low, pred_all, grad_clean, head_stats, row_weight, row_of, sums,
        left(out_left), mixed_own, left(down_left), active, qkv_left, normed_all, table_t, left(up_left),
        grad_up, left(small_left), left(final_left),
    )
    (
        new_slots, slot_first_new, slot_second_new, new_table, table_first_new, table_second_new, loss_pair, emb_norm,
    ) = slot_update(
        kind, unit, column, summed, table_grad, tile_sum, mat_slots, slot_first, slot_second,
        table_own, table_first_moment.T, table_second_moment.T,
    )
    tile_sum = tile_sum.reshape(16 * UNIT)
    vec_share = vec_first.shape[0]
    own_grad = lax.dynamic_slice_in_dim(tile_sum, v * vec_share, vec_share)
    own_vecs = lax.dynamic_slice_in_dim(vec_params, v * vec_share, vec_share)
    new_vecs, vec_first_new, vec_second_new = adamw(own_vecs, own_grad, vec_first, vec_second)
    return (
        loss_pair,
        emb_norm[0],
        new_table.T,
        table_first_new.T,
        table_second_new.T,
        new_slots,
        slot_first_new,
        slot_second_new,
        new_vecs,
        vec_first_new,
        vec_second_new,
    )


def broadcast(value, axis, source):
    kept = jnp.where(lax.axis_index(axis) == source, value, 0).astype(value.dtype)
    return lax.psum(kept, axis)


def merged(value, axis, join):
    pieces = jax.tree.map(lambda part: lax.all_gather(part, axis), value)
    head = jax.tree.map(lambda part: part[0], pieces)
    tail = jax.tree.map(lambda part: part[1:], pieces)
    so_far, _ = lax.scan(lambda so_far, share: (join(so_far, share), None), head, tail)
    return so_far


def matrix_rows():
    return [D, D, D, D, FF, FF] * LAYERS + [EMBED_WIDTH, EMBED_WIDTH, EMBED_WIDTH]


def slot_places(owners):
    counts = jnp.array(matrix_rows(), jnp.int32)
    mat_total = counts.shape[0]
    same_owner = (owners[:, None] == owners[None, :]).astype(jnp.int32)
    earlier_mask = jnp.tril(jnp.ones((mat_total, mat_total), jnp.int32), -1)
    return owners * CAP + jnp.sum(same_owner * earlier_mask * counts[None, :], 1)


def block_scores(query_blk, keys_all, keep_keys, score_scale):
    scores = (
        jnp.einsum("qhd,khd->hqk", query_blk, keys_all, preferred_element_type=jnp.float32)
        * score_scale
    )
    return jnp.where(keep_keys[None, None, :], scores, -1000000000.0)


def attention(queries, keys_all, values_all, keep_keys, score_scale):
    tokens = queries.shape[0]
    width = min(512, tokens)
    query_blocks = queries.reshape(tokens // width, width, HEADS, HDIM)

    def one_block(query_blk):
        scores = block_scores(query_blk, keys_all, keep_keys, score_scale)
        row_max = jnp.max(scores, -1, keepdims=True)
        expo = jnp.exp(scores - row_max)
        exp_total = jnp.sum(expo, -1, keepdims=True)
        probabilities = (expo / exp_total).astype(jnp.bfloat16)
        mixed_out = jnp.einsum(
            "hqk,khd->qhd", probabilities, values_all, preferred_element_type=jnp.float32
        )
        return (mixed_out, (row_max + jnp.log(exp_total))[..., 0])

    mixed_out, log_total = lax.map(one_block, query_blocks)
    return (mixed_out.reshape(tokens, HEADS, HDIM), log_total)


def attention_back(queries, keys_all, values_all, keep_keys, log_total, grad_mixed, score_scale):
    tokens = queries.shape[0]
    width = min(512, tokens)
    query_blocks = queries.reshape(tokens // width, width, HEADS, HDIM)
    grad_blocks = grad_mixed.reshape(tokens // width, width, HEADS, HDIM)

    def one_block(carry_sums, block_data):
        query_blk, total_blk, grad_blk = block_data
        scores = block_scores(query_blk, keys_all, keep_keys, score_scale)
        probabilities = jnp.exp(scores - total_blk[..., None])
        grad_probs = jnp.einsum(
            "qhd,khd->hqk", grad_blk, values_all, preferred_element_type=jnp.float32
        )
        inner_sum = jnp.sum(probabilities * grad_probs, -1, keepdims=True)
        grad_scores = (probabilities * (grad_probs - inner_sum)).astype(jnp.bfloat16)
        grad_query = (
            jnp.einsum("hqk,khd->qhd", grad_scores, keys_all, preferred_element_type=jnp.float32)
            * score_scale
        )
        grad_key = (
            jnp.einsum("hqk,qhd->khd", grad_scores, query_blk, preferred_element_type=jnp.float32)
            * score_scale
        )
        grad_value = jnp.einsum(
            "hqk,qhd->khd",
            probabilities.astype(jnp.bfloat16),
            grad_blk,
            preferred_element_type=jnp.float32,
        )
        return ((carry_sums[0] + grad_key, carry_sums[1] + grad_value), grad_query)

    zero_keys = jnp.zeros(keys_all.shape, jnp.float32)
    grad_kv, grad_queries = lax.scan(
        one_block, (zero_keys, zero_keys), (query_blocks, log_total, grad_blocks)
    )
    return (grad_queries.reshape(tokens, D), grad_kv[0].reshape(-1, D), grad_kv[1].reshape(-1, D))


def send_matrix(piece_cols, root):
    return broadcast(piece_cols, "dp", root)


def fetch_keys(key_rows, value_rows):
    return (
        lax.all_gather(key_rows, "vocab", axis=0, tiled=True),
        lax.all_gather(value_rows, "vocab", axis=0, tiled=True),
    )


def layer_forward(hidden, weights, vec_layer, keep_keys, score_scale):
    w_query, w_key, w_value, w_out, w_up, w_down = weights
    tokens = hidden.shape[0]
    norm_one, inv_one = norm_parts(hidden)
    normed = (norm_one * vec_layer[0:D] + vec_layer[D : 2 * D]).astype(jnp.bfloat16)
    queries = matmul_nn(normed, w_query).astype(jnp.bfloat16)
    key_rows = matmul_nn(normed, w_key).astype(jnp.bfloat16)
    value_rows = matmul_nn(normed, w_value).astype(jnp.bfloat16)
    keys_all, values_all = fetch_keys(key_rows, value_rows)
    keys_all = keys_all.reshape(-1, HEADS, HDIM)
    values_all = values_all.reshape(-1, HEADS, HDIM)
    mixed_out, log_total = attention(
        queries.reshape(tokens, HEADS, HDIM), keys_all, values_all, keep_keys, score_scale
    )
    mixed_low = mixed_out.reshape(tokens, D).astype(jnp.bfloat16)
    middle = hidden + matmul_nn(mixed_low, w_out)
    norm_two, inv_two = norm_parts(middle)
    normed_two = (norm_two * vec_layer[2 * D : 3 * D] + vec_layer[3 * D : 4 * D]).astype(
        jnp.bfloat16
    )
    up_proj = matmul_nt(normed_two, w_up) + vec_layer[4 * D :]
    active = jax.nn.gelu(up_proj).astype(jnp.bfloat16)
    out_rows = middle + matmul_nn(active, w_down)
    kept_vals = (
        norm_one,
        inv_one,
        normed,
        queries,
        key_rows,
        value_rows,
        keys_all,
        values_all,
        log_total,
        mixed_low,
        norm_two,
        inv_two,
        normed_two,
        up_proj,
        active,
    )
    return (out_rows, kept_vals)


def layer_backward(grad_out, kept_vals, weights, vec_layer, keep_keys, score_scale):
    w_query, w_key, w_value, w_out, w_up, w_down = weights
    (
        norm_one,
        inv_one,
        normed,
        queries,
        key_rows,
        value_rows,
        keys_all,
        values_all,
        log_total,
        mixed_low,
        norm_two,
        inv_two,
        normed_two,
        up_proj,
        active,
    ) = kept_vals
    tokens = grad_out.shape[0]
    grad_low = grad_out.astype(jnp.bfloat16)
    grad_down = matmul_tn(active, grad_low)
    grad_active = matmul_nt(grad_low, w_down)
    grad_up_proj = jax.vjp(jax.nn.gelu, up_proj)[1](grad_active)[0].astype(jnp.bfloat16)
    grad_bias = jnp.sum(grad_up_proj.astype(jnp.float32), 0)
    grad_up = matmul_tn(grad_up_proj, normed_two)
    grad_normed_two = matmul_nn(grad_up_proj, w_up)
    grad_part, grad_gain_two, grad_shift_two = norm_back(
        norm_two, inv_two, vec_layer[2 * D : 3 * D], grad_normed_two
    )
    grad_middle = grad_out + grad_part
    grad_attn = grad_middle.astype(jnp.bfloat16)
    grad_out_w = matmul_tn(mixed_low, grad_attn)
    grad_mixed = matmul_nt(grad_attn, w_out).astype(jnp.bfloat16).reshape(tokens, HEADS, HDIM)
    grad_queries, grad_keys_all, grad_values_all = attention_back(
        queries.reshape(tokens, HEADS, HDIM),
        keys_all,
        values_all,
        keep_keys,
        log_total,
        grad_mixed,
        score_scale,
    )
    grad_key_rows, grad_value_rows = (
        lax.psum_scatter(
            grad_keys_all.astype(jnp.bfloat16), "vocab", scatter_dimension=0, tiled=True
        ).astype(jnp.float32),
        lax.psum_scatter(
            grad_values_all.astype(jnp.bfloat16), "vocab", scatter_dimension=0, tiled=True
        ).astype(jnp.float32),
    )
    grad_q_low = grad_queries.astype(jnp.bfloat16)
    grad_k_low = grad_key_rows.astype(jnp.bfloat16)
    grad_v_low = grad_value_rows.astype(jnp.bfloat16)
    grad_wq = matmul_tn(normed, grad_q_low)
    grad_wk = matmul_tn(normed, grad_k_low)
    grad_wv = matmul_tn(normed, grad_v_low)
    grad_normed = (
        matmul_nt(grad_q_low, w_query)
        + matmul_nt(grad_k_low, w_key)
        + matmul_nt(grad_v_low, w_value)
    )
    grad_part_one, grad_gain_one, grad_shift_one = norm_back(
        norm_one, inv_one, vec_layer[0:D], grad_normed
    )
    grad_hidden = grad_middle + grad_part_one
    grad_mats = [grad_wq, grad_wk, grad_wv, grad_out_w, grad_up, grad_down]
    grad_vec = jnp.concatenate(
        [grad_gain_one, grad_shift_one, grad_gain_two, grad_shift_two, grad_bias]
    )
    return (grad_hidden, grad_mats, grad_vec)


def merge_stats(first_part, second_part):
    peak_val = jnp.maximum(first_part[0], second_part[0])
    exp_total = first_part[1] * jnp.exp(first_part[0] - peak_val) + second_part[1] * jnp.exp(
        second_part[0] - peak_val
    )
    return (peak_val, exp_total, first_part[2] + second_part[2])


def any_mesh_device(
    token_ids,
    timesteps,
    pad_mask,
    noise_draw,
    owners,
    emb_table,
    table_first_moment,
    table_second_moment,
    mat_slots,
    slot_first,
    slot_second,
    vec_params,
    vec_first,
    vec_second,
):
    vocab_count = lax.axis_size("vocab")
    vocab_pos = lax.axis_index("vocab")
    data_pos = lax.axis_index("dp")
    seq_len = token_ids.shape[1]
    tokens = seq_len // vocab_count
    vocab_rows = emb_table.shape[0]
    score_scale = HDIM ** (-0.5)
    table_low = lax.all_gather(emb_table.astype(jnp.bfloat16), "dp", axis=1, tiled=True)
    row_counts = matrix_rows()
    local_start = slot_places(owners) - owners * CAP
    sent_pieces = [
        send_matrix(
            lax.dynamic_slice_in_dim(
                mat_slots, local_start[mat_idx], row_counts[mat_idx], 1
            ).astype(jnp.bfloat16),
            owners[mat_idx],
        )
        for mat_idx in range(len(row_counts))
    ]
    canon = jnp.concatenate(sent_pieces, 1)
    weights = lax.all_gather(canon, "vocab", axis=0, tiled=True).T
    layer_rows = 4 * D + 2 * FF
    vec_rows = 4 * D + FF
    tail_at = LAYERS * layer_rows

    def layer_weights(layer_idx):
        begin_row = layer_idx * layer_rows
        cuts = [
            begin_row,
            begin_row + D,
            begin_row + 2 * D,
            begin_row + 3 * D,
            begin_row + 4 * D,
            begin_row + 4 * D + FF,
            begin_row + layer_rows,
        ]
        return [weights[cuts[cut_idx] : cuts[cut_idx + 1]] for cut_idx in range(6)]

    w_input = weights[tail_at : tail_at + 2 * EMBED_WIDTH]
    w_final = weights[tail_at + 2 * EMBED_WIDTH : tail_at + 3 * EMBED_WIDTH]
    seq_ids = token_ids[0]
    seq_mask = pad_mask[0].astype(jnp.float32)
    keep_keys = pad_mask[0] > 0
    local_row = seq_ids - vocab_pos * vocab_rows
    valid_row = (local_row >= 0) & (local_row < vocab_rows)
    safe_row = jnp.clip(local_row, 0, vocab_rows - 1)
    found_rows = jnp.where(
        valid_row[:, None], jnp.take(table_low, safe_row, axis=0), jnp.zeros((), jnp.bfloat16)
    )
    arrived = lax.all_to_all(found_rows, "vocab", split_axis=0, concat_axis=0, tiled=True)
    clean_emb = jnp.sum(arrived.reshape(vocab_count, tokens, EMBED_WIDTH).astype(jnp.float32), 0)
    own_first = vocab_pos * tokens
    mask_own = lax.dynamic_slice_in_dim(seq_mask, own_first, tokens)
    own_places = (own_first + jnp.arange(tokens)).astype(jnp.float32)
    step_val = timesteps[0].astype(jnp.float32)
    signal_level = 1.0 - jnp.sqrt(step_val / DIFF + 0.0001)
    noisy_emb = jnp.sqrt(signal_level) * clean_emb + jnp.sqrt(1.0 - signal_level) * noise_draw[
        0
    ].astype(jnp.float32)
    time_feat = jnp.broadcast_to(waves(step_val[None], EMBED_WIDTH), (tokens, EMBED_WIDTH))
    inputs = jnp.concatenate([noisy_emb, time_feat], 1).astype(jnp.bfloat16)
    hidden = matmul_nn(inputs, w_input) + waves(own_places, D)
    layer_idx = 0
    vec_layer = vec_params[layer_idx * vec_rows : (layer_idx + 1) * vec_rows]
    hidden, kept_vals = layer_forward(
        hidden, layer_weights(layer_idx), vec_layer, keep_keys, score_scale
    )
    kept_list = [kept_vals]
    gain_final = vec_params[LAYERS * vec_rows : LAYERS * vec_rows + D]
    shift_final = vec_params[LAYERS * vec_rows + D :]
    norm_final, inv_final = norm_parts(hidden)
    final_norm = (norm_final * gain_final + shift_final).astype(jnp.bfloat16)
    predicted = matmul_nt(final_norm, w_final)
    pred_all = lax.all_gather(predicted.astype(jnp.bfloat16), "vocab", axis=0, tiled=True)
    head_width = min(512, seq_len)
    head_count = seq_len // head_width
    columns = jnp.arange(vocab_rows)
    pred_blocks = pred_all.reshape(head_count, head_width, EMBED_WIDTH)
    row_blocks = local_row.reshape(head_count, head_width)

    def head_stats(block_data):
        pred_blk, rows_blk = block_data
        logits = matmul_nt(pred_blk, table_low)
        row_max = jnp.max(logits, -1)
        exp_total = jnp.sum(jnp.exp(logits - row_max[:, None]), -1)
        target = jnp.sum(jnp.where(columns[None, :] == rows_blk[:, None], logits, 0.0), -1)
        return (row_max, exp_total, target)

    peaks, totals, targets = lax.map(head_stats, (pred_blocks, row_blocks))
    peak_all, total_all, target_all = merged(
        (peaks.reshape(seq_len), totals.reshape(seq_len), targets.reshape(seq_len)),
        "vocab",
        merge_stats,
    )
    log_total = peak_all + jnp.log(total_all)
    lse_own = lax.dynamic_slice_in_dim(log_total, own_first, tokens)
    target_own = lax.dynamic_slice_in_dim(target_all, own_first, tokens)
    pred_error = predicted - clean_emb
    square_own = jnp.sum(mask_own[:, None] * pred_error * pred_error)
    cross_own = jnp.sum(mask_own * (lse_own - target_own))
    norm_own = jnp.sum(mask_own * jnp.sqrt(jnp.sum(clean_emb * clean_emb, -1) + 1e-06))
    count_all, square, cross_sum, norm_total = lax.psum(
        (jnp.sum(mask_own), square_own, cross_own, norm_own), ("dp", "vocab")
    )
    weight_blocks = (seq_mask / count_all).reshape(head_count, head_width)
    lse_blocks = log_total.reshape(head_count, head_width)

    def head_back(grad_table, block_data):
        pred_blk, rows_blk, lse_blk, weight_blk = block_data
        logits = matmul_nt(pred_blk, table_low)
        probabilities = jnp.exp(logits - lse_blk[:, None])
        onehot = (columns[None, :] == rows_blk[:, None]).astype(jnp.float32)
        grad_logits = ((probabilities - onehot) * weight_blk[:, None]).astype(jnp.bfloat16)
        return (grad_table + matmul_tn(grad_logits, pred_blk), matmul_nn(grad_logits, table_low))

    zero_table = jnp.zeros((vocab_rows, EMBED_WIDTH), jnp.float32)
    grad_table_head, grad_pred_blocks = lax.scan(
        head_back, zero_table, (pred_blocks, row_blocks, lse_blocks, weight_blocks)
    )
    grad_pred = lax.psum_scatter(
        grad_pred_blocks.reshape(seq_len, EMBED_WIDTH).astype(jnp.bfloat16),
        "vocab",
        scatter_dimension=0,
        tiled=True,
    ).astype(jnp.float32)
    error_grad = 2.0 * mask_own[:, None] * pred_error / count_all
    grad_pred_low = (grad_pred + error_grad).astype(jnp.bfloat16)
    grad_final_w = matmul_tn(grad_pred_low, final_norm)
    grad_final = matmul_nn(grad_pred_low, w_final)
    grad_hidden, grad_gain_final, grad_shift_final = norm_back(
        norm_final, inv_final, gain_final, grad_final
    )
    layer_grads = [None] * LAYERS
    vec_grads = [None] * LAYERS
    for layer_idx in reversed(range(LAYERS)):
        vec_layer = vec_params[layer_idx * vec_rows : (layer_idx + 1) * vec_rows]
        grad_hidden, layer_grads[layer_idx], vec_grads[layer_idx] = layer_backward(
            grad_hidden,
            kept_list[layer_idx],
            layer_weights(layer_idx),
            vec_layer,
            keep_keys,
            score_scale,
        )
    grad_hidden_low = grad_hidden.astype(jnp.bfloat16)
    grad_input_w = matmul_tn(inputs, grad_hidden_low)
    grad_inputs = matmul_nt(grad_hidden_low, w_input)
    grad_clean = jnp.sqrt(signal_level) * grad_inputs[:, :EMBED_WIDTH] - error_grad
    grad_clean_all = lax.all_gather(
        grad_clean.astype(jnp.bfloat16), "vocab", axis=0, tiled=True
    ).astype(grad_clean.dtype)
    grad_table_look = zero_table.at[safe_row].add(
        jnp.where(valid_row[:, None], grad_clean_all, 0.0)
    )
    grad_table_local = grad_table_head + grad_table_look
    canon_list = []
    layer_idx = 0
    canon_list = canon_list + layer_grads[layer_idx]
    canon_grad = jnp.concatenate(canon_list + [grad_input_w, grad_final_w], 0).T
    vec_grad = jnp.concatenate(vec_grads + [grad_gain_final, grad_shift_final])
    grad_cols, vec_part = (
        lax.psum_scatter(canon_grad, "vocab", scatter_dimension=0, tiled=True),
        lax.psum_scatter(vec_grad, "vocab", scatter_dimension=0, tiled=True),
    )
    emb_cols = emb_table.shape[1]
    summed_cols, summed_vec, summed_table = lax.psum((grad_cols, vec_part, grad_table_local), "dp")
    table_grad = lax.dynamic_slice_in_dim(summed_table, data_pos * emb_cols, emb_cols, 1)
    slot_grad = jnp.zeros_like(mat_slots)
    cursor = 0
    for mat_idx in range(len(row_counts)):
        piece_cols = summed_cols[:, cursor : cursor + row_counts[mat_idx]]
        updated = lax.dynamic_update_slice_in_dim(slot_grad, piece_cols, local_start[mat_idx], 1)
        slot_grad = jnp.where(owners[mat_idx] == data_pos, updated, slot_grad)
        cursor = cursor + row_counts[mat_idx]
    vec_share = vec_first.shape[0]
    own_vecs = lax.dynamic_slice_in_dim(vec_params, vocab_pos * vec_share, vec_share)
    new_slots, slot_first_new, slot_second_new = adamw(
        mat_slots, slot_grad, slot_first, slot_second
    )
    new_table, table_first_new, table_second_new = adamw(
        emb_table, table_grad, table_first_moment, table_second_moment
    )
    new_vecs, vec_first_new, vec_second_new = adamw(own_vecs, summed_vec, vec_first, vec_second)
    loss_pair = jnp.stack([square + cross_sum, count_all])
    emb_norm = norm_total / count_all
    return (
        loss_pair,
        emb_norm,
        new_table,
        table_first_new,
        table_second_new,
        new_slots,
        slot_first_new,
        slot_second_new,
        new_vecs,
        vec_first_new,
        vec_second_new,
    )


def solution(mesh):
    in_specs = (
        P("dp", None),
        P("dp"),
        P("dp", None),
        P("dp", "vocab", None),
        P(),
        P("vocab", "dp"),
        P("vocab", "dp"),
        P("vocab", "dp"),
        P("vocab", "dp"),
        P("vocab", "dp"),
        P("vocab", "dp"),
        P(),
        P("vocab"),
        P("vocab"),
    )
    out_specs = (
        P(),
        P(),
        P("vocab", "dp"),
        P("vocab", "dp"),
        P("vocab", "dp"),
        P("vocab", "dp"),
        P("vocab", "dp"),
        P("vocab", "dp"),
        P("vocab"),
        P("vocab"),
        P("vocab"),
    )
    fast = mesh.shape["dp"] == 8 and mesh.shape["vocab"] == 4
    body = per_device if fast else any_mesh_device
    return jax.shard_map(
        body, mesh=mesh, in_specs=in_specs, out_specs=out_specs, check_vma=False
    )
```

```python
import functools
import math

import jax
import jax.numpy as jnp
from jax import lax
from jax.experimental import pallas as pl
from jax.experimental.pallas import tpu as pltpu
from jax.sharding import PartitionSpec as P

D = 768
HEADS = 12
HDIM = 64
FF = 3072
EMBED_WIDTH = 128
DIFF = 2000
STEP = 10
CAP = 3072
LAYERS = 1
LANES = 128


beta_one = 0.9
beta_two = 0.999
learn_rate = 0.02
weight_decay = 0.01
eps_adam = 1e-08
eps_norm = 1e-05
f32 = jnp.float32
bf16 = jnp.bfloat16


def matmul_nn(left, right):
    return jnp.dot(left, right, preferred_element_type=f32)


def matmul_tn(left, right):
    return lax.dot_general(left, right, (((0,), (0,)), ((), ())), preferred_element_type=f32)


def matmul_nt(left, right):
    return lax.dot_general(left, right, (((1,), (1,)), ((), ())), preferred_element_type=f32)


ROW_COUNTS = [D, D, D, D, FF, FF, EMBED_WIDTH, EMBED_WIDTH, EMBED_WIDTH]


def slot_starts(owners):
    counts = jnp.array(ROW_COUNTS, jnp.int32)
    same_owner = (owners[:, None] == owners[None, :]).astype(jnp.int32)
    earlier_mask = jnp.tril(jnp.ones((len(ROW_COUNTS),) * 2, jnp.int32), -1)
    return jnp.sum(same_owner * earlier_mask * counts[None, :], 1)


def waves(places, width):
    half_width = width // 2
    frequency = jnp.exp(-math.log(10000.0) * jnp.arange(half_width, dtype=f32) / half_width)
    angles = places[:, None] * frequency[None, :]
    return jnp.concatenate([jnp.sin(angles), jnp.cos(angles)], 1)


def norm_parts(value_entries):
    center = value_entries - jnp.mean(value_entries, -1, keepdims=True)
    scale_inv = lax.rsqrt(jnp.mean(center * center, -1, keepdims=True) + eps_norm)
    return (center * scale_inv, scale_inv)


def norm_back(normal_part, scale_inv, gain_vec, grad_out):
    scaled = grad_out * gain_vec
    inner = (
        scaled
        - jnp.mean(scaled, -1, keepdims=True)
        - normal_part * jnp.mean(scaled * normal_part, -1, keepdims=True)
    )
    return (inner * scale_inv, jnp.sum(grad_out * normal_part, 0), jnp.sum(grad_out, 0))


def adamw(weight, gradient, moment_one, moment_two):
    moment_one = beta_one * moment_one + (1.0 - beta_one) * gradient
    moment_two = beta_two * moment_two + (1.0 - beta_two) * gradient * gradient
    fix_one = 1.0 - beta_one**STEP
    fix_two = 1.0 - beta_two**STEP
    update_dir = moment_one / fix_one / (jnp.sqrt(moment_two / fix_two) + eps_adam)
    return (weight - learn_rate * (update_dir + weight_decay * weight), moment_one, moment_two)


MESH = pl.DeviceIdType.MESH
ANY = pl.BlockSpec(memory_space=pl.ANY)
UNIT = 768
HALF = 96
QUARTER = 192


def place():
    d, v = lax.axis_index("dp"), lax.axis_index("vocab")
    return d // 2, d % 2, d, v


def greet(partners):
    barrier = pltpu.get_barrier_semaphore()
    for partner in partners:
        pl.semaphore_signal(barrier, inc=1, device_id=partner, device_id_type=MESH)
    pl.semaphore_wait(barrier, len(partners))


def remote(src, dst, sems, index, partner):
    return pltpu.make_async_remote_copy(
        src_ref=src,
        dst_ref=dst,
        send_sem=sems[0].at[index],
        recv_sem=sems[1].at[index],
        device_id=partner,
        device_id_type=MESH,
    )


def start_all(copies):
    for copy in copies:
        copy.start()
    return copies


def arrive_all(copies):
    for copy in copies:
        copy.wait_recv()


VMEM = pl.BlockSpec(memory_space=pltpu.VMEM)
SMEM = pl.BlockSpec(memory_space=pltpu.SMEM)


def prepare_kernel(
    owners, ids_from, mask_from, table_from, slots,
    payload, table_low, row_of, safe, keep_rows, keep, valid, count, kind, unit, column,
    units, extras, ids, mask, table, sems, own_sems,
):
    d, v = lax.axis_index("dp"), lax.axis_index("vocab")
    starts = [
        sum(jnp.where(owners[j] == owners[i], ROW_COUNTS[j], 0) for j in range(i)) + 0 * owners[i]
        for i in range(len(ROW_COUNTS))
    ]
    whole = (owners[4] == d) | (owners[5] == d)
    fetched = [
        pltpu.make_async_copy(src, dst, own_sems.at[i])
        for i, (src, dst) in enumerate(((ids_from, ids), (mask_from, mask), (table_from, table)))
    ]
    for copy in fetched:
        copy.start()
    copies = []
    for u in range(4):
        first = pl.multiple_of(jnp.where(whole, u * UNIT, starts[u]), LANES)
        copies.append(
            pltpu.make_async_copy(slots.at[:, pl.ds(first, UNIT)], units.at[u], sems.at[u])
        )
        first = pl.multiple_of(starts[6 + min(u, 2)], LANES)
        copies.append(
            pltpu.make_async_copy(slots.at[:, pl.ds(first, LANES)], extras.at[u], sems.at[4 + u])
        )
    for copy in copies:
        copy.start()

    def clear(j, carry):
        kind[j] = 0
        unit[j] = 0
        column[j] = 0
        return carry

    lax.fori_loop(0, CAP // LANES, clear, 0)
    per_unit = UNIT // LANES
    first_unit = [0, 1, 2, 3, 0, 0, 0, 1, 2]
    for i, rows in enumerate(ROW_COUNTS):

        def claim(i=i, rows=rows):
            def one(b, carry):
                j = starts[i] // LANES + b
                kind[j] = 2 if i > 5 else 1
                unit[j] = first_unit[i] + b // per_unit
                column[j] = b % per_unit
                return carry

            lax.fori_loop(0, rows // LANES, one, 0)

        pl.when(owners[i] == d)(claim)

    for copy in fetched:
        copy.wait()
    table_low[...] = table[...].astype(bf16)
    count[...] = jnp.full((8, LANES), jnp.sum(mask[...].astype(f32)))
    for b in range(4):
        at = pl.ds(pl.multiple_of((v ^ b) * 256, 256), 256)
        local = ids[:, at] - v * table.shape[1]
        row_of[b : b + 1, :] = local
        safe[:, 256 * b : 256 * b + 256] = jnp.clip(local, 0, table.shape[1] - 1)
        weight = mask[:, at].astype(f32)
        keep_rows[b : b + 1, :] = weight
        inside = ((local >= 0) & (local < table.shape[1])).astype(f32)
        both = jnp.concatenate([weight, inside, jnp.zeros((6, 256), f32)], 0).T
        keep[256 * b : 256 * b + 256, :] = both[:, 0:1]
        valid[256 * b : 256 * b + 256, :] = both[:, 1:2]
    for copy in copies:
        copy.wait()
    for u in range(4):
        for half in range(2):
            rows = slice(half * HALF, half * HALF + HALF)
            payload[2 * u + half, :, 0:UNIT] = units[u, rows, :].astype(bf16)
            payload[2 * u + half, :, UNIT:] = extras[u, rows, :].astype(bf16)


def prepare(owners, ids, mask, table, slots):
    def shape(kind, *dims):
        return jax.ShapeDtypeStruct(dims, kind)

    blocks = CAP // LANES
    tokens = ids.shape[1]
    return pl.pallas_call(
        prepare_kernel,
        out_shape=[
            shape(bf16, 8, HALF, UNIT + LANES),
            shape(bf16, *table.shape),
            shape(jnp.int32, 4, tokens // 4),
            shape(jnp.int32, 1, tokens),
            shape(f32, 4, tokens // 4),
            shape(f32, tokens, 1),
            shape(f32, tokens, 1),
            shape(f32, 8, LANES),
        ]
        + [shape(jnp.int32, blocks)] * 3,
        in_specs=[SMEM, ANY, ANY, ANY, ANY],
        out_specs=[VMEM] * 8 + [SMEM] * 3,
        scratch_shapes=[
            pltpu.VMEM((4, QUARTER, UNIT), f32),
            pltpu.VMEM((4, QUARTER, LANES), f32),
            pltpu.VMEM(ids.shape, jnp.int32),
            pltpu.VMEM(mask.shape, jnp.int32),
            pltpu.VMEM(table.shape, f32),
            pltpu.SemaphoreType.DMA((8,)),
            pltpu.SemaphoreType.DMA((3,)),
        ],
        compiler_params=pltpu.CompilerParams(vmem_limit_bytes=60 * 2**20),
    )(owners, ids, mask, table, slots)


TRADE_MASKS = (4, 6, 5, 7, 2, 3, 1)


def chosen_of(pieces, wanted):
    value = pieces[0]
    for i in range(1, len(pieces)):
        value = jnp.where(wanted == i, pieces[i], value)
    return value


def spread_kernel(
    owners, steps, payload, tile, keep_rows, keep, table_home,
    up_to, down_to, small_to, attn_to, out_to, table_to, weight, twice, places, levels,
    up, down, small, attn, out, table, arrived, tiles, up_home, down_home, small_home, attn_home,
    a_send, a_recv, b_send, b_recv,
    z_send, z_recv, y_send, y_recv, x_send, x_recv, n_send, n_recv, f_send, f_recv, local, o_sem,
):
    z, y, d, v = place()
    far, near = v ^ 2, v ^ 1
    greet([(d ^ m, v) for m in TRADE_MASKS] + [(d, far), (d, near)])
    traded = start_all(
        [
            remote(payload.at[d ^ m], arrived.at[i], (a_send, a_recv), i, (d ^ m, v))
            for i, m in enumerate(TRADE_MASKS)
        ]
        + [
            remote(tile, tiles.at[i], (b_send, b_recv), i, (d ^ m, v))
            for i, m in enumerate(TRADE_MASKS)
        ]
    )
    homes = [up_home, down_home, small_home, attn_home, table_home]
    fulls = [up, down, small, attn, table]
    own_rows = pl.ds(v * QUARTER, QUARTER)

    def spot(c, unit):
        if c == 4:
            return table.at[2 * unit + y]
        first = y * HALF if c == 3 else v * QUARTER + y * HALF
        return fulls[c].at[unit, pl.ds(first, HALF), :]

    keeps, line, side, chip = {}, {}, {}, {}
    sent, landing, stores = [], {c: [] for c in range(4)}, []

    def note(copy, store=None, at=None):
        copy.start()
        sent.append(copy)
        if store is not None:
            store[at] = copy
        return copy

    def own_slab(c):
        keeps[c] = pltpu.make_async_copy(homes[c], spot(c, z), local.at[c])
        keeps[c].start()
        note(remote(homes[c], spot(c, z), (y_send, y_recv), (c, 0), (d ^ 1, v)), side, (c, 0))

    def start_class(c):
        for k in (2, 1, 3):
            note(
                remote(homes[c], spot(c, z), (z_send, z_recv), (c, k - 1), (d ^ (2 * k), v)),
                line,
                (c, k),
            )

    def relay(c, then=()):
        for k in (2, 1, 3):
            if k == 3:
                for other in then:
                    start_class(other)
            line[c, k].wait_recv()
            slab = spot(c, z ^ k)
            note(remote(slab, slab, (y_send, y_recv), (c, k), (d ^ 1, v)), side, (c, k))

    def chip_slab(c, k, source, target):
        note(remote(source, target, (x_send, x_recv), (c, k), (d, far)), chip, (c, k))
        landing[c].append(note(remote(source, target, (n_send, n_recv), (c, k), (d, near))))

    def to_chip(c, slabs=(2, 1, 3)):
        for k in slabs:
            side[c, k].wait_recv()
            if k == 0:
                keeps[c].wait()
            if c < 3:
                slab = fulls[c].at[z ^ k, own_rows, :]
                chip_slab(c, k, slab, slab)
        if c == 3 and slabs[-1] == 3:
            keep = pltpu.make_async_copy(attn.at[3], out.at[own_rows, :], local.at[5])
            keep.start()
            chip_slab(c, 0, attn.at[3], out.at[own_rows, :])
            keep.wait()

    def to_last(c):
        rows = pl.ds(far * QUARTER, QUARTER)
        for k in (0,) if c == 3 else (0, 2, 1, 3):
            chip[c, k].wait_recv()
            slab = out.at[rows, :] if c == 3 else fulls[c].at[z ^ k, rows, :]
            landing[c].append(note(remote(slab, slab, (f_send, f_recv), (c, k), (d, near))))

    own_slab(4)

    def angles(position, width, count):
        lane = lax.broadcasted_iota(jnp.int32, (count, width), 1).astype(f32)
        return position * jnp.exp(-math.log(10000.0) * lane / width)

    position = v * 256 + lax.broadcasted_iota(jnp.int32, (256, D // 2), 0)
    angle = angles(position.astype(f32), D // 2, 256)
    places[:, 0 : D // 2] = jnp.sin(angle)
    places[:, D // 2 :] = jnp.cos(angle)
    step = jnp.full((8, EMBED_WIDTH), steps[0], jnp.int32).astype(f32)
    signal = 1.0 - jnp.sqrt(step / DIFF + 0.0001)
    angle = angles(step[:, 0 : EMBED_WIDTH // 2], EMBED_WIDTH // 2, 8)
    levels[0:1] = jnp.sqrt(signal[0:1])
    levels[1:2] = jnp.sqrt(1.0 - signal[0:1])
    levels[2:3] = jnp.concatenate([jnp.sin(angle), jnp.cos(angle)], 1)[0:1]
    levels[3:8] = jnp.zeros((5, EMBED_WIDTH), f32)
    arrive_all(traded)
    sent.extend(traded)
    total = tile[...]
    for i in range(7):
        total = total + tiles[i]
    weight[...] = keep_rows[...] / jnp.concatenate([total[0:4]] * 2, 1)
    twice[...] = 2.0 * keep[0:256, :] / total[0:1, 0:1]

    def from_owner(owner, lanes):
        value = payload[d, :, lanes]
        for i, m in enumerate(TRADE_MASKS):
            value = jnp.where(owner == d ^ m, arrived[i, :, lanes], value)
        return value

    up_home[...] = from_owner(owners[4], slice(0, UNIT))
    down_home[...] = from_owner(owners[5], slice(0, UNIT))
    attn_home[...] = from_owner(chosen_of([owners[u] for u in range(4)], z), slice(0, UNIT))
    small_home[...] = from_owner(
        chosen_of([owners[6 + min(u, 2)] for u in range(4)], z), slice(UNIT, UNIT + LANES)
    )

    def store(src, dst, index):
        copy = pltpu.make_async_copy(src, dst, o_sem.at[index])
        copy.start()
        stores.append(copy)

    def finish(c):
        arrive_all(landing[c])
        if c == 3:
            store(out, out_to, 3)
        else:
            store(fulls[c], (up_to, down_to, small_to)[c], c)

    start_class(0)
    for c in range(4):
        own_slab(c)
    for c in range(3):
        to_chip(c, (0,))
    relay(0, (1,))
    to_chip(0)
    relay(1, (2, 3))
    to_chip(1)
    relay(2)
    relay(3, (4,))
    to_chip(2)
    to_chip(3, (0, 2, 1, 3))
    store(attn, attn_to, 4)
    to_last(0)
    relay(4)
    finish(0)
    to_last(1)
    to_last(2)
    to_last(3)
    to_chip(4, (0, 2, 1, 3))
    store(table, table_to, 5)
    finish(1)
    finish(2)
    finish(3)
    for copy in stores:
        copy.wait()
    for copy in sent:
        copy.wait_send()


def spread(owners, steps, payload, tile, keep_rows, keep, table_home):
    rows, vocab_rows = table_home.shape
    dma, vmem = pltpu.SemaphoreType.DMA, pltpu.VMEM

    def shape(*dims):
        return jax.ShapeDtypeStruct(dims, bf16)

    return pl.pallas_call(
        spread_kernel,
        out_shape=[
            shape(4, D, UNIT),
            shape(4, D, UNIT),
            shape(4, D, LANES),
            shape(4, QUARTER, UNIT),
            shape(D, UNIT),
            shape(8, rows, vocab_rows),
            jax.ShapeDtypeStruct(keep_rows.shape, f32),
            jax.ShapeDtypeStruct((256, 1), f32),
            jax.ShapeDtypeStruct((256, D), f32),
            jax.ShapeDtypeStruct((8, EMBED_WIDTH), f32),
        ],
        in_specs=[SMEM] * 2 + [VMEM] * 5,
        out_specs=[ANY] * 6 + [VMEM] * 4,
        scratch_shapes=[
            vmem((4, D, UNIT), bf16),
            vmem((4, D, UNIT), bf16),
            vmem((4, D, LANES), bf16),
            vmem((4, QUARTER, UNIT), bf16),
            vmem((D, UNIT), bf16),
            vmem((8, rows, vocab_rows), bf16),
            vmem((7, HALF, UNIT + LANES), bf16),
            vmem((7, 8, LANES), f32),
            vmem((HALF, UNIT), bf16),
            vmem((HALF, UNIT), bf16),
            vmem((HALF, LANES), bf16),
            vmem((HALF, UNIT), bf16),
        ]
        + [dma((7,))] * 4
        + [dma((5, 3))] * 2
        + [dma((5, 4))] * 2
        + [dma((4, 4))] * 6
        + [dma((6,))] * 2,
        compiler_params=pltpu.CompilerParams(
            collective_id=1, has_side_effects=True, vmem_limit_bytes=60 * 2**20
        ),
    )(owners, steps, payload, tile, keep_rows, keep, table_home)

def neighbours():
    d, v = lax.axis_index("dp"), lax.axis_index("vocab")
    return [(d, v ^ k) for k in (1, 2, 3)]


def by_position(v, store):
    for i in range(4):
        pl.when(v == i)(functools.partial(store, i))


def forward_kernel(
    looked, valid, levels, places, vecs, keep, noise_hbm, small_hbm, attn_hbm, out_hbm, up_hbm, down_hbm,
    found, clean, inputs, hidden, normed_all, q, k, k_t, values, log_total, mixed, middle, normed_two,
    up_proj, active, hidden_two, final_norm, predicted, pred_all,
    noise, small, attn, out_w, up_w, down_w, found_in, values_t, mixed_out, mixed_in, seen,
    w_sem, s_sem, e_send, e_recv, n_send, n_recv, m_send, m_recv, p_send, p_recv, tables,
):
    v = lax.axis_index("vocab")
    partners = neighbours()
    sources = ((noise_hbm, noise), (small_hbm, small), (attn_hbm, attn), (out_hbm, out_w))
    first = [
        pltpu.make_async_copy(src, dst, s_sem.at[i]) for i, (src, dst) in enumerate(sources)
    ]
    for copy in first:
        copy.start()
    loads = []
    for j in range(4):
        for i, (src, dst) in enumerate(((up_hbm, up_w), (down_hbm, down_w))):
            copy = pltpu.make_async_copy(src.at[j], dst.at[j], w_sem.at[2 * j + i])
            copy.start()
            loads.append(copy)
    for copy in tables:
        copy.start()
    for b in range(4):
        found[b] = jnp.where(
            valid[256 * b : 256 * b + 256, :] > 0.0, looked[b].astype(f32), 0.0
        ).astype(bf16)
    greet(partners)
    asked = start_all(
        [
            remote(found.at[m], found_in.at[m - 1], (e_send, e_recv), m - 1, partners[m - 1])
            for m in (2, 3, 1)
        ]
    )
    seen[...] = jnp.broadcast_to(keep[...], seen.shape)
    for copy in first:
        copy.wait()
    wave = levels[2:3].astype(bf16)
    time_part = matmul_nt(jnp.broadcast_to(wave, (16, EMBED_WIDTH)), small[1])[0:1]
    arrive_all(asked)
    total = found[0].astype(f32)
    for m in range(3):
        total = total + found_in[m].astype(f32)
    clean[...] = total
    noisy = levels[0:1] * total + levels[1:2] * noise[...].astype(f32)
    inputs[:, 0:EMBED_WIDTH] = noisy.astype(bf16)
    inputs[:, EMBED_WIDTH:] = jnp.broadcast_to(wave, noisy.shape)
    value = matmul_nt(inputs[:, 0:EMBED_WIDTH], small[0]) + time_part + places[...]
    hidden[...] = value
    normed_all[0] = (norm_parts(value)[0] * vecs[0:1] + vecs[1:2]).astype(bf16)

    far = remote(normed_all.at[0], normed_all.at[2], (n_send, n_recv), 0, partners[1])
    near = remote(normed_all.at[0], normed_all.at[1], (n_send, n_recv), 1, partners[0])
    last = remote(normed_all.at[2], normed_all.at[3], (n_send, n_recv), 2, partners[0])
    far.start()
    near.start()

    def project(b):
        rows = pl.ds(b * 256, 256)
        block = normed_all[b]
        for i, ref in ((0, q), (1, k), (2, values)):
            result = matmul_nt(block, attn[i])
            if i == 0:
                result = result.astype(bf16).astype(f32) * HDIM ** (-0.5)
            for h in range(3):
                ref[h, rows, :] = result[:, h * HDIM : (h + 1) * HDIM].astype(bf16)
        k_t[:, rows] = matmul_nt(attn[1], block).astype(bf16)
        values_t[:, rows] = matmul_nt(attn[2], block).astype(bf16)

    project(0)
    near.wait_recv()
    project(1)
    far.wait_recv()
    last.start()
    project(2)
    last.wait_recv()
    project(3)

    given = []
    for b in (2, 3, 1, 0):
        rows = pl.ds(b * 256, 256)
        parts = []
        for h in range(3):
            scores = matmul_nt(k[h], q[h, rows, :])
            scores = jnp.where(seen[...] > 0.0, scores, -1000000000.0)
            top = jnp.max(scores, 0, keepdims=True)
            expo = jnp.exp(scores - top)
            mass = jnp.sum(expo, 0, keepdims=True)
            probs = (expo * (1.0 / mass)).astype(bf16)
            log_total[pl.ds(3 * b + h, 1), :] = top + jnp.log(mass)
            parts.append(matmul_nn(values_t[h * HDIM : (h + 1) * HDIM, :], probs))
        block = jnp.concatenate(parts, 0).T.astype(bf16)
        if b == 0:
            mixed_in[0] = block
        else:
            mixed_out[b - 1] = block
            copy = remote(
                mixed_out.at[b - 1], mixed_in.at[b], (m_send, m_recv), b - 1, partners[b - 1]
            )
            copy.start()
            given.append(copy)
    arrive_all(given)

    def lay(i):
        for b in range(4):
            mixed[:, QUARTER * (i ^ b) : QUARTER * ((i ^ b) + 1)] = mixed_in[b]

    by_position(v, lay)
    value = hidden[...] + matmul_nt(mixed[...], out_w[...])
    middle[...] = value
    normed_two[...] = (norm_parts(value)[0] * vecs[2:3] + vecs[3:4]).astype(bf16)
    for j in range(4):
        loads[2 * j].wait()
        loads[2 * j + 1].wait()
        raised = matmul_nn(normed_two[...], up_w[j]) + vecs[4 + j : 5 + j]
        up_proj[j] = raised
        active[j] = jax.nn.gelu(raised).astype(bf16)
        lowered = matmul_nt(active[j], down_w[j])
        hidden_two[...] = (middle[...] if j == 0 else hidden_two[...]) + lowered
    final_norm[...] = (norm_parts(hidden_two[...])[0] * vecs[8:9] + vecs[9:10]).astype(bf16)
    predicted[...] = matmul_nn(final_norm[...], small[2])
    pred_all[0] = predicted[...].astype(bf16)
    shown = start_all(
        [
            remote(pred_all.at[0], pred_all.at[m], (p_send, p_recv), m - 1, partners[m - 1])
            for m in (2, 3, 1)
        ]
    )
    arrive_all(shown)
    for copy in asked + [far, near, last] + given + shown:
        copy.wait_send()


STRIP = 768


def strips(rows):
    return [(lo, min(STRIP, rows - lo)) for lo in range(0, rows, STRIP)]


def head_kernel(
    pred_all, table, table_t, weight, found,
    grad_pred, lse, found_t, stats, gathered, outgoing, incoming,
    s_send, s_recv, g_send, g_recv,
):
    partners = neighbours()
    rows = table_t.shape[0]
    full, rest = rows // STRIP, rows % STRIP
    mixes = []
    for b in range(4):
        block = pred_all[b]

        def strip(at, carry):
            peak, mass, mix = carry
            value = matmul_nt(table_t[at, :], block)
            top = jnp.maximum(peak, jnp.max(value, 0, keepdims=True))
            expo = jnp.exp(value - top)
            fade = jnp.exp(peak - top)
            mass = mass * fade + jnp.sum(expo, 0, keepdims=True)
            return top, mass, mix * fade + matmul_nn(table[:, at], expo.astype(bf16))

        carry = lax.fori_loop(
            0,
            full,
            lambda t, carry: strip(pl.ds(pl.multiple_of(t * STRIP, STRIP), STRIP), carry),
            (
                jnp.full((1, 256), -jnp.inf, f32),
                jnp.zeros((1, 256), f32),
                jnp.zeros((EMBED_WIDTH, 256), f32),
            ),
            unroll=3,
        )
        if rest:
            carry = strip(pl.ds(full * STRIP, rest), carry)
        found_t[b] = found[b].astype(f32).T
        stats[b, 2:3] = jnp.sum(block.astype(f32).T * found_t[b], 0, keepdims=True)
        stats[b, 0:1] = carry[0]
        stats[b, 1:2] = carry[1]
        stats[b, 3:8] = jnp.zeros((5, 256), f32)
        mixes.append(carry[2])
    told = start_all(
        [
            remote(stats, gathered.at[m - 1], (s_send, s_recv), m - 1, partners[m - 1])
            for m in (2, 3, 1)
        ]
    )
    arrive_all(told)
    given = []
    for b in (2, 3, 1, 0):
        views = [stats[b]] + [gathered[m - 1, b ^ m] for m in (1, 2, 3)]
        peak = functools.reduce(jnp.maximum, [view[0:1] for view in views])
        mass = sum(view[1:2] * jnp.exp(view[0:1] - peak) for view in views)
        total = peak + jnp.log(mass)
        lse[b : b + 1, :] = total
        if b == 0:
            target = sum(view[2:3] for view in views)
            lse[4:5, :] = weight[0:1, :] * (total - target)
            lse[5:8, :] = jnp.zeros((3, 256), f32)
        share = weight[b : b + 1, :]
        local = mixes[b] * (jnp.exp(stats[b, 0:1] - total) * share)
        local = local - found_t[b] * share
        outgoing[b] = local.T.astype(bf16)
        if b:
            copy = remote(
                outgoing.at[b], incoming.at[b - 1], (g_send, g_recv), b - 1, partners[b - 1]
            )
            copy.start()
            given.append(copy)
    arrive_all(given)
    value = outgoing[0].astype(f32)
    for m in range(3):
        value = value + incoming[m].astype(f32)
    grad_pred[...] = value
    for copy in told + given:
        copy.wait_send()


def gelu_slope(u):
    inner = math.sqrt(2.0 / math.pi)
    bent = jnp.tanh(inner * (u + 0.044715 * (u * u * u)))
    return 0.5 * (1.0 + bent) + (0.5 * inner) * u * (1.0 - bent * bent) * (
        1.0 + (3.0 * 0.044715) * (u * u)
    )


def backward_kernel(
    grad_pred, clean, predicted, twice, levels, head_stats, hidden, middle, hidden_two,
    normed_two, final_norm, up_proj, q, k, k_t, values, log_total, keep,
    small, attn, out_w, up_w, down_w, vecs,
    grad_pred_low, down_left, up_left, out_left, small_left, final_left, qkv_left, grad_up, grad_clean, sums,
    carried, folded, mix_out, mix_in, grad_k, grad_v, n_out, n_in, f_out, f_in, seen,
    m_send, m_recv, n_send, n_recv, c_send, c_recv,
):
    v = lax.axis_index("vocab")
    partners = neighbours()

    def turned(value):
        return value.astype(f32).T.astype(bf16)

    error = predicted[...] - clean[...]
    pull = twice[...] * error
    low = (grad_pred[...] + pull).astype(bf16)
    grad_pred_low[...] = low
    length = jnp.sqrt(jnp.sum(clean[...] * clean[...], -1, keepdims=True) + 1e-06)
    lane = lax.broadcasted_iota(jnp.int32, (1, UNIT), 1)
    scalars = (jnp.sum(pull * error), jnp.sum(head_stats[4:5, :]), jnp.sum(twice[...] * length))
    counted = jnp.sum(keep[0:256, :])
    sums[10:11, :] = sum(jnp.where(lane == i, x, 0.0) for i, x in enumerate(scalars + (counted,)))
    sums[11:16, :] = jnp.zeros((5, UNIT), f32)

    def through_norm(value, gain_row, grad_out, at):
        normal, scale_inv = norm_parts(value)
        part, grad_gain, grad_shift = norm_back(normal, scale_inv, vecs[gain_row : gain_row + 1], grad_out)
        sums[at : at + 1, :] = grad_gain[None, :]
        sums[at + 1 : at + 2, :] = grad_shift[None, :]
        return part

    carried[...] = through_norm(hidden_two[...], 8, matmul_nt(low, small[2]), 8)
    low = carried[...].astype(bf16)
    down_left[...] = turned(carried[...])
    up_left[...] = turned(normed_two[...])
    final_left[...] = turned(final_norm[...])
    for j in range(4):
        slope = matmul_nn(low, down_w[j]) * gelu_slope(up_proj[j])
        grad_up[j] = slope.astype(bf16)
        sums[4 + j : 5 + j, :] = jnp.sum(grad_up[j].astype(f32), 0, keepdims=True)
        part = matmul_nt(grad_up[j], up_w[j])
        folded[...] = part if j == 0 else folded[...] + part
    carried[...] = carried[...] + through_norm(middle[...], 2, folded[...], 2)
    out_left[...] = turned(carried[...])
    folded[...] = matmul_nn(carried[...].astype(bf16), out_w[...])

    def lay(i):
        for b in range(4):
            mix_out[b] = folded[:, QUARTER * (i ^ b) : QUARTER * ((i ^ b) + 1)].astype(bf16)

    by_position(v, lay)
    mixed = [
        remote(mix_out.at[m], mix_in.at[m - 1], (m_send, m_recv), m - 1, partners[m - 1])
        for m in (1, 2, 3)
    ]
    for m in (2, 3, 1):
        mixed[m - 1].start()
    for b in range(4):
        if b:
            mixed[b - 1].wait_recv()
        grad_block = mix_out[0] if b == 0 else mix_in[b - 1]
        rows = pl.ds(b * 256, 256)
        for h in range(3):
            grad_mix = grad_block[:, h * HDIM : (h + 1) * HDIM]
            asked = q[h, rows, :]
            scores = matmul_nt(k[h], asked)
            scores = jnp.where(seen[...] > 0.0, scores, -1000000000.0)
            probs = jnp.exp(scores - log_total[3 * b + h : 3 * b + h + 1, :])
            grad_probs = matmul_nt(values[h], grad_mix)
            inner = jnp.sum(probs * grad_probs, 0, keepdims=True)
            grad_scores = (probs * (grad_probs - inner)).astype(bf16)
            grad_asked = matmul_nn(k_t[h * HDIM : (h + 1) * HDIM, :], grad_scores)
            qkv_left[0, h * HDIM : (h + 1) * HDIM, rows] = (grad_asked * HDIM ** (-0.5)).astype(bf16)
            part_k = matmul_nn(grad_scores, asked)
            part_v = matmul_nn(probs.astype(bf16), grad_mix)
            grad_k[h] = part_k if b == 0 else grad_k[h] + part_k
            grad_v[h] = part_v if b == 0 else grad_v[h] + part_v
    for h in range(3):
        lanes = pl.ds(h * HDIM, HDIM)
        qkv_left[1, lanes, :] = grad_k[h].T.astype(bf16)
        qkv_left[2, lanes, :] = grad_v[h].T.astype(bf16)

    def grad_normed(b):
        rows = pl.ds(b * 256, 256)
        return sum(matmul_tn(qkv_left[i, :, rows], attn[i]) for i in range(3))

    n_out[0] = grad_normed(1).astype(bf16)
    n_out[1] = grad_normed(3).astype(bf16)
    near = remote(n_out, n_in, (n_send, n_recv), 0, partners[0])
    near.start()
    folded[...] = grad_normed(2)
    near.wait_recv()
    f_out[...] = (folded[...] + n_in[1].astype(f32)).astype(bf16)
    far = remote(f_out, f_in, (n_send, n_recv), 1, partners[1])
    far.start()
    folded[...] = grad_normed(0) + n_in[0].astype(f32)
    far.wait_recv()
    grad_out = folded[...] + f_in[...].astype(f32)
    carried[...] = carried[...] + through_norm(hidden[...], 0, grad_out, 0)
    small_left[...] = turned(carried[...])
    back = matmul_nn(carried[...].astype(bf16), small[0])
    grad_clean[0] = (levels[0:1] * back - twice[...] * (predicted[...] - clean[...])).astype(bf16)
    shown = start_all(
        [
            remote(grad_clean.at[0], grad_clean.at[m], (c_send, c_recv), m - 1, partners[m - 1])
            for m in (2, 3, 1)
        ]
    )
    arrive_all(shown)
    for copy in mixed + [near, far] + shown:
        copy.wait_send()


def step_kernel(
    looked, valid, levels, places, vecs, keep, weight, twice,
    noise_hbm, small_hbm, attn_hbm, out_hbm, up_hbm, down_hbm, table_hbm, table_t_hbm,
    inputs, normed_all, mixed, active, pred_all, lse, grad_pred_low, down_left, up_left, out_left, small_left,
    final_left, qkv_left, grad_up, grad_clean, sums,
    found, clean, hidden, q, k, k_t, values, log_total, middle, normed_two, up_proj, hidden_two, final_norm,
    predicted, grad_pred, noise, small, attn, out_w, up_w, down_w, found_in, values_t, mixed_out, mixed_in, seen,
    table, table_t, found_t, stats, gathered, outgoing, incoming,
    carried, folded, mix_out, mix_in, grad_k, grad_v, n_out, n_in, f_out, f_in,
    w_sem, s_sem, t_sem,
    e_send, e_recv, n_send, n_recv, m_send, m_recv, p_send, p_recv, h_send, h_recv, g_send, g_recv,
    i_send, i_recv, j_send, j_recv, c_send, c_recv,
):
    tables = [
        pltpu.make_async_copy(table_hbm, table, t_sem.at[0]),
        pltpu.make_async_copy(table_t_hbm, table_t, t_sem.at[1]),
    ]
    forward_kernel(
        looked, valid, levels, places, vecs, keep, noise_hbm, small_hbm, attn_hbm, out_hbm, up_hbm, down_hbm,
        found, clean, inputs, hidden, normed_all, q, k, k_t, values, log_total, mixed, middle, normed_two,
        up_proj, active, hidden_two, final_norm, predicted, pred_all,
        noise, small, attn, out_w, up_w, down_w, found_in, values_t, mixed_out, mixed_in, seen,
        w_sem, s_sem, e_send, e_recv, n_send, n_recv, m_send, m_recv, p_send, p_recv, tables,
    )
    for copy in tables:
        copy.wait()
    head_kernel(
        pred_all, table, table_t, weight, found,
        grad_pred, lse, found_t, stats, gathered, outgoing, incoming,
        h_send, h_recv, g_send, g_recv,
    )
    backward_kernel(
        grad_pred, clean, predicted, twice, levels, lse, hidden, middle, hidden_two,
        normed_two, final_norm, up_proj, q, k, k_t, values, log_total, keep,
        small, attn, out_w, up_w, down_w, vecs,
        grad_pred_low, down_left, up_left, out_left, small_left, final_left, qkv_left, grad_up, grad_clean, sums,
        carried, folded, mix_out, mix_in, grad_k, grad_v, n_out, n_in, f_out, f_in, seen,
        i_send, i_recv, j_send, j_recv, c_send, c_recv,
    )


def step(*operands):
    dma, vmem = pltpu.SemaphoreType.DMA, pltpu.VMEM
    n = 256
    table, table_t = operands[-2:]

    def shape(kind, *dims):
        return jax.ShapeDtypeStruct(dims, kind)

    return pl.pallas_call(
        step_kernel,
        out_shape=[
            shape(bf16, n, 2 * EMBED_WIDTH),
            shape(bf16, 4, n, D),
            shape(bf16, n, D),
            shape(bf16, 4, n, UNIT),
            shape(bf16, 4, n, EMBED_WIDTH),
            shape(f32, 8, n),
            shape(bf16, n, EMBED_WIDTH),
        ]
        + [shape(bf16, D, n)] * 5
        + [
            shape(bf16, 3, QUARTER, 4 * n),
            shape(bf16, 4, n, UNIT),
            shape(bf16, 4, n, EMBED_WIDTH),
            shape(f32, 16, UNIT),
        ],
        in_specs=[VMEM] * 8 + [ANY] * 8,
        out_specs=[VMEM] * 16,
        scratch_shapes=[
            vmem((4, n, EMBED_WIDTH), bf16),
            vmem((n, EMBED_WIDTH), f32),
            vmem((n, D), f32),
            vmem((3, 4 * n, HDIM), bf16),
            vmem((3, 4 * n, HDIM), bf16),
            vmem((QUARTER, 4 * n), bf16),
            vmem((3, 4 * n, HDIM), bf16),
            vmem((16, n), f32),
            vmem((n, D), f32),
            vmem((n, D), bf16),
            vmem((4, n, UNIT), f32),
            vmem((n, D), f32),
            vmem((n, D), bf16),
            vmem((n, EMBED_WIDTH), f32),
            vmem((n, EMBED_WIDTH), f32),
            vmem((n, EMBED_WIDTH), bf16),
            vmem((4, D, LANES), bf16),
            vmem((4, QUARTER, UNIT), bf16),
            vmem((D, UNIT), bf16),
            vmem((4, D, UNIT), bf16),
            vmem((4, D, UNIT), bf16),
            vmem((3, n, EMBED_WIDTH), bf16),
            vmem((QUARTER, 4 * n), bf16),
            vmem((3, n, QUARTER), bf16),
            vmem((4, n, QUARTER), bf16),
            vmem((4 * n, n), f32),
            vmem(table.shape, bf16),
            vmem(table_t.shape, bf16),
            vmem((4, EMBED_WIDTH, n), f32),
            vmem((4, 8, n), f32),
            vmem((3, 4, 8, n), f32),
            vmem((4, n, EMBED_WIDTH), bf16),
            vmem((3, n, EMBED_WIDTH), bf16),
            vmem((n, D), f32),
            vmem((n, D), f32),
            vmem((4, n, QUARTER), bf16),
            vmem((3, n, QUARTER), bf16),
            vmem((3, 4 * n, HDIM), f32),
            vmem((3, 4 * n, HDIM), f32),
            vmem((2, n, D), bf16),
            vmem((2, n, D), bf16),
            vmem((n, D), bf16),
            vmem((n, D), bf16),
            dma((8,)),
            dma((4,)),
            dma((2,)),
        ]
        + [dma((3,))] * 18,
        compiler_params=pltpu.CompilerParams(
            collective_id=4, has_side_effects=True, vmem_limit_bytes=60 * 2**20
        ),
    )(*operands)

I16 = jnp.int16
TAIL = 16
TILES = 60
PART_TILES = 30
PART = 3840


def exponent(peak):
    return jnp.ceil(jnp.log2(jnp.maximum(peak, 1e-30))) + 1.0


def coded(value, power):
    return jnp.round(value * jnp.exp2(15.0 - power)).astype(jnp.int32).astype(I16)


def plain(code, power):
    return code.astype(jnp.int32).astype(f32) * jnp.exp2(power - 15.0)


def put(ref, value):
    rows, cols = value.shape
    power = exponent(jnp.max(jnp.abs(value), 0, keepdims=True))
    ref[0:rows, :] = coded(value, power)
    ref[rows : rows + TAIL, :] = (
        jnp.broadcast_to(power, (TAIL, cols)).astype(jnp.int32).astype(I16)
    )


def get(ref, rows):
    power = ref[rows : rows + TAIL, :].astype(jnp.int32).astype(f32)[0:1]
    return plain(ref[0:rows, :], power)


def put_tiles(ref, source, rows):
    lane = lax.broadcasted_iota(jnp.int32, (rows, LANES), 1)

    def body(tile, powers):
        at = pl.ds(pl.multiple_of(tile * LANES, LANES), LANES)
        value = source(at)
        power = exponent(jnp.max(jnp.abs(value), 1, keepdims=True))
        ref[:, at] = coded(value, power)
        return jnp.where(lane == tile, power, powers)

    powers = lax.fori_loop(0, PART_TILES, body, jnp.zeros((rows, LANES), f32), unroll=6)
    ref[:, PART:] = powers.astype(jnp.int32).astype(I16)


def tile_getter(ref, rows):
    lane = lax.broadcasted_iota(jnp.int32, (rows, LANES), 1)
    powers = ref[:, PART:].astype(jnp.int32).astype(f32)

    def read(tile, at):
        power = jnp.sum(jnp.where(lane == tile, powers, 0.0), 1, keepdims=True)
        return plain(ref[:, at], power)

    return read


def grads_kernel(
    owners, inputs, grad_pred, pred_all, grad_clean, lse, weight, row_of, tile,
    out_left_hbm, mixed_hbm, down_left_hbm, active_hbm, qkv_left_hbm, normed_hbm, table_t_hbm, up_left_hbm,
    grad_up_hbm, small_left_hbm, final_left_hbm,
    summed, table_sum, tile_sum,
    out_left, mixed, down_left, active, qkv_left, normed, table_t, up_left, grad_up, small_left, final_left,
    home, small_home, outgoing, cs, cr, xs, xr, ys, yr, zs, zr, part, half,
    small_cs, small_cr, small_xs, small_xr, small_ys, small_yr, small_zs, small_zr, small_half,
    table, pred_t, clean_t, ts, tr, tzs, tzr, tile_at, tile_from,
    c_send, c_recv, x_send, x_recv, y_send, y_recv, z_send, z_recv, t_send, t_recv, a_send, a_recv, local, l_sem,
):
    z, y, d, v = place()
    far, near = v ^ 2, v ^ 1
    pairs = (
        (out_left_hbm, out_left), (mixed_hbm, mixed), (down_left_hbm, down_left), (active_hbm, active),
        (qkv_left_hbm, qkv_left), (normed_hbm, normed), (table_t_hbm, table_t), (up_left_hbm, up_left),
        (grad_up_hbm, grad_up), (small_left_hbm, small_left), (final_left_hbm, final_left),
    )
    loads = [pltpu.make_async_copy(src, dst, l_sem.at[i]) for i, (src, dst) in enumerate(pairs)]
    for copy in loads:
        copy.start()
    loaded = set()

    def need(*which):
        for i in which:
            if i not in loaded:
                loads[i].wait()
                loaded.add(i)

    greet([(d ^ m, v) for m in TRADE_MASKS] + [(d, far), (d, near)])
    sent = []

    def send(src, dst, sems, index, partner):
        copy = remote(src, dst, sems, index, partner)
        copy.start()
        sent.append(copy)
        return copy

    def product(n, who):
        need(*((0, 1) if n == 0 else (2, 3) if n < 5 else (7, 8)))
        if n == 0:
            return matmul_nn(out_left[who], mixed[...])
        if n < 5:
            return matmul_nn(down_left[who], active[n - 1])
        return matmul_nn(up_left[who], grad_up[n - 5])

    core, chip, side, line = {}, {}, {}, {}

    def to_core(n):
        put(cs.at[n, 0], product(n, near))
        put(cs.at[n, 1], product(n, near ^ 2))
        core[n] = send(cs.at[n], cr.at[n], (c_send, c_recv), n, (d, near))

    def to_chip(n):
        core[n].wait_recv()
        put(xs.at[n], product(n, far) + get(cr.at[n, 1], QUARTER))
        chip[n] = send(xs.at[n], xr.at[n], (x_send, x_recv), n, (d, far))

    def halves(slot, value):
        part[...] = value
        put(ys.at[slot], part[pl.ds((1 - y) * HALF, HALF), :])
        half[slot] = part[pl.ds(y * HALF, HALF), :]
        side[slot] = send(ys.at[slot], yr.at[slot], (y_send, y_recv), slot, (d ^ 1, v))

    def to_side(n):
        chip[n].wait_recv()
        value = product(n, v) + get(cr.at[n, 0], QUARTER) + get(xr.at[n], QUARTER)
        halves(3 + n, value)

    def to_line(group):
        for u in range(4):
            slot = 4 * group + u
            side[slot].wait_recv()
            half[slot] = half[slot] + get(yr.at[slot], HALF)
        for k in (2, 1, 3):
            put(zs.at[group, k - 1], half[4 * group + (z ^ k)])
            line[group, k] = send(
                zs.at[group, k - 1], zr.at[group, k - 1], (z_send, z_recv), 3 * group + k - 1, (d ^ (2 * k), v)
            )

    def to_home(group):
        total = half[4 * group + z]
        for k in (2, 1, 3):
            line[group, k].wait_recv()
            total = total + get(zr.at[group, k - 1], HALF)
        put(home.at[group], total)

    def small_product(who):
        need(9, 10)
        return jnp.concatenate(
            [matmul_nn(small_left[who], inputs[...]), matmul_nn(final_left[who], grad_pred[...])], 1
        )

    def small_to_core():
        put(small_cs.at[0], small_product(near))
        put(small_cs.at[1], small_product(near ^ 2))
        core[9] = send(small_cs, small_cr, (c_send, c_recv), 9, (d, near))

    def small_to_chip():
        core[9].wait_recv()
        put(small_xs, small_product(far) + get(small_cr.at[1], QUARTER))
        chip[9] = send(small_xs, small_xr, (x_send, x_recv), 9, (d, far))

    def small_to_side():
        chip[9].wait_recv()
        value = small_product(v) + get(small_cr.at[0], QUARTER) + get(small_xr, QUARTER)
        cols = value.shape[1]
        part[:, 0:cols] = value
        put(small_ys, part[pl.ds((1 - y) * HALF, HALF), 0:cols])
        small_half[0] = part[pl.ds(y * HALF, HALF), 0:LANES]
        small_half[1] = part[pl.ds(y * HALF, HALF), LANES : 2 * LANES]
        small_half[2] = part[pl.ds(y * HALF, HALF), 2 * LANES : cols]
        small_half[3] = jnp.zeros((HALF, LANES), f32)
        side[12] = send(small_ys, small_yr, (y_send, y_recv), 12, (d ^ 1, v))

    def small_to_line():
        side[12].wait_recv()
        value = get(small_yr, HALF)
        for u in range(3):
            small_half[u] = small_half[u] + value[:, u * LANES : (u + 1) * LANES]
        for k in (2, 1, 3):
            put(small_zs.at[k - 1], small_half[z ^ k])
            line[3, k] = send(
                small_zs.at[k - 1], small_zr.at[k - 1], (z_send, z_recv), 9 + k - 1, (d ^ (2 * k), v)
            )

    def small_to_home():
        total = small_half[z]
        for k in (2, 1, 3):
            line[3, k].wait_recv()
            total = total + get(small_zr.at[k - 1], HALF)
        put(small_home, total)

    def turn_tokens():
        for b in range(4):
            pred_t[b] = pred_all[b].astype(f32).T.astype(bf16)
            clean_t[b] = grad_clean[b].astype(f32).T.astype(bf16)

    vocab_rows = table_t.shape[0]

    def table_strip(lo, size):
        need(6)
        total = jnp.zeros((EMBED_WIDTH, size), f32)
        for b in range(4):
            logits = matmul_nt(table_t[lo : lo + size, :], pred_all[b])
            probs = jnp.exp(logits - lse[b : b + 1, :])
            here = lax.broadcasted_iota(jnp.int32, (size, 256), 0) == row_of[b : b + 1, :] - lo
            here = here.astype(f32)
            grad_logits = ((probs - here) * weight[b : b + 1, :]).astype(bf16)
            total = total + matmul_nt(pred_t[b], grad_logits)
            total = total + matmul_nt(clean_t[b], here.astype(bf16))
        for i in range(8):
            rows = slice(16 * (i // 2), 16 * (i // 2) + 16)
            table[i % 2, rows, lo : lo + size] = total[16 * i : 16 * i + 16]
        if lo + size == vocab_rows:
            table[:, :, vocab_rows:] = jnp.zeros((2, 64, TILES * LANES - vocab_rows), f32)

    table_strips = [(lo, min(STRIP, vocab_rows - lo)) for lo in range(0, vocab_rows, STRIP)]

    def shifted(at, p):
        return pl.ds(pl.multiple_of(at.start + p * PART, LANES), LANES)

    def table_to_side(p):
        put_tiles(ts.at[p], lambda at: table[1 - y, :, shifted(at, p)], 64)
        side[13 + p] = send(ts.at[p], tr.at[p], (y_send, y_recv), 13 + p, (d ^ 1, v))

    def table_line_value(which, p):
        rows = pl.ds(pl.multiple_of(which * 16, 16), 16)
        read = tile_getter(tr.at[p, rows, :], 16)
        return rows, read

    def table_to_line(p):
        side[13 + p].wait_recv()
        for k in (2, 1, 3):
            rows, read = table_line_value(z ^ k, p)

            def source(at, rows=rows, read=read):
                return table[y, rows, shifted(at, p)] + read(at.start // LANES, at)

            put_tiles(tzs.at[p, k - 1], source, 16)
            line[4 + p, k] = send(
                tzs.at[p, k - 1],
                tzr.at[p, k - 1],
                (z_send, z_recv),
                12 + 3 * p + k - 1,
                (d ^ (2 * k), v),
            )

    def table_to_home(p):
        for k in (2, 1, 3):
            line[4 + p, k].wait_recv()
        rows, read = table_line_value(z, p)
        others = [tile_getter(tzr.at[p, k], 16) for k in range(3)]

        def body(tile, carry):
            at = pl.ds(pl.multiple_of(tile * LANES, LANES), LANES)
            value = table[y, rows, shifted(at, p)] + read(tile, at)
            for other in others:
                value = value + other(tile, at)
            table_sum[:, shifted(at, p)] = value
            return carry

        lax.fori_loop(0, PART_TILES, body, 0, unroll=5)

    hops = [(d, near), (d, far), (d ^ 1, v), (d ^ 2, v), (d ^ 4, v)]
    tile_copies = {}

    def tile_send(hop):
        if hop == 0:
            tile_at[0] = tile[...]
        else:
            tile_copies[hop - 1].wait_recv()
            tile_at[hop] = tile_at[hop - 1] + tile_from[hop - 1]
        tile_copies[hop] = send(
            tile_at.at[hop], tile_from.at[hop], (t_send, t_recv), hop, hops[hop]
        )

    def token_products():
        need(4, 5)
        for u in range(3):
            halves(
                u,
                sum(matmul_nn(qkv_left[u, :, 256 * b : 256 * b + 256], normed[b]) for b in range(4)),
            )

    to_core(0)
    to_core(1)
    to_chip(0)
    token_products()
    tile_send(0)
    turn_tokens()
    table_strip(*table_strips[0])
    table_strip(*table_strips[1])
    to_core(2)
    to_chip(1)
    to_side(0)
    table_strip(*table_strips[2])
    table_strip(*table_strips[3])
    to_core(3)
    to_chip(2)
    table_strip(*table_strips[4])
    table_to_side(0)
    to_line(0)
    to_side(1)
    table_strip(*table_strips[5])
    table_strip(*table_strips[6])
    to_core(4)
    to_chip(3)
    table_strip(*table_strips[7])
    table_strip(*table_strips[8])
    for strip in table_strips[9:]:
        table_strip(*strip)
    table_to_side(1)
    to_side(2)
    to_core(5)
    to_chip(4)
    tile_send(1)
    table_to_line(0)
    to_core(6)
    to_chip(5)
    to_side(3)
    to_core(7)
    to_chip(6)
    small_to_core()
    to_core(8)
    to_chip(7)
    small_to_chip()
    to_chip(8)
    to_side(4)
    tile_send(2)
    table_to_line(1)
    to_line(1)
    to_side(5)
    to_home(0)
    tile_send(3)
    small_to_side()
    to_side(6)
    table_to_home(0)
    small_to_line()
    tile_send(4)
    to_side(7)
    to_home(1)
    to_side(8)
    to_line(2)
    table_to_home(1)
    small_to_home()
    tile_copies[4].wait_recv()
    tile_sum[...] = tile_at[4] + tile_from[4]
    to_home(2)

    def offer(m):
        taker = d ^ m
        unit = jnp.where(owners[4] == taker, home[2], home[0])
        outgoing[m, :, 0:UNIT] = jnp.where(owners[5] == taker, home[1], unit)
        outgoing[m, :, UNIT:] = small_home[...]

    offered = []
    for i, m in enumerate(TRADE_MASKS):
        offer(m)
        offered.append(send(outgoing.at[m], summed.at[d], (a_send, a_recv), i, (d ^ m, v)))
    offer(0)
    keep = pltpu.make_async_copy(outgoing.at[0], summed.at[d], local)
    keep.start()
    keep.wait()
    arrive_all(offered)
    for copy in sent:
        copy.wait_send()


def reduce_grads(*operands):
    dma = pltpu.SemaphoreType.DMA
    vmem = pltpu.VMEM
    tall, low, wide = QUARTER + TAIL, HALF + TAIL, 3 * LANES
    table_cols = TILES * LANES
    return pl.pallas_call(
        grads_kernel,
        out_shape=[
            jax.ShapeDtypeStruct((8, low, UNIT + LANES), I16),
            jax.ShapeDtypeStruct((16, table_cols), f32),
            jax.ShapeDtypeStruct((16, UNIT), f32),
        ],
        in_specs=[SMEM] + [VMEM] * 8 + [ANY] * 11,
        out_specs=[VMEM] * 3,
        scratch_shapes=[vmem(value.shape, bf16) for value in operands[9:]]
        + [
            vmem((3, low, UNIT), I16),
            vmem((low, LANES), I16),
            vmem((8, low, UNIT + LANES), I16),
            vmem((9, 2, tall, UNIT), I16),
            vmem((9, 2, tall, UNIT), I16),
            vmem((9, tall, UNIT), I16),
            vmem((9, tall, UNIT), I16),
            vmem((12, low, UNIT), I16),
            vmem((12, low, UNIT), I16),
            vmem((3, 3, low, UNIT), I16),
            vmem((3, 3, low, UNIT), I16),
            vmem((QUARTER, UNIT), f32),
            vmem((12, HALF, UNIT), f32),
            vmem((2, tall, wide), I16),
            vmem((2, tall, wide), I16),
            vmem((tall, wide), I16),
            vmem((tall, wide), I16),
            vmem((low, wide), I16),
            vmem((low, wide), I16),
            vmem((3, low, LANES), I16),
            vmem((3, low, LANES), I16),
            vmem((4, HALF, LANES), f32),
            vmem((2, 64, table_cols), f32),
            vmem((4, EMBED_WIDTH, 256), bf16),
            vmem((4, EMBED_WIDTH, 256), bf16),
            vmem((2, 64, PART + LANES), I16),
            vmem((2, 64, PART + LANES), I16),
            vmem((2, 3, 16, PART + LANES), I16),
            vmem((2, 3, 16, PART + LANES), I16),
            vmem((5, 16, UNIT), f32),
            vmem((5, 16, UNIT), f32),
        ]
        + [dma((10,))] * 4
        + [dma((15,))] * 2
        + [dma((18,))] * 2
        + [dma((5,))] * 2
        + [dma((7,))] * 2
        + [dma, dma((11,))],
        compiler_params=pltpu.CompilerParams(
            collective_id=2, has_side_effects=True, vmem_limit_bytes=60 * 2**20
        ),
    )(*operands)


def slot_kernel(
    kind, unit, column, summed, table_grad, sums, w, m1, m2, tw, t1, t2,
    w_out, m1_out, m2_out, tw_out, t1_out, t2_out, loss, norm,
):
    per_unit = UNIT // LANES

    def once():
        g = table_grad[:, 0 : tw.shape[1]]
        tw_out[...], t1_out[...], t2_out[...] = adamw(tw[...], g, t1[...], t2[...])
        row = sums[10:11, :]
        lane = lax.broadcasted_iota(jnp.int32, row.shape, 1)
        square, cross, length, count = [jnp.sum(jnp.where(lane == i, row, 0.0)) for i in range(4)]
        loss[0] = (0.5 * square + cross) * count
        loss[1] = count
        norm[0] = 0.5 * length

    pl.when(pl.program_id(0) == 0)(once)
    for b in range(per_unit):
        j = pl.program_id(0) * per_unit + b
        first = jnp.where(kind[j] == 2, per_unit, column[j])
        at = pl.ds(pl.multiple_of(first * LANES, LANES), LANES)
        lanes = slice(b * LANES, b * LANES + LANES)
        for half in range(2):
            rows = slice(half * HALF, half * HALF + HALF)
            g = get(summed.at[2 * unit[j] + half, :, at], HALF)
            g = jnp.where(kind[j] > 0, g, jnp.zeros_like(g))
            w_out[rows, lanes], m1_out[rows, lanes], m2_out[rows, lanes] = adamw(
                w[rows, lanes], g, m1[rows, lanes], m2[rows, lanes]
            )


def slot_update(kind, unit, column, summed, table_grad, sums, slots, first, second, *table):
    rows = slots.shape[0]
    plain_spec = pl.BlockSpec((rows, UNIT), lambda j, k, u, c: (0, j))

    def whole(value):
        return pl.BlockSpec(value.shape, lambda j, k, u, c: (0,) * len(value.shape))

    return pl.pallas_call(
        slot_kernel,
        grid_spec=pltpu.PrefetchScalarGridSpec(
            num_scalar_prefetch=3,
            grid=(CAP // UNIT,),
            in_specs=[whole(summed), whole(table_grad), whole(sums)]
            + [plain_spec] * 3
            + [whole(value) for value in table],
            out_specs=[plain_spec] * 3 + [whole(value) for value in table] + [SMEM] * 2,
        ),
        out_shape=[jax.ShapeDtypeStruct(slots.shape, f32)] * 3
        + [jax.ShapeDtypeStruct(table[0].shape, f32)] * 3
        + [jax.ShapeDtypeStruct((2,), f32), jax.ShapeDtypeStruct((1,), f32)],
        cost_estimate=pl.CostEstimate(flops=0, bytes_accessed=28 * rows * CAP, transcendentals=0),
        compiler_params=pltpu.CompilerParams(vmem_limit_bytes=60 * 2**20),
    )(kind, unit, column, summed, table_grad, sums, slots, first, second, *table)


def per_device(
    token_ids,
    timesteps,
    pad_mask,
    noise_draw,
    owners,
    emb_table,
    table_first_moment,
    table_second_moment,
    mat_slots,
    slot_first,
    slot_second,
    vec_params,
    vec_first,
    vec_second,
):
    v = lax.axis_index("vocab")
    seq_len = token_ids.shape[1]
    tokens = seq_len // 4
    vocab_rows, emb_cols = emb_table.shape
    table_own = emb_table.T
    (
        payload, table_home, row_of, safe_row, keep_rows, keep_column, valid_column, count_tile,
        kind, unit, column,
    ) = prepare(owners, token_ids, pad_mask, table_own, mat_slots)
    w_up, w_down, w_small, w_attn, w_out, table_low, row_weight, twice, places, levels = spread(
        owners, timesteps, payload, count_tile, keep_rows, keep_column, table_home
    )
    table_low = table_low.reshape(EMBED_WIDTH, vocab_rows)
    table_t = table_low.T
    looked = table_t.at[safe_row[0]].get(mode="promise_in_bounds").reshape(4, tokens, EMBED_WIDTH)
    vecs = vec_params.reshape(10, D)
    (
        inputs, normed_all, mixed_own, active, pred_all, head_stats, grad_pred_low, down_left, up_left, out_left,
        small_left, final_left, qkv_left, grad_up, grad_clean, sums,
    ) = step(
        looked, valid_column, levels, places, vecs, keep_column, row_weight, twice,
        noise_draw[0], w_small, w_attn, w_out, w_up, w_down, table_low, table_t,
    )

    def left(value):
        return value.reshape(4, QUARTER, tokens)

    summed, table_grad, tile_sum = reduce_grads(
        owners, inputs, grad_pred_low, pred_all, grad_clean, head_stats, row_weight, row_of, sums,
        left(out_left), mixed_own, left(down_left), active, qkv_left, normed_all, table_t, left(up_left),
        grad_up, left(small_left), left(final_left),
    )
    (
        new_slots, slot_first_new, slot_second_new, new_table, table_first_new, table_second_new, loss_pair, emb_norm,
    ) = slot_update(
        kind, unit, column, summed, table_grad, tile_sum, mat_slots, slot_first, slot_second,
        table_own, table_first_moment.T, table_second_moment.T,
    )
    tile_sum = tile_sum.reshape(16 * UNIT)
    vec_share = vec_first.shape[0]
    own_grad = lax.dynamic_slice_in_dim(tile_sum, v * vec_share, vec_share)
    own_vecs = lax.dynamic_slice_in_dim(vec_params, v * vec_share, vec_share)
    new_vecs, vec_first_new, vec_second_new = adamw(own_vecs, own_grad, vec_first, vec_second)
    return (
        loss_pair,
        emb_norm[0],
        new_table.T,
        table_first_new.T,
        table_second_new.T,
        new_slots,
        slot_first_new,
        slot_second_new,
        new_vecs,
        vec_first_new,
        vec_second_new,
    )


def broadcast(value, axis, source):
    kept = jnp.where(lax.axis_index(axis) == source, value, 0).astype(value.dtype)
    return lax.psum(kept, axis)


def merged(value, axis, join):
    pieces = jax.tree.map(lambda part: lax.all_gather(part, axis), value)
    head = jax.tree.map(lambda part: part[0], pieces)
    tail = jax.tree.map(lambda part: part[1:], pieces)
    so_far, _ = lax.scan(lambda so_far, share: (join(so_far, share), None), head, tail)
    return so_far


def matrix_rows():
    return [D, D, D, D, FF, FF] * LAYERS + [EMBED_WIDTH, EMBED_WIDTH, EMBED_WIDTH]


def slot_places(owners):
    counts = jnp.array(matrix_rows(), jnp.int32)
    mat_total = counts.shape[0]
    same_owner = (owners[:, None] == owners[None, :]).astype(jnp.int32)
    earlier_mask = jnp.tril(jnp.ones((mat_total, mat_total), jnp.int32), -1)
    return owners * CAP + jnp.sum(same_owner * earlier_mask * counts[None, :], 1)


def block_scores(query_blk, keys_all, keep_keys, score_scale):
    scores = (
        jnp.einsum("qhd,khd->hqk", query_blk, keys_all, preferred_element_type=jnp.float32)
        * score_scale
    )
    return jnp.where(keep_keys[None, None, :], scores, -1000000000.0)


def attention(queries, keys_all, values_all, keep_keys, score_scale):
    tokens = queries.shape[0]
    width = min(512, tokens)
    query_blocks = queries.reshape(tokens // width, width, HEADS, HDIM)

    def one_block(query_blk):
        scores = block_scores(query_blk, keys_all, keep_keys, score_scale)
        row_max = jnp.max(scores, -1, keepdims=True)
        expo = jnp.exp(scores - row_max)
        exp_total = jnp.sum(expo, -1, keepdims=True)
        probabilities = (expo / exp_total).astype(jnp.bfloat16)
        mixed_out = jnp.einsum(
            "hqk,khd->qhd", probabilities, values_all, preferred_element_type=jnp.float32
        )
        return (mixed_out, (row_max + jnp.log(exp_total))[..., 0])

    mixed_out, log_total = lax.map(one_block, query_blocks)
    return (mixed_out.reshape(tokens, HEADS, HDIM), log_total)


def attention_back(queries, keys_all, values_all, keep_keys, log_total, grad_mixed, score_scale):
    tokens = queries.shape[0]
    width = min(512, tokens)
    query_blocks = queries.reshape(tokens // width, width, HEADS, HDIM)
    grad_blocks = grad_mixed.reshape(tokens // width, width, HEADS, HDIM)

    def one_block(carry_sums, block_data):
        query_blk, total_blk, grad_blk = block_data
        scores = block_scores(query_blk, keys_all, keep_keys, score_scale)
        probabilities = jnp.exp(scores - total_blk[..., None])
        grad_probs = jnp.einsum(
            "qhd,khd->hqk", grad_blk, values_all, preferred_element_type=jnp.float32
        )
        inner_sum = jnp.sum(probabilities * grad_probs, -1, keepdims=True)
        grad_scores = (probabilities * (grad_probs - inner_sum)).astype(jnp.bfloat16)
        grad_query = (
            jnp.einsum("hqk,khd->qhd", grad_scores, keys_all, preferred_element_type=jnp.float32)
            * score_scale
        )
        grad_key = (
            jnp.einsum("hqk,qhd->khd", grad_scores, query_blk, preferred_element_type=jnp.float32)
            * score_scale
        )
        grad_value = jnp.einsum(
            "hqk,qhd->khd",
            probabilities.astype(jnp.bfloat16),
            grad_blk,
            preferred_element_type=jnp.float32,
        )
        return ((carry_sums[0] + grad_key, carry_sums[1] + grad_value), grad_query)

    zero_keys = jnp.zeros(keys_all.shape, jnp.float32)
    grad_kv, grad_queries = lax.scan(
        one_block, (zero_keys, zero_keys), (query_blocks, log_total, grad_blocks)
    )
    return (grad_queries.reshape(tokens, D), grad_kv[0].reshape(-1, D), grad_kv[1].reshape(-1, D))


def send_matrix(piece_cols, root):
    return broadcast(piece_cols, "dp", root)


def fetch_keys(key_rows, value_rows):
    return (
        lax.all_gather(key_rows, "vocab", axis=0, tiled=True),
        lax.all_gather(value_rows, "vocab", axis=0, tiled=True),
    )


def layer_forward(hidden, weights, vec_layer, keep_keys, score_scale):
    w_query, w_key, w_value, w_out, w_up, w_down = weights
    tokens = hidden.shape[0]
    norm_one, inv_one = norm_parts(hidden)
    normed = (norm_one * vec_layer[0:D] + vec_layer[D : 2 * D]).astype(jnp.bfloat16)
    queries = matmul_nn(normed, w_query).astype(jnp.bfloat16)
    key_rows = matmul_nn(normed, w_key).astype(jnp.bfloat16)
    value_rows = matmul_nn(normed, w_value).astype(jnp.bfloat16)
    keys_all, values_all = fetch_keys(key_rows, value_rows)
    keys_all = keys_all.reshape(-1, HEADS, HDIM)
    values_all = values_all.reshape(-1, HEADS, HDIM)
    mixed_out, log_total = attention(
        queries.reshape(tokens, HEADS, HDIM), keys_all, values_all, keep_keys, score_scale
    )
    mixed_low = mixed_out.reshape(tokens, D).astype(jnp.bfloat16)
    middle = hidden + matmul_nn(mixed_low, w_out)
    norm_two, inv_two = norm_parts(middle)
    normed_two = (norm_two * vec_layer[2 * D : 3 * D] + vec_layer[3 * D : 4 * D]).astype(
        jnp.bfloat16
    )
    up_proj = matmul_nt(normed_two, w_up) + vec_layer[4 * D :]
    active = jax.nn.gelu(up_proj).astype(jnp.bfloat16)
    out_rows = middle + matmul_nn(active, w_down)
    kept_vals = (
        norm_one,
        inv_one,
        normed,
        queries,
        key_rows,
        value_rows,
        keys_all,
        values_all,
        log_total,
        mixed_low,
        norm_two,
        inv_two,
        normed_two,
        up_proj,
        active,
    )
    return (out_rows, kept_vals)


def layer_backward(grad_out, kept_vals, weights, vec_layer, keep_keys, score_scale):
    w_query, w_key, w_value, w_out, w_up, w_down = weights
    (
        norm_one,
        inv_one,
        normed,
        queries,
        key_rows,
        value_rows,
        keys_all,
        values_all,
        log_total,
        mixed_low,
        norm_two,
        inv_two,
        normed_two,
        up_proj,
        active,
    ) = kept_vals
    tokens = grad_out.shape[0]
    grad_low = grad_out.astype(jnp.bfloat16)
    grad_down = matmul_tn(active, grad_low)
    grad_active = matmul_nt(grad_low, w_down)
    grad_up_proj = jax.vjp(jax.nn.gelu, up_proj)[1](grad_active)[0].astype(jnp.bfloat16)
    grad_bias = jnp.sum(grad_up_proj.astype(jnp.float32), 0)
    grad_up = matmul_tn(grad_up_proj, normed_two)
    grad_normed_two = matmul_nn(grad_up_proj, w_up)
    grad_part, grad_gain_two, grad_shift_two = norm_back(
        norm_two, inv_two, vec_layer[2 * D : 3 * D], grad_normed_two
    )
    grad_middle = grad_out + grad_part
    grad_attn = grad_middle.astype(jnp.bfloat16)
    grad_out_w = matmul_tn(mixed_low, grad_attn)
    grad_mixed = matmul_nt(grad_attn, w_out).astype(jnp.bfloat16).reshape(tokens, HEADS, HDIM)
    grad_queries, grad_keys_all, grad_values_all = attention_back(
        queries.reshape(tokens, HEADS, HDIM),
        keys_all,
        values_all,
        keep_keys,
        log_total,
        grad_mixed,
        score_scale,
    )
    grad_key_rows, grad_value_rows = (
        lax.psum_scatter(
            grad_keys_all.astype(jnp.bfloat16), "vocab", scatter_dimension=0, tiled=True
        ).astype(jnp.float32),
        lax.psum_scatter(
            grad_values_all.astype(jnp.bfloat16), "vocab", scatter_dimension=0, tiled=True
        ).astype(jnp.float32),
    )
    grad_q_low = grad_queries.astype(jnp.bfloat16)
    grad_k_low = grad_key_rows.astype(jnp.bfloat16)
    grad_v_low = grad_value_rows.astype(jnp.bfloat16)
    grad_wq = matmul_tn(normed, grad_q_low)
    grad_wk = matmul_tn(normed, grad_k_low)
    grad_wv = matmul_tn(normed, grad_v_low)
    grad_normed = (
        matmul_nt(grad_q_low, w_query)
        + matmul_nt(grad_k_low, w_key)
        + matmul_nt(grad_v_low, w_value)
    )
    grad_part_one, grad_gain_one, grad_shift_one = norm_back(
        norm_one, inv_one, vec_layer[0:D], grad_normed
    )
    grad_hidden = grad_middle + grad_part_one
    grad_mats = [grad_wq, grad_wk, grad_wv, grad_out_w, grad_up, grad_down]
    grad_vec = jnp.concatenate(
        [grad_gain_one, grad_shift_one, grad_gain_two, grad_shift_two, grad_bias]
    )
    return (grad_hidden, grad_mats, grad_vec)


def merge_stats(first_part, second_part):
    peak_val = jnp.maximum(first_part[0], second_part[0])
    exp_total = first_part[1] * jnp.exp(first_part[0] - peak_val) + second_part[1] * jnp.exp(
        second_part[0] - peak_val
    )
    return (peak_val, exp_total, first_part[2] + second_part[2])


def any_mesh_device(
    token_ids,
    timesteps,
    pad_mask,
    noise_draw,
    owners,
    emb_table,
    table_first_moment,
    table_second_moment,
    mat_slots,
    slot_first,
    slot_second,
    vec_params,
    vec_first,
    vec_second,
):
    vocab_count = lax.axis_size("vocab")
    vocab_pos = lax.axis_index("vocab")
    data_pos = lax.axis_index("dp")
    seq_len = token_ids.shape[1]
    tokens = seq_len // vocab_count
    vocab_rows = emb_table.shape[0]
    score_scale = HDIM ** (-0.5)
    table_low = lax.all_gather(emb_table.astype(jnp.bfloat16), "dp", axis=1, tiled=True)
    row_counts = matrix_rows()
    local_start = slot_places(owners) - owners * CAP
    sent_pieces = [
        send_matrix(
            lax.dynamic_slice_in_dim(
                mat_slots, local_start[mat_idx], row_counts[mat_idx], 1
            ).astype(jnp.bfloat16),
            owners[mat_idx],
        )
        for mat_idx in range(len(row_counts))
    ]
    canon = jnp.concatenate(sent_pieces, 1)
    weights = lax.all_gather(canon, "vocab", axis=0, tiled=True).T
    layer_rows = 4 * D + 2 * FF
    vec_rows = 4 * D + FF
    tail_at = LAYERS * layer_rows

    def layer_weights(layer_idx):
        begin_row = layer_idx * layer_rows
        cuts = [
            begin_row,
            begin_row + D,
            begin_row + 2 * D,
            begin_row + 3 * D,
            begin_row + 4 * D,
            begin_row + 4 * D + FF,
            begin_row + layer_rows,
        ]
        return [weights[cuts[cut_idx] : cuts[cut_idx + 1]] for cut_idx in range(6)]

    w_input = weights[tail_at : tail_at + 2 * EMBED_WIDTH]
    w_final = weights[tail_at + 2 * EMBED_WIDTH : tail_at + 3 * EMBED_WIDTH]
    seq_ids = token_ids[0]
    seq_mask = pad_mask[0].astype(jnp.float32)
    keep_keys = pad_mask[0] > 0
    local_row = seq_ids - vocab_pos * vocab_rows
    valid_row = (local_row >= 0) & (local_row < vocab_rows)
    safe_row = jnp.clip(local_row, 0, vocab_rows - 1)
    found_rows = jnp.where(
        valid_row[:, None], jnp.take(table_low, safe_row, axis=0), jnp.zeros((), jnp.bfloat16)
    )
    arrived = lax.all_to_all(found_rows, "vocab", split_axis=0, concat_axis=0, tiled=True)
    clean_emb = jnp.sum(arrived.reshape(vocab_count, tokens, EMBED_WIDTH).astype(jnp.float32), 0)
    own_first = vocab_pos * tokens
    mask_own = lax.dynamic_slice_in_dim(seq_mask, own_first, tokens)
    own_places = (own_first + jnp.arange(tokens)).astype(jnp.float32)
    step_val = timesteps[0].astype(jnp.float32)
    signal_level = 1.0 - jnp.sqrt(step_val / DIFF + 0.0001)
    noisy_emb = jnp.sqrt(signal_level) * clean_emb + jnp.sqrt(1.0 - signal_level) * noise_draw[
        0
    ].astype(jnp.float32)
    time_feat = jnp.broadcast_to(waves(step_val[None], EMBED_WIDTH), (tokens, EMBED_WIDTH))
    inputs = jnp.concatenate([noisy_emb, time_feat], 1).astype(jnp.bfloat16)
    hidden = matmul_nn(inputs, w_input) + waves(own_places, D)
    layer_idx = 0
    vec_layer = vec_params[layer_idx * vec_rows : (layer_idx + 1) * vec_rows]
    hidden, kept_vals = layer_forward(
        hidden, layer_weights(layer_idx), vec_layer, keep_keys, score_scale
    )
    kept_list = [kept_vals]
    gain_final = vec_params[LAYERS * vec_rows : LAYERS * vec_rows + D]
    shift_final = vec_params[LAYERS * vec_rows + D :]
    norm_final, inv_final = norm_parts(hidden)
    final_norm = (norm_final * gain_final + shift_final).astype(jnp.bfloat16)
    predicted = matmul_nt(final_norm, w_final)
    pred_all = lax.all_gather(predicted.astype(jnp.bfloat16), "vocab", axis=0, tiled=True)
    head_width = min(512, seq_len)
    head_count = seq_len // head_width
    columns = jnp.arange(vocab_rows)
    pred_blocks = pred_all.reshape(head_count, head_width, EMBED_WIDTH)
    row_blocks = local_row.reshape(head_count, head_width)

    def head_stats(block_data):
        pred_blk, rows_blk = block_data
        logits = matmul_nt(pred_blk, table_low)
        row_max = jnp.max(logits, -1)
        exp_total = jnp.sum(jnp.exp(logits - row_max[:, None]), -1)
        target = jnp.sum(jnp.where(columns[None, :] == rows_blk[:, None], logits, 0.0), -1)
        return (row_max, exp_total, target)

    peaks, totals, targets = lax.map(head_stats, (pred_blocks, row_blocks))
    peak_all, total_all, target_all = merged(
        (peaks.reshape(seq_len), totals.reshape(seq_len), targets.reshape(seq_len)),
        "vocab",
        merge_stats,
    )
    log_total = peak_all + jnp.log(total_all)
    lse_own = lax.dynamic_slice_in_dim(log_total, own_first, tokens)
    target_own = lax.dynamic_slice_in_dim(target_all, own_first, tokens)
    pred_error = predicted - clean_emb
    square_own = jnp.sum(mask_own[:, None] * pred_error * pred_error)
    cross_own = jnp.sum(mask_own * (lse_own - target_own))
    norm_own = jnp.sum(mask_own * jnp.sqrt(jnp.sum(clean_emb * clean_emb, -1) + 1e-06))
    count_all, square, cross_sum, norm_total = lax.psum(
        (jnp.sum(mask_own), square_own, cross_own, norm_own), ("dp", "vocab")
    )
    weight_blocks = (seq_mask / count_all).reshape(head_count, head_width)
    lse_blocks = log_total.reshape(head_count, head_width)

    def head_back(grad_table, block_data):
        pred_blk, rows_blk, lse_blk, weight_blk = block_data
        logits = matmul_nt(pred_blk, table_low)
        probabilities = jnp.exp(logits - lse_blk[:, None])
        onehot = (columns[None, :] == rows_blk[:, None]).astype(jnp.float32)
        grad_logits = ((probabilities - onehot) * weight_blk[:, None]).astype(jnp.bfloat16)
        return (grad_table + matmul_tn(grad_logits, pred_blk), matmul_nn(grad_logits, table_low))

    zero_table = jnp.zeros((vocab_rows, EMBED_WIDTH), jnp.float32)
    grad_table_head, grad_pred_blocks = lax.scan(
        head_back, zero_table, (pred_blocks, row_blocks, lse_blocks, weight_blocks)
    )
    grad_pred = lax.psum_scatter(
        grad_pred_blocks.reshape(seq_len, EMBED_WIDTH).astype(jnp.bfloat16),
        "vocab",
        scatter_dimension=0,
        tiled=True,
    ).astype(jnp.float32)
    error_grad = 2.0 * mask_own[:, None] * pred_error / count_all
    grad_pred_low = (grad_pred + error_grad).astype(jnp.bfloat16)
    grad_final_w = matmul_tn(grad_pred_low, final_norm)
    grad_final = matmul_nn(grad_pred_low, w_final)
    grad_hidden, grad_gain_final, grad_shift_final = norm_back(
        norm_final, inv_final, gain_final, grad_final
    )
    layer_grads = [None] * LAYERS
    vec_grads = [None] * LAYERS
    for layer_idx in reversed(range(LAYERS)):
        vec_layer = vec_params[layer_idx * vec_rows : (layer_idx + 1) * vec_rows]
        grad_hidden, layer_grads[layer_idx], vec_grads[layer_idx] = layer_backward(
            grad_hidden,
            kept_list[layer_idx],
            layer_weights(layer_idx),
            vec_layer,
            keep_keys,
            score_scale,
        )
    grad_hidden_low = grad_hidden.astype(jnp.bfloat16)
    grad_input_w = matmul_tn(inputs, grad_hidden_low)
    grad_inputs = matmul_nt(grad_hidden_low, w_input)
    grad_clean = jnp.sqrt(signal_level) * grad_inputs[:, :EMBED_WIDTH] - error_grad
    grad_clean_all = lax.all_gather(
        grad_clean.astype(jnp.bfloat16), "vocab", axis=0, tiled=True
    ).astype(grad_clean.dtype)
    grad_table_look = zero_table.at[safe_row].add(
        jnp.where(valid_row[:, None], grad_clean_all, 0.0)
    )
    grad_table_local = grad_table_head + grad_table_look
    canon_list = []
    layer_idx = 0
    canon_list = canon_list + layer_grads[layer_idx]
    canon_grad = jnp.concatenate(canon_list + [grad_input_w, grad_final_w], 0).T
    vec_grad = jnp.concatenate(vec_grads + [grad_gain_final, grad_shift_final])
    grad_cols, vec_part = (
        lax.psum_scatter(canon_grad, "vocab", scatter_dimension=0, tiled=True),
        lax.psum_scatter(vec_grad, "vocab", scatter_dimension=0, tiled=True),
    )
    emb_cols = emb_table.shape[1]
    summed_cols, summed_vec, summed_table = lax.psum((grad_cols, vec_part, grad_table_local), "dp")
    table_grad = lax.dynamic_slice_in_dim(summed_table, data_pos * emb_cols, emb_cols, 1)
    slot_grad = jnp.zeros_like(mat_slots)
    cursor = 0
    for mat_idx in range(len(row_counts)):
        piece_cols = summed_cols[:, cursor : cursor + row_counts[mat_idx]]
        updated = lax.dynamic_update_slice_in_dim(slot_grad, piece_cols, local_start[mat_idx], 1)
        slot_grad = jnp.where(owners[mat_idx] == data_pos, updated, slot_grad)
        cursor = cursor + row_counts[mat_idx]
    vec_share = vec_first.shape[0]
    own_vecs = lax.dynamic_slice_in_dim(vec_params, vocab_pos * vec_share, vec_share)
    new_slots, slot_first_new, slot_second_new = adamw(
        mat_slots, slot_grad, slot_first, slot_second
    )
    new_table, table_first_new, table_second_new = adamw(
        emb_table, table_grad, table_first_moment, table_second_moment
    )
    new_vecs, vec_first_new, vec_second_new = adamw(own_vecs, summed_vec, vec_first, vec_second)
    loss_pair = jnp.stack([square + cross_sum, count_all])
    emb_norm = norm_total / count_all
    return (
        loss_pair,
        emb_norm,
        new_table,
        table_first_new,
        table_second_new,
        new_slots,
        slot_first_new,
        slot_second_new,
        new_vecs,
        vec_first_new,
        vec_second_new,
    )


def solution(mesh):
    in_specs = (
        P("dp", None),
        P("dp"),
        P("dp", None),
        P("dp", "vocab", None),
        P(),
        P("vocab", "dp"),
        P("vocab", "dp"),
        P("vocab", "dp"),
        P("vocab", "dp"),
        P("vocab", "dp"),
        P("vocab", "dp"),
        P(),
        P("vocab"),
        P("vocab"),
    )
    out_specs = (
        P(),
        P(),
        P("vocab", "dp"),
        P("vocab", "dp"),
        P("vocab", "dp"),
        P("vocab", "dp"),
        P("vocab", "dp"),
        P("vocab", "dp"),
        P("vocab"),
        P("vocab"),
        P("vocab"),
    )
    fast = mesh.shape["dp"] == 8 and mesh.shape["vocab"] == 4
    body = per_device if fast else any_mesh_device
    return jax.shard_map(
        body, mesh=mesh, in_specs=in_specs, out_specs=out_specs, check_vma=False
    )
```
